32 devices in a mesh: dp: 4 (over z), seq: 2 (over y), tensor: 4 (over x, core).
Axes of the slice: x: 2, y: 2, z: 4, core: 2. Of those that a mesh axis runs over, the one named last changes fastest.
Arguments:
- block_input: float32 [8192, 768], P(('dp', 'seq', 'tensor')), may hold values from -6 to 6
- attn_in_weight: bfloat16 [3, 768, 768], P(None, ('dp', 'seq'), 'tensor'), may hold values from -0.21875 to 0.21875
- attn_out_weight: bfloat16 [768, 768], P('tensor', ('dp', 'seq')), may hold values from -3.5 to 3.5
- position_bias: float32 [32, 12], P(None, 'tensor'), may hold values from -6 to 6
- norm_gains: float32 [2, 768], replicated, may hold values from 0.1 to 1.9
- router_weight: bfloat16 [768, 8], replicated, may hold values from -0.15625 to 0.15625
- expert_in: bfloat16 [8, 768, 3072], P(('dp', 'seq'), None, 'tensor'), may hold values from -0.21875 to 0.21875
- expert_out: bfloat16 [8, 3072, 768], P(('dp', 'seq'), 'tensor'), may hold values from -10 to 10
- segment_ids: int32 [4, 2048], P('dp', ('seq', 'tensor')), may hold values from 0 to 2, as said below
- expert_ids: int32 [8192, 1], P(('dp', 'seq')), may hold values from 0 to 7; in each aligned block of 1024 rows (0 to 1023, 1024 to 2047, ...) at most 256 rows name the same one
- out_grad: float32 [8192, 768], P(('dp', 'seq', 'tensor')), may hold values from -6 to 6
Outputs:
- block_out: float32 [8192, 768], P(('dp', 'seq', 'tensor'))
- input_grad: float32 [8192, 768], P(('dp', 'seq', 'tensor'))
- grad_attn_in: float32 [3, 768, 768], P(None, ('dp', 'seq'), 'tensor')
- grad_attn_out: float32 [768, 768], P('tensor', ('dp', 'seq'))
- grad_bias: float32 [32, 12], P(None, 'tensor')
- grad_gains: float32 [2, 768], replicated
- grad_router: float32 [768, 8], replicated
- grad_expert_in: float32 [8, 768, 3072], P(('dp', 'seq'), None, 'tensor')
- grad_expert_out: float32 [8, 3072, 768], P(('dp', 'seq'), 'tensor')
The draws below stay inside these ranges and needn't reach their ends.
Inputs may be any that keep to these rules, and one draw needn't show every extreme that they name: `segment_ids`: along a sequence the ids never fall; every sequence holds documents 0, 1 and 2, each one run of positions. In some sequence document 1 begins within the first 1024 positions and ends within the last 1024. `expert_ids`: in each aligned block of 1024 rows no expert is named by more than 256 rows.
All inputs are finite; a program needn't handle non-finite values.
Results may differ from the reference program's by a relative error of at most 0.035.
Values may be sent and summed in bfloat16 or wider, within the bound.
No kernel may reach another device: no remote copies, remote signals or barrier semaphores. Data moves between devices by JAX's collectives and lax.ppermute only.
A program may use at most 448 MiB of HBM per device.

```python
import math
import jax
import jax.numpy as jnp
import numpy as np
from jax import lax

D = 768
H = 12
HD = 64
FF = 3072
BUCKETS = 32
SEQ_LEN = 2048
ROWS = 1024
TOKENS = 8192
EXPERTS = 8
CAP = 256
N_DP = 4


def draw_segment_ids(key, part):
    key = jax.random.fold_in(key, 11)
    pick_key, first_key, last_key, wide_first_key, wide_last_key = jax.random.split(key, 5)
    shortest = max(1, SEQ_LEN * 25 // 256)
    opening = jax.random.randint(first_key, (N_DP, 1), shortest, SEQ_LEN - 2 * shortest + 1)
    closing = jax.random.randint(last_key, (N_DP, 1), opening + shortest, SEQ_LEN - shortest + 1)
    wide_opening = jax.random.randint(wide_first_key, (N_DP, 1), shortest, ROWS)
    wide_closing = jax.random.randint(wide_last_key, (N_DP, 1), SEQ_LEN - ROWS + 1, SEQ_LEN - shortest + 1)
    spanned = jax.random.randint(pick_key, (), 0, N_DP)
    spanning = (jnp.arange(N_DP, dtype=jnp.int32) == spanned)[:, None]
    opening = jnp.where(spanning, wide_opening, opening)
    closing = jnp.where(spanning, wide_closing, closing)
    places = jnp.arange(SEQ_LEN, dtype=jnp.int32)[None, :]
    return (places >= opening).astype(jnp.int32) + (places >= closing).astype(jnp.int32)


def levels(rng, shape, pieces, least, largest):
    gain = 1.0
    for axis_at, shards_of in pieces:
        heights = jax.random.uniform(jax.random.fold_in(jax.random.fold_in(rng, 6), axis_at), (shards_of,), jnp.float32, least / len(pieces), largest / len(pieces))
        gain = gain * jnp.repeat(jnp.exp(heights), shape[axis_at] // shards_of).reshape((-1,) + (1,) * (len(shape) - 1 - axis_at))
    return gain


def shared_out(rng, own, number, rows, number_of, top, bound, slope):
    ranking = jax.random.permutation(rng, number_of)
    packed, ordinary = load_shares(number_of, rows * top, bound, slope, True), load_shares(number_of, rows * top, bound, slope, False)
    places = jnp.arange(number_of)

    def named(sizes, turn):
        used = int((sizes > 0).sum())
        fixed = max(1, used // 4)
        moved = fixed + (places - fixed + turn * (used - fixed)) % max(1, number_of - fixed)
        return jnp.zeros((number_of,), jnp.int32).at[ranking[jnp.where(places < fixed, places, moved)]].set(jnp.asarray(sizes, jnp.int32))

    sizes = jnp.where(number % 4 == 0, named(packed, number // 4), named(ordinary, number - number // 4 - 1))
    mixed = jax.random.permutation(jax.random.fold_in(own, 3), number_of)
    donor, sink = mixed[0:number_of // 2 * 2:2], mixed[1:number_of // 2 * 2:2]
    room = jnp.minimum(sizes[donor] - 1, bound - sizes[sink]) // 2
    room = jnp.where((donor == ranking[0]) | (sink == ranking[0]) | (sizes[sink] == 0), 0, jnp.maximum(room, 0))
    moved = jax.random.randint(jax.random.fold_in(own, 4), (number_of // 2,), 0, 1 << 20) % (room + 1)
    sizes = sizes.at[donor].add(-moved).at[sink].add(moved)
    members = jnp.searchsorted(jnp.cumsum(sizes), jnp.arange(rows * top), side="right").astype(jnp.int32)
    table = members.reshape(top, rows).T
    table = table[jax.random.permutation(jax.random.fold_in(own, 1), rows)]
    turn = jax.random.randint(jax.random.fold_in(own, 2), (rows, 1), 0, top)
    return jnp.take_along_axis(table, (jnp.arange(top)[None, :] + turn) % top, axis=1)


def load_shares(amount, total, bound, slope, full):
    portions = [(1 << 20) // math.isqrt(rank ** slope) + 1 for rank in range(1, amount + 1)]
    largest = bound if full else min(bound, max(-(-total // amount), total * portions[0] // sum(portions)))
    least = 1 if total - largest >= amount - 1 else 0
    holding, spare = [largest] + [least] * (amount - 1), total - largest - least * (amount - 1)
    while spare > 0:
        candidates = [i for i in range(1, amount) if holding[i] < largest] or [i for i in range(1, amount) if holding[i] < bound]
        mass, left = sum([portions[i] for i in candidates]), spare
        for i in candidates:
            more = min(bound - holding[i], max(1, left * portions[i] // mass), spare)
            holding[i] = holding[i] + more
            spare = spare - more
    return np.array(holding)


def normal_values(rng, shape, scale, limit, pieces=(), kind=jnp.bfloat16):
    values = jax.random.normal(rng, shape, jnp.float32) * scale
    if len(pieces) > 0:
        values = levels(rng, shape, pieces, -0.22, 0.18) * values
    return jnp.clip(values, min=-limit, max=limit).astype(kind)


def setup_inputs(seed: int = 0) -> dict:
    keys = jax.random.split(jax.random.key(seed), 12)
    block_input = normal_values(keys[0], (TOKENS, D), 1.0, 6.0, ((0, 32),), jnp.float32)
    attn_in_weight = normal_values(keys[1], (3, D, D), D ** -0.5, 0.21875, ((1, 8), (2, 4)))
    attn_out_weight = normal_values(keys[2], (D, D), 0.6, 3.5, ((0, 4), (1, 8)))
    position_bias = normal_values(keys[3], (BUCKETS, H), 1.0, 6.0, ((1, 4),), jnp.float32)
    norm_gains = jnp.clip(1.0 + 0.18 * jax.random.normal(keys[4], (2, D), jnp.float32), 0.1, 1.9)
    router_weight = normal_values(keys[5], (D, EXPERTS), (2 * D) ** -0.5, 0.15625)
    expert_in = normal_values(keys[6], (EXPERTS, D, FF), D ** -0.5, 0.21875, ((0, 8), (2, 4)))
    expert_out = normal_values(keys[7], (EXPERTS, FF, D), 1.8, 10.0, ((0, 8), (1, 4)))
    segment_ids = draw_segment_ids(jax.random.fold_in(keys[11], 71), 0)
    expert_ids_keys = jax.random.split(jax.random.fold_in(keys[9], 1), TOKENS // ROWS)
    expert_ids_turns = jax.random.permutation(jax.random.fold_in(keys[9], 3), TOKENS // ROWS)
    expert_ids = jax.vmap(lambda own, number: shared_out(jax.random.fold_in(keys[9], 2), own, number, ROWS, EXPERTS, 1, CAP, 1))(expert_ids_keys, expert_ids_turns).reshape((TOKENS, 1))
    out_grad = normal_values(keys[10], (TOKENS, D), 1.0, 6.0, ((0, 32),), jnp.float32)
    return dict(block_input=block_input, attn_in_weight=attn_in_weight, attn_out_weight=attn_out_weight, position_bias=position_bias, norm_gains=norm_gains, router_weight=router_weight, expert_in=expert_in, expert_out=expert_out, segment_ids=segment_ids, expert_ids=expert_ids, out_grad=out_grad)


EPSILON = 1e-06
EDGES = (1, 2, 3, 4, 5, 6, 7, 8, 12, 16, 23, 32, 46, 64, 91)
HIGHEST = lax.Precision.HIGHEST

@jax.custom_vjp
def low(v):
    return lax.optimization_barrier(v.astype(jnp.bfloat16)).astype(jnp.float32)

@jax.custom_vjp
def low_back(v):
    return v

def low_keep(v):
    return (low(v), None)

def low_pass(kept, grad):
    return (grad,)

def back_keep(v):
    return (v, None)

def back_low(kept, grad):
    return (low(grad),)
low.defvjp(low_keep, low_pass)
low_back.defvjp(back_keep, back_low)

def matmul(left_side, right_side):
    return jnp.dot(left_side, right_side, precision=HIGHEST)

def normalize(values, gain_row):
    return values * lax.rsqrt(lax.optimization_barrier(jnp.mean(values * values, axis=-1, keepdims=True)) + EPSILON) * gain_row

def bucket_of(relative):
    magnitude = jnp.abs(relative)
    counted = jnp.zeros(relative.shape, jnp.int32)
    for edge_value in EDGES:
        counted = counted + (magnitude >= edge_value).astype(jnp.int32)
    return counted + jnp.where(relative > 0, BUCKETS // 2, 0).astype(jnp.int32)

def attend_sequence(normed, segment, w_first, w_second, bias_table):
    projected = [low_back(low(matmul(normed, w_first[which]))) for which in range(3)]
    queries = projected[0].reshape(SEQ_LEN, H, HD)
    keys_all = projected[1].reshape(SEQ_LEN, H, HD)
    values_all = projected[2].reshape(SEQ_LEN, H, HD)
    q_block = min(512, SEQ_LEN)
    key_pos = jnp.arange(SEQ_LEN, dtype=jnp.int32)

    def one_block(start):
        query_part = lax.dynamic_slice_in_dim(queries, start, q_block, 0)
        query_seg = lax.dynamic_slice_in_dim(segment, start, q_block, 0)
        query_pos = start + jnp.arange(q_block, dtype=jnp.int32)
        looked = bias_table[bucket_of(key_pos[None, :] - query_pos[:, None])]
        scores = jnp.einsum('qhd,khd->hqk', query_part, keys_all, precision=HIGHEST) * 0.125 + jnp.transpose(looked, (2, 0, 1))
        scores = low_back(scores)
        allowed = query_seg[:, None] == segment[None, :]
        scores = jnp.where(allowed[None, :, :], scores, -1000000000.0)
        attn_probs = jax.nn.softmax(scores, axis=-1)
        return jnp.einsum('hqk,khd->qhd', low(attn_probs), values_all, precision=HIGHEST)
    starts = jnp.arange(SEQ_LEN // q_block, dtype=jnp.int32) * q_block
    blocks = lax.map(jax.checkpoint(one_block), starts)
    attended = low_back(low(blocks.reshape(SEQ_LEN, D)))
    return matmul(attended, w_second)

def forward(block_input, w_first, w_second, bias_table, gains, router, exp_first, exp_second, segment_ids, expert_ids):
    sequences = block_input.reshape(N_DP, SEQ_LEN, D)
    normed_one = low(normalize(sequences, gains[0]))
    attn_rows = lax.map(lambda pair_item: attend_sequence(pair_item[0], pair_item[1], w_first, w_second, bias_table), (normed_one, segment_ids))
    state_rows = block_input + low_back(attn_rows.reshape(TOKENS, D))
    normed_two = low(normalize(state_rows, gains[1]))
    router_probs = jax.nn.softmax(matmul(normed_two, router), axis=-1)
    chosen = expert_ids[:, 0]
    onehot = chosen[:, None] == jnp.arange(EXPERTS, dtype=jnp.int32)[None, :]
    gate_value = lax.optimization_barrier(jnp.sum(jnp.where(onehot, router_probs, 0.0), axis=-1, keepdims=True))
    blocks = TOKENS // ROWS
    grouped = onehot.astype(jnp.int32).reshape(blocks, ROWS, EXPERTS)
    slot_rank = lax.optimization_barrier(jnp.sum(jnp.cumsum(grouped, axis=1, dtype=jnp.int32) * grouped, axis=-1, dtype=jnp.int32)) - 1
    block_id = jnp.arange(blocks, dtype=jnp.int32)[:, None]
    target = (chosen.reshape(blocks, ROWS) * (blocks * CAP) + block_id * CAP + slot_rank).reshape(TOKENS).astype(jnp.int32)
    buffer = jnp.zeros((EXPERTS * blocks * CAP, D), jnp.float32).at[target].set(normed_two)
    buffer = buffer.reshape(EXPERTS, blocks * CAP, D)

    def one_expert(expert_item):
        inputs, weight_first, weight_second = expert_item
        pre_act = low_back(matmul(inputs, weight_first))
        activated = low(jax.nn.gelu(pre_act))
        return low_back(matmul(activated, weight_second))
    results = lax.map(jax.checkpoint(one_expert), (buffer, exp_first, exp_second))
    expert_rows = results.reshape(EXPERTS * blocks * CAP, D)[target]
    return state_rows + gate_value * expert_rows

def reference(block_input, attn_in_weight, attn_out_weight, position_bias, norm_gains, router_weight, expert_in, expert_out, segment_ids, expert_ids, out_grad):

    def closed(value_in, w_first, w_second, bias_table, gains, router, exp_first, exp_second):
        return forward(value_in, w_first, w_second, bias_table, gains, router, exp_first, exp_second, segment_ids, expert_ids)
    block_out, pullback = jax.vjp(closed, block_input, attn_in_weight.astype(jnp.float32), attn_out_weight.astype(jnp.float32), position_bias, norm_gains, router_weight.astype(jnp.float32), expert_in.astype(jnp.float32), expert_out.astype(jnp.float32))
    grads = pullback(out_grad)
    return (block_out, grads[0], grads[1], grads[2], grads[3], grads[4], grads[5], grads[6], grads[7])
```

```python
import functools
import math

import jax
import jax.numpy as jnp
from jax import lax
from jax.experimental import pallas as pl
from jax.experimental.pallas import tpu as pltpu
from jax.sharding import PartitionSpec as P

EPSILON = 1e-06
EDGES = (1, 2, 3, 4, 5, 6, 7, 8, 12, 16, 23, 32, 46, 64, 91)
TILE = 256
HALF = TILE // 2
LOG2E = math.log2(math.e)
SCALE = 0.125
MASKED = -1e30
LOWEST = -1e29
VMEM_BYTES = 48 * 1024 * 1024
GELU_A = math.sqrt(2.0 / math.pi)
GELU_B = 0.044715
BF16 = jnp.bfloat16
F32 = jnp.float32


def dot(left_side, right_side):
    return jnp.dot(left_side, right_side, preferred_element_type=F32)


def dot_rows(left_side, right_side):
    return lax.dot_general(
        left_side, right_side, (((1,), (1,)), ((), ())), preferred_element_type=F32
    )


def einsum(formula, *operands):
    return jnp.einsum(formula, *operands, preferred_element_type=F32)


def swap(values, axis, bit):
    count = lax.axis_size(axis)
    return lax.ppermute(values, axis, [(i, i ^ bit) for i in range(count)])


def bits_of(count):
    return [1 << i for i in range(count.bit_length() - 1)]


def gather_relative(values, axis):
    pieces = {0: values}
    for bit in reversed(bits_of(lax.axis_size(axis))):
        for place in list(pieces):
            pieces[place ^ bit] = swap(pieces[place], axis, bit)
    return [pieces[place] for place in range(len(pieces))]


def sum_relative(blocks, axis):
    blocks = dict(enumerate(blocks))
    for bit in bits_of(lax.axis_size(axis)):
        for place in [k for k in blocks if k & bit]:
            sent = swap(blocks.pop(place).astype(BF16), axis, bit)
            blocks[place ^ bit] = blocks[place ^ bit].astype(F32) + sent.astype(F32)
    return blocks[0]


def reorder(pieces, own_index):
    for bit in bits_of(len(pieces)):
        flip = (own_index & bit) != 0
        pieces = [
            jnp.where(flip, pieces[place ^ bit], pieces[place]) for place in range(len(pieces))
        ]
    return pieces


def gather_grid(values):
    dp_count, seq_count = lax.axis_size("dp"), lax.axis_size("seq")
    if dp_count > 4 or seq_count > 2:
        return lax.all_gather(values, ("dp", "seq"), axis=0, tiled=False)
    columns = [values] + [swap(values, "dp", place) for place in range(1, dp_count)]
    pieces = []
    for column in columns:
        pieces.append(column)
        if seq_count == 2:
            pieces.append(swap(column, "seq", 1))
    own = lax.axis_index("dp") * seq_count + lax.axis_index("seq")
    return jnp.stack(reorder(pieces, own))


def scatter_grid(blocks):
    dp_count, seq_count = lax.axis_size("dp"), lax.axis_size("seq")
    if dp_count > 4 or seq_count > 2:
        return lax.psum_scatter(
            blocks.astype(BF16), ("dp", "seq"), scatter_dimension=0, tiled=False
        ).astype(F32)
    own = lax.axis_index("dp") * seq_count + lax.axis_index("seq")
    parts = reorder([blocks[place] for place in range(dp_count * seq_count)], own)
    if seq_count == 2:
        sent = swap(jnp.stack(parts[1::2]).astype(BF16), "seq", 1)
        parts = [parts[2 * place] + sent[place].astype(F32) for place in range(dp_count)]
    total = parts[0]
    for place in range(1, dp_count):
        total = total + swap(parts[place].astype(BF16), "dp", place).astype(F32)
    return total


def sum_all(values, axes):
    for axis in axes:
        for bit in bits_of(lax.axis_size(axis)):
            values = values + swap(values, axis, bit)
    return values


def bucket_of(relative, half_count):
    magnitude = jnp.abs(relative)
    counted = jnp.zeros(relative.shape, jnp.int32)
    for edge_value in EDGES:
        counted = counted + (magnitude >= edge_value).astype(jnp.int32)
    return counted + jnp.where(relative > 0, half_count, 0).astype(jnp.int32)


def near_buckets(half_count):
    shape = (3, HALF, HALF)
    relative = (
        (lax.broadcasted_iota(jnp.int32, shape, 0) - 1) * HALF
        + lax.broadcasted_iota(jnp.int32, shape, 1)
        - lax.broadcasted_iota(jnp.int32, shape, 2)
    )
    return bucket_of(relative, half_count)


def bias_tiles(position_bias):
    bucket_count, heads = position_bias.shape
    half_count = bucket_count // 2
    grid = near_buckets(half_count)
    near = jnp.zeros((heads, 3, HALF, HALF), F32)
    for bucket_index in range(bucket_count):
        near = near + jnp.where(
            (grid == bucket_index)[None], position_bias[bucket_index][:, None, None, None], 0.0
        )
    before, same, after = near[:, 0], near[:, 1], near[:, 2]
    far_before = jnp.broadcast_to(
        position_bias[half_count - 1][:, None, None], (heads, HALF, HALF)
    )
    far_after = jnp.broadcast_to(
        position_bias[bucket_count - 1][:, None, None], (heads, HALF, HALF)
    )

    def square(a, b, c, d):
        return jnp.concatenate(
            [jnp.concatenate([a, b], axis=2), jnp.concatenate([c, d], axis=2)], axis=1
        )

    tiles = jnp.stack(
        [
            square(far_before, far_before, far_before, far_before),
            square(far_before, far_before, before, far_before),
            square(same, before, after, same),
            square(far_after, after, far_after, far_after),
            square(far_after, far_after, far_after, far_after),
        ]
    )
    return tiles * LOG2E


def bias_sums(tiles, bucket_count):
    half_count = bucket_count // 2
    first, last = slice(0, HALF), slice(HALF, TILE)
    same = tiles[2][:, first, first] + tiles[2][:, last, last]
    before = tiles[2][:, first, last] + tiles[1][:, last, first]
    after = tiles[2][:, last, first] + tiles[3][:, first, last]
    near = jnp.stack([before, same, after], axis=1)
    grid = near_buckets(half_count)
    rows = [
        jnp.sum(jnp.where((grid == bucket_index)[None], near, 0.0), axis=(1, 2, 3))
        for bucket_index in range(bucket_count)
    ]
    rows[half_count - 1] = (
        rows[half_count - 1]
        + jnp.sum(tiles[0], axis=(1, 2))
        + jnp.sum(tiles[1][:, first, :], axis=(1, 2))
        + jnp.sum(tiles[1][:, last, last], axis=(1, 2))
    )
    rows[bucket_count - 1] = (
        rows[bucket_count - 1]
        + jnp.sum(tiles[4], axis=(1, 2))
        + jnp.sum(tiles[3][:, last, :], axis=(1, 2))
        + jnp.sum(tiles[3][:, first, first], axis=(1, 2))
    )
    return jnp.stack(rows)


def span_of(meta_ref, query_tile, key_tiles):
    opening, closing = meta_ref[1], meta_ref[2]
    first = query_tile * TILE
    last = first + TILE - 1
    begin = jnp.where(first < opening, 0, jnp.where(first < closing, opening, closing))
    end = jnp.where(last < opening, opening, jnp.where(last < closing, closing, key_tiles * TILE))
    return begin // TILE, (end + TILE - 1) // TILE


def document_of(meta_ref, tile, dimension):
    place = tile * TILE + lax.broadcasted_iota(jnp.int32, (TILE, TILE), dimension)
    return (place >= meta_ref[1]).astype(jnp.int32) + (place >= meta_ref[2]).astype(jnp.int32)


def attend_kernel(meta_ref, q_ref, kv_ref, bias_ref, exact_ref, out_ref, log_ref, key_ref, sum_ref):
    key_tiles = kv_ref.shape[0]
    heads = bias_ref.shape[1]
    size = q_ref.shape[1] // heads

    def turn(tile, carry):
        for h in range(heads):
            key_ref[tile, h] = kv_ref[tile, h * size : (h + 1) * size, :].T
        return carry

    lax.fori_loop(0, key_tiles, turn, 0)

    def query_body(i, carry):
        tile = meta_ref[0] + i
        begin, end = span_of(meta_ref, tile, key_tiles)
        own_document = document_of(meta_ref, tile, 1)
        sum_ref[...] = jnp.zeros_like(sum_ref)

        def key_body(j, stats):
            allowed = document_of(meta_ref, j, 0) == own_document
            kind = jnp.clip(j - tile, -2, 2) + 2
            stats = list(stats)
            for h in range(heads):
                peak, total = stats[2 * h], stats[2 * h + 1]
                rows = slice(h * size, (h + 1) * size)
                scores = dot(key_ref[j, h], q_ref[i, rows, :]) * LOG2E + bias_ref[kind, h]
                scores = jnp.where(allowed, scores, MASKED)
                new_peak = jnp.maximum(peak, jnp.max(scores, axis=0, keepdims=True))
                kept = jnp.exp2(peak - new_peak)
                weights = jnp.exp2(scores - new_peak)
                stats[2 * h] = new_peak
                stats[2 * h + 1] = total * kept + jnp.sum(weights, axis=0, keepdims=True)
                values = kv_ref[j, (heads + h) * size : (heads + h + 1) * size, :]
                sum_ref[rows, :] = sum_ref[rows, :] * kept + dot(values, weights.astype(BF16))
            return tuple(stats)

        start = []
        for h in range(heads):
            start += [jnp.full((1, TILE), LOWEST, F32), jnp.zeros((1, TILE), F32)]
        stats = lax.fori_loop(begin, end, key_body, tuple(start))
        for h in range(heads):
            rows = slice(h * size, (h + 1) * size)
            result = sum_ref[rows, :] * (1.0 / stats[2 * h + 1])
            exact_ref[i, rows, :] = result
            out_ref[i, rows, :] = result.astype(BF16)
            log_ref[i, h] = stats[2 * h] + jnp.log2(stats[2 * h + 1])
        return carry

    lax.fori_loop(0, q_ref.shape[0], query_body, 0)


def whole_specs(count):
    return [pl.BlockSpec(memory_space=pltpu.VMEM)] * count


def attend(meta, queries, keys_values, bias):
    query_tiles, width, _ = queries.shape
    key_tiles = keys_values.shape[0]
    heads = bias.shape[1]
    return pl.pallas_call(
        attend_kernel,
        out_shape=(
            jax.ShapeDtypeStruct(queries.shape, F32),
            jax.ShapeDtypeStruct(queries.shape, BF16),
            jax.ShapeDtypeStruct((query_tiles, heads, 1, TILE), F32),
        ),
        in_specs=[pl.BlockSpec(memory_space=pltpu.SMEM)] + whole_specs(3),
        out_specs=tuple(whole_specs(3)),
        scratch_shapes=[
            pltpu.VMEM((key_tiles, heads, TILE, width // heads), BF16),
            pltpu.VMEM((width, TILE), F32),
        ],
        compiler_params=pltpu.CompilerParams(vmem_limit_bytes=VMEM_BYTES),
        name="attend",
    )(meta, queries, keys_values, bias)


def attend_back_kernel(
    meta_ref,
    q_ref,
    kv_ref,
    bias_ref,
    grad_ref,
    exact_ref,
    log_ref,
    dq_ref,
    dkv_ref,
    tiles_ref,
    key_ref,
    value_ref,
    dq_sum,
    dkv_sum,
):
    key_tiles = kv_ref.shape[0]
    heads = bias_ref.shape[1]
    size = q_ref.shape[1] // heads

    def turn(tile, carry):
        for h in range(heads):
            key_ref[tile, h] = kv_ref[tile, h * size : (h + 1) * size, :].T
            value_ref[tile, h] = kv_ref[tile, (heads + h) * size : (heads + h + 1) * size, :].T
        return carry

    lax.fori_loop(0, key_tiles, turn, 0)
    dkv_sum[...] = jnp.zeros_like(dkv_sum)
    tiles_ref[...] = jnp.zeros_like(tiles_ref)

    def query_body(i, carry):
        tile = meta_ref[0] + i
        begin, end = span_of(meta_ref, tile, key_tiles)
        own_document = document_of(meta_ref, tile, 1)
        dq_sum[...] = jnp.zeros_like(dq_sum)
        centres = []
        for h in range(heads):
            rows = slice(h * size, (h + 1) * size)
            centres.append(
                jnp.sum(grad_ref[i, rows, :].astype(F32) * exact_ref[i, rows, :], axis=0, keepdims=True)
            )

        def key_body(j, inner):
            allowed = document_of(meta_ref, j, 0) == own_document
            kind = jnp.clip(j - tile, -2, 2) + 2
            for h in range(heads):
                rows = slice(h * size, (h + 1) * size)
                value_rows = slice((heads + h) * size, (heads + h + 1) * size)
                query = q_ref[i, rows, :]
                grad = grad_ref[i, rows, :]
                scores = dot(key_ref[j, h], query) * LOG2E + bias_ref[kind, h]
                probs = jnp.where(allowed, jnp.exp2(scores - log_ref[i, h]), 0.0)
                prob_grad = dot(value_ref[j, h], grad)
                score_grad = probs * (prob_grad - centres[h])
                tiles_ref[kind, h] += score_grad
                low_grad = score_grad.astype(BF16)
                dkv_sum[j, rows, :] += dot_rows(query, low_grad)
                dkv_sum[j, value_rows, :] += dot_rows(grad, probs.astype(BF16))
                dq_sum[rows, :] += dot(kv_ref[j, rows, :], low_grad)
            return inner

        lax.fori_loop(begin, end, key_body, 0)
        dq_ref[i] = (dq_sum[...] * SCALE).astype(BF16)
        return carry

    lax.fori_loop(0, q_ref.shape[0], query_body, 0)
    dkv_ref[...] = dkv_sum[...].astype(BF16)


def attend_back(meta, queries, keys_values, bias, grad, exact, logs):
    key_tiles = keys_values.shape[0]
    heads = bias.shape[1]
    size = queries.shape[1] // heads
    return pl.pallas_call(
        attend_back_kernel,
        out_shape=(
            jax.ShapeDtypeStruct(queries.shape, BF16),
            jax.ShapeDtypeStruct(keys_values.shape, BF16),
            jax.ShapeDtypeStruct(bias.shape, F32),
        ),
        in_specs=[pl.BlockSpec(memory_space=pltpu.SMEM)] + whole_specs(6),
        out_specs=tuple(whole_specs(3)),
        scratch_shapes=[
            pltpu.VMEM((key_tiles, heads, TILE, size), BF16),
            pltpu.VMEM((key_tiles, heads, TILE, size), BF16),
            pltpu.VMEM(queries.shape[1:], F32),
            pltpu.VMEM(keys_values.shape, F32),
        ],
        compiler_params=pltpu.CompilerParams(vmem_limit_bytes=VMEM_BYTES),
        name="attend_back",
    )(meta, queries, keys_values, bias, grad, exact, logs)


def split_low(values):
    high = values.astype(BF16)
    return high, (values - high.astype(F32)).astype(BF16)


def expert_kernel(
    parts,
    own_ref,
    *refs,
):
    state_refs, grad_refs = refs[:parts], refs[parts : 2 * parts]
    (in_ref, in_t_ref, out_ref, out_t_ref, router_ref, router_t_ref, gain_ref) = refs[
        2 * parts : 2 * parts + 7
    ]
    (
        back_ref,
        result_ref,
        normed_ref,
        scaled_ref,
        act_ref,
        pre_ref,
        gain_sum,
        router_sum,
    ) = refs[2 * parts + 7 :]

    @pl.when(pl.program_id(0) == 0)
    def _():
        gain_sum[...] = jnp.zeros_like(gain_sum)
        router_sum[...] = jnp.zeros_like(router_sum)

    width = gain_ref.shape[0]
    state = jnp.concatenate([ref[0] for ref in state_refs], axis=0).astype(F32)
    root = lax.rsqrt(jnp.sum(state * state, axis=0, keepdims=True) * (1.0 / width) + EPSILON)
    gain = gain_ref[...]
    normed = (state * root * gain).astype(BF16)
    normed_ref[0] = normed
    logits = dot(router_t_ref[...], normed)
    raised = jnp.exp(logits - jnp.max(logits, axis=0, keepdims=True))
    router_probs = raised / jnp.sum(raised, axis=0, keepdims=True)
    chosen = lax.broadcasted_iota(jnp.int32, logits.shape, 0) == own_ref[0]
    gate = jnp.sum(jnp.where(chosen, router_probs, 0.0), axis=0, keepdims=True)
    grad = jnp.concatenate([ref[0] for ref in grad_refs], axis=0)
    scaled_ref[0] = (grad.astype(F32) * gate).astype(BF16)
    pre_act = dot(in_t_ref[...], normed)
    square = pre_act * pre_act
    bent = jnp.tanh(GELU_A * pre_act * (1.0 + GELU_B * square))
    cdf = 0.5 + 0.5 * bent
    activated = (pre_act * cdf).astype(BF16)
    act_ref[0] = activated
    slope = cdf + (0.5 * GELU_A) * pre_act * (1.0 - bent * bent) * (1.0 + (3.0 * GELU_B) * square)
    act_grad = dot(out_ref[...], grad)
    pre_grad = (act_grad * gate * slope).astype(BF16)
    pre_ref[0] = pre_grad
    gate_grad = jnp.sum(activated.astype(F32) * act_grad, axis=0, keepdims=True)
    logit_grad = gate_grad * gate * (chosen.astype(F32) - router_probs)
    high, low = split_low(logit_grad)
    router = router_ref[...]
    normed_grad = dot(in_ref[...], pre_grad) + dot(router, high) + dot(router, low)
    router_sum[...] += dot_rows(high, normed) + dot_rows(low, normed)
    plain = normed.astype(F32)
    product = normed_grad * plain
    gain_sum[...] += product
    centre = jnp.sum(product, axis=0, keepdims=True) * (1.0 / width)
    back = root * (normed_grad * gain - plain * (centre * (1.0 / gain)))
    share = width // parts
    result = dot(out_t_ref[...], activated) * gate
    for k in range(parts):
        rows = slice(k * share, (k + 1) * share)
        back_ref[k, 0] = back[rows].astype(BF16)
        result_ref[k, 0] = result[rows].astype(BF16)


def run_expert(own, states, grads, weights):
    parts = len(states)
    count, share, slots = states[0].shape
    width = share * parts
    hidden = weights[0].shape[1]
    experts = weights[4].shape[1]

    def fixed(shape):
        return pl.BlockSpec(shape, lambda g: (0,) * len(shape))

    piece = pl.BlockSpec((1, share, slots), lambda g: (g, 0, 0))
    split = pl.BlockSpec((parts, 1, share, slots), lambda g: (0, g, 0, 0))
    wide = pl.BlockSpec((1, width, slots), lambda g: (g, 0, 0))
    deep = pl.BlockSpec((1, hidden, slots), lambda g: (g, 0, 0))
    return pl.pallas_call(
        functools.partial(expert_kernel, parts),
        grid=(count,),
        out_shape=(
            jax.ShapeDtypeStruct((parts, count, share, slots), BF16),
            jax.ShapeDtypeStruct((parts, count, share, slots), BF16),
            jax.ShapeDtypeStruct((count, width, slots), BF16),
            jax.ShapeDtypeStruct((count, width, slots), BF16),
            jax.ShapeDtypeStruct((count, hidden, slots), BF16),
            jax.ShapeDtypeStruct((count, hidden, slots), BF16),
            jax.ShapeDtypeStruct((width, slots), F32),
            jax.ShapeDtypeStruct((experts, width), F32),
        ),
        in_specs=[pl.BlockSpec(memory_space=pltpu.SMEM)]
        + [piece] * (2 * parts)
        + [fixed(weight.shape) for weight in weights],
        out_specs=(
            split,
            split,
            wide,
            wide,
            deep,
            deep,
            fixed((width, slots)),
            fixed((experts, width)),
        ),
        compiler_params=pltpu.CompilerParams(vmem_limit_bytes=VMEM_BYTES),
        name="expert",
    )(own, *states, *grads, *weights)


def norm_back(values, gain_row, grad):
    root = lax.rsqrt(jnp.mean(values * values, axis=-1, keepdims=True) + EPSILON)
    scaled = grad * gain_row
    return root * scaled - values * root**3 * jnp.mean(scaled * values, axis=-1, keepdims=True)


def shards(
    block_input,
    attn_in_weight,
    attn_out_weight,
    position_bias,
    norm_gains,
    router_weight,
    expert_in,
    expert_out,
    segment_ids,
    expert_ids,
    out_grad,
):
    tensor_count, seq_count = lax.axis_size("tensor"), lax.axis_size("seq")
    tensor_place, seq_place = lax.axis_index("tensor"), lax.axis_index("seq")
    grid_place = lax.axis_index("dp") * seq_count + seq_place
    local_count, width = block_input.shape
    group_count = local_count * tensor_count
    share = width // tensor_count
    bucket_count, heads = position_bias.shape
    head_cols = attn_in_weight.shape[2]
    experts = router_weight.shape[1]
    capacity = max(2, 2 * group_count // experts)
    tiles = group_count // TILE

    def relative(values, axis=0):
        shape = values.shape
        blocks = values.reshape(
            shape[:axis] + (tensor_count, shape[axis] // tensor_count) + shape[axis + 1 :]
        )
        return [
            lax.dynamic_index_in_dim(blocks, tensor_place ^ k, axis, keepdims=False)
            for k in range(tensor_count)
        ]

    group_input = jnp.concatenate(
        reorder(gather_relative(block_input.astype(BF16), "tensor"), tensor_place)
    )
    in_full = gather_grid(jnp.transpose(attn_in_weight, (1, 0, 2)))
    in_full = in_full.reshape(width, 3, head_cols)
    counts = jnp.stack([jnp.sum(segment_ids < 1), jnp.sum(segment_ids < 2)]).astype(jnp.int32)
    bounds = sum_all(counts, ("tensor", "seq"))
    meta = jnp.concatenate([(seq_place * tiles).astype(jnp.int32)[None], bounds])
    bias = bias_tiles(position_bias)

    wide_input = group_input.astype(F32)
    root_one = lax.rsqrt(jnp.mean(wide_input * wide_input, axis=-1, keepdims=True) + EPSILON)
    normed_one = (wide_input * root_one * norm_gains[0]).astype(BF16)
    normed_tiles = normed_one.reshape(tiles, TILE, width)
    projected = einsum("nrd,dkc->nkcr", normed_tiles, in_full)
    keys_values = (
        projected[:, 1:].astype(BF16).reshape(tiles, 2 * head_cols, TILE)
    )
    queries = (projected[:, 0] * SCALE).astype(BF16)
    if seq_count == 2:
        other = swap(keys_values, "seq", 1)
        keys_values_all = jnp.concatenate(reorder([keys_values, other], seq_place))
    else:
        keys_values_all = lax.all_gather(keys_values, "seq", axis=0, tiled=True)

    route_all = expert_ids[:, 0]
    expert_range = jnp.arange(experts, dtype=jnp.int32)
    route_hot = (route_all[:, None] == expert_range[None, :]).astype(jnp.int32)
    slot_rank = jnp.sum(jnp.cumsum(route_hot, axis=0) * route_hot, axis=-1) - 1
    target = route_all * capacity + slot_rank
    places = jnp.arange(experts * capacity, dtype=jnp.int32).reshape(experts, 1, capacity)
    onehot = (target[None, :, None] == places).astype(BF16)
    merged = max(1, TILE // capacity)

    def to_experts(features):
        buffer = einsum("dr,ers->eds", features, onehot).astype(BF16)
        arrived = lax.all_to_all(
            buffer, ("dp", "seq"), split_axis=0, concat_axis=0, tiled=True
        )
        if merged > 1:
            arrived = arrived.reshape(-1, merged, share, capacity)
            arrived = jnp.transpose(arrived, (0, 2, 1, 3)).reshape(-1, share, merged * capacity)
        return arrived

    def from_experts(blocks):
        total = sum_relative([blocks[k] for k in range(tensor_count)], "tensor").astype(BF16)
        if merged > 1:
            total = total.reshape(-1, share, merged, capacity)
            total = jnp.transpose(total, (0, 2, 1, 3)).reshape(-1, share, capacity)
        returned = lax.all_to_all(
            total, ("dp", "seq"), split_axis=0, concat_axis=0, tiled=True
        )
        return einsum("eds,ers->dr", returned, onehot)

    grad_rows, keys_values_all = lax.optimization_barrier(
        (out_grad.astype(BF16), keys_values_all)
    )
    grad_share = lax.all_to_all(grad_rows, "tensor", split_axis=1, concat_axis=0, tiled=True)
    grad_features = jnp.transpose(grad_share)
    grad_arrived = to_experts(grad_features)

    exact, attended, logs = attend(meta, queries, keys_values_all, bias)

    out_full = gather_grid(jnp.transpose(attn_out_weight)).reshape(width, head_cols)
    out_blocks = jnp.stack(relative(out_full))
    input_share = jnp.transpose(
        lax.dynamic_slice_in_dim(group_input, tensor_place * share, share, 1)
    ).astype(F32)
    attn_blocks = einsum("kec,ncq->kenq", out_blocks, attended)
    attn_blocks = attn_blocks.reshape(tensor_count, share, group_count)
    attn_share = sum_relative([attn_blocks[k] for k in range(tensor_count)], "tensor")
    state_share = (input_share + attn_share).astype(BF16)
    state_share, grad_arrived = lax.optimization_barrier((state_share, grad_arrived))
    grad_pieces = gather_relative(grad_arrived, "tensor")
    state_pieces = gather_relative(to_experts(state_share), "tensor")

    in_blocks = jnp.concatenate(relative(expert_in[0]))
    out_cols = jnp.concatenate(relative(expert_out[0], 1), axis=1)
    router_blocks = jnp.concatenate(relative(router_weight))
    gain_two = jnp.concatenate(relative(norm_gains[1]))[:, None]
    back, result, normed_two, scaled_grad, activated, pre_grad, gain_sum, router_sum = run_expert(
        grid_place.astype(jnp.int32)[None],
        state_pieces,
        grad_pieces,
        (
            in_blocks,
            jnp.transpose(in_blocks),
            out_cols,
            jnp.transpose(out_cols),
            router_blocks,
            jnp.transpose(router_blocks),
            gain_two,
        ),
    )
    state_grad = (grad_features.astype(F32) + from_experts(back)).astype(BF16)
    branch = gather_relative(state_grad, "tensor")
    branch_tiles = jnp.stack(branch).reshape(tensor_count, share, tiles, TILE)
    attended_grad = einsum("kec,kenq->ncq", out_blocks, branch_tiles).astype(BF16)
    dq, dkv, bias_grad = attend_back(
        meta, queries, keys_values_all, bias, attended_grad, exact, logs
    )

    result, branch_tiles = lax.optimization_barrier((result, branch_tiles))
    result_share = attn_share + from_experts(result)
    result_rows = lax.all_to_all(
        jnp.transpose(result_share.astype(BF16)), "tensor", split_axis=0, concat_axis=1, tiled=True
    )
    block_out = block_input + result_rows.astype(F32)
    grad_expert_in = jnp.concatenate(
        reorder(
            [
                einsum("gds,gfs->df", normed_two[:, k * share : (k + 1) * share], pre_grad)
                for k in range(tensor_count)
            ],
            tensor_place,
        )
    )[None]
    grad_expert_out = jnp.concatenate(
        reorder(
            [
                einsum("gfs,gds->fd", activated, scaled_grad[:, k * share : (k + 1) * share])
                for k in range(tensor_count)
            ],
            tensor_place,
        ),
        axis=1,
    )[None]
    attended_rows = attended
    out_grads = [
        einsum("ncq,enq->ec", attended_rows, branch_tiles[k]) for k in range(tensor_count)
    ]
    out_grads = jnp.concatenate(reorder(out_grads, tensor_place))
    grad_attn_out = jnp.transpose(scatter_grid(out_grads.reshape(-1, attn_out_weight.shape[1], head_cols)))
    own_branch = jnp.concatenate(
        reorder(
            [
                lax.dynamic_slice_in_dim(piece, tensor_place * local_count, local_count, 1)
                for piece in branch
            ],
            tensor_place,
        )
    )
    state_rows_grad = jnp.transpose(own_branch).astype(F32)

    if seq_count == 2:
        halves = dkv.reshape(2, tiles, 2 * head_cols, TILE)
        mine = lax.dynamic_index_in_dim(halves, seq_place, 0, keepdims=False)
        theirs = lax.dynamic_index_in_dim(halves, seq_place ^ 1, 0, keepdims=False)
        dkv_own = (mine.astype(F32) + swap(theirs, "seq", 1).astype(F32)).astype(BF16)
    else:
        dkv_own = lax.psum_scatter(dkv, "seq", scatter_dimension=0, tiled=True)
    proj_grad = jnp.concatenate([dq, dkv_own], axis=1).reshape(tiles, 3, head_cols, TILE)
    normed_one_part = einsum("nkcq,dkc->nqd", proj_grad, in_full)
    normed_one_grad = sum_relative(
        relative(normed_one_part.reshape(group_count, width)), "tensor"
    )
    grad_in_full = einsum("nqd,nkcq->dkc", normed_tiles, proj_grad)
    gain_one_part = jnp.sum(grad_in_full * in_full.astype(F32), axis=(1, 2)) / norm_gains[0]
    grad_attn_in = jnp.transpose(
        scatter_grid(grad_in_full.reshape(-1, attn_in_weight.shape[1], 3, head_cols)), (1, 0, 2)
    )
    input_grad = state_rows_grad + norm_back(block_input, norm_gains[0], normed_one_grad)

    gain_two_part = jnp.sum(gain_sum, axis=1)
    small = jnp.concatenate([router_sum, gain_two_part[None]])
    small = small.reshape(experts + 1, tensor_count, share)
    small = jnp.concatenate(
        reorder([small[:, k] for k in range(tensor_count)], tensor_place), axis=1
    )
    small = sum_all(small, ("tensor", "seq", "dp"))
    bias_part = bias_sums(bias_grad, bucket_count)
    bias_padded = lax.dynamic_update_slice_in_dim(
        jnp.zeros((bucket_count, heads * tensor_count), F32), bias_part, tensor_place * heads, 1
    )
    late = sum_all(
        jnp.concatenate([gain_one_part, bias_padded.reshape(-1)]), ("tensor", "seq", "dp")
    )
    bias_sum = late[width:].reshape(bucket_count, heads * tensor_count)
    grad_bias = lax.dynamic_slice_in_dim(bias_sum, tensor_place * heads, heads, 1)
    grad_gains = jnp.stack([late[:width], small[experts] / norm_gains[1]])
    return (
        block_out,
        input_grad,
        grad_attn_in,
        grad_attn_out,
        grad_bias,
        grad_gains,
        jnp.transpose(small[:experts]),
        grad_expert_in,
        grad_expert_out,
    )


def solution(mesh):
    return jax.shard_map(
        shards,
        mesh=mesh,
        in_specs=(
            P(("dp", "seq", "tensor"), None),
            P(None, ("dp", "seq"), "tensor"),
            P("tensor", ("dp", "seq")),
            P(None, "tensor"),
            P(),
            P(),
            P(("dp", "seq"), None, "tensor"),
            P(("dp", "seq"), "tensor", None),
            P("dp", ("seq", "tensor")),
            P(("dp", "seq"), None),
            P(("dp", "seq", "tensor"), None),
        ),
        out_specs=(
            P(("dp", "seq", "tensor"), None),
            P(("dp", "seq", "tensor"), None),
            P(None, ("dp", "seq"), "tensor"),
            P("tensor", ("dp", "seq")),
            P(None, "tensor"),
            P(),
            P(),
            P(("dp", "seq"), None, "tensor"),
            P(("dp", "seq"), "tensor", None),
        ),
        check_vma=False,
    )
```

```python
import functools
import math

import jax
import jax.numpy as jnp
from jax import lax
from jax.experimental import pallas as pl
from jax.experimental.pallas import tpu as pltpu
from jax.sharding import PartitionSpec as P

EPSILON = 1e-06
EDGES = (1, 2, 3, 4, 5, 6, 7, 8, 12, 16, 23, 32, 46, 64, 91)
TILE = 256
HALF = TILE // 2
LOG2E = math.log2(math.e)
SCALE = 0.125
MASKED = -1e30
LOWEST = -1e29
VMEM_BYTES = 48 * 1024 * 1024
GELU_A = math.sqrt(2.0 / math.pi)
GELU_B = 0.044715
BF16 = jnp.bfloat16
F32 = jnp.float32


def dot(left_side, right_side):
    return jnp.dot(left_side, right_side, preferred_element_type=F32)


def dot_rows(left_side, right_side):
    return lax.dot_general(
        left_side, right_side, (((1,), (1,)), ((), ())), preferred_element_type=F32
    )


def einsum(formula, *operands):
    return jnp.einsum(formula, *operands, preferred_element_type=F32)


def swap(values, axis, bit):
    count = lax.axis_size(axis)
    return lax.ppermute(values, axis, [(i, i ^ bit) for i in range(count)])


def bits_of(count):
    return [1 << i for i in range(count.bit_length() - 1)]


def gather_relative(values, axis):
    pieces = {0: values}
    for bit in reversed(bits_of(lax.axis_size(axis))):
        for place in list(pieces):
            pieces[place ^ bit] = swap(pieces[place], axis, bit)
    return [pieces[place] for place in range(len(pieces))]


def sum_relative(kept, sent, axis):
    total = kept.astype(F32) + swap(sent.astype(BF16), axis, 1).astype(F32)
    bit = 2
    while bit < lax.axis_size(axis):
        pairs = total.reshape((-1, 2) + total.shape[1:])
        total = pairs[:, 0] + swap(pairs[:, 1].astype(BF16), axis, bit).astype(F32)
        bit *= 2
    return total[0]


def reorder(pieces, own_index):
    for bit in bits_of(len(pieces)):
        flip = (own_index & bit) != 0
        pieces = [
            jnp.where(flip, pieces[place ^ bit], pieces[place]) for place in range(len(pieces))
        ]
    return pieces


def gather_grid(values):
    dp_count, seq_count = lax.axis_size("dp"), lax.axis_size("seq")
    if dp_count > 4 or seq_count != 2:
        return lax.all_gather(values, ("dp", "seq"), axis=0, tiled=False)
    columns = [values] + [swap(values, "dp", place) for place in range(1, dp_count)]
    near = swap(values, "seq", 1)
    far = swap(jnp.stack(columns[1:]), "seq", 1)
    pieces = [values, near]
    for place in range(1, dp_count):
        pieces += [columns[place], far[place - 1]]
    own = lax.axis_index("dp") * seq_count + lax.axis_index("seq")
    return jnp.stack(reorder(pieces, own))


def scatter_grid(blocks):
    dp_count, seq_count = lax.axis_size("dp"), lax.axis_size("seq")
    if dp_count > 4 or seq_count != 2:
        return lax.psum_scatter(
            blocks.astype(BF16), ("dp", "seq"), scatter_dimension=0, tiled=False
        ).astype(F32)
    own = lax.axis_index("dp") * seq_count + lax.axis_index("seq")
    parts = reorder([blocks[place] for place in range(dp_count * seq_count)], own)
    sent = swap(jnp.stack(parts[1::2]).astype(BF16), "seq", 1)
    parts = [parts[2 * place] + sent[place].astype(F32) for place in range(dp_count)]
    total = parts[0]
    for place in range(1, dp_count):
        total = total + swap(parts[place].astype(BF16), "dp", place).astype(F32)
    return total


def sum_all(values, axes):
    for axis in axes:
        for bit in bits_of(lax.axis_size(axis)):
            values = values + swap(values, axis, bit)
    return values


def bucket_of(relative, half_count):
    magnitude = jnp.abs(relative)
    counted = jnp.zeros(relative.shape, jnp.int32)
    for edge_value in EDGES:
        counted = counted + (magnitude >= edge_value).astype(jnp.int32)
    return counted + jnp.where(relative > 0, half_count, 0).astype(jnp.int32)


def near_buckets(half_count):
    shape = (3, HALF, HALF)
    relative = (
        (lax.broadcasted_iota(jnp.int32, shape, 0) - 1) * HALF
        + lax.broadcasted_iota(jnp.int32, shape, 1)
        - lax.broadcasted_iota(jnp.int32, shape, 2)
    )
    return bucket_of(relative, half_count)


def bias_tiles(position_bias):
    bucket_count, heads = position_bias.shape
    half_count = bucket_count // 2
    grid = near_buckets(half_count)
    near = jnp.zeros((heads, 3, HALF, HALF), F32)
    for bucket_index in range(bucket_count):
        near = near + jnp.where(
            (grid == bucket_index)[None], position_bias[bucket_index][:, None, None, None], 0.0
        )
    before, same, after = near[:, 0], near[:, 1], near[:, 2]
    far_before = jnp.broadcast_to(
        position_bias[half_count - 1][:, None, None], (heads, HALF, HALF)
    )
    far_after = jnp.broadcast_to(
        position_bias[bucket_count - 1][:, None, None], (heads, HALF, HALF)
    )

    def square(a, b, c, d):
        return jnp.concatenate(
            [jnp.concatenate([a, b], axis=2), jnp.concatenate([c, d], axis=2)], axis=1
        )

    tiles = jnp.stack(
        [
            square(far_before, far_before, far_before, far_before),
            square(far_before, far_before, before, far_before),
            square(same, before, after, same),
            square(far_after, after, far_after, far_after),
            square(far_after, far_after, far_after, far_after),
        ]
    )
    return tiles * LOG2E


def bias_sums(tiles, bucket_count):
    half_count = bucket_count // 2
    first, last = slice(0, HALF), slice(HALF, TILE)
    same = tiles[2][:, first, first] + tiles[2][:, last, last]
    before = tiles[2][:, first, last] + tiles[1][:, last, first]
    after = tiles[2][:, last, first] + tiles[3][:, first, last]
    near = jnp.stack([before, same, after], axis=1)
    grid = near_buckets(half_count)
    rows = [
        jnp.sum(jnp.where((grid == bucket_index)[None], near, 0.0), axis=(1, 2, 3))
        for bucket_index in range(bucket_count)
    ]
    rows[half_count - 1] = (
        rows[half_count - 1]
        + jnp.sum(tiles[0], axis=(1, 2))
        + jnp.sum(tiles[1][:, first, :], axis=(1, 2))
        + jnp.sum(tiles[1][:, last, last], axis=(1, 2))
    )
    rows[bucket_count - 1] = (
        rows[bucket_count - 1]
        + jnp.sum(tiles[4], axis=(1, 2))
        + jnp.sum(tiles[3][:, last, :], axis=(1, 2))
        + jnp.sum(tiles[3][:, first, first], axis=(1, 2))
    )
    return jnp.stack(rows)


def span_of(meta_ref, query_tile, key_tiles):
    opening, closing = meta_ref[1], meta_ref[2]
    first = query_tile * TILE
    last = first + TILE - 1
    begin = jnp.where(first < opening, 0, jnp.where(first < closing, opening, closing))
    end = jnp.where(last < opening, opening, jnp.where(last < closing, closing, key_tiles * TILE))
    return begin // TILE, (end + TILE - 1) // TILE


def document_of(meta_ref, tile, dimension):
    place = tile * TILE + lax.broadcasted_iota(jnp.int32, (TILE, TILE), dimension)
    return (place >= meta_ref[1]).astype(jnp.int32) + (place >= meta_ref[2]).astype(jnp.int32)


def attend_kernel(meta_ref, q_ref, kv_ref, bias_ref, exact_ref, out_ref, log_ref, key_ref, sum_ref):
    key_tiles = kv_ref.shape[0]
    heads = bias_ref.shape[1]
    size = q_ref.shape[1] // heads

    def turn(tile, carry):
        for h in range(heads):
            key_ref[tile, h] = kv_ref[tile, h * size : (h + 1) * size, :].T
        return carry

    lax.fori_loop(0, key_tiles, turn, 0)

    def query_body(i, carry):
        tile = meta_ref[3 + key_tiles + i]
        place = tile % meta_ref[0]
        begin, end = span_of(meta_ref, tile, key_tiles)
        own_document = document_of(meta_ref, tile, 1)
        sum_ref[...] = jnp.zeros_like(sum_ref)

        def key_body(j, stats):
            allowed = document_of(meta_ref, j, 0) == own_document
            kind = jnp.clip(j - tile, -2, 2) + 2
            stats = list(stats)
            kept = meta_ref[3 + j]
            for h in range(heads):
                peak, total = stats[2 * h], stats[2 * h + 1]
                rows = slice(h * size, (h + 1) * size)
                scores = dot(key_ref[kept, h], q_ref[i, rows, :]) * LOG2E + bias_ref[kind, h]
                scores = jnp.where(allowed, scores, MASKED)
                new_peak = jnp.maximum(peak, jnp.max(scores, axis=0, keepdims=True))
                faded = jnp.exp2(peak - new_peak)
                weights = jnp.exp2(scores - new_peak)
                stats[2 * h] = new_peak
                stats[2 * h + 1] = total * faded + jnp.sum(weights, axis=0, keepdims=True)
                values = kv_ref[kept, (heads + h) * size : (heads + h + 1) * size, :]
                sum_ref[rows, :] = sum_ref[rows, :] * faded + dot(values, weights.astype(BF16))
            return tuple(stats)

        start = []
        for h in range(heads):
            start += [jnp.full((1, TILE), LOWEST, F32), jnp.zeros((1, TILE), F32)]
        stats = lax.fori_loop(begin, end, key_body, tuple(start))
        for h in range(heads):
            rows = slice(h * size, (h + 1) * size)
            result = sum_ref[rows, :] * (1.0 / stats[2 * h + 1])
            exact_ref[i, rows, :] = result
            out_ref[place, rows, :] = result.astype(BF16)
            log_ref[i, h] = stats[2 * h] + jnp.log2(stats[2 * h + 1])
        return carry

    lax.fori_loop(0, q_ref.shape[0], query_body, 0)


def estimate(queries, key_tiles, products):
    pairs = queries.shape[0] * TILE * key_tiles * TILE
    return pl.CostEstimate(
        flops=2 * products * pairs * queries.shape[1],
        bytes_accessed=8 * pairs,
        transcendentals=3 * pairs,
    )


def whole_specs(count):
    return [pl.BlockSpec(memory_space=pltpu.VMEM)] * count


def attend(meta, queries, keys_values, bias):
    query_tiles, width, _ = queries.shape
    key_tiles = keys_values.shape[0]
    heads = bias.shape[1]
    return pl.pallas_call(
        attend_kernel,
        out_shape=(
            jax.ShapeDtypeStruct(queries.shape, F32),
            jax.ShapeDtypeStruct(queries.shape, BF16),
            jax.ShapeDtypeStruct((query_tiles, heads, 1, TILE), F32),
        ),
        in_specs=[pl.BlockSpec(memory_space=pltpu.SMEM)] + whole_specs(3),
        out_specs=tuple(whole_specs(3)),
        scratch_shapes=[
            pltpu.VMEM((key_tiles, heads, TILE, width // heads), BF16),
            pltpu.VMEM((width, TILE), F32),
        ],
        compiler_params=pltpu.CompilerParams(vmem_limit_bytes=VMEM_BYTES),
        cost_estimate=estimate(queries, key_tiles, 2),
        name="attend",
    )(meta, queries, keys_values, bias)


def attend_back_kernel(
    meta_ref,
    q_ref,
    kv_ref,
    bias_ref,
    grad_ref,
    exact_ref,
    log_ref,
    dq_ref,
    dkv_ref,
    tiles_ref,
    key_ref,
    value_ref,
    dq_sum,
    dkv_sum,
):
    key_tiles = kv_ref.shape[0]
    heads = bias_ref.shape[1]
    size = q_ref.shape[1] // heads

    def turn(tile, carry):
        for h in range(heads):
            key_ref[tile, h] = kv_ref[tile, h * size : (h + 1) * size, :].T
            value_ref[tile, h] = kv_ref[tile, (heads + h) * size : (heads + h + 1) * size, :].T
        return carry

    lax.fori_loop(0, key_tiles, turn, 0)
    dkv_sum[...] = jnp.zeros_like(dkv_sum)
    tiles_ref[...] = jnp.zeros_like(tiles_ref)

    def query_body(i, carry):
        tile = meta_ref[3 + key_tiles + i]
        place = tile % meta_ref[0]
        begin, end = span_of(meta_ref, tile, key_tiles)
        own_document = document_of(meta_ref, tile, 1)
        dq_sum[...] = jnp.zeros_like(dq_sum)
        centres = []
        for h in range(heads):
            rows = slice(h * size, (h + 1) * size)
            centres.append(
                jnp.sum(grad_ref[place, rows, :].astype(F32) * exact_ref[i, rows, :], axis=0, keepdims=True)
            )

        def key_body(j, inner):
            allowed = document_of(meta_ref, j, 0) == own_document
            kept = meta_ref[3 + j]
            kind = jnp.clip(j - tile, -2, 2) + 2
            for h in range(heads):
                rows = slice(h * size, (h + 1) * size)
                value_rows = slice((heads + h) * size, (heads + h + 1) * size)
                query = q_ref[i, rows, :]
                grad = grad_ref[place, rows, :]
                scores = dot(key_ref[kept, h], query) * LOG2E + bias_ref[kind, h]
                probs = jnp.where(allowed, jnp.exp2(scores - log_ref[i, h]), 0.0)
                prob_grad = dot(value_ref[kept, h], grad)
                score_grad = probs * (prob_grad - centres[h])
                tiles_ref[kind, h] += score_grad
                low_grad = score_grad.astype(BF16)
                dkv_sum[kept, rows, :] += dot_rows(query, low_grad)
                dkv_sum[kept, value_rows, :] += dot_rows(grad, probs.astype(BF16))
                dq_sum[rows, :] += dot(kv_ref[kept, rows, :], low_grad)
            return inner

        lax.fori_loop(begin, end, key_body, 0)
        dq_ref[i] = (dq_sum[...] * SCALE).astype(BF16)
        return carry

    lax.fori_loop(0, q_ref.shape[0], query_body, 0)
    dkv_ref[...] = dkv_sum[...].astype(BF16)


def attend_back(meta, queries, keys_values, bias, grad, exact, logs):
    key_tiles = keys_values.shape[0]
    heads = bias.shape[1]
    size = queries.shape[1] // heads
    return pl.pallas_call(
        attend_back_kernel,
        out_shape=(
            jax.ShapeDtypeStruct(queries.shape, BF16),
            jax.ShapeDtypeStruct(keys_values.shape, BF16),
            jax.ShapeDtypeStruct(bias.shape, F32),
        ),
        in_specs=[pl.BlockSpec(memory_space=pltpu.SMEM)] + whole_specs(6),
        out_specs=tuple(whole_specs(3)),
        scratch_shapes=[
            pltpu.VMEM((key_tiles, heads, TILE, size), BF16),
            pltpu.VMEM((key_tiles, heads, TILE, size), BF16),
            pltpu.VMEM(queries.shape[1:], F32),
            pltpu.VMEM(keys_values.shape, F32),
        ],
        compiler_params=pltpu.CompilerParams(vmem_limit_bytes=VMEM_BYTES),
        cost_estimate=estimate(queries, key_tiles, 5),
        name="attend_back",
    )(meta, queries, keys_values, bias, grad, exact, logs)


def split_low(values):
    high = values.astype(BF16)
    return high, (values - high.astype(F32)).astype(BF16)


def load_tile(ref, *place):
    return jnp.concatenate([ref[(m, *place)] for m in range(ref.shape[0])], axis=-1)


def expert_kernel(
    parts,
    own_ref,
    *refs,
):
    state_refs = refs[:parts]
    (grad_ref, other_ref, in_ref, in_t_ref, out_ref, router_ref, router_t_ref, gain_ref) = refs[
        parts : parts + 8
    ]
    (
        kept_ref,
        sent_ref,
        normed_ref,
        full_ref,
        act_ref,
        pre_ref,
        gate_ref,
        gain_sum,
        router_sum,
        state_ref,
        back_ref,
    ) = refs[parts + 8 :]

    @pl.when(pl.program_id(0) == 0)
    def _():
        gain_sum[...] = jnp.zeros_like(gain_sum)
        router_sum[...] = jnp.zeros_like(router_sum)

    width = gain_ref.shape[0]
    share = width // parts
    expert, own = own_ref[0], own_ref[1]
    for k in range(parts):
        state_ref[own ^ k] = load_tile(state_refs[k])
        full_ref[0, own ^ k] = load_tile(other_ref if k & 1 else grad_ref, k // 2)
    columns = state_ref.shape[-1]
    state = state_ref[...].reshape(width, columns).astype(F32)
    root = lax.rsqrt(jnp.sum(state * state, axis=0, keepdims=True) * (1.0 / width) + EPSILON)
    gain = gain_ref[...]
    normed = (state * root * gain).astype(BF16)
    normed_ref[0] = normed
    logits = dot(router_t_ref[...], normed)
    raised = jnp.exp(logits - jnp.max(logits, axis=0, keepdims=True))
    router_probs = raised / jnp.sum(raised, axis=0, keepdims=True)
    chosen = lax.broadcasted_iota(jnp.int32, logits.shape, 0) == expert
    gate = jnp.sum(jnp.where(chosen, router_probs, 0.0), axis=0, keepdims=True)
    gate_ref[0] = gate
    act_grad = dot(out_ref[...], full_ref[0].reshape(width, columns))
    pre_act = dot(in_t_ref[...], normed)
    square = pre_act * pre_act
    bent = jnp.tanh(GELU_A * pre_act * (1.0 + GELU_B * square))
    cdf = 0.5 + 0.5 * bent
    activated = (pre_act * cdf).astype(BF16)
    act_ref[0] = activated
    slope = cdf + (0.5 * GELU_A) * pre_act * (1.0 - bent * bent) * (1.0 + (3.0 * GELU_B) * square)
    pre_grad = (act_grad * gate * slope).astype(BF16)
    pre_ref[0] = pre_grad
    gate_grad = jnp.sum(activated.astype(F32) * act_grad, axis=0, keepdims=True)
    logit_grad = gate_grad * gate * (chosen.astype(F32) - router_probs)
    high, low = split_low(logit_grad)
    router = router_ref[...]
    normed_grad = dot(in_ref[...], pre_grad) + dot(router, high) + dot(router, low)
    router_sum[...] += dot_rows(high, normed) + dot_rows(low, normed)
    plain = normed.astype(F32)
    product = normed_grad * plain
    gain_sum[...] += product
    centre = jnp.sum(product, axis=0, keepdims=True) * (1.0 / width)
    back = root * (normed_grad * gain - plain * (centre * (1.0 / gain)))
    back_ref[...] = back.astype(BF16).reshape(parts, share, columns)
    merged = kept_ref.shape[1]
    slots = columns // merged
    for k in range(parts):
        block = back_ref[own ^ k]
        target = sent_ref if k & 1 else kept_ref
        for m in range(merged):
            target[k // 2, m] = block[:, m * slots : (m + 1) * slots]


def result_kernel(parts, own_ref, *refs):
    chunks = (len(refs) - 7) // 5
    sets = [refs[5 * c : 5 * c + 5] for c in range(chunks)]
    out_t_ref, kept_ref, sent_ref, in_sum, out_sum, result_ref, _ = refs[5 * chunks :]

    @pl.when(pl.program_id(0) == 0)
    def _():
        in_sum[...] = jnp.zeros_like(in_sum)
        out_sum[...] = jnp.zeros_like(out_sum)

    own = own_ref[1]
    width = out_t_ref.shape[0]
    share = width // parts
    for c in range(chunks):
        normed_ref, full_ref, act_ref, pre_ref, gate_ref = sets[c]
        gate, activated = gate_ref[0], act_ref[0]
        columns = activated.shape[-1]
        in_sum[...] += dot_rows(normed_ref[0], pre_ref[0])
        scaled = (full_ref[0].reshape(width, columns).astype(F32) * gate).astype(BF16)
        out_sum[...] += dot_rows(activated, scaled)
        result = dot(out_t_ref[...], activated) * gate
        result_ref[...] = result.astype(BF16).reshape(parts, share, columns)
        merged = kept_ref.shape[1]
        slots = columns // merged
        for k in range(parts):
            block = result_ref[own ^ k]
            target = sent_ref if k & 1 else kept_ref
            for m in range(merged):
                target[k // 2, m, :, c * slots : (c + 1) * slots] = block[
                    :, m * slots : (m + 1) * slots
                ]


def fixed_spec(shape):
    return pl.BlockSpec(shape, lambda g: (0,) * len(shape))


def run_expert(own, states, grads, chunk, merged, weights):
    parts = len(states)
    count, share, slots = states[0].shape
    width = share * parts
    columns = merged * slots
    steps = count // merged
    hidden = weights[0].shape[1]
    experts = weights[3].shape[1]
    half = parts // 2
    piece = pl.BlockSpec((merged, share, slots), lambda g: (g, 0, 0))
    grad_piece = pl.BlockSpec((merged, half, share, slots), lambda g: (g, 0, 0, chunk))
    split = pl.BlockSpec((half, merged, share, slots), lambda g: (0, g, 0, 0))
    wide = pl.BlockSpec((1, width, columns), lambda g: (g, 0, 0))
    deep = pl.BlockSpec((1, hidden, columns), lambda g: (g, 0, 0))
    tall = pl.BlockSpec((1, parts, share, columns), lambda g: (g, 0, 0, 0))
    flat = pl.BlockSpec((1, 1, columns), lambda g: (g, 0, 0))
    return pl.pallas_call(
        functools.partial(expert_kernel, parts),
        grid=(steps,),
        out_shape=(
            jax.ShapeDtypeStruct((half, count, share, slots), BF16),
            jax.ShapeDtypeStruct((half, count, share, slots), BF16),
            jax.ShapeDtypeStruct((steps, width, columns), BF16),
            jax.ShapeDtypeStruct((steps, parts, share, columns), BF16),
            jax.ShapeDtypeStruct((steps, hidden, columns), BF16),
            jax.ShapeDtypeStruct((steps, hidden, columns), BF16),
            jax.ShapeDtypeStruct((steps, 1, columns), F32),
            jax.ShapeDtypeStruct((width, columns), F32),
            jax.ShapeDtypeStruct((experts, width), F32),
        ),
        in_specs=[pl.BlockSpec(memory_space=pltpu.SMEM)]
        + [piece] * parts
        + [grad_piece] * 2
        + [fixed_spec(weight.shape) for weight in weights],
        out_specs=(
            split,
            split,
            wide,
            tall,
            deep,
            deep,
            flat,
            fixed_spec((width, columns)),
            fixed_spec((experts, width)),
        ),
        scratch_shapes=[
            pltpu.VMEM((parts, share, columns), BF16),
            pltpu.VMEM((parts, share, columns), BF16),
        ],
        compiler_params=pltpu.CompilerParams(vmem_limit_bytes=VMEM_BYTES),
        cost_estimate=pl.CostEstimate(
            flops=6 * steps * columns * width * hidden,
            bytes_accessed=16 * steps * columns * width,
            transcendentals=steps * columns * hidden,
        ),
        name="expert",
    )(own, *states, *grads, *weights)


def run_result(own, saved, merged, out_t):
    chunks = len(saved)
    steps, parts, share, columns = saved[0][1].shape
    width = parts * share
    hidden = saved[0][2].shape[1]
    slots = columns // merged
    half = parts // 2
    wide = pl.BlockSpec((1, width, columns), lambda g: (g, 0, 0))
    deep = pl.BlockSpec((1, hidden, columns), lambda g: (g, 0, 0))
    tall = pl.BlockSpec((1, parts, share, columns), lambda g: (g, 0, 0, 0))
    flat = pl.BlockSpec((1, 1, columns), lambda g: (g, 0, 0))
    split = pl.BlockSpec((half, merged, share, slots * chunks), lambda g: (0, g, 0, 0))
    total = jax.ShapeDtypeStruct((half, steps * merged, share, slots * chunks), BF16)
    return pl.pallas_call(
        functools.partial(result_kernel, parts),
        grid=(steps,),
        out_shape=(
            total,
            total,
            jax.ShapeDtypeStruct((width, hidden), F32),
            jax.ShapeDtypeStruct((hidden, width), F32),
        ),
        in_specs=[pl.BlockSpec(memory_space=pltpu.SMEM)]
        + [wide, tall, deep, deep, flat] * chunks
        + [fixed_spec(out_t.shape)],
        out_specs=(split, split, fixed_spec((width, hidden)), fixed_spec((hidden, width))),
        scratch_shapes=[
            pltpu.VMEM((parts, share, columns), BF16),
            pltpu.SMEM((1,), jnp.int32),
        ],
        compiler_params=pltpu.CompilerParams(vmem_limit_bytes=VMEM_BYTES),
        cost_estimate=pl.CostEstimate(
            flops=6 * chunks * steps * columns * width * hidden,
            bytes_accessed=12 * chunks * steps * columns * width,
            transcendentals=0,
        ),
        name="result",
    )(own, *[array for arrays in saved for array in arrays], out_t)


def norm_back(values, gain_row, grad):
    root = lax.rsqrt(jnp.mean(values * values, axis=-1, keepdims=True) + EPSILON)
    scaled = grad * gain_row
    return root * scaled - values * root**3 * jnp.mean(scaled * values, axis=-1, keepdims=True)


def shards(
    block_input,
    attn_in_weight,
    attn_out_weight,
    position_bias,
    norm_gains,
    router_weight,
    expert_in,
    expert_out,
    segment_ids,
    expert_ids,
    out_grad,
):
    tensor_count, seq_count = lax.axis_size("tensor"), lax.axis_size("seq")
    tensor_place, seq_place = lax.axis_index("tensor"), lax.axis_index("seq")
    grid_place = lax.axis_index("dp") * seq_count + seq_place
    local_count, width = block_input.shape
    group_count = local_count * tensor_count
    share = width // tensor_count
    bucket_count, heads = position_bias.shape
    head_cols = attn_in_weight.shape[2]
    experts = router_weight.shape[1]
    capacity = max(2, 2 * group_count // experts)
    tiles = group_count // TILE
    key_tiles = tiles * seq_count
    fast = seq_count == 2 and local_count == TILE

    def relative(values, axis=0):
        shape = values.shape
        blocks = values.reshape(
            shape[:axis] + (tensor_count, shape[axis] // tensor_count) + shape[axis + 1 :]
        )
        return [
            lax.dynamic_index_in_dim(blocks, tensor_place ^ k, axis, keepdims=False)
            for k in range(tensor_count)
        ]

    id_row = jnp.pad(segment_ids.astype(BF16), ((0, 15), (0, width - local_count)))
    own_rows = jnp.concatenate([block_input.astype(BF16), id_row])
    if seq_count == 2:
        both_rows = jnp.stack([own_rows, swap(own_rows, "seq", 1)])
    else:
        both_rows = lax.all_gather(own_rows, "seq", axis=0, tiled=False)
    row_pieces = gather_relative(both_rows, "tensor")
    weight_pieces = jnp.concatenate(
        [jnp.transpose(attn_in_weight, (1, 0, 2)), jnp.transpose(attn_out_weight)[:, None]], axis=1
    )
    weights_full = gather_grid(weight_pieces).reshape(width, 4, head_cols)
    in_full, out_full = weights_full[:, :3], weights_full[:, 3]
    all_ids = jnp.stack([piece[:, local_count, :local_count] for piece in row_pieces])
    opening = jnp.sum((all_ids < 0.5).astype(jnp.int32))
    closing = jnp.sum((all_ids < 1.5).astype(jnp.int32))
    slots_of_keys = jnp.arange(key_tiles, dtype=jnp.int32)
    tile_of_queries = seq_place * tiles + jnp.arange(tiles, dtype=jnp.int32)
    if fast:
        input_tiles = jnp.stack(
            [piece[s, :local_count] for s in range(seq_count) for piece in row_pieces]
        )
        slots_of_keys = ((slots_of_keys // tiles) ^ seq_place) * tiles + (
            (slots_of_keys % tiles) ^ tensor_place
        )
        tile_of_queries = seq_place * tiles + (
            jnp.arange(tiles, dtype=jnp.int32) ^ tensor_place
        )
        own_tiles = input_tiles[:tiles]
    else:
        ordered = reorder([piece[:, :local_count] for piece in row_pieces], tensor_place)
        ordered = jnp.stack(ordered, axis=1).reshape(seq_count, group_count, width)
        if seq_count == 2:
            ordered = jnp.stack(reorder([ordered[0], ordered[1]], seq_place))
        input_tiles = ordered.reshape(key_tiles, TILE, width)
        own_tiles = lax.dynamic_slice_in_dim(input_tiles, seq_place * tiles, tiles, 0)
    meta = jnp.concatenate(
        [
            jnp.stack([jnp.int32(tiles), opening, closing]),
            slots_of_keys.astype(jnp.int32),
            tile_of_queries.astype(jnp.int32),
        ]
    )
    bias = bias_tiles(position_bias)

    def normed_of(rows):
        wide_rows = rows.astype(F32)
        root = lax.rsqrt(jnp.mean(wide_rows * wide_rows, axis=-1, keepdims=True) + EPSILON)
        return (wide_rows * root * norm_gains[0]).astype(BF16)

    normed_tiles = normed_of(input_tiles)
    own_normed = normed_tiles[:tiles] if fast else normed_of(own_tiles)

    route_all = expert_ids[:, 0]
    expert_range = jnp.arange(experts, dtype=jnp.int32)
    route_hot = (route_all[:, None] == expert_range[None, :]).astype(jnp.int32)
    slot_rank = jnp.sum(jnp.cumsum(route_hot, axis=0) * route_hot, axis=-1) - 1
    target = (route_all * capacity + slot_rank).reshape(1, tiles, TILE, 1)
    places = jnp.arange(experts * capacity, dtype=jnp.int32).reshape(experts, 1, 1, capacity)
    onehot = (target == places).astype(BF16)
    chunks = 2 if capacity >= TILE else 1
    slots = capacity // chunks
    spread = max(1, TILE // capacity)
    merged = max(1, TILE // (slots * spread))

    def exchange(values):
        return lax.all_to_all(values, ("dp", "seq"), split_axis=0, concat_axis=0, tiled=True)

    def joined(values):
        if spread == 1:
            return values
        shape = values.shape
        values = values.reshape((-1, spread) + shape[1:])
        return jnp.moveaxis(values, 1, -2).reshape(
            (shape[0] // spread,) + shape[1:-1] + (spread * shape[-1],)
        )

    def parted(values):
        if spread == 1:
            return values
        shape = values.shape
        values = values.reshape(shape[:-1] + (spread, shape[-1] // spread))
        return jnp.moveaxis(values, -2, 1).reshape((-1,) + shape[1:-1] + (shape[-1] // spread,))

    half = tensor_count // 2
    grad_rows, row_pieces = lax.optimization_barrier((out_grad.astype(BF16), row_pieces))
    grad_shares = jnp.transpose(grad_rows.reshape(local_count, tensor_count, share), (1, 0, 2))
    grad_sent = jnp.stack(
        [grad_shares[jnp.array([j ^ (2 * k) for j in range(tensor_count)])] for k in range(half)],
        axis=1,
    )
    grad_here = lax.all_to_all(grad_sent, "tensor", split_axis=0, concat_axis=0, tiled=True)
    grad_here = jnp.moveaxis(grad_here, 1, 0).reshape(half, tiles, TILE, share)
    grad_buffer = einsum("knqd,enqs->ekds", grad_here, onehot).astype(BF16)

    queries = (einsum("nrd,dc->ncr", own_normed, in_full[:, 0]) * SCALE).astype(BF16)
    queries, grad_buffer = lax.optimization_barrier((queries, grad_buffer))
    keys_values = einsum("nrd,dkc->nkcr", normed_tiles, in_full[:, 1:]).astype(BF16)
    keys_values = keys_values.reshape(key_tiles, 2 * head_cols, TILE)
    grad_arrived = joined(exchange(grad_buffer))
    exact, attended, logs = attend(meta, queries, keys_values, bias)

    out_blocks = jnp.stack(relative(out_full))
    input_share = jnp.concatenate(
        [
            lax.dynamic_slice(
                own_tiles,
                (n ^ tensor_place if fast else n, 0, tensor_place * share),
                (1, TILE, share),
            )
            for n in range(tiles)
        ]
    )
    input_share = jnp.transpose(input_share, (0, 2, 1)).astype(F32)
    attn_kept = einsum("kec,ncq->kneq", out_blocks[0::2], attended)
    attn_sent = einsum("kec,ncq->kneq", out_blocks[1::2], attended)
    attn_share = sum_relative(attn_kept, attn_sent, "tensor")
    state_share = (input_share + attn_share).astype(BF16)
    grad_other = swap(grad_arrived, "tensor", 1)

    own = jnp.stack([grid_place, tensor_place]).astype(jnp.int32)
    router_t = jnp.transpose(router_weight)
    in_t, out_t = jnp.transpose(expert_in[0]), jnp.transpose(expert_out[0])
    weights = (
        expert_in[0],
        in_t,
        expert_out[0],
        router_weight,
        router_t,
        norm_gains[1][:, None],
    )
    arrivals = []
    for c in range(chunks):
        buffer = einsum("ndq,enqs->eds", state_share, onehot[..., c * slots : (c + 1) * slots])
        arrivals.append(joined(exchange(buffer.astype(BF16))))
    saved, parts_back = [], []
    small = jnp.zeros((experts + 1, width), F32)
    for c in range(chunks):
        kept, sent, normed_two, full, activated, pre_grad, gate, gain_sum, router_sum = run_expert(
            own,
            gather_relative(arrivals[c], "tensor"),
            (grad_arrived, grad_other),
            c,
            merged,
            weights,
        )
        saved.append((normed_two, full, activated, pre_grad, gate))
        parts_back.append((kept, sent))
        gain_part = jnp.sum(gain_sum, axis=1) / norm_gains[1]
        small = small + jnp.concatenate([router_sum, gain_part[None]])
    state_grad = jnp.transpose(grad_here[0], (0, 2, 1)).astype(F32)
    for c in range(chunks):
        total = parted(sum_relative(*parts_back[c], "tensor").astype(BF16))
        state_grad = state_grad + einsum(
            "eds,enqs->ndq", exchange(total), onehot[..., c * slots : (c + 1) * slots]
        )
    state_grad = state_grad.astype(BF16)
    result_kept, result_sent, grad_expert_in, grad_expert_out = run_result(
        own, saved, merged, out_t
    )
    result_total = sum_relative(result_kept, result_sent, "tensor").astype(BF16)
    state_grad, result_total = lax.optimization_barrier((state_grad, result_total))
    result_back = exchange(parted(result_total))

    branch = gather_relative(state_grad, "tensor")
    branch_tiles = jnp.stack(branch)
    attended_grad = einsum("kec,kneq->ncq", out_blocks, branch_tiles).astype(BF16)
    dq, dkv, bias_grad = attend_back(
        meta, queries, keys_values, bias, attended_grad, exact, logs
    )
    dq, dkv, bias_grad, result_back = lax.optimization_barrier((dq, dkv, bias_grad, result_back))

    own_slots = dkv[:tiles] if fast else lax.dynamic_slice_in_dim(dkv, seq_place * tiles, tiles, 0)
    in_flat = in_full.reshape(width, 3 * head_cols)
    own_part = einsum("ncq,dc->nqd", jnp.concatenate([dq, own_slots], axis=1), in_flat)
    in_grad = jnp.concatenate(
        [
            einsum("nqd,ncq->dc", own_normed, dq),
            einsum("nqd,ncq->dc", normed_tiles, dkv),
        ],
        axis=1,
    )
    if fast:
        far_part = einsum("ncq,dc->nqd", dkv[tiles:], in_flat[:, head_cols:])
        far_sum = sum_relative(far_part[0::2], far_part[1::2], "tensor")
        normed_one_grad = sum_relative(own_part[0::2], own_part[1::2], "tensor")
        normed_one_grad = normed_one_grad + swap(far_sum.astype(BF16), "seq", 1).astype(F32)
    else:
        all_part = einsum("ncq,dc->nqd", dkv, in_flat[:, head_cols:])
        own_part = einsum("ncq,dc->nqd", dq, in_flat[:, :head_cols])
        own_part = own_part + lax.psum_scatter(
            all_part.astype(BF16), "seq", scatter_dimension=0, tiled=True
        ).astype(F32)
        blocks = relative(own_part.reshape(group_count, width))
        normed_one_grad = sum_relative(jnp.stack(blocks[0::2]), jnp.stack(blocks[1::2]), "tensor")
    grad_attn_in = scatter_grid(in_grad.reshape(-1, attn_in_weight.shape[1], 3, head_cols))
    grad_attn_in = jnp.transpose(grad_attn_in, (1, 0, 2))
    gain_one_part = jnp.sum(in_grad * in_flat.astype(F32), axis=1) / norm_gains[0]
    own_branch = jnp.concatenate(
        reorder(
            [
                piece.reshape(tiles, share, TILE)[0]
                if tiles == 1
                else lax.dynamic_index_in_dim(piece, tensor_place, 0, keepdims=False)
                for piece in branch
            ],
            tensor_place,
        )
    )
    if local_count != TILE:
        own_branch = lax.dynamic_slice_in_dim(
            own_branch, tensor_place * local_count % TILE, local_count, 1
        )
    input_grad = jnp.transpose(own_branch).astype(F32) + norm_back(
        block_input, norm_gains[0], normed_one_grad
    )

    result_share = attn_share + einsum("eds,enqs->ndq", result_back, onehot)
    result_share = jnp.transpose(result_share.astype(BF16), (0, 2, 1)).reshape(group_count, share)
    result_rows = lax.all_to_all(
        result_share, "tensor", split_axis=0, concat_axis=1, tiled=True
    )
    block_out = block_input + result_rows.astype(F32)
    out_grads = einsum("ncq,kneq->kec", attended, branch_tiles)
    out_grads = jnp.concatenate(
        reorder([out_grads[k] for k in range(tensor_count)], tensor_place)
    )
    grad_attn_out = jnp.transpose(
        scatter_grid(out_grads.reshape(-1, attn_out_weight.shape[1], head_cols))
    )

    bias_padded = lax.dynamic_update_slice_in_dim(
        jnp.zeros((bucket_count, heads * tensor_count), F32),
        bias_sums(bias_grad, bucket_count),
        tensor_place * heads,
        1,
    )
    small = sum_all(
        jnp.concatenate([small.reshape(-1), gain_one_part, bias_padded.reshape(-1)]),
        ("tensor", "seq", "dp"),
    )
    first, second = experts * width, (experts + 1) * width
    grad_router = jnp.transpose(small[:first].reshape(experts, width))
    grad_gains = jnp.stack([small[second : second + width], small[first:second]])
    bias_sum = small[second + width :].reshape(bucket_count, heads * tensor_count)
    grad_bias = lax.dynamic_slice_in_dim(bias_sum, tensor_place * heads, heads, 1)
    return (
        block_out,
        input_grad,
        grad_attn_in,
        grad_attn_out,
        grad_bias,
        grad_gains,
        grad_router,
        grad_expert_in[None],
        grad_expert_out[None],
    )


def solution(mesh):
    return jax.shard_map(
        shards,
        mesh=mesh,
        in_specs=(
            P(("dp", "seq", "tensor"), None),
            P(None, ("dp", "seq"), "tensor"),
            P("tensor", ("dp", "seq")),
            P(None, "tensor"),
            P(),
            P(),
            P(("dp", "seq"), None, "tensor"),
            P(("dp", "seq"), "tensor", None),
            P("dp", ("seq", "tensor")),
            P(("dp", "seq"), None),
            P(("dp", "seq", "tensor"), None),
        ),
        out_specs=(
            P(("dp", "seq", "tensor"), None),
            P(("dp", "seq", "tensor"), None),
            P(None, ("dp", "seq"), "tensor"),
            P("tensor", ("dp", "seq")),
            P(None, "tensor"),
            P(),
            P(),
            P(("dp", "seq"), None, "tensor"),
            P(("dp", "seq"), "tensor", None),
        ),
        check_vma=False,
    )
```

```python
import functools
import math

import jax
import jax.numpy as jnp
from jax import lax
from jax.experimental import pallas as pl
from jax.experimental.pallas import tpu as pltpu
from jax.sharding import PartitionSpec as P

EPSILON = 1e-06
EDGES = (1, 2, 3, 4, 5, 6, 7, 8, 12, 16, 23, 32, 46, 64, 91)
TILE = 256
HALF = TILE // 2
LOG2E = math.log2(math.e)
SCALE = 0.125
MASKED = -1e30
LOWEST = -1e29
VMEM_BYTES = 48 * 1024 * 1024
GELU_A = math.sqrt(2.0 / math.pi)
GELU_B = 0.044715
BF16 = jnp.bfloat16
F32 = jnp.float32


def dot(left_side, right_side):
    return jnp.dot(left_side, right_side, preferred_element_type=F32)


def dot_rows(left_side, right_side):
    return lax.dot_general(
        left_side, right_side, (((1,), (1,)), ((), ())), preferred_element_type=F32
    )


def einsum(formula, *operands):
    return jnp.einsum(formula, *operands, preferred_element_type=F32)


def swap(values, axis, bit):
    count = lax.axis_size(axis)
    return lax.ppermute(values, axis, [(i, i ^ bit) for i in range(count)])


def bits_of(count):
    return [1 << i for i in range(count.bit_length() - 1)]


def gather_relative(values, axis):
    pieces = {0: values}
    for bit in reversed(bits_of(lax.axis_size(axis))):
        for place in list(pieces):
            pieces[place ^ bit] = swap(pieces[place], axis, bit)
    return [pieces[place] for place in range(len(pieces))]


def sum_cores(kept, sent, axis):
    return kept.astype(F32) + swap(sent.astype(BF16), axis, 1).astype(F32)


def sum_chips(total, axis):
    bit = 2
    while bit < lax.axis_size(axis):
        pairs = total.reshape((-1, 2) + total.shape[1:])
        total = pairs[:, 0] + swap(pairs[:, 1].astype(BF16), axis, bit).astype(F32)
        bit *= 2
    return total[0]


def reorder(pieces, own_index):
    for bit in bits_of(len(pieces)):
        flip = (own_index & bit) != 0
        pieces = [
            jnp.where(flip, pieces[place ^ bit], pieces[place]) for place in range(len(pieces))
        ]
    return pieces


def gather_grid(values):
    dp_count, seq_count = lax.axis_size("dp"), lax.axis_size("seq")
    if dp_count > 4 or seq_count != 2:
        return [lax.all_gather(values, ("dp", "seq"), axis=0, tiled=True)]
    columns = [swap(values, "dp", place) for place in range(1, dp_count)]
    pieces = [values, swap(values, "seq", 1)]
    for column in columns:
        pieces += [column, swap(column, "seq", 1)]
    return pieces


def sum_all(values, axes):
    for axis in axes:
        for bit in bits_of(lax.axis_size(axis)):
            values = values + swap(values, axis, bit)
    return values


def bucket_of(relative, half_count):
    magnitude = jnp.abs(relative)
    counted = jnp.zeros(relative.shape, jnp.int32)
    for edge_value in EDGES:
        counted = counted + (magnitude >= edge_value).astype(jnp.int32)
    return counted + jnp.where(relative > 0, half_count, 0).astype(jnp.int32)


def near_buckets(half_count):
    shape = (3, HALF, HALF)
    relative = (
        (lax.broadcasted_iota(jnp.int32, shape, 0) - 1) * HALF
        + lax.broadcasted_iota(jnp.int32, shape, 1)
        - lax.broadcasted_iota(jnp.int32, shape, 2)
    )
    return bucket_of(relative, half_count)


def bias_tiles(position_bias):
    bucket_count, heads = position_bias.shape
    half_count = bucket_count // 2
    grid = near_buckets(half_count)
    near = jnp.zeros((heads, 3, HALF, HALF), F32)
    for bucket_index in range(bucket_count):
        near = near + jnp.where(
            (grid == bucket_index)[None], position_bias[bucket_index][:, None, None, None], 0.0
        )
    before, same, after = near[:, 0], near[:, 1], near[:, 2]
    far_before = jnp.broadcast_to(
        position_bias[half_count - 1][:, None, None], (heads, HALF, HALF)
    )
    far_after = jnp.broadcast_to(
        position_bias[bucket_count - 1][:, None, None], (heads, HALF, HALF)
    )

    def square(a, b, c, d):
        return jnp.concatenate(
            [jnp.concatenate([a, b], axis=2), jnp.concatenate([c, d], axis=2)], axis=1
        )

    tiles = jnp.stack(
        [
            square(far_before, far_before, far_before, far_before),
            square(far_before, far_before, before, far_before),
            square(same, before, after, same),
            square(far_after, after, far_after, far_after),
            square(far_after, far_after, far_after, far_after),
        ]
    )
    return tiles * LOG2E


def span_of(meta_ref, query_tile, key_tiles):
    opening, closing = meta_ref[1], meta_ref[2]
    first = query_tile * TILE
    last = first + TILE - 1
    begin = jnp.where(first < opening, 0, jnp.where(first < closing, opening, closing))
    end = jnp.where(last < opening, opening, jnp.where(last < closing, closing, key_tiles * TILE))
    return begin // TILE, (end + TILE - 1) // TILE


def document_of(meta_ref, tile, dimension):
    place = tile * TILE + lax.broadcasted_iota(jnp.int32, (TILE, TILE), dimension)
    return (place >= meta_ref[1]).astype(jnp.int32) + (place >= meta_ref[2]).astype(jnp.int32)


def attend_kernel(
    meta_ref,
    q_ref,
    kv_ref,
    bias_ref,
    weight_ref,
    exact_ref,
    out_ref,
    log_ref,
    even_ref,
    odd_ref,
    key_ref,
    sum_ref,
):
    key_tiles = kv_ref.shape[0]
    heads = bias_ref.shape[1]
    size = q_ref.shape[1] // heads

    def turn(tile, carry):
        for h in range(heads):
            key_ref[tile, h] = kv_ref[tile, h * size : (h + 1) * size, :].T
        return carry

    lax.fori_loop(0, key_tiles, turn, 0)

    def query_body(i, carry):
        tile = meta_ref[3 + key_tiles + i]
        place = tile % meta_ref[0]
        begin, end = span_of(meta_ref, tile, key_tiles)
        own_document = document_of(meta_ref, tile, 1)
        sum_ref[...] = jnp.zeros_like(sum_ref)

        def key_body(j, stats):
            allowed = document_of(meta_ref, j, 0) == own_document
            kind = jnp.clip(j - tile, -2, 2) + 2
            stats = list(stats)
            kept = meta_ref[3 + j]
            for h in range(heads):
                peak, total = stats[2 * h], stats[2 * h + 1]
                rows = slice(h * size, (h + 1) * size)
                scores = dot(key_ref[kept, h], q_ref[i, rows, :]) * LOG2E + bias_ref[kind, h]
                scores = jnp.where(allowed, scores, MASKED)
                new_peak = jnp.maximum(peak, jnp.max(scores, axis=0, keepdims=True))
                faded = jnp.exp2(peak - new_peak)
                weights = jnp.exp2(scores - new_peak)
                stats[2 * h] = new_peak
                stats[2 * h + 1] = total * faded + jnp.sum(weights, axis=0, keepdims=True)
                values = kv_ref[kept, (heads + h) * size : (heads + h + 1) * size, :]
                sum_ref[rows, :] = sum_ref[rows, :] * faded + dot(values, weights.astype(BF16))
            return tuple(stats)

        start = []
        for h in range(heads):
            start += [jnp.full((1, TILE), LOWEST, F32), jnp.zeros((1, TILE), F32)]
        stats = lax.fori_loop(begin, end, key_body, tuple(start))
        for h in range(heads):
            rows = slice(h * size, (h + 1) * size)
            result = sum_ref[rows, :] * (1.0 / stats[2 * h + 1])
            exact_ref[i, rows, :] = result
            out_ref[place, rows, :] = result.astype(BF16)
            log_ref[i, h] = stats[2 * h] + jnp.log2(stats[2 * h + 1])
        attended = out_ref[place]
        for k in range(weight_ref.shape[0]):
            block = dot(weight_ref[k], attended).astype(BF16)
            (odd_ref if k & 1 else even_ref)[k // 2, place] = block
        return carry

    lax.fori_loop(0, q_ref.shape[0], query_body, 0)


def estimate(queries, key_tiles, products):
    pairs = queries.shape[0] * TILE * key_tiles * TILE
    return pl.CostEstimate(
        flops=2 * products * pairs * queries.shape[1],
        bytes_accessed=8 * pairs,
        transcendentals=3 * pairs,
    )


def whole_specs(count):
    return [pl.BlockSpec(memory_space=pltpu.VMEM)] * count


def attend(meta, queries, keys_values, bias, out_blocks):
    query_tiles, width, _ = queries.shape
    key_tiles = keys_values.shape[0]
    heads = bias.shape[1]
    parts, share, _ = out_blocks.shape
    blocks = jax.ShapeDtypeStruct((parts // 2, query_tiles, share, TILE), BF16)
    return pl.pallas_call(
        attend_kernel,
        out_shape=(
            jax.ShapeDtypeStruct(queries.shape, F32),
            jax.ShapeDtypeStruct(queries.shape, BF16),
            jax.ShapeDtypeStruct((query_tiles, heads, 1, TILE), F32),
            blocks,
            blocks,
        ),
        in_specs=[pl.BlockSpec(memory_space=pltpu.SMEM)] + whole_specs(4),
        out_specs=tuple(whole_specs(5)),
        scratch_shapes=[
            pltpu.VMEM((key_tiles, heads, TILE, width // heads), BF16),
            pltpu.VMEM((width, TILE), F32),
        ],
        compiler_params=pltpu.CompilerParams(vmem_limit_bytes=VMEM_BYTES),
        cost_estimate=estimate(queries, key_tiles, 2),
        name="attend",
    )(meta, queries, keys_values, bias, out_blocks)


def bucket_rows(tiles_ref, rows_ref):
    heads, bucket_count = rows_ref.shape[:2]
    half_count = bucket_count // 2
    offset = lax.broadcasted_iota(jnp.int32, (HALF, HALF), 0) - lax.broadcasted_iota(
        jnp.int32, (HALF, HALF), 1
    )
    grids = [bucket_of(offset + shift * HALF, half_count) for shift in (-1, 0, 1)]
    first, last = slice(0, HALF), slice(HALF, TILE)

    def column_sums(values):
        return jnp.sum(values, axis=0, keepdims=True)

    def head_body(h, carry):
        before = tiles_ref[2, h, first, last] + tiles_ref[1, h, last, first]
        same = tiles_ref[2, h, first, first] + tiles_ref[2, h, last, last]
        after = tiles_ref[2, h, last, first] + tiles_ref[3, h, first, last]
        far_before = column_sums(tiles_ref[0, h, :, first] + tiles_ref[0, h, :, last])
        far_before += column_sums(tiles_ref[1, h, first, first] + tiles_ref[1, h, first, last])
        far_before += column_sums(tiles_ref[1, h, last, last])
        far_after = column_sums(tiles_ref[4, h, :, first] + tiles_ref[4, h, :, last])
        far_after += column_sums(tiles_ref[3, h, last, first] + tiles_ref[3, h, last, last])
        far_after += column_sums(tiles_ref[3, h, first, first])
        for bucket_index in range(bucket_count):
            row = column_sums(jnp.where(grids[1] == bucket_index, same, 0.0))
            if 0 < bucket_index < half_count:
                row += column_sums(jnp.where(grids[0] == bucket_index, before, 0.0))
            if bucket_index > half_count:
                row += column_sums(jnp.where(grids[2] == bucket_index, after, 0.0))
            if bucket_index == half_count - 1:
                row += far_before
            if bucket_index == bucket_count - 1:
                row += far_after
            rows_ref[h, bucket_index : bucket_index + 1, :] = row
        return carry

    lax.fori_loop(0, heads, head_body, 0)


def attend_back_kernel(
    meta_ref,
    q_ref,
    kv_ref,
    bias_ref,
    weight_ref,
    exact_ref,
    log_ref,
    *refs,
):
    parts = weight_ref.shape[0]
    branch_refs = refs[:parts]
    (
        dq_ref,
        dkv_ref,
        rows_ref,
        tiles_ref,
        key_ref,
        value_ref,
        grad_ref,
        dq_sum,
        dkv_sum,
    ) = refs[parts:]
    key_tiles = kv_ref.shape[0]
    heads = bias_ref.shape[1]
    size = q_ref.shape[1] // heads

    def turn(tile, carry):
        for h in range(heads):
            key_ref[tile, h] = kv_ref[tile, h * size : (h + 1) * size, :].T
            value_ref[tile, h] = kv_ref[tile, (heads + h) * size : (heads + h + 1) * size, :].T
        return carry

    lax.fori_loop(0, key_tiles, turn, 0)
    dkv_sum[...] = jnp.zeros_like(dkv_sum)
    tiles_ref[...] = jnp.zeros_like(tiles_ref)

    def query_body(i, carry):
        tile = meta_ref[3 + key_tiles + i]
        place = tile % meta_ref[0]
        begin, end = span_of(meta_ref, tile, key_tiles)
        own_document = document_of(meta_ref, tile, 1)
        dq_sum[...] = jnp.zeros_like(dq_sum)
        grad_sum = dot(weight_ref[0], branch_refs[0][place])
        for k in range(1, parts):
            grad_sum += dot(weight_ref[k], branch_refs[k][place])
        grad_ref[...] = grad_sum.astype(BF16)
        centres = []
        for h in range(heads):
            rows = slice(h * size, (h + 1) * size)
            centres.append(
                jnp.sum(grad_ref[rows, :].astype(F32) * exact_ref[i, rows, :], axis=0, keepdims=True)
            )

        def key_body(j, inner):
            allowed = document_of(meta_ref, j, 0) == own_document
            kept = meta_ref[3 + j]
            kind = jnp.clip(j - tile, -2, 2) + 2
            for h in range(heads):
                rows = slice(h * size, (h + 1) * size)
                value_rows = slice((heads + h) * size, (heads + h + 1) * size)
                query = q_ref[i, rows, :]
                grad = grad_ref[rows, :]
                scores = dot(key_ref[kept, h], query) * LOG2E + bias_ref[kind, h]
                probs = jnp.where(allowed, jnp.exp2(scores - log_ref[i, h]), 0.0)
                prob_grad = dot(value_ref[kept, h], grad)
                score_grad = probs * (prob_grad - centres[h])
                tiles_ref[kind, h] += score_grad
                low_grad = score_grad.astype(BF16)
                dkv_sum[kept, rows, :] += dot_rows(query, low_grad)
                dkv_sum[kept, value_rows, :] += dot_rows(grad, probs.astype(BF16))
                dq_sum[rows, :] += dot(kv_ref[kept, rows, :], low_grad)
            return inner

        lax.fori_loop(begin, end, key_body, 0)
        dq_ref[i] = (dq_sum[...] * SCALE).astype(BF16)
        return carry

    lax.fori_loop(0, q_ref.shape[0], query_body, 0)
    dkv_ref[...] = dkv_sum[...].astype(BF16)
    bucket_rows(tiles_ref, rows_ref)


def attend_back(meta, queries, keys_values, bias, out_blocks, exact, logs, branch, buckets):
    key_tiles = keys_values.shape[0]
    heads = bias.shape[1]
    size = queries.shape[1] // heads
    return pl.pallas_call(
        attend_back_kernel,
        out_shape=(
            jax.ShapeDtypeStruct(queries.shape, BF16),
            jax.ShapeDtypeStruct(keys_values.shape, BF16),
            jax.ShapeDtypeStruct((heads, buckets, HALF), F32),
        ),
        in_specs=[pl.BlockSpec(memory_space=pltpu.SMEM)] + whole_specs(6 + len(branch)),
        out_specs=tuple(whole_specs(3)),
        scratch_shapes=[
            pltpu.VMEM(bias.shape, F32),
            pltpu.VMEM((key_tiles, heads, TILE, size), BF16),
            pltpu.VMEM((key_tiles, heads, TILE, size), BF16),
            pltpu.VMEM(queries.shape[1:], BF16),
            pltpu.VMEM(queries.shape[1:], F32),
            pltpu.VMEM(keys_values.shape, F32),
        ],
        compiler_params=pltpu.CompilerParams(vmem_limit_bytes=VMEM_BYTES),
        cost_estimate=estimate(queries, key_tiles, 5),
        name="attend_back",
    )(meta, queries, keys_values, bias, out_blocks, exact, logs, *branch)


def project_kernel(piece_count, weight_count, tiles, share, own_ref, *refs):
    piece_refs = refs[:piece_count]
    weight_refs = refs[piece_count : piece_count + weight_count]
    gain_ref = refs[piece_count + weight_count]
    (
        meta_ref,
        q_ref,
        kv_ref,
        normed_ref,
        input_ref,
        in_ref,
        out_ref,
        out_t_ref,
        block_ref,
        turned_ref,
    ) = refs[piece_count + weight_count + 1 :]
    grid_place, tensor_place, seq_place, own_first = (own_ref[i] for i in range(4))
    width = gain_ref.shape[0]
    head_cols = q_ref.shape[1]
    columns = turned_ref.shape[0]
    for k in range(weight_count):
        place = grid_place ^ k if weight_count > 1 else 0
        block_ref[place] = weight_refs[k][...]
    full = block_ref[...].reshape(width, columns)
    in_ref[...] = full[:, : 3 * head_cols]
    turned_ref[...] = full.T
    blocks_here = width // share
    tall = block_ref.shape[1]
    per = share // tall if weight_count > 1 else 1
    for k in range(blocks_here):
        if weight_count > 1:
            block = block_ref[pl.ds((tensor_place ^ k) * per, per), :, 3 * head_cols :]
            block = block.reshape(share, head_cols)
        else:
            start = pl.multiple_of((tensor_place ^ k) * share, share)
            block = block_ref[0, pl.ds(start, share), 3 * head_cols :]
        out_ref[k] = block
        out_t_ref[k] = block.T
    key_tiles = kv_ref.shape[0]
    early = jnp.zeros((1, TILE), F32)
    late = jnp.zeros((1, TILE), F32)
    gain = gain_ref[...]
    turns = key_tiles // tiles
    for s in range(piece_refs[0].shape[0]):
        for k in range(piece_count):
            kept = s * piece_count + k
            rows = piece_refs[k][s, :width, :].astype(F32)
            ids = piece_refs[k][s, width : width + 16, :][:1].astype(F32)
            early += (ids < 0.5).astype(F32)
            late += (ids < 1.5).astype(F32)
            root = lax.rsqrt(jnp.sum(rows * rows, axis=0, keepdims=True) * (1.0 / width) + EPSILON)
            normed = (rows * root * gain).astype(BF16)
            normed_ref[kept] = normed
            kv_ref[kept] = dot(turned_ref[head_cols : 3 * head_cols, :], normed).astype(BF16)
    for i in range(tiles):
        normed = normed_ref[own_first + i]
        q_ref[i] = (dot(turned_ref[:head_cols, :], normed) * SCALE).astype(BF16)
        start = pl.multiple_of(tensor_place * share, share)
        if piece_count > 1:
            input_ref[tensor_place ^ i] = piece_refs[i][0, pl.ds(start, share), :]
        else:
            input_ref[i] = piece_refs[0][own_first + i, pl.ds(start, share), :]
    meta_ref[0] = tiles
    meta_ref[1] = jnp.sum(early).astype(jnp.int32)
    meta_ref[2] = jnp.sum(late).astype(jnp.int32)
    for j in range(key_tiles):
        if piece_count > 1:
            meta_ref[3 + j] = ((j // tiles) ^ seq_place) * tiles + ((j % tiles) ^ tensor_place)
        else:
            meta_ref[3 + j] = j
    for i in range(tiles):
        shift = tensor_place ^ i if piece_count > 1 else i
        meta_ref[3 + key_tiles + i] = seq_place * tiles + shift


def project(own, pieces, weight_pieces, gain, tiles, key_tiles, share):
    width = gain.shape[0]
    columns = weight_pieces[0].shape[1]
    head_cols = columns // 4
    parts = width // share
    return pl.pallas_call(
        functools.partial(project_kernel, len(pieces), len(weight_pieces), tiles, share),
        out_shape=(
            jax.ShapeDtypeStruct((3 + key_tiles + tiles,), jnp.int32),
            jax.ShapeDtypeStruct((tiles, head_cols, TILE), BF16),
            jax.ShapeDtypeStruct((key_tiles, 2 * head_cols, TILE), BF16),
            jax.ShapeDtypeStruct((key_tiles, width, TILE), BF16),
            jax.ShapeDtypeStruct((tiles, share, TILE), BF16),
            jax.ShapeDtypeStruct((width, 3 * head_cols), BF16),
            jax.ShapeDtypeStruct((parts, share, head_cols), BF16),
            jax.ShapeDtypeStruct((parts, head_cols, share), BF16),
        ),
        in_specs=[pl.BlockSpec(memory_space=pltpu.SMEM)]
        + whole_specs(len(pieces) + len(weight_pieces) + 1),
        out_specs=(pl.BlockSpec(memory_space=pltpu.SMEM),) + tuple(whole_specs(7)),
        scratch_shapes=[
            pltpu.VMEM((len(weight_pieces),) + weight_pieces[0].shape, BF16),
            pltpu.VMEM((columns, width), BF16),
        ],
        compiler_params=pltpu.CompilerParams(vmem_limit_bytes=VMEM_BYTES),
        cost_estimate=pl.CostEstimate(
            flops=6 * key_tiles * TILE * width * head_cols,
            bytes_accessed=8 * key_tiles * TILE * width,
            transcendentals=0,
        ),
        name="project",
    )(own, *pieces, *weight_pieces, gain)


def project_back_kernel(fast, parts, own_ref, dq_ref, dkv_ref, normed_ref, in_ref, attended_ref, *refs):
    branch_refs = refs[:parts]
    if fast:
        far_even, far_odd, own_even, own_odd, weight_even, weight_odd, gain_ref, full_ref = refs[
            parts:
        ]
    else:
        part_ref, weight_ref, gain_ref, full_ref = refs[parts:]
    grid_place, tensor_place, seq_place, own_first = (own_ref[i] for i in range(4))
    tiles, head_cols, _ = dq_ref.shape
    key_tiles = dkv_ref.shape[0]
    width = in_ref.shape[0]
    share = width // parts
    key_weight = in_ref[:, head_cols:]
    query_weight = in_ref[:, :head_cols]
    if fast:
        for n in range(tiles):
            block = dot(key_weight, dkv_ref[tiles + n]).astype(BF16)
            (far_odd if n & 1 else far_even)[n // 2] = block
        for n in range(tiles):
            block = dot(key_weight, dkv_ref[n]) + dot(query_weight, dq_ref[n])
            (own_odd if n & 1 else own_even)[n // 2] = block.astype(BF16)
    else:
        for n in range(key_tiles):
            part_ref[n] = dot(key_weight, dkv_ref[n]).astype(BF16)
        for n in range(tiles):
            block = part_ref[own_first + n].astype(F32) + dot(query_weight, dq_ref[n])
            part_ref[own_first + n] = block.astype(BF16)
    query_sum = dot_rows(normed_ref[own_first], dq_ref[0])
    for n in range(1, tiles):
        query_sum += dot_rows(normed_ref[own_first + n], dq_ref[n])
    key_sum = dot_rows(normed_ref[0], dkv_ref[0])
    for n in range(1, key_tiles):
        key_sum += dot_rows(normed_ref[n], dkv_ref[n])
    gain_ref[...] = jnp.sum(
        query_sum * query_weight.astype(F32), axis=1, keepdims=True
    ) + jnp.sum(key_sum * key_weight.astype(F32), axis=1, keepdims=True)
    full_ref[:, :head_cols] = query_sum.astype(BF16)
    full_ref[:, head_cols : 3 * head_cols] = key_sum.astype(BF16)
    for k in range(parts):
        block = dot_rows(branch_refs[k][0], attended_ref[0])
        for n in range(1, tiles):
            block += dot_rows(branch_refs[k][n], attended_ref[n])
        start = pl.multiple_of((tensor_place ^ k) * share, share)
        full_ref[pl.ds(start, share), 3 * head_cols :] = block.astype(BF16)
    if fast:
        tall = weight_even.shape[1]
        for k in range(weight_even.shape[0]):
            place = grid_place ^ (2 * k)
            weight_even[k] = full_ref[pl.ds(pl.multiple_of(place * tall, tall), tall), :]
            weight_odd[k] = full_ref[pl.ds(pl.multiple_of((place ^ 1) * tall, tall), tall), :]
    else:
        weight_ref[...] = full_ref[...]


def project_back(fast, own, dq, dkv, normed, in_flat, attended, branch, grid_count):
    tiles, head_cols, _ = dq.shape
    key_tiles = dkv.shape[0]
    width = in_flat.shape[0]
    parts = len(branch)
    columns = 4 * head_cols
    if fast:
        block = jax.ShapeDtypeStruct((parts // 2, width, TILE), BF16)
        weight = jax.ShapeDtypeStruct((grid_count // 2, width // grid_count, columns), BF16)
        shapes = (block,) * 4 + (weight,) * 2
    else:
        shapes = (
            jax.ShapeDtypeStruct((key_tiles, width, TILE), BF16),
            jax.ShapeDtypeStruct((width, columns), BF16),
        )
    shapes = shapes + (jax.ShapeDtypeStruct((width, 1), F32),)
    return pl.pallas_call(
        functools.partial(project_back_kernel, fast, parts),
        out_shape=shapes,
        in_specs=[pl.BlockSpec(memory_space=pltpu.SMEM)] + whole_specs(5 + parts),
        out_specs=tuple(whole_specs(len(shapes))),
        scratch_shapes=[pltpu.VMEM((width, columns), BF16)],
        compiler_params=pltpu.CompilerParams(vmem_limit_bytes=VMEM_BYTES),
        cost_estimate=pl.CostEstimate(
            flops=12 * key_tiles * TILE * width * head_cols,
            bytes_accessed=8 * key_tiles * TILE * width,
            transcendentals=0,
        ),
        name="project_back",
    )(own, dq, dkv, normed, in_flat, attended, *branch)


def finish_kernel(input_ref, gain_ref, branch_ref, result_ref, *refs):
    sum_refs = refs[:-2]
    out_ref, grad_ref = refs[-2:]
    rows = input_ref[...]
    width = rows.shape[1]
    values = rows.T
    gain = gain_ref[...]
    grad = sum_refs[0][...].astype(F32)
    for ref in sum_refs[1:]:
        grad += ref[...].astype(F32)
    root = lax.rsqrt(jnp.sum(values * values, axis=0, keepdims=True) * (1.0 / width) + EPSILON)
    scaled = grad * gain
    centre = jnp.sum(scaled * values, axis=0, keepdims=True) * (1.0 / width)
    total = root * scaled - values * (root * root * root * centre)
    grad_ref[...] = (total + branch_ref[...].astype(F32)).T
    out_ref[...] = rows + result_ref[...].astype(F32).T


def finish(block_input, gain, branch, result, sums):
    shape = jax.ShapeDtypeStruct(block_input.shape, F32)
    return pl.pallas_call(
        finish_kernel,
        out_shape=(shape, shape),
        in_specs=whole_specs(4 + len(sums)),
        out_specs=tuple(whole_specs(2)),
        compiler_params=pltpu.CompilerParams(vmem_limit_bytes=VMEM_BYTES),
        name="finish",
    )(block_input, gain, branch, result, *sums)


def split_low(values):
    high = values.astype(BF16)
    return high, (values - high.astype(F32)).astype(BF16)


def load_tile(ref, first, count, *place):
    return jnp.concatenate([ref[(first + m, *place)] for m in range(count)], axis=-1)


def expert_kernel(
    parts,
    own_ref,
    *refs,
):
    state_refs = refs[:parts]
    (grad_ref, other_ref, in_ref, in_t_ref, out_ref, router_ref, router_t_ref, gain_ref) = refs[
        parts : parts + 8
    ]
    (
        kept_ref,
        sent_ref,
        normed_ref,
        full_ref,
        act_ref,
        pre_ref,
        gate_ref,
        gain_sum,
        router_sum,
        state_ref,
        back_ref,
    ) = refs[parts + 8 :]

    @pl.when(pl.program_id(0) == 0)
    def _():
        gain_sum[...] = jnp.zeros_like(gain_sum)
        router_sum[...] = jnp.zeros_like(router_sum)

    width = gain_ref.shape[0]
    share = width // parts
    expert, own = own_ref[0], own_ref[1]
    chains, columns = state_ref.shape[0], state_ref.shape[-1]
    merged = kept_ref.shape[1] // chains
    for a in range(chains):
        for k in range(parts):
            state_ref[a, own ^ k] = load_tile(state_refs[k], a * merged, merged)
            near = 2 * (k // 2) + ((own & 1) ^ (k & 1))
            full_ref[a, near] = load_tile(
                other_ref if k & 1 else grad_ref, a * merged, merged, k // 2
            )
    for a in range(chains):
        state = state_ref[a].reshape(width, columns).astype(F32)
        root = lax.rsqrt(jnp.sum(state * state, axis=0, keepdims=True) * (1.0 / width) + EPSILON)
        gain = gain_ref[...]
        normed = (state * root * gain).astype(BF16)
        normed_ref[a] = normed
        logits = dot(router_t_ref[...], normed)
        raised = jnp.exp(logits - jnp.max(logits, axis=0, keepdims=True))
        router_probs = raised / jnp.sum(raised, axis=0, keepdims=True)
        chosen = lax.broadcasted_iota(jnp.int32, logits.shape, 0) == expert
        gate = jnp.sum(jnp.where(chosen, router_probs, 0.0), axis=0, keepdims=True)
        gate_ref[a] = gate
        act_grad = dot(out_ref[...], full_ref[a].reshape(width, columns))
        pre_act = dot(in_t_ref[...], normed)
        square = pre_act * pre_act
        bent = jnp.tanh(GELU_A * pre_act * (1.0 + GELU_B * square))
        cdf = 0.5 + 0.5 * bent
        activated = (pre_act * cdf).astype(BF16)
        act_ref[a] = activated
        slope = cdf + (0.5 * GELU_A) * pre_act * (1.0 - bent * bent) * (1.0 + (3.0 * GELU_B) * square)
        pre_grad = (act_grad * gate * slope).astype(BF16)
        pre_ref[a] = pre_grad
        gate_grad = jnp.sum(activated.astype(F32) * act_grad, axis=0, keepdims=True)
        logit_grad = gate_grad * gate * (chosen.astype(F32) - router_probs)
        high, low = split_low(logit_grad)
        router = router_ref[...]
        normed_grad = dot(in_ref[...], pre_grad) + dot(router, high) + dot(router, low)
        router_sum[...] += dot_rows(high, normed) + dot_rows(low, normed)
        plain = normed.astype(F32)
        product = normed_grad * plain
        gain_sum[...] += product
        centre = jnp.sum(product, axis=0, keepdims=True) * (1.0 / width)
        back = root * (normed_grad * gain - plain * (centre * (1.0 / gain)))
        back_ref[a] = back.astype(BF16).reshape(parts, share, columns)
        slots = columns // merged
        for k in range(parts):
            block = back_ref[a, own ^ k]
            target = sent_ref if k & 1 else kept_ref
            for m in range(merged):
                target[k // 2, a * merged + m] = block[:, m * slots : (m + 1) * slots]


def result_kernel(parts, own_ref, *refs):
    chunks = (len(refs) - 6) // 5
    sets = [refs[5 * c : 5 * c + 5] for c in range(chunks)]
    out_t_ref, kept_ref, sent_ref, in_sum, out_sum, result_ref = refs[5 * chunks :]

    @pl.when(pl.program_id(0) == 0)
    def _():
        in_sum[...] = jnp.zeros_like(in_sum)
        out_sum[...] = jnp.zeros_like(out_sum)

    own = own_ref[1]
    width = out_t_ref.shape[0]
    share = width // parts
    for c in range(chunks):
        normed_ref, full_ref, act_ref, pre_ref, gate_ref = sets[c]
        gate, activated = gate_ref[0], act_ref[0]
        columns = activated.shape[-1]
        in_sum[...] += dot_rows(normed_ref[0], pre_ref[0])
        scaled = (full_ref[0].reshape(width, columns).astype(F32) * gate).astype(BF16)
        out_sum[...] += dot_rows(activated, scaled)
        result = dot(out_t_ref[...], activated) * gate
        result_ref[...] = result.astype(BF16).reshape(parts, share, columns)
        merged = kept_ref.shape[1]
        slots = columns // merged
        for k in range(parts):
            block = result_ref[own ^ k]
            target = sent_ref if k & 1 else kept_ref
            for m in range(merged):
                target[k // 2, m, :, c * slots : (c + 1) * slots] = block[
                    :, m * slots : (m + 1) * slots
                ]


def fixed_spec(shape):
    return pl.BlockSpec(shape, lambda g: (0,) * len(shape))


def run_expert(own, states, grads, chunk, merged, chains, weights):
    parts = len(states)
    count, share, slots = states[0].shape
    width = share * parts
    columns = merged * slots
    steps = count // merged
    hidden = weights[0].shape[1]
    experts = weights[3].shape[1]
    half = parts // 2
    taken = merged * chains
    piece = pl.BlockSpec((taken, share, slots), lambda g: (g, 0, 0))
    grad_piece = pl.BlockSpec((taken, half, share, slots), lambda g: (g, 0, 0, chunk))
    split = pl.BlockSpec((half, taken, share, slots), lambda g: (0, g, 0, 0))
    wide = pl.BlockSpec((chains, width, columns), lambda g: (g, 0, 0))
    deep = pl.BlockSpec((chains, hidden, columns), lambda g: (g, 0, 0))
    tall = pl.BlockSpec((chains, parts, share, columns), lambda g: (g, 0, 0, 0))
    flat = pl.BlockSpec((chains, 1, columns), lambda g: (g, 0, 0))
    return pl.pallas_call(
        functools.partial(expert_kernel, parts),
        grid=(steps // chains,),
        out_shape=(
            jax.ShapeDtypeStruct((half, count, share, slots), BF16),
            jax.ShapeDtypeStruct((half, count, share, slots), BF16),
            jax.ShapeDtypeStruct((steps, width, columns), BF16),
            jax.ShapeDtypeStruct((steps, parts, share, columns), BF16),
            jax.ShapeDtypeStruct((steps, hidden, columns), BF16),
            jax.ShapeDtypeStruct((steps, hidden, columns), BF16),
            jax.ShapeDtypeStruct((steps, 1, columns), F32),
            jax.ShapeDtypeStruct((width, columns), F32),
            jax.ShapeDtypeStruct((experts, width), F32),
        ),
        in_specs=[pl.BlockSpec(memory_space=pltpu.SMEM)]
        + [piece] * parts
        + [grad_piece] * 2
        + [fixed_spec(weight.shape) for weight in weights],
        out_specs=(
            split,
            split,
            wide,
            tall,
            deep,
            deep,
            flat,
            fixed_spec((width, columns)),
            fixed_spec((experts, width)),
        ),
        scratch_shapes=[
            pltpu.VMEM((chains, parts, share, columns), BF16),
            pltpu.VMEM((chains, parts, share, columns), BF16),
        ],
        compiler_params=pltpu.CompilerParams(vmem_limit_bytes=VMEM_BYTES),
        cost_estimate=pl.CostEstimate(
            flops=6 * steps * columns * width * hidden,
            bytes_accessed=16 * steps * columns * width,
            transcendentals=steps * columns * hidden,
        ),
        name="expert",
    )(own, *states, *grads, *weights)


def run_result(own, saved, merged, out_t):
    chunks = len(saved)
    steps, parts, share, columns = saved[0][1].shape
    width = parts * share
    hidden = saved[0][2].shape[1]
    slots = columns // merged
    half = parts // 2
    wide = pl.BlockSpec((1, width, columns), lambda g: (g, 0, 0))
    deep = pl.BlockSpec((1, hidden, columns), lambda g: (g, 0, 0))
    tall = pl.BlockSpec((1, parts, share, columns), lambda g: (g, 0, 0, 0))
    flat = pl.BlockSpec((1, 1, columns), lambda g: (g, 0, 0))
    split = pl.BlockSpec((half, merged, share, slots * chunks), lambda g: (0, g, 0, 0))
    total = jax.ShapeDtypeStruct((half, steps * merged, share, slots * chunks), BF16)
    return pl.pallas_call(
        functools.partial(result_kernel, parts),
        grid=(steps,),
        out_shape=(
            total,
            total,
            jax.ShapeDtypeStruct((width, hidden), F32),
            jax.ShapeDtypeStruct((hidden, width), F32),
        ),
        in_specs=[pl.BlockSpec(memory_space=pltpu.SMEM)]
        + [wide, tall, deep, deep, flat] * chunks
        + [fixed_spec(out_t.shape)],
        out_specs=(split, split, fixed_spec((width, hidden)), fixed_spec((hidden, width))),
        scratch_shapes=[
            pltpu.VMEM((parts, share, columns), BF16),
        ],
        compiler_params=pltpu.CompilerParams(vmem_limit_bytes=VMEM_BYTES),
        cost_estimate=pl.CostEstimate(
            flops=6 * chunks * steps * columns * width * hidden,
            bytes_accessed=12 * chunks * steps * columns * width,
            transcendentals=0,
        ),
        name="result",
    )(own, *[array for arrays in saved for array in arrays], out_t)


def shards(
    block_input,
    attn_in_weight,
    attn_out_weight,
    position_bias,
    norm_gains,
    router_weight,
    expert_in,
    expert_out,
    segment_ids,
    expert_ids,
    out_grad,
):
    tensor_count, seq_count = lax.axis_size("tensor"), lax.axis_size("seq")
    tensor_place, seq_place = lax.axis_index("tensor"), lax.axis_index("seq")
    grid_count = lax.axis_size("dp") * seq_count
    grid_place = lax.axis_index("dp") * seq_count + seq_place
    local_count, width = block_input.shape
    group_count = local_count * tensor_count
    share = width // tensor_count
    bucket_count, heads = position_bias.shape
    head_cols = attn_in_weight.shape[2]
    experts = router_weight.shape[1]
    capacity = max(2, 2 * group_count // experts)
    tiles = group_count // TILE
    key_tiles = tiles * seq_count
    fast = seq_count == 2 and local_count == TILE and grid_count == 8

    def tiled(pieces):
        pieces = reorder(pieces, tensor_place)
        if local_count == TILE:
            return jnp.stack(pieces)
        return jnp.concatenate(pieces, axis=-1)[None]

    own_rows = jnp.concatenate(
        [
            jnp.transpose(block_input.astype(BF16)),
            jnp.pad(segment_ids.astype(BF16), ((0, 15), (0, 0))),
        ]
    )
    weight_piece = jnp.concatenate(
        [attn_in_weight[0], attn_in_weight[1], attn_in_weight[2], jnp.transpose(attn_out_weight)],
        axis=1,
    )
    if seq_count == 2:
        both_rows = jnp.stack([own_rows, swap(own_rows, "seq", 1)])
    else:
        both_rows = lax.all_gather(own_rows, "seq", axis=0, tiled=False)
    weight_pieces = gather_grid(weight_piece)
    row_pieces = gather_relative(both_rows, "tensor")
    if fast:
        own_first = jnp.int32(0)
    else:
        own_first = seq_place * tiles
        row_pieces = jnp.concatenate(reorder(row_pieces, tensor_place), axis=-1)
        if seq_count == 2:
            row_pieces = jnp.stack(reorder([row_pieces[0], row_pieces[1]], seq_place))
        row_pieces = row_pieces.reshape(seq_count, -1, tiles, TILE)
        row_pieces = [jnp.moveaxis(row_pieces, 2, 1).reshape(key_tiles, -1, TILE)]
    own = jnp.stack([grid_place, tensor_place, seq_place, own_first]).astype(jnp.int32)

    bias = bias_tiles(position_bias)
    in_t, out_t = jnp.transpose(expert_in[0]), jnp.transpose(expert_out[0])
    route_all = expert_ids[:, 0]
    expert_range = jnp.arange(experts, dtype=jnp.int32)
    route_hot = (route_all[:, None] == expert_range[None, :]).astype(jnp.int32)
    slot_rank = jnp.sum(jnp.cumsum(route_hot, axis=0) * route_hot, axis=-1) - 1
    target = (route_all * capacity + slot_rank).reshape(1, tiles, TILE, 1)
    places = jnp.arange(experts * capacity, dtype=jnp.int32).reshape(experts, 1, 1, capacity)
    onehot = (target == places).astype(BF16)
    chunks = 2 if capacity >= TILE else 1
    slots = capacity // chunks
    spread = max(1, TILE // capacity)
    merged = max(1, TILE // (slots * spread))

    def exchange(values):
        return lax.all_to_all(values, ("dp", "seq"), split_axis=0, concat_axis=0, tiled=True)

    def joined(values):
        if spread == 1:
            return values
        shape = values.shape
        values = values.reshape((-1, spread) + shape[1:])
        return jnp.moveaxis(values, 1, -2).reshape(
            (shape[0] // spread,) + shape[1:-1] + (spread * shape[-1],)
        )

    def parted(values):
        if spread == 1:
            return values
        shape = values.shape
        values = values.reshape(shape[:-1] + (spread, shape[-1] // spread))
        return jnp.moveaxis(values, -2, 1).reshape((-1,) + shape[1:-1] + (shape[-1] // spread,))

    half = tensor_count // 2
    grad_rows = jnp.transpose(out_grad.astype(BF16)).reshape(half, 2, share, local_count)
    core = tensor_place & 1
    grad_mine = lax.dynamic_index_in_dim(grad_rows, core, 1, keepdims=False)
    grad_theirs = lax.dynamic_index_in_dim(grad_rows, core ^ 1, 1, keepdims=False)
    grad_pair = jnp.stack([grad_mine, swap(grad_theirs, "tensor", 1)])
    grad_far = swap(grad_pair, "tensor", 2)
    grad_here = tiled([grad_pair[0], grad_pair[1], grad_far[0], grad_far[1]])
    grad_buffer = einsum("nkdq,enqs->ekds", grad_here, onehot).astype(BF16)

    gain_one = norm_gains[0][:, None]
    gain_two = norm_gains[1][:, None]
    gain_one, bias, in_t, out_t, target, gain_two = lax.optimization_barrier(
        (gain_one, bias, in_t, out_t, target, gain_two)
    )
    meta, queries, keys_values, normed_tiles, input_share, in_flat, out_blocks, out_t_blocks = (
        project(own, row_pieces, weight_pieces, gain_one, tiles, key_tiles, share)
    )
    queries, grad_buffer = lax.optimization_barrier((queries, grad_buffer))
    grad_arrived = joined(exchange(grad_buffer))
    exact, attended, logs, attn_even, attn_odd = attend(
        meta, queries, keys_values, bias, out_blocks
    )
    attn_share = sum_chips(sum_cores(attn_even, attn_odd, "tensor"), "tensor")
    state_share = (input_share.astype(F32) + attn_share).astype(BF16)
    state_share, grad_arrived = lax.optimization_barrier((state_share, grad_arrived))
    grad_other = swap(grad_arrived, "tensor", 1)

    weights = (
        expert_in[0],
        in_t,
        expert_out[0],
        router_weight,
        jnp.transpose(router_weight),
        gain_two,
    )
    arrivals = []
    for c in range(chunks):
        buffer = einsum("ndq,enqs->eds", state_share, onehot[..., c * slots : (c + 1) * slots])
        arrivals.append(joined(exchange(buffer.astype(BF16))))
    chains = 2 if arrivals[0].shape[0] // merged % 2 == 0 else 1
    saved, halves = [], []
    small = jnp.zeros((experts + 1, width), F32)
    for c in range(chunks):
        pieces = gather_relative(arrivals[c], "tensor")
        if halves:
            pieces[0], halves[-1] = lax.optimization_barrier((pieces[0], halves[-1]))
        kept, sent, normed_two, full, activated, pre_grad, gate, gain_sum, router_sum = run_expert(
            own, pieces, (grad_arrived, grad_other), c, merged, chains, weights
        )
        saved.append((normed_two, full, activated, pre_grad, gate))
        halves.append(sum_cores(kept, sent, "tensor"))
        gain_part = jnp.sum(gain_sum, axis=1) / norm_gains[1]
        small = small + jnp.concatenate([router_sum, gain_part[None]])
    own_late, halves[-1] = lax.optimization_barrier((own, halves[-1]))
    result_even, result_odd, grad_expert_in, grad_expert_out = run_result(
        own_late, saved, merged, out_t
    )
    state_grad = lax.dynamic_index_in_dim(grad_here, tensor_place // 2, 1, keepdims=False)
    state_grad = state_grad.astype(F32)
    for c in range(chunks):
        total = parted(sum_chips(halves[c], "tensor").astype(BF16))
        state_grad = state_grad + einsum(
            "eds,enqs->ndq", exchange(total), onehot[..., c * slots : (c + 1) * slots]
        )
    state_grad = state_grad.astype(BF16)
    result_total = sum_chips(sum_cores(result_even, result_odd, "tensor"), "tensor").astype(BF16)
    state_grad, result_total = lax.optimization_barrier((state_grad, result_total))
    result_back = exchange(parted(result_total))

    branch = gather_relative(state_grad, "tensor")
    dq, dkv, bias_rows = attend_back(
        meta, queries, keys_values, bias, out_t_blocks, exact, logs, branch, bucket_count
    )
    dq, dkv, bias_rows, result_back = lax.optimization_barrier((dq, dkv, bias_rows, result_back))

    if fast:
        far_even, far_odd, own_even, own_odd, weight_even, weight_odd, gain_part = project_back(
            True, own, dq, dkv, normed_tiles, in_flat, attended, branch, grid_count
        )
        far_half = sum_cores(far_even, far_odd, "tensor")
        own_half = sum_cores(own_even, own_odd, "tensor")
        weight_half = weight_even.astype(F32) + swap(weight_odd, "seq", 1).astype(F32)
        far_half, own_half, weight_half, small, gain_part, bias_rows, result_back = (
            lax.optimization_barrier(
                (far_half, own_half, weight_half, small, gain_part, bias_rows, result_back)
            )
        )
        far_sum = sum_chips(far_half, "tensor").astype(BF16)
        sums = [
            own_half[0],
            swap(own_half[1].astype(BF16), "tensor", 2),
            swap(far_sum, "seq", 1),
        ]
        weight_grad = weight_half[0]
        for k in range(1, grid_count // 2):
            weight_grad = weight_grad + swap(weight_half[k].astype(BF16), "dp", k).astype(F32)
    else:
        row_part, weight_part, gain_part = project_back(
            False, own, dq, dkv, normed_tiles, in_flat, attended, branch, grid_count
        )
        row_part = lax.psum_scatter(row_part, "seq", scatter_dimension=0, tiled=True)
        row_part = jnp.moveaxis(row_part, 0, 1).reshape(width, tensor_count, local_count)
        blocks = [
            lax.dynamic_index_in_dim(row_part, tensor_place ^ k, 1, keepdims=False)
            for k in range(tensor_count)
        ]
        halved = sum_cores(jnp.stack(blocks[0::2]), jnp.stack(blocks[1::2]), "tensor")
        sums = [sum_chips(halved, "tensor")]
        weight_grad = lax.psum_scatter(
            weight_part, ("dp", "seq"), scatter_dimension=0, tiled=True
        ).astype(F32)
    grad_attn_in = jnp.stack(
        [weight_grad[:, c * head_cols : (c + 1) * head_cols] for c in range(3)]
    )
    grad_attn_out = jnp.transpose(weight_grad[:, 3 * head_cols :])

    bias_padded = lax.dynamic_update_slice_in_dim(
        jnp.zeros((heads * tensor_count, bucket_count), F32),
        jnp.sum(bias_rows, axis=2),
        tensor_place * heads,
        0,
    )
    small = sum_all(
        jnp.concatenate(
            [small.reshape(-1), gain_part[:, 0] / norm_gains[0], bias_padded.reshape(-1)]
        ),
        ("tensor", "seq", "dp"),
    )
    first, second = experts * width, (experts + 1) * width
    grad_router = jnp.transpose(small[:first].reshape(experts, width))
    grad_gains = jnp.stack([small[second : second + width], small[first:second]])
    bias_sum = small[second + width :].reshape(heads * tensor_count, bucket_count)
    grad_bias = jnp.transpose(lax.dynamic_slice_in_dim(bias_sum, tensor_place * heads, heads, 0))

    result_share = attn_share + einsum("eds,enqs->ndq", result_back, onehot)
    result_share = jnp.moveaxis(result_share.astype(BF16), 0, 1).reshape(
        share, tensor_count, local_count
    )
    result_rows = lax.all_to_all(
        jnp.moveaxis(result_share, 1, 0), "tensor", split_axis=0, concat_axis=0, tiled=True
    ).reshape(width, local_count)
    if local_count == TILE:
        own_branch = [
            lax.dynamic_index_in_dim(piece, tensor_place, 0, keepdims=False) for piece in branch
        ]
    else:
        own_branch = [
            lax.dynamic_slice_in_dim(piece[0], tensor_place * local_count, local_count, 1)
            for piece in branch
        ]
    own_branch = jnp.concatenate(reorder(own_branch, tensor_place))
    block_out, input_grad = finish(block_input, gain_one, own_branch, result_rows, sums)
    return (
        block_out,
        input_grad,
        grad_attn_in,
        grad_attn_out,
        grad_bias,
        grad_gains,
        grad_router,
        grad_expert_in[None],
        grad_expert_out[None],
    )


def solution(mesh):
    return jax.shard_map(
        shards,
        mesh=mesh,
        in_specs=(
            P(("dp", "seq", "tensor"), None),
            P(None, ("dp", "seq"), "tensor"),
            P("tensor", ("dp", "seq")),
            P(None, "tensor"),
            P(),
            P(),
            P(("dp", "seq"), None, "tensor"),
            P(("dp", "seq"), "tensor", None),
            P("dp", ("seq", "tensor")),
            P(("dp", "seq"), None),
            P(("dp", "seq", "tensor"), None),
        ),
        out_specs=(
            P(("dp", "seq", "tensor"), None),
            P(("dp", "seq", "tensor"), None),
            P(None, ("dp", "seq"), "tensor"),
            P("tensor", ("dp", "seq")),
            P(None, "tensor"),
            P(),
            P(),
            P(("dp", "seq"), None, "tensor"),
            P(("dp", "seq"), "tensor", None),
        ),
        check_vma=False,
    )
```

```python
import functools
import math

import jax
import jax.numpy as jnp
from jax import lax
from jax.experimental import pallas as pl
from jax.experimental.pallas import tpu as pltpu
from jax.sharding import PartitionSpec as P

EPSILON = 1e-06
EDGES = (1, 2, 3, 4, 5, 6, 7, 8, 12, 16, 23, 32, 46, 64, 91)
TILE = 256
HALF = TILE // 2
LOG2E = math.log2(math.e)
SCALE = 0.125
MASKED = -1e30
LOWEST = -1e29
EXTRA = 16
VMEM_BYTES = 48 * 1024 * 1024
GELU_A = math.sqrt(2.0 / math.pi)
GELU_B = 0.044715
BF16 = jnp.bfloat16
F32 = jnp.float32


def dot(left_side, right_side):
    return jnp.dot(left_side, right_side, preferred_element_type=F32)


def dot_rows(left_side, right_side):
    return lax.dot_general(
        left_side, right_side, (((1,), (1,)), ((), ())), preferred_element_type=F32
    )


def einsum(formula, *operands):
    return jnp.einsum(formula, *operands, preferred_element_type=F32)


def swap(values, axis, bit):
    count = lax.axis_size(axis)
    return lax.ppermute(values, axis, [(i, i ^ bit) for i in range(count)])


def bits_of(count):
    return [1 << i for i in range(count.bit_length() - 1)]


def gather_relative(values, axis):
    pieces = {0: values}
    for bit in reversed(bits_of(lax.axis_size(axis))):
        for place in list(pieces):
            pieces[place ^ bit] = swap(pieces[place], axis, bit)
    return [pieces[place] for place in range(len(pieces))]


def sum_cores(kept, sent, axis):
    return kept.astype(F32) + swap(sent.astype(BF16), axis, 1).astype(F32)


def sum_chips(total, axis):
    bit = 2
    while bit < lax.axis_size(axis):
        pairs = total.reshape((-1, 2) + total.shape[1:])
        total = pairs[:, 0] + swap(pairs[:, 1].astype(BF16), axis, bit).astype(F32)
        bit *= 2
    return total[0]


def reorder(pieces, own_index):
    for bit in bits_of(len(pieces)):
        flip = (own_index & bit) != 0
        pieces = [
            jnp.where(flip, pieces[place ^ bit], pieces[place]) for place in range(len(pieces))
        ]
    return pieces


def gather_grid(values):
    dp_count, seq_count = lax.axis_size("dp"), lax.axis_size("seq")
    if dp_count > 4 or seq_count != 2:
        return [lax.all_gather(values, ("dp", "seq"), axis=0, tiled=True)]
    columns = [values] + [swap(values, "dp", place) for place in range(1, dp_count)]
    near = swap(values, "seq", 1)
    far = swap(jnp.stack(columns[1:]), "seq", 1)
    pieces = [values, near]
    for place in range(1, dp_count):
        pieces += [columns[place], far[place - 1]]
    return pieces


def sum_all(values, axes):
    for axis in axes:
        for bit in bits_of(lax.axis_size(axis)):
            values = values + swap(values, axis, bit)
    return values


def bucket_of(relative, half_count):
    magnitude = jnp.abs(relative)
    counted = jnp.zeros(relative.shape, jnp.int32)
    for edge_value in EDGES:
        counted = counted + (magnitude >= edge_value).astype(jnp.int32)
    return counted + jnp.where(relative > 0, half_count, 0).astype(jnp.int32)


def near_buckets(half_count):
    shape = (3, HALF, HALF)
    relative = (
        (lax.broadcasted_iota(jnp.int32, shape, 0) - 1) * HALF
        + lax.broadcasted_iota(jnp.int32, shape, 1)
        - lax.broadcasted_iota(jnp.int32, shape, 2)
    )
    return bucket_of(relative, half_count)


def bias_tiles(position_bias):
    bucket_count, heads = position_bias.shape
    half_count = bucket_count // 2
    grid = near_buckets(half_count)
    near = jnp.zeros((heads, 3, HALF, HALF), F32)
    for bucket_index in range(bucket_count):
        near = near + jnp.where(
            (grid == bucket_index)[None], position_bias[bucket_index][:, None, None, None], 0.0
        )
    before, same, after = near[:, 0], near[:, 1], near[:, 2]
    far_before = jnp.broadcast_to(
        position_bias[half_count - 1][:, None, None], (heads, HALF, HALF)
    )
    far_after = jnp.broadcast_to(
        position_bias[bucket_count - 1][:, None, None], (heads, HALF, HALF)
    )

    def square(a, b, c, d):
        return jnp.concatenate(
            [jnp.concatenate([a, b], axis=2), jnp.concatenate([c, d], axis=2)], axis=1
        )

    tiles = jnp.stack(
        [
            square(far_before, far_before, far_before, far_before),
            square(far_before, far_before, before, far_before),
            square(same, before, after, same),
            square(far_after, after, far_after, far_after),
            square(far_after, far_after, far_after, far_after),
        ]
    )
    return tiles * LOG2E


def span_of(meta_ref, query_tile, key_tiles):
    opening, closing = meta_ref[1], meta_ref[2]
    first = query_tile * TILE
    last = first + TILE - 1
    begin = jnp.where(first < opening, 0, jnp.where(first < closing, opening, closing))
    end = jnp.where(last < opening, opening, jnp.where(last < closing, closing, key_tiles * TILE))
    return begin // TILE, (end + TILE - 1) // TILE


def document_row(meta_ref, tile):
    place = tile * TILE + lax.broadcasted_iota(jnp.int32, (EXTRA, TILE), 1)
    return (place >= meta_ref[1]).astype(jnp.int32) + (place >= meta_ref[2]).astype(jnp.int32)


def key_rows(meta_ref, tile):
    row = lax.broadcasted_iota(jnp.int32, (EXTRA, TILE), 0)
    differs = jnp.where(document_row(meta_ref, tile) != row, MASKED, 0.0)
    return jnp.where(row < 3, differs, jnp.where(row < 6, 1.0, 0.0)).astype(BF16)


def query_rows(meta_ref, tile, terms):
    row = lax.broadcasted_iota(jnp.int32, (EXTRA, TILE), 0)
    agrees = jnp.where(document_row(meta_ref, tile) == row, 1.0, 0.0)
    return jnp.where(row < 3, agrees, three_rows(row - 3, terms)).astype(BF16)


def three_rows(row, terms):
    result = jnp.zeros(row.shape, F32)
    for i, term in enumerate(terms):
        result = jnp.where(row == i, term, result)
    return result


def split_three(values):
    first = values.astype(BF16).astype(F32)
    second = (values - first).astype(BF16).astype(F32)
    return first, second, values - first - second


def attend_kernel(
    meta_ref,
    q_ref,
    kv_ref,
    bias_ref,
    weight_ref,
    exact_ref,
    out_ref,
    log_ref,
    even_ref,
    odd_ref,
    key_ref,
    query_ref,
    sum_ref,
):
    key_tiles = kv_ref.shape[0]
    heads = bias_ref.shape[1]
    size = q_ref.shape[1] // heads

    def turn(j, carry):
        kept = meta_ref[3 + j]
        extra = key_rows(meta_ref, j)
        for h in range(heads):
            rows = kv_ref[kept, h * size : (h + 1) * size, :]
            key_ref[kept, h] = jnp.concatenate([rows, extra], axis=0).T
        return carry

    lax.fori_loop(0, key_tiles, turn, 0)
    ones = jnp.ones((EXTRA, TILE), BF16)

    def query_body(i, carry):
        tile = meta_ref[3 + key_tiles + i]
        place = tile % meta_ref[0]
        begin, end = span_of(meta_ref, tile, key_tiles)
        extra = query_rows(meta_ref, tile, ())
        for h in range(heads):
            rows = q_ref[i, h * size : (h + 1) * size, :]
            query_ref[h] = jnp.concatenate([rows, extra], axis=0)
        sum_ref[...] = jnp.zeros_like(sum_ref)

        def key_body(j, peaks):
            kept = meta_ref[3 + j]
            kind = jnp.clip(j - tile, -2, 2) + 2
            scores = [
                dot(key_ref[kept, h], query_ref[h]) + bias_ref[kind, h] for h in range(heads)
            ]
            new_peaks = [
                jnp.maximum(peaks[h], jnp.max(scores[h], axis=0, keepdims=True))
                for h in range(heads)
            ]
            weights = [jnp.exp2(scores[h] - new_peaks[h]).astype(BF16) for h in range(heads)]
            added = []
            for h in range(heads):
                values = kv_ref[kept, (heads + h) * size : (heads + h + 1) * size, :]
                added.append(dot(jnp.concatenate([values, ones], axis=0), weights[h]))
            for h in range(heads):
                sum_ref[h] = sum_ref[h] * jnp.exp2(peaks[h] - new_peaks[h]) + added[h]
            return tuple(new_peaks)

        start = tuple(jnp.full((1, TILE), LOWEST, F32) for _ in range(heads))
        peaks = lax.fori_loop(begin, end, key_body, start)
        for h in range(heads):
            rows = slice(h * size, (h + 1) * size)
            total = sum_ref[h, size : size + 1, :]
            result = sum_ref[h, :size, :] * (1.0 / total)
            exact_ref[i, rows, :] = result
            out_ref[place, rows, :] = result.astype(BF16)
            log_ref[i, h] = peaks[h] + jnp.log2(total)
        attended = out_ref[place]
        for k in range(weight_ref.shape[0]):
            block = dot(weight_ref[k], attended).astype(BF16)
            (odd_ref if k & 1 else even_ref)[k // 2, place] = block
        return carry

    lax.fori_loop(0, q_ref.shape[0], query_body, 0)


def estimate(queries, key_tiles, products):
    pairs = queries.shape[0] * TILE * key_tiles * TILE
    return pl.CostEstimate(
        flops=2 * products * pairs * queries.shape[1],
        bytes_accessed=8 * pairs,
        transcendentals=3 * pairs,
    )


def whole_specs(count):
    return [pl.BlockSpec(memory_space=pltpu.VMEM)] * count


def attend(meta, queries, keys_values, bias, out_blocks):
    query_tiles, width, _ = queries.shape
    key_tiles = keys_values.shape[0]
    heads = bias.shape[1]
    parts, share, _ = out_blocks.shape
    blocks = jax.ShapeDtypeStruct((parts // 2, query_tiles, share, TILE), BF16)
    return pl.pallas_call(
        attend_kernel,
        out_shape=(
            jax.ShapeDtypeStruct(queries.shape, F32),
            jax.ShapeDtypeStruct(queries.shape, BF16),
            jax.ShapeDtypeStruct((query_tiles, heads, 1, TILE), F32),
            blocks,
            blocks,
        ),
        in_specs=[pl.BlockSpec(memory_space=pltpu.SMEM)] + whole_specs(4),
        out_specs=tuple(whole_specs(5)),
        scratch_shapes=[
            pltpu.VMEM((key_tiles, heads, TILE, width // heads + EXTRA), BF16),
            pltpu.VMEM((heads, width // heads + EXTRA, TILE), BF16),
            pltpu.VMEM((heads, width // heads + EXTRA, TILE), F32),
        ],
        compiler_params=pltpu.CompilerParams(vmem_limit_bytes=VMEM_BYTES),
        cost_estimate=estimate(queries, key_tiles, 2),
        name="attend",
    )(meta, queries, keys_values, bias, out_blocks)


def bucket_rows(tiles_ref, rows_ref):
    heads, bucket_count = rows_ref.shape[:2]
    half_count = bucket_count // 2
    offset = lax.broadcasted_iota(jnp.int32, (HALF, HALF), 0) - lax.broadcasted_iota(
        jnp.int32, (HALF, HALF), 1
    )
    grids = [bucket_of(offset + shift * HALF, half_count) for shift in (-1, 0, 1)]
    first, last = slice(0, HALF), slice(HALF, TILE)

    def column_sums(values):
        return jnp.sum(values, axis=0, keepdims=True)

    def head_body(h, carry):
        before = tiles_ref[2, h, first, last] + tiles_ref[1, h, last, first]
        same = tiles_ref[2, h, first, first] + tiles_ref[2, h, last, last]
        after = tiles_ref[2, h, last, first] + tiles_ref[3, h, first, last]
        far_before = column_sums(tiles_ref[0, h, :, first] + tiles_ref[0, h, :, last])
        far_before += column_sums(tiles_ref[1, h, first, first] + tiles_ref[1, h, first, last])
        far_before += column_sums(tiles_ref[1, h, last, last])
        far_after = column_sums(tiles_ref[4, h, :, first] + tiles_ref[4, h, :, last])
        far_after += column_sums(tiles_ref[3, h, last, first] + tiles_ref[3, h, last, last])
        far_after += column_sums(tiles_ref[3, h, first, first])
        for bucket_index in range(bucket_count):
            row = column_sums(jnp.where(grids[1] == bucket_index, same, 0.0))
            if 0 < bucket_index < half_count:
                row += column_sums(jnp.where(grids[0] == bucket_index, before, 0.0))
            if bucket_index > half_count:
                row += column_sums(jnp.where(grids[2] == bucket_index, after, 0.0))
            if bucket_index == half_count - 1:
                row += far_before
            if bucket_index == bucket_count - 1:
                row += far_after
            rows_ref[h, bucket_index : bucket_index + 1, :] = row
        return carry

    lax.fori_loop(0, heads, head_body, 0)


def attend_back_kernel(
    meta_ref,
    q_ref,
    kv_ref,
    bias_ref,
    weight_ref,
    exact_ref,
    log_ref,
    *refs,
):
    parts = weight_ref.shape[0]
    branch_refs = refs[:parts]
    (
        dq_ref,
        dkv_ref,
        rows_ref,
        tiles_ref,
        key_ref,
        value_ref,
        query_ref,
        grad_ref,
        dq_sum,
        dkv_sum,
    ) = refs[parts:]
    key_tiles = kv_ref.shape[0]
    heads = bias_ref.shape[1]
    size = q_ref.shape[1] // heads

    row = lax.broadcasted_iota(jnp.int32, (EXTRA, TILE), 0)
    ones = jnp.where(row < 3, 1.0, 0.0).astype(BF16)

    def turn(j, carry):
        kept = meta_ref[3 + j]
        extra = key_rows(meta_ref, j)
        for h in range(heads):
            rows = kv_ref[kept, h * size : (h + 1) * size, :]
            key_ref[kept, h] = jnp.concatenate([rows, extra], axis=0).T
            rows = kv_ref[kept, (heads + h) * size : (heads + h + 1) * size, :]
            value_ref[kept, h] = jnp.concatenate([rows, ones], axis=0).T
        return carry

    lax.fori_loop(0, key_tiles, turn, 0)
    dkv_sum[...] = jnp.zeros_like(dkv_sum)
    tiles_ref[...] = jnp.zeros_like(tiles_ref)

    def query_body(i, carry):
        tile = meta_ref[3 + key_tiles + i]
        place = tile % meta_ref[0]
        begin, end = span_of(meta_ref, tile, key_tiles)
        dq_sum[...] = jnp.zeros_like(dq_sum)
        grad_sum = dot(weight_ref[0], branch_refs[0][place])
        for k in range(1, parts):
            grad_sum += dot(weight_ref[k], branch_refs[k][place])
        for h in range(heads):
            rows = slice(h * size, (h + 1) * size)
            grad = grad_sum[rows].astype(BF16)
            centre = jnp.sum(grad.astype(F32) * exact_ref[i, rows, :], axis=0, keepdims=True)
            extra = three_rows(row, split_three(-centre)).astype(BF16)
            grad_ref[h] = jnp.concatenate([grad, extra], axis=0)
            extra = query_rows(meta_ref, tile, split_three(-log_ref[i, h]))
            query_ref[h] = jnp.concatenate([q_ref[i, rows, :], extra], axis=0)

        def key_body(j, inner):
            kept = meta_ref[3 + j]
            kind = jnp.clip(j - tile, -2, 2) + 2
            probs = [
                jnp.exp2(dot(key_ref[kept, h], query_ref[h]) + bias_ref[kind, h])
                for h in range(heads)
            ]
            score_grads = [probs[h] * dot(value_ref[kept, h], grad_ref[h]) for h in range(heads)]
            low_probs = [prob.astype(BF16) for prob in probs]
            low_grads = [score_grad.astype(BF16) for score_grad in score_grads]
            key_adds, value_adds, query_adds = [], [], []
            for h in range(heads):
                rows = slice(h * size, (h + 1) * size)
                key_adds.append(dot_rows(q_ref[i, rows, :], low_grads[h]))
                value_adds.append(dot_rows(grad_ref[h, :size, :], low_probs[h]))
                query_adds.append(dot(kv_ref[kept, rows, :], low_grads[h]))
            for h in range(heads):
                rows = slice(h * size, (h + 1) * size)
                value_rows = slice((heads + h) * size, (heads + h + 1) * size)
                tiles_ref[kind, h] += score_grads[h]
                dkv_sum[kept, rows, :] += key_adds[h]
                dkv_sum[kept, value_rows, :] += value_adds[h]
                dq_sum[rows, :] += query_adds[h]
            return inner

        lax.fori_loop(begin, end, key_body, 0)
        dq_ref[i] = (dq_sum[...] * SCALE).astype(BF16)
        return carry

    lax.fori_loop(0, q_ref.shape[0], query_body, 0)
    middle = heads * size
    dkv_ref[:, :middle, :] = (dkv_sum[:, :middle, :] * (1.0 / LOG2E)).astype(BF16)
    dkv_ref[:, middle:, :] = dkv_sum[:, middle:, :].astype(BF16)
    bucket_rows(tiles_ref, rows_ref)


def attend_back(meta, queries, keys_values, bias, out_blocks, exact, logs, branch, buckets):
    key_tiles = keys_values.shape[0]
    heads = bias.shape[1]
    size = queries.shape[1] // heads
    return pl.pallas_call(
        attend_back_kernel,
        out_shape=(
            jax.ShapeDtypeStruct(queries.shape, BF16),
            jax.ShapeDtypeStruct(keys_values.shape, BF16),
            jax.ShapeDtypeStruct((heads, buckets, HALF), F32),
        ),
        in_specs=[pl.BlockSpec(memory_space=pltpu.SMEM)] + whole_specs(6 + len(branch)),
        out_specs=tuple(whole_specs(3)),
        scratch_shapes=[
            pltpu.VMEM(bias.shape, F32),
            pltpu.VMEM((key_tiles, heads, TILE, size + EXTRA), BF16),
            pltpu.VMEM((key_tiles, heads, TILE, size + EXTRA), BF16),
            pltpu.VMEM((heads, size + EXTRA, TILE), BF16),
            pltpu.VMEM((heads, size + EXTRA, TILE), BF16),
            pltpu.VMEM(queries.shape[1:], F32),
            pltpu.VMEM(keys_values.shape, F32),
        ],
        compiler_params=pltpu.CompilerParams(vmem_limit_bytes=VMEM_BYTES),
        cost_estimate=estimate(queries, key_tiles, 5),
        name="attend_back",
    )(meta, queries, keys_values, bias, out_blocks, exact, logs, *branch)


def project_kernel(piece_count, weight_count, tiles, share, own_ref, *refs):
    piece_refs = refs[:piece_count]
    weight_refs = refs[piece_count : piece_count + weight_count]
    gain_ref = refs[piece_count + weight_count]
    (
        meta_ref,
        q_ref,
        kv_ref,
        normed_ref,
        input_ref,
        in_ref,
        out_ref,
        out_t_ref,
        block_ref,
        turned_ref,
    ) = refs[piece_count + weight_count + 1 :]
    grid_place, tensor_place, seq_place, own_first = (own_ref[i] for i in range(4))
    width = gain_ref.shape[0]
    head_cols = q_ref.shape[1]
    columns = turned_ref.shape[0]
    for k in range(weight_count):
        place = grid_place ^ k if weight_count > 1 else 0
        block_ref[place] = weight_refs[k][...]
    full = block_ref[...].reshape(width, columns)
    in_ref[...] = full[:, : 3 * head_cols]
    turned_ref[...] = full.T
    blocks_here = width // share
    tall = block_ref.shape[1]
    per = share // tall if weight_count > 1 else 1
    for k in range(blocks_here):
        if weight_count > 1:
            block = block_ref[pl.ds((tensor_place ^ k) * per, per), :, 3 * head_cols :]
            block = block.reshape(share, head_cols)
        else:
            start = pl.multiple_of((tensor_place ^ k) * share, share)
            block = block_ref[0, pl.ds(start, share), 3 * head_cols :]
        out_ref[k] = block
        out_t_ref[k] = block.T
    key_tiles = kv_ref.shape[0]
    early = jnp.zeros((1, TILE), F32)
    late = jnp.zeros((1, TILE), F32)
    gain = gain_ref[...]
    for k in range(piece_count):
        for s in range(piece_refs[0].shape[0]):
            kept = s + k
            rows = piece_refs[k][s, :width, :].astype(F32)
            ids = piece_refs[k][s, width : width + 16, :][:1].astype(F32)
            early += (ids < 0.5).astype(F32)
            late += (ids < 1.5).astype(F32)
            root = lax.rsqrt(jnp.sum(rows * rows, axis=0, keepdims=True) * (1.0 / width) + EPSILON)
            normed = (rows * root * gain).astype(BF16)
            normed_ref[kept] = normed
            kv_ref[kept] = dot(turned_ref[head_cols : 3 * head_cols, :], normed).astype(BF16)
    for i in range(tiles):
        normed = normed_ref[own_first + i]
        q_ref[i] = (dot(turned_ref[:head_cols, :], normed) * (SCALE * LOG2E)).astype(BF16)
        start = pl.multiple_of(tensor_place * share, share)
        if piece_count > 1:
            input_ref[tensor_place ^ i] = piece_refs[i][0, pl.ds(start, share), :]
        else:
            input_ref[i] = piece_refs[0][own_first + i, pl.ds(start, share), :]
    meta_ref[0] = tiles
    meta_ref[1] = jnp.sum(early).astype(jnp.int32)
    meta_ref[2] = jnp.sum(late).astype(jnp.int32)
    for j in range(key_tiles):
        if piece_count > 1:
            meta_ref[3 + j] = ((j // tiles) ^ seq_place) * tiles + ((j % tiles) ^ tensor_place)
        else:
            meta_ref[3 + j] = j
    for i in range(tiles):
        shift = tensor_place ^ i if piece_count > 1 else i
        meta_ref[3 + key_tiles + i] = seq_place * tiles + shift


def project(own, pieces, weight_pieces, gain, tiles, key_tiles, share):
    width = gain.shape[0]
    columns = weight_pieces[0].shape[1]
    head_cols = columns // 4
    parts = width // share
    return pl.pallas_call(
        functools.partial(project_kernel, len(pieces), len(weight_pieces), tiles, share),
        out_shape=(
            jax.ShapeDtypeStruct((3 + key_tiles + tiles,), jnp.int32),
            jax.ShapeDtypeStruct((tiles, head_cols, TILE), BF16),
            jax.ShapeDtypeStruct((key_tiles, 2 * head_cols, TILE), BF16),
            jax.ShapeDtypeStruct((key_tiles, width, TILE), BF16),
            jax.ShapeDtypeStruct((tiles, share, TILE), BF16),
            jax.ShapeDtypeStruct((width, 3 * head_cols), BF16),
            jax.ShapeDtypeStruct((parts, share, head_cols), BF16),
            jax.ShapeDtypeStruct((parts, head_cols, share), BF16),
        ),
        in_specs=[pl.BlockSpec(memory_space=pltpu.SMEM)]
        + whole_specs(len(pieces) + len(weight_pieces) + 1),
        out_specs=(pl.BlockSpec(memory_space=pltpu.SMEM),) + tuple(whole_specs(7)),
        scratch_shapes=[
            pltpu.VMEM((len(weight_pieces),) + weight_pieces[0].shape, BF16),
            pltpu.VMEM((columns, width), BF16),
        ],
        compiler_params=pltpu.CompilerParams(vmem_limit_bytes=VMEM_BYTES),
        cost_estimate=pl.CostEstimate(
            flops=6 * key_tiles * TILE * width * head_cols,
            bytes_accessed=8 * key_tiles * TILE * width,
            transcendentals=0,
        ),
        name="project",
    )(own, *pieces, *weight_pieces, gain)


def project_back_kernel(fast, parts, own_ref, dq_ref, dkv_ref, normed_ref, in_ref, attended_ref, *refs):
    branch_refs = refs[:parts]
    if fast:
        far_even, far_odd, own_even, own_odd, weight_even, weight_odd, gain_ref, full_ref = refs[
            parts:
        ]
    else:
        part_ref, weight_ref, gain_ref, full_ref = refs[parts:]
    grid_place, tensor_place, seq_place, own_first = (own_ref[i] for i in range(4))
    tiles, head_cols, _ = dq_ref.shape
    key_tiles = dkv_ref.shape[0]
    width = in_ref.shape[0]
    share = width // parts
    key_weight = in_ref[:, head_cols:]
    query_weight = in_ref[:, :head_cols]
    if fast:
        for n in range(tiles):
            block = dot(key_weight, dkv_ref[tiles + n]).astype(BF16)
            (far_odd if n & 1 else far_even)[n // 2] = block
        for n in range(tiles):
            block = dot(key_weight, dkv_ref[n]) + dot(query_weight, dq_ref[n])
            (own_odd if n & 1 else own_even)[n // 2] = block.astype(BF16)
    else:
        for n in range(key_tiles):
            part_ref[n] = dot(key_weight, dkv_ref[n]).astype(BF16)
        for n in range(tiles):
            block = part_ref[own_first + n].astype(F32) + dot(query_weight, dq_ref[n])
            part_ref[own_first + n] = block.astype(BF16)
    query_sum = dot_rows(normed_ref[own_first], dq_ref[0])
    for n in range(1, tiles):
        query_sum += dot_rows(normed_ref[own_first + n], dq_ref[n])
    key_sum = dot_rows(normed_ref[0], dkv_ref[0])
    for n in range(1, key_tiles):
        key_sum += dot_rows(normed_ref[n], dkv_ref[n])
    gain_ref[...] = jnp.sum(
        query_sum * query_weight.astype(F32), axis=1, keepdims=True
    ) + jnp.sum(key_sum * key_weight.astype(F32), axis=1, keepdims=True)
    full_ref[:, :head_cols] = query_sum.astype(BF16)
    full_ref[:, head_cols : 3 * head_cols] = key_sum.astype(BF16)
    for k in range(parts):
        block = dot_rows(branch_refs[k][0], attended_ref[0])
        for n in range(1, tiles):
            block += dot_rows(branch_refs[k][n], attended_ref[n])
        start = pl.multiple_of((tensor_place ^ k) * share, share)
        full_ref[pl.ds(start, share), 3 * head_cols :] = block.astype(BF16)
    if fast:
        tall = weight_even.shape[1]
        for k in range(weight_even.shape[0]):
            place = grid_place ^ (2 * k)
            weight_even[k] = full_ref[pl.ds(pl.multiple_of(place * tall, tall), tall), :]
            weight_odd[k] = full_ref[pl.ds(pl.multiple_of((place ^ 1) * tall, tall), tall), :]
    else:
        weight_ref[...] = full_ref[...]


def project_back(fast, own, dq, dkv, normed, in_flat, attended, branch, grid_count):
    tiles, head_cols, _ = dq.shape
    key_tiles = dkv.shape[0]
    width = in_flat.shape[0]
    parts = len(branch)
    columns = 4 * head_cols
    if fast:
        block = jax.ShapeDtypeStruct((parts // 2, width, TILE), BF16)
        weight = jax.ShapeDtypeStruct((grid_count // 2, width // grid_count, columns), BF16)
        shapes = (block,) * 4 + (weight,) * 2
    else:
        shapes = (
            jax.ShapeDtypeStruct((key_tiles, width, TILE), BF16),
            jax.ShapeDtypeStruct((width, columns), BF16),
        )
    shapes = shapes + (jax.ShapeDtypeStruct((width, 1), F32),)
    return pl.pallas_call(
        functools.partial(project_back_kernel, fast, parts),
        out_shape=shapes,
        in_specs=[pl.BlockSpec(memory_space=pltpu.SMEM)] + whole_specs(5 + parts),
        out_specs=tuple(whole_specs(len(shapes))),
        scratch_shapes=[pltpu.VMEM((width, columns), BF16)],
        compiler_params=pltpu.CompilerParams(vmem_limit_bytes=VMEM_BYTES),
        cost_estimate=pl.CostEstimate(
            flops=12 * key_tiles * TILE * width * head_cols,
            bytes_accessed=8 * key_tiles * TILE * width,
            transcendentals=0,
        ),
        name="project_back",
    )(own, dq, dkv, normed, in_flat, attended, *branch)


def finish_kernel(input_ref, gain_ref, branch_ref, result_ref, *refs):
    sum_refs = refs[:-2]
    out_ref, grad_ref = refs[-2:]
    rows = input_ref[...]
    width = rows.shape[1]
    values = rows.T
    gain = gain_ref[...]
    grad = sum_refs[0][...].astype(F32)
    for ref in sum_refs[1:]:
        grad += ref[...].astype(F32)
    root = lax.rsqrt(jnp.sum(values * values, axis=0, keepdims=True) * (1.0 / width) + EPSILON)
    scaled = grad * gain
    centre = jnp.sum(scaled * values, axis=0, keepdims=True) * (1.0 / width)
    total = root * scaled - values * (root * root * root * centre)
    grad_ref[...] = (total + branch_ref[...].astype(F32)).T
    out_ref[...] = rows + result_ref[...].astype(F32).T


def finish(block_input, gain, branch, result, sums):
    shape = jax.ShapeDtypeStruct(block_input.shape, F32)
    return pl.pallas_call(
        finish_kernel,
        out_shape=(shape, shape),
        in_specs=whole_specs(4 + len(sums)),
        out_specs=tuple(whole_specs(2)),
        compiler_params=pltpu.CompilerParams(vmem_limit_bytes=VMEM_BYTES),
        name="finish",
    )(block_input, gain, branch, result, *sums)


def split_low(values):
    high = values.astype(BF16)
    return high, (values - high.astype(F32)).astype(BF16)


def load_tile(ref, first, count, *place):
    return jnp.concatenate([ref[(first + m, *place)] for m in range(count)], axis=-1)


def expert_kernel(parts, own_ref, *refs):
    state_refs = refs[:parts]
    (grad_ref, other_ref, in_ref, in_t_ref, out_ref, gain_ref) = refs[parts : parts + 6]
    (
        kept_ref,
        sent_ref,
        normed_ref,
        act_ref,
        pre_ref,
        gate_ref,
        router_sum,
        state_ref,
        full_ref,
        back_ref,
        joint_ref,
    ) = refs[parts + 6 :]

    @pl.when(pl.program_id(0) == 0)
    def _():
        router_sum[...] = jnp.zeros_like(router_sum)

    width = gain_ref.shape[0]
    share = width // parts
    hidden = act_ref.shape[1]
    experts = router_sum.shape[0]
    expert, own = own_ref[0], own_ref[1]
    chains, columns = state_ref.shape[0], state_ref.shape[-1]
    merged = kept_ref.shape[1] // chains
    slots = columns // merged
    gain = gain_ref[...]
    for a in range(chains):
        for k in range(parts):
            state_ref[a, own ^ k] = load_tile(state_refs[k], a * merged, merged)
            near = 2 * (k // 2) + ((own & 1) ^ (k & 1))
            full_ref[a, near] = load_tile(
                other_ref if k & 1 else grad_ref, a * merged, merged, k // 2
            )
    for a in range(chains):
        state = state_ref[a].reshape(width, columns).astype(F32)
        root = lax.rsqrt(jnp.sum(state * state, axis=0, keepdims=True) * (1.0 / width) + EPSILON)
        normed = (state * root * gain).astype(BF16)
        normed_ref[a] = normed
        both = dot(in_t_ref[...], normed)
        pre_act, logits = both[:hidden], both[hidden : hidden + experts]
        act_grad = dot(out_ref[...], full_ref[a].reshape(width, columns))
        raised = jnp.exp(logits - jnp.max(logits, axis=0, keepdims=True))
        router_probs = raised / jnp.sum(raised, axis=0, keepdims=True)
        chosen = lax.broadcasted_iota(jnp.int32, logits.shape, 0) == expert
        gate = jnp.sum(jnp.where(chosen, router_probs, 0.0), axis=0, keepdims=True)
        gate_ref[a] = gate
        square = pre_act * pre_act
        cdf = 0.5 + 0.5 * jnp.tanh(pre_act * (GELU_A + (GELU_A * GELU_B) * square))
        activated = pre_act * cdf
        act_ref[a] = activated.astype(BF16)
        rise = (2.0 * GELU_A) + (6.0 * GELU_A * GELU_B) * square
        pre_grad = act_grad * (cdf + activated * (1.0 - cdf) * rise)
        low_grad = pre_grad.astype(BF16)
        pre_ref[a] = low_grad
        gate_grad = jnp.sum(activated * act_grad, axis=0, keepdims=True)
        logit_grad = gate_grad * (chosen.astype(F32) - router_probs)
        centre = jnp.sum(pre_grad * pre_act, axis=0, keepdims=True)
        centre += jnp.sum(logit_grad * logits, axis=0, keepdims=True)
        joint_ref[a, :hidden, :] = low_grad
        joint_ref[a, hidden:, :] = jnp.concatenate(split_low(logit_grad), axis=0)
        high, low = split_low(logit_grad * gate)
        router_sum[...] += dot_rows(high, normed) + dot_rows(low, normed)
        normed_grad = dot(in_ref[...], joint_ref[a])
        state = state_ref[a].reshape(width, columns).astype(F32)
        back = (root * gate) * (normed_grad * gain - state * (root * centre * (1.0 / width)))
        back_ref[a] = back.astype(BF16).reshape(parts, share, columns)
        for k in range(parts):
            block = back_ref[a, own ^ k]
            target = sent_ref if k & 1 else kept_ref
            for m in range(merged):
                target[k // 2, a * merged + m] = block[:, m * slots : (m + 1) * slots]


def result_kernel(parts, own_ref, *refs):
    chunks = (len(refs) - 11) // 4
    sets = [refs[4 * c : 4 * c + 4] for c in range(chunks)]
    (
        grad_ref,
        other_ref,
        in_ref,
        out_t_ref,
        kept_ref,
        sent_ref,
        in_sum,
        out_sum,
        gain_sum,
        result_ref,
        full_ref,
    ) = refs[4 * chunks :]

    @pl.when(pl.program_id(0) == 0)
    def _():
        in_sum[...] = jnp.zeros_like(in_sum)
        out_sum[...] = jnp.zeros_like(out_sum)

    own = own_ref[1]
    width = out_t_ref.shape[0]
    share = width // parts
    merged = kept_ref.shape[1]
    for c in range(chunks):
        normed_ref, act_ref, pre_ref, gate_ref = sets[c]
        gate, activated = gate_ref[0], act_ref[0]
        columns = activated.shape[-1]
        slots = columns // merged
        for k in range(parts):
            near = 2 * (k // 2) + ((own & 1) ^ (k & 1))
            source = other_ref if k & 1 else grad_ref
            full_ref[c, near] = jnp.concatenate(
                [source[m, k // 2, :, c * slots : (c + 1) * slots] for m in range(merged)], axis=-1
            )
        result = dot(out_t_ref[...], activated) * gate
        result_ref[c] = result.astype(BF16).reshape(parts, share, columns)
        for k in range(parts):
            block = result_ref[c, own ^ k]
            target = sent_ref if k & 1 else kept_ref
            for m in range(merged):
                target[k // 2, m, :, c * slots : (c + 1) * slots] = block[
                    :, m * slots : (m + 1) * slots
                ]
        normed = (normed_ref[0].astype(F32) * gate).astype(BF16)
        in_sum[...] += dot_rows(normed, pre_ref[0])
        scaled = (full_ref[c].reshape(width, columns).astype(F32) * gate).astype(BF16)
        out_sum[...] += dot_rows(activated, scaled)

    @pl.when(pl.program_id(0) == pl.num_programs(0) - 1)
    def _():
        gain_sum[...] = jnp.sum(in_sum[...] * in_ref[...].astype(F32), axis=1, keepdims=True)


def fixed_spec(shape):
    return pl.BlockSpec(shape, lambda g: (0,) * len(shape))


def run_expert(own, states, grads, chunk, merged, chains, weights):
    parts = len(states)
    count, share, slots = states[0].shape
    width = share * parts
    columns = merged * slots
    steps = count // merged
    hidden = weights[2].shape[0]
    joint = weights[0].shape[1]
    experts = (joint - hidden) // 2
    half = parts // 2
    taken = merged * chains
    piece = pl.BlockSpec((taken, share, slots), lambda g: (g, 0, 0))
    grad_piece = pl.BlockSpec((taken, half, share, slots), lambda g: (g, 0, 0, chunk))
    split = pl.BlockSpec((half, taken, share, slots), lambda g: (0, g, 0, 0))
    wide = pl.BlockSpec((chains, width, columns), lambda g: (g, 0, 0))
    deep = pl.BlockSpec((chains, hidden, columns), lambda g: (g, 0, 0))
    flat = pl.BlockSpec((chains, 1, columns), lambda g: (g, 0, 0))
    return pl.pallas_call(
        functools.partial(expert_kernel, parts),
        grid=(steps // chains,),
        out_shape=(
            jax.ShapeDtypeStruct((half, count, share, slots), BF16),
            jax.ShapeDtypeStruct((half, count, share, slots), BF16),
            jax.ShapeDtypeStruct((steps, width, columns), BF16),
            jax.ShapeDtypeStruct((steps, hidden, columns), BF16),
            jax.ShapeDtypeStruct((steps, hidden, columns), BF16),
            jax.ShapeDtypeStruct((steps, 1, columns), F32),
            jax.ShapeDtypeStruct((experts, width), F32),
        ),
        in_specs=[pl.BlockSpec(memory_space=pltpu.SMEM)]
        + [piece] * parts
        + [grad_piece] * 2
        + [fixed_spec(weight.shape) for weight in weights],
        out_specs=(split, split, wide, deep, deep, flat, fixed_spec((experts, width))),
        scratch_shapes=[
            pltpu.VMEM((chains, parts, share, columns), BF16),
            pltpu.VMEM((chains, parts, share, columns), BF16),
            pltpu.VMEM((chains, parts, share, columns), BF16),
            pltpu.VMEM((chains, joint, columns), BF16),
        ],
        compiler_params=pltpu.CompilerParams(vmem_limit_bytes=VMEM_BYTES),
        cost_estimate=pl.CostEstimate(
            flops=16 * steps * columns * width * hidden,
            bytes_accessed=16 * steps * columns * width,
            transcendentals=steps * columns * hidden,
        ),
        name="expert",
    )(own, *states, *grads, *weights)


def run_result(own, saved, grads, merged, weights):
    chunks = len(saved)
    steps, width, columns = saved[0][0].shape
    hidden = saved[0][1].shape[1]
    _, half, share, _ = grads[0].shape
    parts = 2 * half
    slots = columns // merged
    wide = pl.BlockSpec((1, width, columns), lambda g: (g, 0, 0))
    deep = pl.BlockSpec((1, hidden, columns), lambda g: (g, 0, 0))
    flat = pl.BlockSpec((1, 1, columns), lambda g: (g, 0, 0))
    grad_piece = pl.BlockSpec((merged, half, share, slots * chunks), lambda g: (g, 0, 0, 0))
    split = pl.BlockSpec((half, merged, share, slots * chunks), lambda g: (0, g, 0, 0))
    total = jax.ShapeDtypeStruct((half, steps * merged, share, slots * chunks), BF16)
    return pl.pallas_call(
        functools.partial(result_kernel, parts),
        grid=(steps,),
        out_shape=(
            total,
            total,
            jax.ShapeDtypeStruct((width, hidden), F32),
            jax.ShapeDtypeStruct((hidden, width), F32),
            jax.ShapeDtypeStruct((width, 1), F32),
        ),
        in_specs=[pl.BlockSpec(memory_space=pltpu.SMEM)]
        + [wide, deep, deep, flat] * chunks
        + [grad_piece] * 2
        + [fixed_spec(weight.shape) for weight in weights],
        out_specs=(
            split,
            split,
            fixed_spec((width, hidden)),
            fixed_spec((hidden, width)),
            fixed_spec((width, 1)),
        ),
        scratch_shapes=[
            pltpu.VMEM((chunks, parts, share, columns), BF16),
            pltpu.VMEM((chunks, parts, share, columns), BF16),
        ],
        compiler_params=pltpu.CompilerParams(vmem_limit_bytes=VMEM_BYTES),
        cost_estimate=pl.CostEstimate(
            flops=16 * chunks * steps * columns * width * hidden,
            bytes_accessed=12 * chunks * steps * columns * width,
            transcendentals=0,
        ),
        name="result",
    )(own, *[array for arrays in saved for array in arrays], *grads, *weights)


def shards(
    block_input,
    attn_in_weight,
    attn_out_weight,
    position_bias,
    norm_gains,
    router_weight,
    expert_in,
    expert_out,
    segment_ids,
    expert_ids,
    out_grad,
):
    tensor_count, seq_count = lax.axis_size("tensor"), lax.axis_size("seq")
    tensor_place, seq_place = lax.axis_index("tensor"), lax.axis_index("seq")
    grid_count = lax.axis_size("dp") * seq_count
    grid_place = lax.axis_index("dp") * seq_count + seq_place
    local_count, width = block_input.shape
    group_count = local_count * tensor_count
    share = width // tensor_count
    bucket_count, heads = position_bias.shape
    head_cols = attn_in_weight.shape[2]
    experts = router_weight.shape[1]
    capacity = max(2, 2 * group_count // experts)
    tiles = group_count // TILE
    key_tiles = tiles * seq_count
    fast = seq_count == 2 and local_count == TILE and grid_count == 8

    def tiled(pieces):
        pieces = reorder(pieces, tensor_place)
        if local_count == TILE:
            return jnp.stack(pieces)
        return jnp.concatenate(pieces, axis=-1)[None]

    own_rows = jnp.concatenate(
        [
            jnp.transpose(block_input.astype(BF16)),
            jnp.pad(segment_ids.astype(BF16), ((0, 15), (0, 0))),
        ]
    )
    weight_piece = jnp.concatenate(
        [attn_in_weight[0], attn_in_weight[1], attn_in_weight[2], jnp.transpose(attn_out_weight)],
        axis=1,
    )
    weight_pieces = gather_grid(weight_piece)
    if fast:
        own_first = jnp.int32(0)
        far_rows = swap(own_rows, "seq", 1)
        near_two, far_two = swap(own_rows, "tensor", 2), swap(far_rows, "tensor", 2)
        near_one, far_one = swap(own_rows, "tensor", 1), swap(far_rows, "tensor", 1)
        far_two, weight_pieces = lax.optimization_barrier((far_two, weight_pieces))
        near_three, far_three = swap(near_two, "tensor", 1), swap(far_two, "tensor", 1)
        row_pieces = [
            rows[None]
            for rows in (
                own_rows,
                near_one,
                near_two,
                near_three,
                far_rows,
                far_one,
                far_two,
                far_three,
            )
        ]
    else:
        both_rows = lax.all_gather(own_rows, "seq", axis=0, tiled=False)
        row_pieces = gather_relative(both_rows, "tensor")
        own_first = seq_place * tiles
        row_pieces = jnp.concatenate(reorder(row_pieces, tensor_place), axis=-1)
        row_pieces = row_pieces.reshape(seq_count, -1, tiles, TILE)
        row_pieces = [jnp.moveaxis(row_pieces, 2, 1).reshape(key_tiles, -1, TILE)]
    own = jnp.stack([grid_place, tensor_place, seq_place, own_first]).astype(jnp.int32)

    bias = bias_tiles(position_bias)
    in_t, out_t = jnp.transpose(expert_in[0]), jnp.transpose(expert_out[0])
    router_t = jnp.transpose(router_weight)
    in_joint = jnp.concatenate([expert_in[0], router_weight, router_weight], axis=1)
    in_t = jnp.concatenate([in_t, router_t, router_t])
    route_all = expert_ids[:, 0]
    expert_range = jnp.arange(experts, dtype=jnp.int32)
    route_hot = (route_all[:, None] == expert_range[None, :]).astype(jnp.int32)
    slot_rank = jnp.sum(jnp.cumsum(route_hot, axis=0) * route_hot, axis=-1) - 1
    target = (route_all * capacity + slot_rank).reshape(1, tiles, TILE, 1)
    places = jnp.arange(experts * capacity, dtype=jnp.int32).reshape(experts, 1, 1, capacity)
    onehot = (target == places).astype(BF16)
    chunks = 2 if capacity >= TILE else 1
    slots = capacity // chunks
    spread = max(1, TILE // capacity)
    merged = max(1, TILE // (slots * spread))

    def exchange(values):
        return lax.all_to_all(values, ("dp", "seq"), split_axis=0, concat_axis=0, tiled=True)

    def joined(values):
        if spread == 1:
            return values
        shape = values.shape
        values = values.reshape((-1, spread) + shape[1:])
        return jnp.moveaxis(values, 1, -2).reshape(
            (shape[0] // spread,) + shape[1:-1] + (spread * shape[-1],)
        )

    def parted(values):
        if spread == 1:
            return values
        shape = values.shape
        values = values.reshape(shape[:-1] + (spread, shape[-1] // spread))
        return jnp.moveaxis(values, -2, 1).reshape((-1,) + shape[1:-1] + (shape[-1] // spread,))

    half = tensor_count // 2
    grad_rows = jnp.transpose(out_grad.astype(BF16)).reshape(half, 2, share, local_count)
    core = tensor_place & 1
    grad_mine = lax.dynamic_index_in_dim(grad_rows, core, 1, keepdims=False)
    grad_theirs = lax.dynamic_index_in_dim(grad_rows, core ^ 1, 1, keepdims=False)
    if fast:
        grad_theirs, far_two = lax.optimization_barrier((grad_theirs, far_two))
    grad_pair = jnp.stack([grad_mine, swap(grad_theirs, "tensor", 1)])
    grad_far = swap(grad_pair, "tensor", 2)
    grad_here = tiled([grad_pair[0], grad_pair[1], grad_far[0], grad_far[1]])
    grad_buffer = einsum("nkdq,enqs->ekds", grad_here, onehot).astype(BF16)

    gain_one = norm_gains[0][:, None]
    gain_two = norm_gains[1][:, None]
    gain_one, bias, in_t, in_joint, out_t, target, gain_two = lax.optimization_barrier(
        (gain_one, bias, in_t, in_joint, out_t, target, gain_two)
    )
    meta, queries, keys_values, normed_tiles, input_share, in_flat, out_blocks, out_t_blocks = (
        project(own, row_pieces, weight_pieces, gain_one, tiles, key_tiles, share)
    )
    queries, grad_buffer = lax.optimization_barrier((queries, grad_buffer))
    grad_arrived = joined(exchange(grad_buffer))
    exact, attended, logs, attn_even, attn_odd = attend(
        meta, queries, keys_values, bias, out_blocks
    )
    attn_share = sum_chips(sum_cores(attn_even, attn_odd, "tensor"), "tensor")
    state_share = (input_share.astype(F32) + attn_share).astype(BF16)
    state_share, grad_arrived = lax.optimization_barrier((state_share, grad_arrived))
    grad_other = swap(grad_arrived, "tensor", 1)

    weights = (in_joint, in_t, expert_out[0], gain_two)
    grads = (grad_arrived, grad_other)
    buffers = [
        einsum("ndq,enqs->eds", state_share, onehot[..., c * slots : (c + 1) * slots]).astype(BF16)
        for c in range(chunks)
    ]
    buffers = list(lax.optimization_barrier(tuple(buffers)))
    arrivals = [joined(exchange(buffer)) for buffer in buffers]
    chains = 2 if arrivals[0].shape[0] // merged % 2 == 0 else 1
    gathered = [gather_relative(arrival, "tensor") for arrival in arrivals]
    gathered[0][0], gathered[-1][0] = lax.optimization_barrier((gathered[0][0], gathered[-1][0]))
    saved, halves = [], []
    small = jnp.zeros((experts, width), F32)
    for c in range(chunks):
        if halves:
            gathered[c][0], halves[-1] = lax.optimization_barrier((gathered[c][0], halves[-1]))
        kept, sent, normed_two, activated, pre_grad, gate, router_sum = run_expert(
            own, gathered[c], grads, c, merged, chains, weights
        )
        saved.append((normed_two, activated, pre_grad, gate))
        halves.append(sum_cores(kept, sent, "tensor"))
        small = small + router_sum
    totals = [sum_chips(half_sum, "tensor") for half_sum in halves[:-1]]
    late = lax.optimization_barrier((own, halves[-1], *totals))
    own_late, halves[-1], totals = late[0], late[1], list(late[2:])
    totals.append(sum_chips(halves[-1], "tensor"))
    result_even, result_odd, grad_expert_in, grad_expert_out, in_gain = run_result(
        own_late, saved, grads, merged, (expert_in[0], out_t)
    )
    gain_part = in_gain[:, 0] + jnp.sum(small * router_t.astype(F32), axis=0)
    small = jnp.concatenate([small, (gain_part / norm_gains[1])[None]])
    state_grad = lax.dynamic_index_in_dim(grad_here, tensor_place // 2, 1, keepdims=False)
    state_grad = state_grad.astype(F32)
    for c in range(chunks):
        state_grad = state_grad + einsum(
            "eds,enqs->ndq",
            exchange(parted(totals[c].astype(BF16))),
            onehot[..., c * slots : (c + 1) * slots],
        )
    state_grad = state_grad.astype(BF16)
    result_total = sum_chips(sum_cores(result_even, result_odd, "tensor"), "tensor").astype(BF16)

    branch = gather_relative(state_grad, "tensor")
    result_total, branch[1] = lax.optimization_barrier((result_total, branch[1]))
    result_back = exchange(parted(result_total))
    dq, dkv, bias_rows = attend_back(
        meta, queries, keys_values, bias, out_t_blocks, exact, logs, branch, bucket_count
    )
    dq, dkv, bias_rows, result_back = lax.optimization_barrier((dq, dkv, bias_rows, result_back))

    if fast:
        far_even, far_odd, own_even, own_odd, weight_even, weight_odd, gain_part = project_back(
            True, own, dq, dkv, normed_tiles, in_flat, attended, branch, grid_count
        )
        far_half = sum_cores(far_even, far_odd, "tensor")
        own_half = sum_cores(own_even, own_odd, "tensor")
        weight_half = weight_even.astype(F32) + swap(weight_odd, "seq", 1).astype(F32)
        far_half, own_half, small, gain_part, bias_rows, result_back = lax.optimization_barrier(
            (far_half, own_half, small, gain_part, bias_rows, result_back)
        )
        far_sum = sum_chips(far_half, "tensor").astype(BF16)
        sums = [
            own_half[0],
            swap(own_half[1].astype(BF16), "tensor", 2),
            swap(far_sum, "seq", 1),
        ]
        weight_grad = weight_half[0]
        for k in range(1, grid_count // 2):
            weight_grad = weight_grad + swap(weight_half[k].astype(BF16), "dp", k).astype(F32)
    else:
        row_part, weight_part, gain_part = project_back(
            False, own, dq, dkv, normed_tiles, in_flat, attended, branch, grid_count
        )
        row_part = lax.psum_scatter(row_part, "seq", scatter_dimension=0, tiled=True)
        row_part = jnp.moveaxis(row_part, 0, 1).reshape(width, tensor_count, local_count)
        blocks = [
            lax.dynamic_index_in_dim(row_part, tensor_place ^ k, 1, keepdims=False)
            for k in range(tensor_count)
        ]
        halved = sum_cores(jnp.stack(blocks[0::2]), jnp.stack(blocks[1::2]), "tensor")
        sums = [sum_chips(halved, "tensor")]
        weight_grad = lax.psum_scatter(
            weight_part, ("dp", "seq"), scatter_dimension=0, tiled=True
        ).astype(F32)
    grad_attn_in = jnp.stack(
        [weight_grad[:, c * head_cols : (c + 1) * head_cols] for c in range(3)]
    )
    grad_attn_out = jnp.transpose(weight_grad[:, 3 * head_cols :])

    bias_padded = lax.dynamic_update_slice_in_dim(
        jnp.zeros((heads * tensor_count, bucket_count), F32),
        jnp.sum(bias_rows, axis=2),
        tensor_place * heads,
        0,
    )
    small = sum_all(
        jnp.concatenate(
            [small.reshape(-1), gain_part[:, 0] / norm_gains[0], bias_padded.reshape(-1)]
        ),
        ("tensor", "seq", "dp"),
    )
    first, second = experts * width, (experts + 1) * width
    grad_router = jnp.transpose(small[:first].reshape(experts, width))
    grad_gains = jnp.stack([small[second : second + width], small[first:second]])
    bias_sum = small[second + width :].reshape(heads * tensor_count, bucket_count)
    grad_bias = jnp.transpose(lax.dynamic_slice_in_dim(bias_sum, tensor_place * heads, heads, 0))

    result_share = attn_share + einsum("eds,enqs->ndq", result_back, onehot)
    result_share = jnp.moveaxis(result_share.astype(BF16), 0, 1).reshape(
        share, tensor_count, local_count
    )
    result_rows = lax.all_to_all(
        jnp.moveaxis(result_share, 1, 0), "tensor", split_axis=0, concat_axis=0, tiled=True
    ).reshape(width, local_count)
    if local_count == TILE:
        own_branch = [
            lax.dynamic_index_in_dim(piece, tensor_place, 0, keepdims=False) for piece in branch
        ]
    else:
        own_branch = [
            lax.dynamic_slice_in_dim(piece[0], tensor_place * local_count, local_count, 1)
            for piece in branch
        ]
    own_branch = jnp.concatenate(reorder(own_branch, tensor_place))
    block_out, input_grad = finish(block_input, gain_one, own_branch, result_rows, sums)
    return (
        block_out,
        input_grad,
        grad_attn_in,
        grad_attn_out,
        grad_bias,
        grad_gains,
        grad_router,
        grad_expert_in[None],
        grad_expert_out[None],
    )


def solution(mesh):
    return jax.shard_map(
        shards,
        mesh=mesh,
        in_specs=(
            P(("dp", "seq", "tensor"), None),
            P(None, ("dp", "seq"), "tensor"),
            P("tensor", ("dp", "seq")),
            P(None, "tensor"),
            P(),
            P(),
            P(("dp", "seq"), None, "tensor"),
            P(("dp", "seq"), "tensor", None),
            P("dp", ("seq", "tensor")),
            P(("dp", "seq"), None),
            P(("dp", "seq", "tensor"), None),
        ),
        out_specs=(
            P(("dp", "seq", "tensor"), None),
            P(("dp", "seq", "tensor"), None),
            P(None, ("dp", "seq"), "tensor"),
            P("tensor", ("dp", "seq")),
            P(None, "tensor"),
            P(),
            P(),
            P(("dp", "seq"), None, "tensor"),
            P(("dp", "seq"), "tensor", None),
        ),
        check_vma=False,
    )
```

```python
import functools
import math

import jax
import jax.numpy as jnp
from jax import lax
from jax.experimental import pallas as pl
from jax.experimental.pallas import tpu as pltpu
from jax.sharding import PartitionSpec as P

EPSILON = 1e-06
EDGES = (1, 2, 3, 4, 5, 6, 7, 8, 12, 16, 23, 32, 46, 64, 91)
TILE = 256
HALF = TILE // 2
LOG2E = math.log2(math.e)
SCALE = 0.125
MASKED = -1e30
LOWEST = -1e29
EXTRA = 16
VMEM_BYTES = 48 * 1024 * 1024
GELU_A = math.sqrt(2.0 / math.pi)
GELU_B = 0.044715
BF16 = jnp.bfloat16
F32 = jnp.float32


def dot(left_side, right_side):
    return jnp.dot(left_side, right_side, preferred_element_type=F32)


def dot_rows(left_side, right_side):
    return lax.dot_general(
        left_side, right_side, (((1,), (1,)), ((), ())), preferred_element_type=F32
    )


def einsum(formula, *operands):
    return jnp.einsum(formula, *operands, preferred_element_type=F32)


def swap(values, axis, bit):
    count = lax.axis_size(axis)
    return lax.ppermute(values, axis, [(i, i ^ bit) for i in range(count)])


def bits_of(count):
    return [1 << i for i in range(count.bit_length() - 1)]


def gather_relative(values, axis):
    pieces = {0: values}
    for bit in reversed(bits_of(lax.axis_size(axis))):
        for place in list(pieces):
            pieces[place ^ bit] = swap(pieces[place], axis, bit)
    return [pieces[place] for place in range(len(pieces))]


def sum_cores(kept, sent, axis):
    return kept.astype(F32) + swap(sent.astype(BF16), axis, 1).astype(F32)


def sum_chips(total, axis):
    bit = 2
    while bit < lax.axis_size(axis):
        pairs = total.reshape((-1, 2) + total.shape[1:])
        total = pairs[:, 0] + swap(pairs[:, 1].astype(BF16), axis, bit).astype(F32)
        bit *= 2
    return total[0]


def reorder(pieces, own_index):
    for bit in bits_of(len(pieces)):
        flip = (own_index & bit) != 0
        pieces = [
            jnp.where(flip, pieces[place ^ bit], pieces[place]) for place in range(len(pieces))
        ]
    return pieces


def gather_grid(values):
    dp_count, seq_count = lax.axis_size("dp"), lax.axis_size("seq")
    if dp_count > 4 or seq_count != 2:
        return [lax.all_gather(values, ("dp", "seq"), axis=0, tiled=True)]
    columns = [values] + [swap(values, "dp", place) for place in range(1, dp_count)]
    near = swap(values, "seq", 1)
    far = swap(jnp.stack(columns[1:]), "seq", 1)
    pieces = [values, near]
    for place in range(1, dp_count):
        pieces += [columns[place], far[place - 1]]
    return pieces


def sum_all(values, axes):
    for axis in axes:
        for bit in bits_of(lax.axis_size(axis)):
            values = values + swap(values, axis, bit)
    return values


def bucket_of(relative, half_count):
    magnitude = jnp.abs(relative)
    counted = jnp.zeros(relative.shape, jnp.int32)
    for edge_value in EDGES:
        counted = counted + (magnitude >= edge_value).astype(jnp.int32)
    return counted + jnp.where(relative > 0, half_count, 0).astype(jnp.int32)


def near_buckets(half_count):
    shape = (3, HALF, HALF)
    relative = (
        (lax.broadcasted_iota(jnp.int32, shape, 0) - 1) * HALF
        + lax.broadcasted_iota(jnp.int32, shape, 1)
        - lax.broadcasted_iota(jnp.int32, shape, 2)
    )
    return bucket_of(relative, half_count)


def bias_tiles(position_bias):
    bucket_count, heads = position_bias.shape
    half_count = bucket_count // 2
    grid = near_buckets(half_count)
    near = jnp.zeros((heads, 3, HALF, HALF), F32)
    for bucket_index in range(bucket_count):
        near = near + jnp.where(
            (grid == bucket_index)[None], position_bias[bucket_index][:, None, None, None], 0.0
        )
    before, same, after = near[:, 0], near[:, 1], near[:, 2]
    far_before = jnp.broadcast_to(
        position_bias[half_count - 1][:, None, None], (heads, HALF, HALF)
    )
    far_after = jnp.broadcast_to(
        position_bias[bucket_count - 1][:, None, None], (heads, HALF, HALF)
    )

    def square(a, b, c, d):
        return jnp.concatenate(
            [jnp.concatenate([a, b], axis=2), jnp.concatenate([c, d], axis=2)], axis=1
        )

    tiles = jnp.stack(
        [
            square(far_before, far_before, far_before, far_before),
            square(far_before, far_before, before, far_before),
            square(same, before, after, same),
            square(far_after, after, far_after, far_after),
            square(far_after, far_after, far_after, far_after),
        ]
    )
    return tiles * LOG2E


def span_of(meta_ref, query_tile, key_tiles):
    opening, closing = meta_ref[1], meta_ref[2]
    first = query_tile * TILE
    last = first + TILE - 1
    begin = jnp.where(first < opening, 0, jnp.where(first < closing, opening, closing))
    end = jnp.where(last < opening, opening, jnp.where(last < closing, closing, key_tiles * TILE))
    return begin // TILE, (end + TILE - 1) // TILE


def document_row(meta_ref, tile):
    place = tile * TILE + lax.broadcasted_iota(jnp.int32, (EXTRA, TILE), 1)
    return (place >= meta_ref[1]).astype(jnp.int32) + (place >= meta_ref[2]).astype(jnp.int32)


def key_rows(meta_ref, tile):
    row = lax.broadcasted_iota(jnp.int32, (EXTRA, TILE), 0)
    differs = jnp.where(document_row(meta_ref, tile) != row, MASKED, 0.0)
    return jnp.where(row < 3, differs, jnp.where(row < 6, 1.0, 0.0)).astype(BF16)


def query_rows(meta_ref, tile, terms):
    row = lax.broadcasted_iota(jnp.int32, (EXTRA, TILE), 0)
    agrees = jnp.where(document_row(meta_ref, tile) == row, 1.0, 0.0)
    return jnp.where(row < 3, agrees, three_rows(row - 3, terms)).astype(BF16)


def three_rows(row, terms):
    result = jnp.zeros(row.shape, F32)
    for i, term in enumerate(terms):
        result = jnp.where(row == i, term, result)
    return result


def split_three(values):
    first = values.astype(BF16).astype(F32)
    second = (values - first).astype(BF16).astype(F32)
    return first, second, values - first - second


def attend_kernel(
    meta_ref,
    q_ref,
    kv_ref,
    bias_ref,
    weight_ref,
    exact_ref,
    out_ref,
    log_ref,
    even_ref,
    odd_ref,
    key_ref,
    query_ref,
    sum_ref,
):
    key_tiles = kv_ref.shape[0]
    heads = bias_ref.shape[1]
    size = q_ref.shape[1] // heads

    def turn(j, carry):
        kept = meta_ref[3 + j]
        extra = key_rows(meta_ref, j)
        for h in range(heads):
            rows = kv_ref[kept, h * size : (h + 1) * size, :]
            key_ref[kept, h] = jnp.concatenate([rows, extra], axis=0).T
        return carry

    lax.fori_loop(0, key_tiles, turn, 0)
    ones = jnp.ones((EXTRA, TILE), BF16)

    def query_body(i, carry):
        tile = meta_ref[3 + key_tiles + i]
        place = tile % meta_ref[0]
        begin, end = span_of(meta_ref, tile, key_tiles)
        extra = query_rows(meta_ref, tile, ())
        for h in range(heads):
            rows = q_ref[i, h * size : (h + 1) * size, :]
            query_ref[h] = jnp.concatenate([rows, extra], axis=0)
        sum_ref[...] = jnp.zeros_like(sum_ref)

        def key_body(j, peaks):
            kept = meta_ref[3 + j]
            kind = jnp.clip(j - tile, -2, 2) + 2
            scores = [
                dot(key_ref[kept, h], query_ref[h]) + bias_ref[kind, h] for h in range(heads)
            ]
            new_peaks = [
                jnp.maximum(peaks[h], jnp.max(scores[h], axis=0, keepdims=True))
                for h in range(heads)
            ]
            weights = [jnp.exp2(scores[h] - new_peaks[h]).astype(BF16) for h in range(heads)]
            added = []
            for h in range(heads):
                values = kv_ref[kept, (heads + h) * size : (heads + h + 1) * size, :]
                added.append(dot(jnp.concatenate([values, ones], axis=0), weights[h]))
            for h in range(heads):
                sum_ref[h] = sum_ref[h] * jnp.exp2(peaks[h] - new_peaks[h]) + added[h]
            return tuple(new_peaks)

        start = tuple(jnp.full((1, TILE), LOWEST, F32) for _ in range(heads))
        peaks = lax.fori_loop(begin, end, key_body, start)
        for h in range(heads):
            rows = slice(h * size, (h + 1) * size)
            total = sum_ref[h, size : size + 1, :]
            result = sum_ref[h, :size, :] * (1.0 / total)
            exact_ref[i, rows, :] = result
            out_ref[place, rows, :] = result.astype(BF16)
            log_ref[i, h] = peaks[h] + jnp.log2(total)
        attended = out_ref[place]
        for k in range(weight_ref.shape[0]):
            block = dot(weight_ref[k], attended).astype(BF16)
            (odd_ref if k & 1 else even_ref)[k // 2, place] = block
        return carry

    lax.fori_loop(0, q_ref.shape[0], query_body, 0)


def estimate(queries, key_tiles, products):
    pairs = queries.shape[0] * TILE * key_tiles * TILE
    return pl.CostEstimate(
        flops=2 * products * pairs * queries.shape[1],
        bytes_accessed=8 * pairs,
        transcendentals=3 * pairs,
    )


def whole_specs(count):
    return [pl.BlockSpec(memory_space=pltpu.VMEM)] * count


def attend(meta, queries, keys_values, bias, out_blocks):
    query_tiles, width, _ = queries.shape
    key_tiles = keys_values.shape[0]
    heads = bias.shape[1]
    parts, share, _ = out_blocks.shape
    blocks = jax.ShapeDtypeStruct((parts // 2, query_tiles, share, TILE), BF16)
    return pl.pallas_call(
        attend_kernel,
        out_shape=(
            jax.ShapeDtypeStruct(queries.shape, F32),
            jax.ShapeDtypeStruct(queries.shape, BF16),
            jax.ShapeDtypeStruct((query_tiles, heads, 1, TILE), F32),
            blocks,
            blocks,
        ),
        in_specs=[pl.BlockSpec(memory_space=pltpu.SMEM)] + whole_specs(4),
        out_specs=tuple(whole_specs(5)),
        scratch_shapes=[
            pltpu.VMEM((key_tiles, heads, TILE, width // heads + EXTRA), BF16),
            pltpu.VMEM((heads, width // heads + EXTRA, TILE), BF16),
            pltpu.VMEM((heads, width // heads + EXTRA, TILE), F32),
        ],
        compiler_params=pltpu.CompilerParams(vmem_limit_bytes=VMEM_BYTES),
        cost_estimate=estimate(queries, key_tiles, 2),
        name="attend",
    )(meta, queries, keys_values, bias, out_blocks)


def bucket_rows(tiles_ref, rows_ref):
    heads, bucket_count = rows_ref.shape[:2]
    half_count = bucket_count // 2
    offset = lax.broadcasted_iota(jnp.int32, (HALF, HALF), 0) - lax.broadcasted_iota(
        jnp.int32, (HALF, HALF), 1
    )
    grids = [bucket_of(offset + shift * HALF, half_count) for shift in (-1, 0, 1)]
    first, last = slice(0, HALF), slice(HALF, TILE)

    def column_sums(values):
        return jnp.sum(values, axis=0, keepdims=True)

    def head_body(h, carry):
        before = tiles_ref[2, h, first, last] + tiles_ref[1, h, last, first]
        same = tiles_ref[2, h, first, first] + tiles_ref[2, h, last, last]
        after = tiles_ref[2, h, last, first] + tiles_ref[3, h, first, last]
        far_before = column_sums(tiles_ref[0, h, :, first] + tiles_ref[0, h, :, last])
        far_before += column_sums(tiles_ref[1, h, first, first] + tiles_ref[1, h, first, last])
        far_before += column_sums(tiles_ref[1, h, last, last])
        far_after = column_sums(tiles_ref[4, h, :, first] + tiles_ref[4, h, :, last])
        far_after += column_sums(tiles_ref[3, h, last, first] + tiles_ref[3, h, last, last])
        far_after += column_sums(tiles_ref[3, h, first, first])
        for bucket_index in range(bucket_count):
            row = column_sums(jnp.where(grids[1] == bucket_index, same, 0.0))
            if 0 < bucket_index < half_count:
                row += column_sums(jnp.where(grids[0] == bucket_index, before, 0.0))
            if bucket_index > half_count:
                row += column_sums(jnp.where(grids[2] == bucket_index, after, 0.0))
            if bucket_index == half_count - 1:
                row += far_before
            if bucket_index == bucket_count - 1:
                row += far_after
            rows_ref[h, bucket_index : bucket_index + 1, :] = row
        return carry

    lax.fori_loop(0, heads, head_body, 0)


def attend_back_kernel(
    meta_ref,
    q_ref,
    kv_ref,
    bias_ref,
    weight_ref,
    exact_ref,
    log_ref,
    *refs,
):
    parts = weight_ref.shape[0]
    branch_refs = refs[:parts]
    (
        dq_ref,
        dkv_ref,
        rows_ref,
        tiles_ref,
        key_ref,
        value_ref,
        query_ref,
        grad_ref,
        dq_sum,
        dkv_sum,
    ) = refs[parts:]
    key_tiles = kv_ref.shape[0]
    heads = bias_ref.shape[1]
    size = q_ref.shape[1] // heads

    row = lax.broadcasted_iota(jnp.int32, (EXTRA, TILE), 0)
    ones = jnp.where(row < 3, 1.0, 0.0).astype(BF16)

    def turn(j, carry):
        kept = meta_ref[3 + j]
        extra = key_rows(meta_ref, j)
        for h in range(heads):
            rows = kv_ref[kept, h * size : (h + 1) * size, :]
            key_ref[kept, h] = jnp.concatenate([rows, extra], axis=0).T
            rows = kv_ref[kept, (heads + h) * size : (heads + h + 1) * size, :]
            value_ref[kept, h] = jnp.concatenate([rows, ones], axis=0).T
        return carry

    lax.fori_loop(0, key_tiles, turn, 0)
    dkv_sum[...] = jnp.zeros_like(dkv_sum)
    tiles_ref[...] = jnp.zeros_like(tiles_ref)

    def query_body(i, carry):
        tile = meta_ref[3 + key_tiles + i]
        place = tile % meta_ref[0]
        begin, end = span_of(meta_ref, tile, key_tiles)
        dq_sum[...] = jnp.zeros_like(dq_sum)
        grad_sum = dot(weight_ref[0], branch_refs[0][place])
        for k in range(1, parts):
            grad_sum += dot(weight_ref[k], branch_refs[k][place])
        for h in range(heads):
            rows = slice(h * size, (h + 1) * size)
            grad = grad_sum[rows].astype(BF16)
            centre = jnp.sum(grad.astype(F32) * exact_ref[i, rows, :], axis=0, keepdims=True)
            extra = three_rows(row, split_three(-centre)).astype(BF16)
            grad_ref[h] = jnp.concatenate([grad, extra], axis=0)
            extra = query_rows(meta_ref, tile, split_three(-log_ref[i, h]))
            query_ref[h] = jnp.concatenate([q_ref[i, rows, :], extra], axis=0)

        def key_body(j, inner):
            kept = meta_ref[3 + j]
            kind = jnp.clip(j - tile, -2, 2) + 2
            probs = [
                jnp.exp2(dot(key_ref[kept, h], query_ref[h]) + bias_ref[kind, h])
                for h in range(heads)
            ]
            score_grads = [probs[h] * dot(value_ref[kept, h], grad_ref[h]) for h in range(heads)]
            low_probs = [prob.astype(BF16) for prob in probs]
            low_grads = [score_grad.astype(BF16) for score_grad in score_grads]
            key_adds, value_adds, query_adds = [], [], []
            for h in range(heads):
                rows = slice(h * size, (h + 1) * size)
                key_adds.append(dot_rows(q_ref[i, rows, :], low_grads[h]))
                value_adds.append(dot_rows(grad_ref[h, :size, :], low_probs[h]))
                query_adds.append(dot(kv_ref[kept, rows, :], low_grads[h]))
            for h in range(heads):
                rows = slice(h * size, (h + 1) * size)
                value_rows = slice((heads + h) * size, (heads + h + 1) * size)
                tiles_ref[kind, h] += score_grads[h]
                dkv_sum[kept, rows, :] += key_adds[h]
                dkv_sum[kept, value_rows, :] += value_adds[h]
                dq_sum[rows, :] += query_adds[h]
            return inner

        lax.fori_loop(begin, end, key_body, 0)
        dq_ref[i] = (dq_sum[...] * SCALE).astype(BF16)
        return carry

    lax.fori_loop(0, q_ref.shape[0], query_body, 0)
    middle = heads * size
    dkv_ref[:, :middle, :] = (dkv_sum[:, :middle, :] * (1.0 / LOG2E)).astype(BF16)
    dkv_ref[:, middle:, :] = dkv_sum[:, middle:, :].astype(BF16)
    bucket_rows(tiles_ref, rows_ref)


def attend_back(meta, queries, keys_values, bias, out_blocks, exact, logs, branch, buckets):
    key_tiles = keys_values.shape[0]
    heads = bias.shape[1]
    size = queries.shape[1] // heads
    return pl.pallas_call(
        attend_back_kernel,
        out_shape=(
            jax.ShapeDtypeStruct(queries.shape, BF16),
            jax.ShapeDtypeStruct(keys_values.shape, BF16),
            jax.ShapeDtypeStruct((heads, buckets, HALF), F32),
        ),
        in_specs=[pl.BlockSpec(memory_space=pltpu.SMEM)] + whole_specs(6 + len(branch)),
        out_specs=tuple(whole_specs(3)),
        scratch_shapes=[
            pltpu.VMEM(bias.shape, F32),
            pltpu.VMEM((key_tiles, heads, TILE, size + EXTRA), BF16),
            pltpu.VMEM((key_tiles, heads, TILE, size + EXTRA), BF16),
            pltpu.VMEM((heads, size + EXTRA, TILE), BF16),
            pltpu.VMEM((heads, size + EXTRA, TILE), BF16),
            pltpu.VMEM(queries.shape[1:], F32),
            pltpu.VMEM(keys_values.shape, F32),
        ],
        compiler_params=pltpu.CompilerParams(vmem_limit_bytes=VMEM_BYTES),
        cost_estimate=estimate(queries, key_tiles, 5),
        name="attend_back",
    )(meta, queries, keys_values, bias, out_blocks, exact, logs, *branch)


def project_kernel(piece_count, weight_count, tiles, share, own_ref, *refs):
    piece_refs = refs[:piece_count]
    weight_refs = refs[piece_count : piece_count + weight_count]
    gain_ref = refs[piece_count + weight_count]
    (
        meta_ref,
        q_ref,
        kv_ref,
        normed_ref,
        input_ref,
        in_ref,
        out_ref,
        out_t_ref,
        block_ref,
        turned_ref,
    ) = refs[piece_count + weight_count + 1 :]
    grid_place, tensor_place, seq_place, own_first = (own_ref[i] for i in range(4))
    width = gain_ref.shape[0]
    head_cols = q_ref.shape[1]
    columns = turned_ref.shape[0]
    for k in range(weight_count):
        place = grid_place ^ k if weight_count > 1 else 0
        block_ref[place] = weight_refs[k][...]
    full = block_ref[...].reshape(width, columns)
    in_ref[...] = full[:, : 3 * head_cols]
    turned_ref[...] = full.T
    blocks_here = width // share
    tall = block_ref.shape[1]
    per = share // tall if weight_count > 1 else 1
    for k in range(blocks_here):
        if weight_count > 1:
            block = block_ref[pl.ds((tensor_place ^ k) * per, per), :, 3 * head_cols :]
            block = block.reshape(share, head_cols)
        else:
            start = pl.multiple_of((tensor_place ^ k) * share, share)
            block = block_ref[0, pl.ds(start, share), 3 * head_cols :]
        out_ref[k] = block
        out_t_ref[k] = block.T
    key_tiles = kv_ref.shape[0]
    early = jnp.zeros((1, TILE), F32)
    late = jnp.zeros((1, TILE), F32)
    gain = gain_ref[...]
    for k in range(piece_count):
        for s in range(piece_refs[0].shape[0]):
            kept = s + k
            rows = piece_refs[k][s, :width, :].astype(F32)
            ids = piece_refs[k][s, width : width + 16, :][:1].astype(F32)
            early += (ids < 0.5).astype(F32)
            late += (ids < 1.5).astype(F32)
            root = lax.rsqrt(jnp.sum(rows * rows, axis=0, keepdims=True) * (1.0 / width) + EPSILON)
            normed = (rows * root * gain).astype(BF16)
            normed_ref[kept] = normed
            kv_ref[kept] = dot(turned_ref[head_cols : 3 * head_cols, :], normed).astype(BF16)
    for i in range(tiles):
        normed = normed_ref[own_first + i]
        q_ref[i] = (dot(turned_ref[:head_cols, :], normed) * (SCALE * LOG2E)).astype(BF16)
        start = pl.multiple_of(tensor_place * share, share)
        if piece_count > 1:
            input_ref[tensor_place ^ i] = piece_refs[i][0, pl.ds(start, share), :]
        else:
            input_ref[i] = piece_refs[0][own_first + i, pl.ds(start, share), :]
    meta_ref[0] = tiles
    meta_ref[1] = jnp.sum(early).astype(jnp.int32)
    meta_ref[2] = jnp.sum(late).astype(jnp.int32)
    for j in range(key_tiles):
        if piece_count > 1:
            meta_ref[3 + j] = ((j // tiles) ^ seq_place) * tiles + ((j % tiles) ^ tensor_place)
        else:
            meta_ref[3 + j] = j
    for i in range(tiles):
        shift = tensor_place ^ i if piece_count > 1 else i
        meta_ref[3 + key_tiles + i] = seq_place * tiles + shift


def project(own, pieces, weight_pieces, gain, tiles, key_tiles, share):
    width = gain.shape[0]
    columns = weight_pieces[0].shape[1]
    head_cols = columns // 4
    parts = width // share
    return pl.pallas_call(
        functools.partial(project_kernel, len(pieces), len(weight_pieces), tiles, share),
        out_shape=(
            jax.ShapeDtypeStruct((3 + key_tiles + tiles,), jnp.int32),
            jax.ShapeDtypeStruct((tiles, head_cols, TILE), BF16),
            jax.ShapeDtypeStruct((key_tiles, 2 * head_cols, TILE), BF16),
            jax.ShapeDtypeStruct((key_tiles, width, TILE), BF16),
            jax.ShapeDtypeStruct((tiles, share, TILE), BF16),
            jax.ShapeDtypeStruct((width, 3 * head_cols), BF16),
            jax.ShapeDtypeStruct((parts, share, head_cols), BF16),
            jax.ShapeDtypeStruct((parts, head_cols, share), BF16),
        ),
        in_specs=[pl.BlockSpec(memory_space=pltpu.SMEM)]
        + whole_specs(len(pieces) + len(weight_pieces) + 1),
        out_specs=(pl.BlockSpec(memory_space=pltpu.SMEM),) + tuple(whole_specs(7)),
        scratch_shapes=[
            pltpu.VMEM((len(weight_pieces),) + weight_pieces[0].shape, BF16),
            pltpu.VMEM((columns, width), BF16),
        ],
        compiler_params=pltpu.CompilerParams(vmem_limit_bytes=VMEM_BYTES),
        cost_estimate=pl.CostEstimate(
            flops=6 * key_tiles * TILE * width * head_cols,
            bytes_accessed=8 * key_tiles * TILE * width,
            transcendentals=0,
        ),
        name="project",
    )(own, *pieces, *weight_pieces, gain)


def project_back_kernel(fast, parts, own_ref, dq_ref, dkv_ref, normed_ref, in_ref, attended_ref, *refs):
    branch_refs = refs[:parts]
    if fast:
        far_even, far_odd, own_even, own_odd, weight_even, weight_odd, gain_ref, full_ref = refs[
            parts:
        ]
    else:
        part_ref, weight_ref, gain_ref, full_ref = refs[parts:]
    grid_place, tensor_place, seq_place, own_first = (own_ref[i] for i in range(4))
    tiles, head_cols, _ = dq_ref.shape
    key_tiles = dkv_ref.shape[0]
    width = in_ref.shape[0]
    share = width // parts
    key_weight = in_ref[:, head_cols:]
    query_weight = in_ref[:, :head_cols]
    if fast:
        for n in range(tiles):
            block = dot(key_weight, dkv_ref[tiles + n]).astype(BF16)
            (far_odd if n & 1 else far_even)[n // 2] = block
        for n in range(tiles):
            block = dot(key_weight, dkv_ref[n]) + dot(query_weight, dq_ref[n])
            (own_odd if n & 1 else own_even)[n // 2] = block.astype(BF16)
    else:
        for n in range(key_tiles):
            part_ref[n] = dot(key_weight, dkv_ref[n]).astype(BF16)
        for n in range(tiles):
            block = part_ref[own_first + n].astype(F32) + dot(query_weight, dq_ref[n])
            part_ref[own_first + n] = block.astype(BF16)
    query_sum = dot_rows(normed_ref[own_first], dq_ref[0])
    for n in range(1, tiles):
        query_sum += dot_rows(normed_ref[own_first + n], dq_ref[n])
    key_sum = dot_rows(normed_ref[0], dkv_ref[0])
    for n in range(1, key_tiles):
        key_sum += dot_rows(normed_ref[n], dkv_ref[n])
    gain_ref[...] = jnp.sum(
        query_sum * query_weight.astype(F32), axis=1, keepdims=True
    ) + jnp.sum(key_sum * key_weight.astype(F32), axis=1, keepdims=True)
    full_ref[:, :head_cols] = query_sum.astype(BF16)
    full_ref[:, head_cols : 3 * head_cols] = key_sum.astype(BF16)
    for k in range(parts):
        block = dot_rows(branch_refs[k][0], attended_ref[0])
        for n in range(1, tiles):
            block += dot_rows(branch_refs[k][n], attended_ref[n])
        start = pl.multiple_of((tensor_place ^ k) * share, share)
        full_ref[pl.ds(start, share), 3 * head_cols :] = block.astype(BF16)
    if fast:
        tall = weight_even.shape[1]
        for k in range(weight_even.shape[0]):
            place = grid_place ^ (2 * k)
            weight_even[k] = full_ref[pl.ds(pl.multiple_of(place * tall, tall), tall), :]
            weight_odd[k] = full_ref[pl.ds(pl.multiple_of((place ^ 1) * tall, tall), tall), :]
    else:
        weight_ref[...] = full_ref[...]


def project_back(fast, own, dq, dkv, normed, in_flat, attended, branch, grid_count):
    tiles, head_cols, _ = dq.shape
    key_tiles = dkv.shape[0]
    width = in_flat.shape[0]
    parts = len(branch)
    columns = 4 * head_cols
    if fast:
        block = jax.ShapeDtypeStruct((parts // 2, width, TILE), BF16)
        weight = jax.ShapeDtypeStruct((grid_count // 2, width // grid_count, columns), BF16)
        shapes = (block,) * 4 + (weight,) * 2
    else:
        shapes = (
            jax.ShapeDtypeStruct((key_tiles, width, TILE), BF16),
            jax.ShapeDtypeStruct((width, columns), BF16),
        )
    shapes = shapes + (jax.ShapeDtypeStruct((width, 1), F32),)
    return pl.pallas_call(
        functools.partial(project_back_kernel, fast, parts),
        out_shape=shapes,
        in_specs=[pl.BlockSpec(memory_space=pltpu.SMEM)] + whole_specs(5 + parts),
        out_specs=tuple(whole_specs(len(shapes))),
        scratch_shapes=[pltpu.VMEM((width, columns), BF16)],
        compiler_params=pltpu.CompilerParams(vmem_limit_bytes=VMEM_BYTES),
        cost_estimate=pl.CostEstimate(
            flops=12 * key_tiles * TILE * width * head_cols,
            bytes_accessed=8 * key_tiles * TILE * width,
            transcendentals=0,
        ),
        name="project_back",
    )(own, dq, dkv, normed, in_flat, attended, *branch)


def finish_kernel(input_ref, gain_ref, branch_ref, result_ref, *refs):
    sum_refs = refs[:-2]
    out_ref, grad_ref = refs[-2:]
    rows = input_ref[...]
    width = rows.shape[1]
    values = rows.T
    gain = gain_ref[...]
    grad = sum_refs[0][...].astype(F32)
    for ref in sum_refs[1:]:
        grad += ref[...].astype(F32)
    root = lax.rsqrt(jnp.sum(values * values, axis=0, keepdims=True) * (1.0 / width) + EPSILON)
    scaled = grad * gain
    centre = jnp.sum(scaled * values, axis=0, keepdims=True) * (1.0 / width)
    total = root * scaled - values * (root * root * root * centre)
    grad_ref[...] = (total + branch_ref[...].astype(F32)).T
    out_ref[...] = rows + result_ref[...].astype(F32).T


def finish(block_input, gain, branch, result, sums):
    shape = jax.ShapeDtypeStruct(block_input.shape, F32)
    return pl.pallas_call(
        finish_kernel,
        out_shape=(shape, shape),
        in_specs=whole_specs(4 + len(sums)),
        out_specs=tuple(whole_specs(2)),
        compiler_params=pltpu.CompilerParams(vmem_limit_bytes=VMEM_BYTES),
        name="finish",
    )(block_input, gain, branch, result, *sums)


def split_low(values):
    high = values.astype(BF16)
    return high, (values - high.astype(F32)).astype(BF16)


def load_tile(ref, first, count, *place):
    return jnp.concatenate([ref[(first + m, *place)] for m in range(count)], axis=-1)


def expert_kernel(parts, own_ref, *refs):
    state_refs = refs[:parts]
    (grad_ref, other_ref, in_ref, in_t_ref, out_ref, gain_ref) = refs[parts : parts + 6]
    (
        kept_ref,
        sent_ref,
        normed_ref,
        act_ref,
        pre_ref,
        gate_ref,
        router_sum,
        state_ref,
        full_ref,
        back_ref,
        joint_ref,
    ) = refs[parts + 6 :]

    @pl.when(pl.program_id(0) == 0)
    def _():
        router_sum[...] = jnp.zeros_like(router_sum)

    width = gain_ref.shape[0]
    share = width // parts
    hidden = act_ref.shape[1]
    experts = router_sum.shape[0]
    expert, own = own_ref[0], own_ref[1]
    chains, columns = state_ref.shape[0], state_ref.shape[-1]
    merged = kept_ref.shape[1] // chains
    slots = columns // merged
    gain = gain_ref[...]
    for a in range(chains):
        for k in range(parts):
            state_ref[a, own ^ k] = load_tile(state_refs[k], a * merged, merged)
            near = 2 * (k // 2) + ((own & 1) ^ (k & 1))
            full_ref[a, near] = load_tile(
                other_ref if k & 1 else grad_ref, a * merged, merged, k // 2
            )
    for a in range(chains):
        state = state_ref[a].reshape(width, columns).astype(F32)
        root = lax.rsqrt(jnp.sum(state * state, axis=0, keepdims=True) * (1.0 / width) + EPSILON)
        normed = (state * root * gain).astype(BF16)
        normed_ref[a] = normed
        both = dot(in_t_ref[...], normed)
        pre_act, logits = both[:hidden], both[hidden : hidden + experts]
        act_grad = dot(out_ref[...], full_ref[a].reshape(width, columns))
        raised = jnp.exp(logits - jnp.max(logits, axis=0, keepdims=True))
        router_probs = raised / jnp.sum(raised, axis=0, keepdims=True)
        chosen = lax.broadcasted_iota(jnp.int32, logits.shape, 0) == expert
        gate = jnp.sum(jnp.where(chosen, router_probs, 0.0), axis=0, keepdims=True)
        gate_ref[a] = gate
        square = pre_act * pre_act
        cdf = 0.5 + 0.5 * jnp.tanh(pre_act * (GELU_A + (GELU_A * GELU_B) * square))
        activated = pre_act * cdf
        act_ref[a] = activated.astype(BF16)
        rise = (2.0 * GELU_A) + (6.0 * GELU_A * GELU_B) * square
        pre_grad = act_grad * (cdf + activated * (1.0 - cdf) * rise)
        low_grad = pre_grad.astype(BF16)
        pre_ref[a] = low_grad
        gate_grad = jnp.sum(activated * act_grad, axis=0, keepdims=True)
        logit_grad = gate_grad * (chosen.astype(F32) - router_probs)
        centre = jnp.sum(pre_grad * pre_act, axis=0, keepdims=True)
        centre += jnp.sum(logit_grad * logits, axis=0, keepdims=True)
        joint_ref[a, :hidden, :] = low_grad
        joint_ref[a, hidden:, :] = jnp.concatenate(split_low(logit_grad), axis=0)
        high, low = split_low(logit_grad * gate)
        router_sum[...] += dot_rows(high, normed) + dot_rows(low, normed)
        normed_grad = dot(in_ref[...], joint_ref[a])
        state = state_ref[a].reshape(width, columns).astype(F32)
        back = (root * gate) * (normed_grad * gain - state * (root * centre * (1.0 / width)))
        back_ref[a] = back.astype(BF16).reshape(parts, share, columns)
        for k in range(parts):
            block = back_ref[a, own ^ k]
            target = sent_ref if k & 1 else kept_ref
            for m in range(merged):
                target[k // 2, a * merged + m] = block[:, m * slots : (m + 1) * slots]


def result_kernel(parts, own_ref, *refs):
    chunks = (len(refs) - 11) // 4
    sets = [refs[4 * c : 4 * c + 4] for c in range(chunks)]
    (
        grad_ref,
        other_ref,
        in_ref,
        out_t_ref,
        kept_ref,
        sent_ref,
        in_sum,
        out_sum,
        gain_sum,
        result_ref,
        full_ref,
    ) = refs[4 * chunks :]

    @pl.when(pl.program_id(0) == 0)
    def _():
        in_sum[...] = jnp.zeros_like(in_sum)
        out_sum[...] = jnp.zeros_like(out_sum)

    own = own_ref[1]
    width = out_t_ref.shape[0]
    share = width // parts
    merged = kept_ref.shape[1]
    for c in range(chunks):
        normed_ref, act_ref, pre_ref, gate_ref = sets[c]
        gate, activated = gate_ref[0], act_ref[0]
        columns = activated.shape[-1]
        slots = columns // merged
        for k in range(parts):
            near = 2 * (k // 2) + ((own & 1) ^ (k & 1))
            source = other_ref if k & 1 else grad_ref
            full_ref[c, near] = jnp.concatenate(
                [source[m, k // 2, :, c * slots : (c + 1) * slots] for m in range(merged)], axis=-1
            )
        result = dot(out_t_ref[...], activated) * gate
        result_ref[c] = result.astype(BF16).reshape(parts, share, columns)
        for k in range(parts):
            block = result_ref[c, own ^ k]
            target = sent_ref if k & 1 else kept_ref
            for m in range(merged):
                target[k // 2, m, :, c * slots : (c + 1) * slots] = block[
                    :, m * slots : (m + 1) * slots
                ]
        normed = (normed_ref[0].astype(F32) * gate).astype(BF16)
        in_sum[...] += dot_rows(normed, pre_ref[0])
        scaled = (full_ref[c].reshape(width, columns).astype(F32) * gate).astype(BF16)
        out_sum[...] += dot_rows(activated, scaled)

    @pl.when(pl.program_id(0) == pl.num_programs(0) - 1)
    def _():
        gain_sum[...] = jnp.sum(in_sum[...] * in_ref[...].astype(F32), axis=1, keepdims=True)


def fixed_spec(shape):
    return pl.BlockSpec(shape, lambda g: (0,) * len(shape))


def run_expert(own, states, grads, chunk, merged, chains, weights):
    parts = len(states)
    count, share, slots = states[0].shape
    width = share * parts
    columns = merged * slots
    steps = count // merged
    hidden = weights[2].shape[0]
    joint = weights[0].shape[1]
    experts = (joint - hidden) // 2
    half = parts // 2
    taken = merged * chains
    piece = pl.BlockSpec((taken, share, slots), lambda g: (g, 0, 0))
    grad_piece = pl.BlockSpec((taken, half, share, slots), lambda g: (g, 0, 0, chunk))
    split = pl.BlockSpec((half, taken, share, slots), lambda g: (0, g, 0, 0))
    wide = pl.BlockSpec((chains, width, columns), lambda g: (g, 0, 0))
    deep = pl.BlockSpec((chains, hidden, columns), lambda g: (g, 0, 0))
    flat = pl.BlockSpec((chains, 1, columns), lambda g: (g, 0, 0))
    return pl.pallas_call(
        functools.partial(expert_kernel, parts),
        grid=(steps // chains,),
        out_shape=(
            jax.ShapeDtypeStruct((half, count, share, slots), BF16),
            jax.ShapeDtypeStruct((half, count, share, slots), BF16),
            jax.ShapeDtypeStruct((steps, width, columns), BF16),
            jax.ShapeDtypeStruct((steps, hidden, columns), BF16),
            jax.ShapeDtypeStruct((steps, hidden, columns), BF16),
            jax.ShapeDtypeStruct((steps, 1, columns), F32),
            jax.ShapeDtypeStruct((experts, width), F32),
        ),
        in_specs=[pl.BlockSpec(memory_space=pltpu.SMEM)]
        + [piece] * parts
        + [grad_piece] * 2
        + [fixed_spec(weight.shape) for weight in weights],
        out_specs=(split, split, wide, deep, deep, flat, fixed_spec((experts, width))),
        scratch_shapes=[
            pltpu.VMEM((chains, parts, share, columns), BF16),
            pltpu.VMEM((chains, parts, share, columns), BF16),
            pltpu.VMEM((chains, parts, share, columns), BF16),
            pltpu.VMEM((chains, joint, columns), BF16),
        ],
        compiler_params=pltpu.CompilerParams(vmem_limit_bytes=VMEM_BYTES),
        cost_estimate=pl.CostEstimate(
            flops=16 * steps * columns * width * hidden,
            bytes_accessed=16 * steps * columns * width,
            transcendentals=steps * columns * hidden,
        ),
        name="expert",
    )(own, *states, *grads, *weights)


def run_result(own, saved, grads, merged, weights):
    chunks = len(saved)
    steps, width, columns = saved[0][0].shape
    hidden = saved[0][1].shape[1]
    _, half, share, _ = grads[0].shape
    parts = 2 * half
    slots = columns // merged
    wide = pl.BlockSpec((1, width, columns), lambda g: (g, 0, 0))
    deep = pl.BlockSpec((1, hidden, columns), lambda g: (g, 0, 0))
    flat = pl.BlockSpec((1, 1, columns), lambda g: (g, 0, 0))
    grad_piece = pl.BlockSpec((merged, half, share, slots * chunks), lambda g: (g, 0, 0, 0))
    split = pl.BlockSpec((half, merged, share, slots * chunks), lambda g: (0, g, 0, 0))
    total = jax.ShapeDtypeStruct((half, steps * merged, share, slots * chunks), BF16)
    return pl.pallas_call(
        functools.partial(result_kernel, parts),
        grid=(steps,),
        out_shape=(
            total,
            total,
            jax.ShapeDtypeStruct((width, hidden), F32),
            jax.ShapeDtypeStruct((hidden, width), F32),
            jax.ShapeDtypeStruct((width, 1), F32),
        ),
        in_specs=[pl.BlockSpec(memory_space=pltpu.SMEM)]
        + [wide, deep, deep, flat] * chunks
        + [grad_piece] * 2
        + [fixed_spec(weight.shape) for weight in weights],
        out_specs=(
            split,
            split,
            fixed_spec((width, hidden)),
            fixed_spec((hidden, width)),
            fixed_spec((width, 1)),
        ),
        scratch_shapes=[
            pltpu.VMEM((chunks, parts, share, columns), BF16),
            pltpu.VMEM((chunks, parts, share, columns), BF16),
        ],
        compiler_params=pltpu.CompilerParams(vmem_limit_bytes=VMEM_BYTES),
        cost_estimate=pl.CostEstimate(
            flops=16 * chunks * steps * columns * width * hidden,
            bytes_accessed=12 * chunks * steps * columns * width,
            transcendentals=0,
        ),
        name="result",
    )(own, *[array for arrays in saved for array in arrays], *grads, *weights)


def shards(
    block_input,
    attn_in_weight,
    attn_out_weight,
    position_bias,
    norm_gains,
    router_weight,
    expert_in,
    expert_out,
    segment_ids,
    expert_ids,
    out_grad,
):
    tensor_count, seq_count = lax.axis_size("tensor"), lax.axis_size("seq")
    tensor_place, seq_place = lax.axis_index("tensor"), lax.axis_index("seq")
    grid_count = lax.axis_size("dp") * seq_count
    grid_place = lax.axis_index("dp") * seq_count + seq_place
    local_count, width = block_input.shape
    group_count = local_count * tensor_count
    share = width // tensor_count
    bucket_count, heads = position_bias.shape
    head_cols = attn_in_weight.shape[2]
    experts = router_weight.shape[1]
    capacity = max(2, 2 * group_count // experts)
    tiles = group_count // TILE
    key_tiles = tiles * seq_count
    fast = seq_count == 2 and local_count == TILE and grid_count == 8

    def tiled(pieces):
        pieces = reorder(pieces, tensor_place)
        if local_count == TILE:
            return jnp.stack(pieces)
        return jnp.concatenate(pieces, axis=-1)[None]

    half = tensor_count // 2
    core = tensor_place & 1
    grad_rows = jnp.transpose(out_grad.astype(BF16)).reshape(half, 2, share, local_count)
    grad_mine = lax.dynamic_index_in_dim(grad_rows, core, 1, keepdims=False)
    grad_theirs = lax.dynamic_index_in_dim(grad_rows, core ^ 1, 1, keepdims=False)
    grad_other = swap(grad_theirs, "tensor", 1)
    grad_far, grad_last = swap(grad_mine, "tensor", 2), swap(grad_other, "tensor", 2)

    own_rows = jnp.concatenate(
        [
            jnp.transpose(block_input.astype(BF16)),
            jnp.pad(segment_ids.astype(BF16), ((0, 15), (0, 0))),
        ]
    )
    weight_piece = jnp.concatenate(
        [attn_in_weight[0], attn_in_weight[1], attn_in_weight[2], jnp.transpose(attn_out_weight)],
        axis=1,
    )
    weight_pieces = gather_grid(weight_piece)
    if fast:
        own_first = jnp.int32(0)
        far_rows = swap(own_rows, "seq", 1)
        far_rows, grad_far = lax.optimization_barrier((far_rows, grad_far))
        near_two, far_two = swap(own_rows, "tensor", 2), swap(far_rows, "tensor", 2)
        near_one, far_one = swap(own_rows, "tensor", 1), swap(far_rows, "tensor", 1)
        far_two, weight_pieces = lax.optimization_barrier((far_two, weight_pieces))
        near_three, far_three = swap(near_two, "tensor", 1), swap(far_two, "tensor", 1)
        row_pieces = [
            rows[None]
            for rows in (
                own_rows,
                near_one,
                near_two,
                near_three,
                far_rows,
                far_one,
                far_two,
                far_three,
            )
        ]
    else:
        both_rows = lax.all_gather(own_rows, "seq", axis=0, tiled=False)
        row_pieces = gather_relative(both_rows, "tensor")
        own_first = seq_place * tiles
        row_pieces = jnp.concatenate(reorder(row_pieces, tensor_place), axis=-1)
        row_pieces = row_pieces.reshape(seq_count, -1, tiles, TILE)
        row_pieces = [jnp.moveaxis(row_pieces, 2, 1).reshape(key_tiles, -1, TILE)]
    own = jnp.stack([grid_place, tensor_place, seq_place, own_first]).astype(jnp.int32)

    bias = bias_tiles(position_bias)
    in_t, out_t = jnp.transpose(expert_in[0]), jnp.transpose(expert_out[0])
    router_t = jnp.transpose(router_weight)
    in_joint = jnp.concatenate([expert_in[0], router_weight, router_weight], axis=1)
    in_t = jnp.concatenate([in_t, router_t, router_t])
    route_all = expert_ids[:, 0]
    expert_range = jnp.arange(experts, dtype=jnp.int32)
    route_hot = (route_all[:, None] == expert_range[None, :]).astype(jnp.int32)
    slot_rank = jnp.sum(jnp.cumsum(route_hot, axis=0) * route_hot, axis=-1) - 1
    target = (route_all * capacity + slot_rank).reshape(1, tiles, TILE, 1)
    places = jnp.arange(experts * capacity, dtype=jnp.int32).reshape(experts, 1, 1, capacity)
    onehot = (target == places).astype(BF16)
    chunks = 2 if capacity >= TILE else 1
    slots = capacity // chunks
    spread = max(1, TILE // capacity)
    merged = max(1, TILE // (slots * spread))

    def exchange(values):
        return lax.all_to_all(values, ("dp", "seq"), split_axis=0, concat_axis=0, tiled=True)

    def joined(values):
        if spread == 1:
            return values
        shape = values.shape
        values = values.reshape((-1, spread) + shape[1:])
        return jnp.moveaxis(values, 1, -2).reshape(
            (shape[0] // spread,) + shape[1:-1] + (spread * shape[-1],)
        )

    def parted(values):
        if spread == 1:
            return values
        shape = values.shape
        values = values.reshape(shape[:-1] + (spread, shape[-1] // spread))
        return jnp.moveaxis(values, -2, 1).reshape((-1,) + shape[1:-1] + (shape[-1] // spread,))

    grad_here = tiled([grad_mine, grad_other, grad_far, grad_last])
    grad_buffer = einsum("nkdq,enqs->ekds", grad_here, onehot).astype(BF16)

    gain_one = norm_gains[0][:, None]
    gain_two = norm_gains[1][:, None]
    gain_one, bias, in_t, in_joint, out_t, target, gain_two, grad_buffer = (
        lax.optimization_barrier(
            (gain_one, bias, in_t, in_joint, out_t, target, gain_two, grad_buffer)
        )
    )
    meta, queries, keys_values, normed_tiles, input_share, in_flat, out_blocks, out_t_blocks = (
        project(own, row_pieces, weight_pieces, gain_one, tiles, key_tiles, share)
    )
    grad_arrived = joined(exchange(grad_buffer))
    exact, attended, logs, attn_even, attn_odd = attend(
        meta, queries, keys_values, bias, out_blocks
    )
    attn_share = sum_chips(sum_cores(attn_even, attn_odd, "tensor"), "tensor")
    state_share = (input_share.astype(F32) + attn_share).astype(BF16)
    state_share, grad_arrived = lax.optimization_barrier((state_share, grad_arrived))
    grad_other = swap(grad_arrived, "tensor", 1)

    weights = (in_joint, in_t, expert_out[0], gain_two)
    grads = (grad_arrived, grad_other)
    buffers = [
        einsum("ndq,enqs->eds", state_share, onehot[..., c * slots : (c + 1) * slots]).astype(BF16)
        for c in range(chunks)
    ]
    buffers = list(lax.optimization_barrier(tuple(buffers)))
    arrivals = [joined(exchange(buffer)) for buffer in buffers]
    chains = 2 if arrivals[0].shape[0] // merged % 2 == 0 else 1
    gathered = []
    for arrival in arrivals:
        gathered.append(
            [arrival, swap(arrival, "tensor", 1), swap(arrival, "tensor", 2)]
        )
    gathered[0][0], gathered[-1][0] = lax.optimization_barrier((gathered[0][0], gathered[-1][0]))
    saved, halves, crossed = [], [], []
    small = jnp.zeros((experts, width), F32)
    for c in range(chunks):
        gathered[c].append(swap(gathered[c][2], "tensor", 1))
        kept, sent, normed_two, activated, pre_grad, gate, router_sum = run_expert(
            own, gathered[c], grads, c, merged, chains, weights
        )
        saved.append((normed_two, activated, pre_grad, gate))
        if c + 1 < chunks:
            sent, gathered[c + 1][2] = lax.optimization_barrier((sent, gathered[c + 1][2]))
        if c > 0:
            sent, crossed[c - 1] = lax.optimization_barrier((sent, crossed[c - 1]))
        halves.append(sum_cores(kept, sent, "tensor"))
        if c + 1 == chunks:
            own_late, halves[c] = lax.optimization_barrier((own, halves[c]))
        crossed.append(swap(halves[c][1].astype(BF16), "tensor", 2))
        small = small + router_sum
    returned = [
        exchange(parted((halves[c][0] + crossed[c].astype(F32)).astype(BF16)))
        for c in range(chunks - 1)
    ]
    result_even, result_odd, grad_expert_in, grad_expert_out, in_gain = run_result(
        own_late, saved, grads, merged, (expert_in[0], out_t)
    )
    tied = lax.optimization_barrier((result_odd, crossed[-1], *returned))
    result_odd, crossed[-1], returned = tied[0], tied[1], list(tied[2:])
    returned.append(
        exchange(parted((halves[-1][0] + crossed[-1].astype(F32)).astype(BF16)))
    )
    gain_part = in_gain[:, 0] + jnp.sum(small * router_t.astype(F32), axis=0)
    router_gains = jnp.concatenate([small, (gain_part / norm_gains[1])[None]])
    state_grad = lax.dynamic_index_in_dim(grad_here, tensor_place // 2, 1, keepdims=False)
    state_grad = state_grad.astype(F32)
    for c in range(chunks):
        state_grad = state_grad + einsum(
            "eds,enqs->ndq", returned[c], onehot[..., c * slots : (c + 1) * slots]
        )
    state_grad = state_grad.astype(BF16)
    result_half = sum_cores(result_even, result_odd, "tensor")
    result_far = swap(result_half[1].astype(BF16), "tensor", 2)

    branch = [state_grad, swap(state_grad, "tensor", 1), swap(state_grad, "tensor", 2)]
    result_far, branch[1] = lax.optimization_barrier((result_far, branch[1]))
    branch.append(swap(branch[2], "tensor", 1))
    result_total = (result_half[0] + result_far.astype(F32)).astype(BF16)
    result_back = exchange(parted(result_total))
    dq, dkv, bias_rows = attend_back(
        meta, queries, keys_values, bias, out_t_blocks, exact, logs, branch, bucket_count
    )
    dq, dkv, bias_rows, result_back = lax.optimization_barrier((dq, dkv, bias_rows, result_back))

    def joined_small():
        bias_padded = lax.dynamic_update_slice_in_dim(
            jnp.zeros((heads * tensor_count, bucket_count), F32),
            jnp.sum(bias_rows, axis=2),
            tensor_place * heads,
            0,
        )
        return jnp.concatenate(
            [router_gains.reshape(-1), gain_part[:, 0] / norm_gains[0], bias_padded.reshape(-1)]
        )

    def result_rows_of():
        shares = attn_share + einsum("eds,enqs->ndq", result_back, onehot)
        return jnp.moveaxis(shares.astype(BF16), 0, 1).reshape(share, tensor_count, local_count)

    if fast:
        far_even, far_odd, own_even, own_odd, weight_even, weight_odd, gain_part = project_back(
            True, own, dq, dkv, normed_tiles, in_flat, attended, branch, grid_count
        )
        far_half = sum_cores(far_even, far_odd, "tensor")
        own_half = sum_cores(own_even, own_odd, "tensor")
        weight_sent = swap(weight_odd, "seq", 1)
        far_half, own_half, gain_part, result_back = lax.optimization_barrier(
            (far_half, own_half, gain_part, result_back)
        )
        far_sent = swap(far_half[1].astype(BF16), "tensor", 2)
        own_sent = swap(own_half[1].astype(BF16), "tensor", 2)
        small = sum_all(joined_small(), ("tensor",))
        result_share = result_rows_of()
        far_sent, weight_sent, small, result_share = lax.optimization_barrier(
            (far_sent, weight_sent, small, result_share)
        )
        far_sum = (far_half[0] + far_sent.astype(F32)).astype(BF16)
        sums = [own_half[0], own_sent, swap(far_sum, "seq", 1)]
        weight_half = weight_even.astype(F32) + weight_sent.astype(F32)
        weight_grad = weight_half[0]
        for k in range(1, grid_count // 2):
            weight_grad = weight_grad + swap(weight_half[k].astype(BF16), "dp", k).astype(F32)
    else:
        row_part, weight_part, gain_part = project_back(
            False, own, dq, dkv, normed_tiles, in_flat, attended, branch, grid_count
        )
        row_part = lax.psum_scatter(row_part, "seq", scatter_dimension=0, tiled=True)
        row_part = jnp.moveaxis(row_part, 0, 1).reshape(width, tensor_count, local_count)
        blocks = [
            lax.dynamic_index_in_dim(row_part, tensor_place ^ k, 1, keepdims=False)
            for k in range(tensor_count)
        ]
        halved = sum_cores(jnp.stack(blocks[0::2]), jnp.stack(blocks[1::2]), "tensor")
        sums = [sum_chips(halved, "tensor")]
        small = sum_all(joined_small(), ("tensor",))
        result_share = result_rows_of()
        weight_grad = lax.psum_scatter(
            weight_part, ("dp", "seq"), scatter_dimension=0, tiled=True
        ).astype(F32)
    grad_attn_in = jnp.stack(
        [weight_grad[:, c * head_cols : (c + 1) * head_cols] for c in range(3)]
    )
    grad_attn_out = jnp.transpose(weight_grad[:, 3 * head_cols :])

    small = sum_all(small, ("seq", "dp"))
    first, second = experts * width, (experts + 1) * width
    grad_router = jnp.transpose(small[:first].reshape(experts, width))
    grad_gains = jnp.stack([small[second : second + width], small[first:second]])
    bias_sum = small[second + width :].reshape(heads * tensor_count, bucket_count)
    grad_bias = jnp.transpose(lax.dynamic_slice_in_dim(bias_sum, tensor_place * heads, heads, 0))

    result_rows = lax.all_to_all(
        jnp.moveaxis(result_share, 1, 0), "tensor", split_axis=0, concat_axis=0, tiled=True
    ).reshape(width, local_count)
    if local_count == TILE:
        own_branch = [
            lax.dynamic_index_in_dim(piece, tensor_place, 0, keepdims=False) for piece in branch
        ]
    else:
        own_branch = [
            lax.dynamic_slice_in_dim(piece[0], tensor_place * local_count, local_count, 1)
            for piece in branch
        ]
    own_branch = jnp.concatenate(reorder(own_branch, tensor_place))
    block_out, input_grad = finish(block_input, gain_one, own_branch, result_rows, sums)
    return (
        block_out,
        input_grad,
        grad_attn_in,
        grad_attn_out,
        grad_bias,
        grad_gains,
        grad_router,
        grad_expert_in[None],
        grad_expert_out[None],
    )


def solution(mesh):
    return jax.shard_map(
        shards,
        mesh=mesh,
        in_specs=(
            P(("dp", "seq", "tensor"), None),
            P(None, ("dp", "seq"), "tensor"),
            P("tensor", ("dp", "seq")),
            P(None, "tensor"),
            P(),
            P(),
            P(("dp", "seq"), None, "tensor"),
            P(("dp", "seq"), "tensor", None),
            P("dp", ("seq", "tensor")),
            P(("dp", "seq"), None),
            P(("dp", "seq", "tensor"), None),
        ),
        out_specs=(
            P(("dp", "seq", "tensor"), None),
            P(("dp", "seq", "tensor"), None),
            P(None, ("dp", "seq"), "tensor"),
            P("tensor", ("dp", "seq")),
            P(None, "tensor"),
            P(),
            P(),
            P(("dp", "seq"), None, "tensor"),
            P(("dp", "seq"), "tensor", None),
        ),
        check_vma=False,
    )
```

```python
import functools
import math

import jax
import jax.numpy as jnp
from jax import lax
from jax.experimental import pallas as pl
from jax.experimental.pallas import tpu as pltpu
from jax.sharding import PartitionSpec as P

EPSILON = 1e-06
EDGES = (1, 2, 3, 4, 5, 6, 7, 8, 12, 16, 23, 32, 46, 64, 91)
TILE = 256
HALF = TILE // 2
LOG2E = math.log2(math.e)
SCALE = 0.125
MASKED = -1e30
LOWEST = -1e29
EXTRA = 16
VMEM_BYTES = 48 * 1024 * 1024
GELU_A = math.sqrt(2.0 / math.pi)
GELU_B = 0.044715
BF16 = jnp.bfloat16
F32 = jnp.float32


def dot(left_side, right_side):
    return jnp.dot(left_side, right_side, preferred_element_type=F32)


def dot_rows(left_side, right_side):
    return lax.dot_general(
        left_side, right_side, (((1,), (1,)), ((), ())), preferred_element_type=F32
    )


def einsum(formula, *operands):
    return jnp.einsum(formula, *operands, preferred_element_type=F32)


def swap(values, axis, bit):
    count = lax.axis_size(axis)
    return lax.ppermute(values, axis, [(i, i ^ bit) for i in range(count)])


def bits_of(count):
    return [1 << i for i in range(count.bit_length() - 1)]


def gather_relative(values, axis):
    pieces = {0: values}
    for bit in reversed(bits_of(lax.axis_size(axis))):
        for place in list(pieces):
            pieces[place ^ bit] = swap(pieces[place], axis, bit)
    return [pieces[place] for place in range(len(pieces))]


def core_step(kept, sent):
    got = swap(sent, "tensor", 1)
    to_send = (kept[1].astype(F32) + got[1].astype(F32)).astype(BF16)
    return kept[0], got[0], to_send


def chip_step(near, got, far):
    return near.astype(F32) + got.astype(F32) + far.astype(F32)


def sum_tensor(kept, sent):
    near, got, to_send = core_step(kept, sent)
    return chip_step(near, got, swap(to_send, "tensor", 2))


def reorder(pieces, own_index):
    for bit in bits_of(len(pieces)):
        flip = (own_index & bit) != 0
        pieces = [
            jnp.where(flip, pieces[place ^ bit], pieces[place]) for place in range(len(pieces))
        ]
    return pieces


def sum_all(values, axes):
    for axis in axes:
        for bit in bits_of(lax.axis_size(axis)):
            values = values + swap(values, axis, bit)
    return values


def bucket_of(relative, half_count):
    magnitude = jnp.abs(relative)
    counted = jnp.zeros(relative.shape, jnp.int32)
    for edge_value in EDGES:
        counted = counted + (magnitude >= edge_value).astype(jnp.int32)
    return counted + jnp.where(relative > 0, half_count, 0).astype(jnp.int32)


def near_buckets(half_count):
    shape = (3, HALF, HALF)
    relative = (
        (lax.broadcasted_iota(jnp.int32, shape, 0) - 1) * HALF
        + lax.broadcasted_iota(jnp.int32, shape, 1)
        - lax.broadcasted_iota(jnp.int32, shape, 2)
    )
    return bucket_of(relative, half_count)


def bias_tiles(position_bias):
    bucket_count, heads = position_bias.shape
    half_count = bucket_count // 2
    grid = near_buckets(half_count)
    near = jnp.zeros((heads, 3, HALF, HALF), F32)
    for bucket_index in range(bucket_count):
        near = near + jnp.where(
            (grid == bucket_index)[None], position_bias[bucket_index][:, None, None, None], 0.0
        )
    before, same, after = near[:, 0], near[:, 1], near[:, 2]
    far_before = jnp.broadcast_to(
        position_bias[half_count - 1][:, None, None], (heads, HALF, HALF)
    )
    far_after = jnp.broadcast_to(
        position_bias[bucket_count - 1][:, None, None], (heads, HALF, HALF)
    )

    def square(a, b, c, d):
        return jnp.concatenate(
            [jnp.concatenate([a, b], axis=2), jnp.concatenate([c, d], axis=2)], axis=1
        )

    tiles = jnp.stack(
        [
            square(far_before, far_before, far_before, far_before),
            square(far_before, far_before, before, far_before),
            square(same, before, after, same),
            square(far_after, after, far_after, far_after),
            square(far_after, far_after, far_after, far_after),
        ]
    )
    return tiles * LOG2E


def span_of(meta_ref, query_tile, key_tiles):
    opening, closing = meta_ref[1], meta_ref[2]
    first = query_tile * TILE
    last = first + TILE - 1
    begin = jnp.where(first < opening, 0, jnp.where(first < closing, opening, closing))
    end = jnp.where(last < opening, opening, jnp.where(last < closing, closing, key_tiles * TILE))
    return begin // TILE, (end + TILE - 1) // TILE


def document_row(meta_ref, tile):
    place = tile * TILE + lax.broadcasted_iota(jnp.int32, (EXTRA, TILE), 1)
    return (place >= meta_ref[1]).astype(jnp.int32) + (place >= meta_ref[2]).astype(jnp.int32)


def key_rows(meta_ref, tile):
    row = lax.broadcasted_iota(jnp.int32, (EXTRA, TILE), 0)
    differs = jnp.where(document_row(meta_ref, tile) != row, MASKED, 0.0)
    return jnp.where(row < 3, differs, jnp.where(row < 6, 1.0, 0.0)).astype(BF16)


def query_rows(meta_ref, tile, terms):
    row = lax.broadcasted_iota(jnp.int32, (EXTRA, TILE), 0)
    agrees = jnp.where(document_row(meta_ref, tile) == row, 1.0, 0.0)
    return jnp.where(row < 3, agrees, three_rows(row - 3, terms)).astype(BF16)


def three_rows(row, terms):
    result = jnp.zeros(row.shape, F32)
    for i, term in enumerate(terms):
        result = jnp.where(row == i, term, result)
    return result


def split_three(values):
    first = values.astype(BF16).astype(F32)
    second = (values - first).astype(BF16).astype(F32)
    return first, second, values - first - second


def attend_kernel(
    meta_ref,
    q_ref,
    kv_ref,
    bias_ref,
    weight_ref,
    exact_ref,
    out_ref,
    log_ref,
    even_ref,
    odd_ref,
    key_ref,
    query_ref,
    sum_ref,
):
    key_tiles = kv_ref.shape[0]
    heads = bias_ref.shape[1]
    size = q_ref.shape[1] // heads

    def turn(j, carry):
        kept = meta_ref[3 + j]
        extra = key_rows(meta_ref, j)
        for h in range(heads):
            rows = kv_ref[kept, h * size : (h + 1) * size, :]
            key_ref[kept, h] = jnp.concatenate([rows, extra], axis=0).T
        return carry

    lax.fori_loop(0, key_tiles, turn, 0)
    ones = jnp.ones((EXTRA, TILE), BF16)

    def query_body(i, carry):
        tile = meta_ref[3 + key_tiles + i]
        place = tile % meta_ref[0]
        begin, end = span_of(meta_ref, tile, key_tiles)
        extra = query_rows(meta_ref, tile, ())
        for h in range(heads):
            rows = q_ref[i, h * size : (h + 1) * size, :]
            query_ref[h] = jnp.concatenate([rows, extra], axis=0)
        sum_ref[...] = jnp.zeros_like(sum_ref)

        def key_body(j, peaks):
            kept = meta_ref[3 + j]
            kind = jnp.clip(j - tile, -2, 2) + 2
            scores = [
                dot(key_ref[kept, h], query_ref[h]) + bias_ref[kind, h] for h in range(heads)
            ]
            new_peaks = [
                jnp.maximum(peaks[h], jnp.max(scores[h], axis=0, keepdims=True))
                for h in range(heads)
            ]
            weights = [jnp.exp2(scores[h] - new_peaks[h]).astype(BF16) for h in range(heads)]
            added = []
            for h in range(heads):
                values = kv_ref[kept, (heads + h) * size : (heads + h + 1) * size, :]
                added.append(dot(jnp.concatenate([values, ones], axis=0), weights[h]))
            for h in range(heads):
                sum_ref[h] = sum_ref[h] * jnp.exp2(peaks[h] - new_peaks[h]) + added[h]
            return tuple(new_peaks)

        start = tuple(jnp.full((1, TILE), LOWEST, F32) for _ in range(heads))
        peaks = lax.fori_loop(begin, end, key_body, start)
        for h in range(heads):
            rows = slice(h * size, (h + 1) * size)
            total = sum_ref[h, size : size + 1, :]
            result = sum_ref[h, :size, :] * (1.0 / total)
            exact_ref[i, rows, :] = result
            out_ref[place, rows, :] = result.astype(BF16)
            log_ref[i, h] = peaks[h] + jnp.log2(total)
        attended = out_ref[place]
        for k in range(weight_ref.shape[0]):
            block = dot(weight_ref[k], attended).astype(BF16)
            (odd_ref if k & 1 else even_ref)[k // 2, place] = block
        return carry

    lax.fori_loop(0, q_ref.shape[0], query_body, 0)


def estimate(queries, key_tiles, products):
    pairs = queries.shape[0] * TILE * key_tiles * TILE
    return pl.CostEstimate(
        flops=2 * products * pairs * queries.shape[1],
        bytes_accessed=8 * pairs,
        transcendentals=3 * pairs,
    )


def whole_specs(arrays):
    return [pl.BlockSpec(array.shape, functools.partial(origin, len(array.shape))) for array in arrays]


def origin(dimensions, step):
    return (0,) * dimensions


def attend(meta, queries, keys_values, bias, out_blocks):
    query_tiles, width, _ = queries.shape
    key_tiles = keys_values.shape[0]
    heads = bias.shape[1]
    parts, share, _ = out_blocks.shape
    blocks = jax.ShapeDtypeStruct((parts // 2, query_tiles, share, TILE), BF16)
    shapes = (
        jax.ShapeDtypeStruct(queries.shape, F32),
        jax.ShapeDtypeStruct(queries.shape, BF16),
        jax.ShapeDtypeStruct((query_tiles, heads, 1, TILE), F32),
        blocks,
        blocks,
    )
    operands = (queries, keys_values, bias, out_blocks)
    return pl.pallas_call(
        attend_kernel,
        grid=(1,),
        out_shape=shapes,
        in_specs=[pl.BlockSpec(memory_space=pltpu.SMEM)] + whole_specs(operands),
        out_specs=tuple(whole_specs(shapes)),
        scratch_shapes=[
            pltpu.VMEM((key_tiles, heads, TILE, width // heads + EXTRA), BF16),
            pltpu.VMEM((heads, width // heads + EXTRA, TILE), BF16),
            pltpu.VMEM((heads, width // heads + EXTRA, TILE), F32),
        ],
        compiler_params=pltpu.CompilerParams(vmem_limit_bytes=VMEM_BYTES),
        cost_estimate=estimate(queries, key_tiles, 2),
        name="attend",
    )(meta, *operands)


def bucket_rows(tiles_ref, rows_ref):
    heads, bucket_count = rows_ref.shape[:2]
    half_count = bucket_count // 2
    offset = lax.broadcasted_iota(jnp.int32, (HALF, HALF), 0) - lax.broadcasted_iota(
        jnp.int32, (HALF, HALF), 1
    )
    grids = [bucket_of(offset + shift * HALF, half_count) for shift in (-1, 0, 1)]
    first, last = slice(0, HALF), slice(HALF, TILE)

    def column_sums(values):
        return jnp.sum(values, axis=0, keepdims=True)

    def head_body(h, carry):
        before = tiles_ref[2, h, first, last] + tiles_ref[1, h, last, first]
        same = tiles_ref[2, h, first, first] + tiles_ref[2, h, last, last]
        after = tiles_ref[2, h, last, first] + tiles_ref[3, h, first, last]
        far_before = column_sums(tiles_ref[0, h, :, first] + tiles_ref[0, h, :, last])
        far_before += column_sums(tiles_ref[1, h, first, first] + tiles_ref[1, h, first, last])
        far_before += column_sums(tiles_ref[1, h, last, last])
        far_after = column_sums(tiles_ref[4, h, :, first] + tiles_ref[4, h, :, last])
        far_after += column_sums(tiles_ref[3, h, last, first] + tiles_ref[3, h, last, last])
        far_after += column_sums(tiles_ref[3, h, first, first])
        for bucket_index in range(bucket_count):
            row = column_sums(jnp.where(grids[1] == bucket_index, same, 0.0))
            if 0 < bucket_index < half_count:
                row += column_sums(jnp.where(grids[0] == bucket_index, before, 0.0))
            if bucket_index > half_count:
                row += column_sums(jnp.where(grids[2] == bucket_index, after, 0.0))
            if bucket_index == half_count - 1:
                row += far_before
            if bucket_index == bucket_count - 1:
                row += far_after
            rows_ref[h, bucket_index : bucket_index + 1, :] = row
        return carry

    lax.fori_loop(0, heads, head_body, 0)


def attend_back_kernel(
    meta_ref,
    q_ref,
    kv_ref,
    bias_ref,
    weight_ref,
    exact_ref,
    log_ref,
    *refs,
):
    parts = weight_ref.shape[0]
    branch_refs = refs[:parts]
    (
        dq_ref,
        dkv_ref,
        rows_ref,
        tiles_ref,
        key_ref,
        value_ref,
        query_ref,
        grad_ref,
        dq_sum,
        dkv_sum,
    ) = refs[parts:]
    key_tiles = kv_ref.shape[0]
    heads = bias_ref.shape[1]
    size = q_ref.shape[1] // heads

    row = lax.broadcasted_iota(jnp.int32, (EXTRA, TILE), 0)
    ones = jnp.where(row < 3, 1.0, 0.0).astype(BF16)

    def turn(j, carry):
        kept = meta_ref[3 + j]
        extra = key_rows(meta_ref, j)
        for h in range(heads):
            rows = kv_ref[kept, h * size : (h + 1) * size, :]
            key_ref[kept, h] = jnp.concatenate([rows, extra], axis=0).T
            rows = kv_ref[kept, (heads + h) * size : (heads + h + 1) * size, :]
            value_ref[kept, h] = jnp.concatenate([rows, ones], axis=0).T
        return carry

    lax.fori_loop(0, key_tiles, turn, 0)
    dkv_sum[...] = jnp.zeros_like(dkv_sum)
    tiles_ref[...] = jnp.zeros_like(tiles_ref)

    def query_body(i, carry):
        tile = meta_ref[3 + key_tiles + i]
        place = tile % meta_ref[0]
        begin, end = span_of(meta_ref, tile, key_tiles)
        dq_sum[...] = jnp.zeros_like(dq_sum)
        grad_sum = dot(weight_ref[0], branch_refs[0][place])
        for k in range(1, parts):
            grad_sum += dot(weight_ref[k], branch_refs[k][place])
        for h in range(heads):
            rows = slice(h * size, (h + 1) * size)
            grad = grad_sum[rows].astype(BF16)
            centre = jnp.sum(grad.astype(F32) * exact_ref[i, rows, :], axis=0, keepdims=True)
            extra = three_rows(row, split_three(-centre)).astype(BF16)
            grad_ref[h] = jnp.concatenate([grad, extra], axis=0)
            extra = query_rows(meta_ref, tile, split_three(-log_ref[i, h]))
            query_ref[h] = jnp.concatenate([q_ref[i, rows, :], extra], axis=0)

        def key_body(j, inner):
            kept = meta_ref[3 + j]
            kind = jnp.clip(j - tile, -2, 2) + 2
            probs = [
                jnp.exp2(dot(key_ref[kept, h], query_ref[h]) + bias_ref[kind, h])
                for h in range(heads)
            ]
            score_grads = [probs[h] * dot(value_ref[kept, h], grad_ref[h]) for h in range(heads)]
            low_probs = [prob.astype(BF16) for prob in probs]
            low_grads = [score_grad.astype(BF16) for score_grad in score_grads]
            key_adds, value_adds, query_adds = [], [], []
            for h in range(heads):
                rows = slice(h * size, (h + 1) * size)
                key_adds.append(dot_rows(q_ref[i, rows, :], low_grads[h]))
                value_adds.append(dot_rows(grad_ref[h, :size, :], low_probs[h]))
                query_adds.append(dot(kv_ref[kept, rows, :], low_grads[h]))
            for h in range(heads):
                rows = slice(h * size, (h + 1) * size)
                value_rows = slice((heads + h) * size, (heads + h + 1) * size)
                tiles_ref[kind, h] += score_grads[h]
                dkv_sum[kept, rows, :] += key_adds[h]
                dkv_sum[kept, value_rows, :] += value_adds[h]
                dq_sum[rows, :] += query_adds[h]
            return inner

        lax.fori_loop(begin, end, key_body, 0)
        dq_ref[i] = (dq_sum[...] * SCALE).astype(BF16)
        return carry

    lax.fori_loop(0, q_ref.shape[0], query_body, 0)
    middle = heads * size
    dkv_ref[:, :middle, :] = (dkv_sum[:, :middle, :] * (1.0 / LOG2E)).astype(BF16)
    dkv_ref[:, middle:, :] = dkv_sum[:, middle:, :].astype(BF16)
    bucket_rows(tiles_ref, rows_ref)


def attend_back(meta, queries, keys_values, bias, out_blocks, exact, logs, branch, buckets):
    key_tiles = keys_values.shape[0]
    heads = bias.shape[1]
    size = queries.shape[1] // heads
    shapes = (
        jax.ShapeDtypeStruct(queries.shape, BF16),
        jax.ShapeDtypeStruct(keys_values.shape, BF16),
        jax.ShapeDtypeStruct((heads, buckets, HALF), F32),
    )
    operands = (queries, keys_values, bias, out_blocks, exact, logs, *branch)
    return pl.pallas_call(
        attend_back_kernel,
        grid=(1,),
        out_shape=shapes,
        in_specs=[pl.BlockSpec(memory_space=pltpu.SMEM)] + whole_specs(operands),
        out_specs=tuple(whole_specs(shapes)),
        scratch_shapes=[
            pltpu.VMEM(bias.shape, F32),
            pltpu.VMEM((key_tiles, heads, TILE, size + EXTRA), BF16),
            pltpu.VMEM((key_tiles, heads, TILE, size + EXTRA), BF16),
            pltpu.VMEM((heads, size + EXTRA, TILE), BF16),
            pltpu.VMEM((heads, size + EXTRA, TILE), BF16),
            pltpu.VMEM(queries.shape[1:], F32),
            pltpu.VMEM(keys_values.shape, F32),
        ],
        compiler_params=pltpu.CompilerParams(vmem_limit_bytes=VMEM_BYTES),
        cost_estimate=estimate(queries, key_tiles, 5),
        name="attend_back",
    )(meta, *operands)


def project_kernel(piece_count, weight_count, tiles, share, own_ref, *refs):
    piece_refs = refs[:piece_count]
    weight_refs = refs[piece_count : piece_count + weight_count]
    gain_ref = refs[piece_count + weight_count]
    (
        meta_ref,
        q_ref,
        kv_ref,
        normed_ref,
        input_ref,
        in_ref,
        out_ref,
        out_t_ref,
        block_ref,
        turned_ref,
    ) = refs[piece_count + weight_count + 1 :]
    grid_place, tensor_place, seq_place, own_first = (own_ref[i] for i in range(4))
    width = gain_ref.shape[0]
    head_cols = q_ref.shape[1]
    columns = turned_ref.shape[0]
    for k in range(weight_count):
        place = grid_place ^ k if weight_count > 1 else 0
        block_ref[place] = weight_refs[k][...]
    full = block_ref[...].reshape(width, columns)
    in_ref[...] = full[:, : 3 * head_cols]
    turned_ref[...] = full.T
    blocks_here = width // share
    tall = block_ref.shape[1]
    per = share // tall if weight_count > 1 else 1
    for k in range(blocks_here):
        if weight_count > 1:
            block = block_ref[pl.ds((tensor_place ^ k) * per, per), :, 3 * head_cols :]
            block = block.reshape(share, head_cols)
        else:
            start = pl.multiple_of((tensor_place ^ k) * share, share)
            block = block_ref[0, pl.ds(start, share), 3 * head_cols :]
        out_ref[k] = block
        out_t_ref[k] = block.T
    key_tiles = kv_ref.shape[0]
    early = jnp.zeros((1, TILE), F32)
    late = jnp.zeros((1, TILE), F32)
    gain = gain_ref[...]
    for k in range(piece_count):
        for s in range(piece_refs[0].shape[0]):
            kept = s + k
            rows = piece_refs[k][s, :width, :].astype(F32)
            ids = piece_refs[k][s, width : width + 16, :][:1].astype(F32)
            early += (ids < 0.5).astype(F32)
            late += (ids < 1.5).astype(F32)
            root = lax.rsqrt(jnp.sum(rows * rows, axis=0, keepdims=True) * (1.0 / width) + EPSILON)
            normed = (rows * root * gain).astype(BF16)
            normed_ref[kept] = normed
            kv_ref[kept] = dot(turned_ref[head_cols : 3 * head_cols, :], normed).astype(BF16)
    for i in range(tiles):
        normed = normed_ref[own_first + i]
        q_ref[i] = (dot(turned_ref[:head_cols, :], normed) * (SCALE * LOG2E)).astype(BF16)
        start = pl.multiple_of(tensor_place * share, share)
        if piece_count > 1:
            input_ref[tensor_place ^ i] = piece_refs[i][0, pl.ds(start, share), :]
        else:
            input_ref[i] = piece_refs[0][own_first + i, pl.ds(start, share), :]
    meta_ref[0] = tiles
    meta_ref[1] = jnp.sum(early).astype(jnp.int32)
    meta_ref[2] = jnp.sum(late).astype(jnp.int32)
    for j in range(key_tiles):
        if piece_count > 1:
            meta_ref[3 + j] = ((j // tiles) ^ seq_place) * tiles + ((j % tiles) ^ tensor_place)
        else:
            meta_ref[3 + j] = j
    for i in range(tiles):
        shift = tensor_place ^ i if piece_count > 1 else i
        meta_ref[3 + key_tiles + i] = seq_place * tiles + shift


def project(own, pieces, weight_pieces, gain, tiles, key_tiles, share):
    width = gain.shape[0]
    columns = weight_pieces[0].shape[1]
    head_cols = columns // 4
    parts = width // share
    shapes = (
        jax.ShapeDtypeStruct((tiles, head_cols, TILE), BF16),
        jax.ShapeDtypeStruct((key_tiles, 2 * head_cols, TILE), BF16),
        jax.ShapeDtypeStruct((key_tiles, width, TILE), BF16),
        jax.ShapeDtypeStruct((tiles, share, TILE), BF16),
        jax.ShapeDtypeStruct((width, 3 * head_cols), BF16),
        jax.ShapeDtypeStruct((parts, share, head_cols), BF16),
        jax.ShapeDtypeStruct((parts, head_cols, share), BF16),
    )
    operands = (*pieces, *weight_pieces, gain)
    return pl.pallas_call(
        functools.partial(project_kernel, len(pieces), len(weight_pieces), tiles, share),
        grid=(1,),
        out_shape=(jax.ShapeDtypeStruct((3 + key_tiles + tiles,), jnp.int32),) + shapes,
        in_specs=[pl.BlockSpec(memory_space=pltpu.SMEM)] + whole_specs(operands),
        out_specs=(pl.BlockSpec(memory_space=pltpu.SMEM),) + tuple(whole_specs(shapes)),
        scratch_shapes=[
            pltpu.VMEM((len(weight_pieces),) + weight_pieces[0].shape, BF16),
            pltpu.VMEM((columns, width), BF16),
        ],
        compiler_params=pltpu.CompilerParams(vmem_limit_bytes=VMEM_BYTES),
        cost_estimate=pl.CostEstimate(
            flops=6 * key_tiles * TILE * width * head_cols,
            bytes_accessed=8 * key_tiles * TILE * width,
            transcendentals=0,
        ),
        name="project",
    )(own, *operands)


def project_back_kernel(fast, parts, own_ref, dq_ref, dkv_ref, normed_ref, in_ref, attended_ref, *refs):
    branch_refs = refs[:parts]
    if fast:
        far_even, far_odd, own_even, own_odd, weight_even, weight_odd, gain_ref, full_ref = refs[
            parts:
        ]
    else:
        part_ref, weight_ref, gain_ref, full_ref = refs[parts:]
    grid_place, tensor_place, seq_place, own_first = (own_ref[i] for i in range(4))
    tiles, head_cols, _ = dq_ref.shape
    key_tiles = dkv_ref.shape[0]
    width = in_ref.shape[0]
    share = width // parts
    key_weight = in_ref[:, head_cols:]
    query_weight = in_ref[:, :head_cols]
    if fast:
        for n in range(tiles):
            block = dot(key_weight, dkv_ref[tiles + n]).astype(BF16)
            (far_odd if n & 1 else far_even)[n // 2] = block
        for n in range(tiles):
            block = dot(key_weight, dkv_ref[n]) + dot(query_weight, dq_ref[n])
            (own_odd if n & 1 else own_even)[n // 2] = block.astype(BF16)
    else:
        for n in range(key_tiles):
            part_ref[n] = dot(key_weight, dkv_ref[n]).astype(BF16)
        for n in range(tiles):
            block = part_ref[own_first + n].astype(F32) + dot(query_weight, dq_ref[n])
            part_ref[own_first + n] = block.astype(BF16)
    query_sum = dot_rows(normed_ref[own_first], dq_ref[0])
    for n in range(1, tiles):
        query_sum += dot_rows(normed_ref[own_first + n], dq_ref[n])
    key_sum = dot_rows(normed_ref[0], dkv_ref[0])
    for n in range(1, key_tiles):
        key_sum += dot_rows(normed_ref[n], dkv_ref[n])
    gain_ref[...] = jnp.sum(
        query_sum * query_weight.astype(F32), axis=1, keepdims=True
    ) + jnp.sum(key_sum * key_weight.astype(F32), axis=1, keepdims=True)
    full_ref[:, :head_cols] = query_sum.astype(BF16)
    full_ref[:, head_cols : 3 * head_cols] = key_sum.astype(BF16)
    for k in range(parts):
        block = dot_rows(branch_refs[k][0], attended_ref[0])
        for n in range(1, tiles):
            block += dot_rows(branch_refs[k][n], attended_ref[n])
        start = pl.multiple_of((tensor_place ^ k) * share, share)
        full_ref[pl.ds(start, share), 3 * head_cols :] = block.astype(BF16)
    if fast:
        tall = weight_even.shape[1]
        for k in range(weight_even.shape[0]):
            place = grid_place ^ (2 * k)
            weight_even[k] = full_ref[pl.ds(pl.multiple_of(place * tall, tall), tall), :]
            weight_odd[k] = full_ref[pl.ds(pl.multiple_of((place ^ 1) * tall, tall), tall), :]
    else:
        weight_ref[...] = full_ref[...]


def project_back(fast, own, dq, dkv, normed, in_flat, attended, branch, grid_count):
    tiles, head_cols, _ = dq.shape
    key_tiles = dkv.shape[0]
    width = in_flat.shape[0]
    parts = len(branch)
    columns = 4 * head_cols
    if fast:
        block = jax.ShapeDtypeStruct((parts // 2, width, TILE), BF16)
        weight = jax.ShapeDtypeStruct((grid_count // 2, width // grid_count, columns), BF16)
        shapes = (block,) * 4 + (weight,) * 2
    else:
        shapes = (
            jax.ShapeDtypeStruct((key_tiles, width, TILE), BF16),
            jax.ShapeDtypeStruct((width, columns), BF16),
        )
    shapes = shapes + (jax.ShapeDtypeStruct((width, 1), F32),)
    operands = (dq, dkv, normed, in_flat, attended, *branch)
    return pl.pallas_call(
        functools.partial(project_back_kernel, fast, parts),
        grid=(1,),
        out_shape=shapes,
        in_specs=[pl.BlockSpec(memory_space=pltpu.SMEM)] + whole_specs(operands),
        out_specs=tuple(whole_specs(shapes)),
        scratch_shapes=[pltpu.VMEM((width, columns), BF16)],
        compiler_params=pltpu.CompilerParams(vmem_limit_bytes=VMEM_BYTES),
        cost_estimate=pl.CostEstimate(
            flops=12 * key_tiles * TILE * width * head_cols,
            bytes_accessed=8 * key_tiles * TILE * width,
            transcendentals=0,
        ),
        name="project_back",
    )(own, *operands)


def finish_kernel(input_ref, gain_ref, branch_ref, result_ref, *refs):
    sum_refs = refs[:-2]
    out_ref, grad_ref = refs[-2:]
    rows = input_ref[...]
    width = rows.shape[1]
    values = rows.T
    gain = gain_ref[...]
    grad = sum_refs[0][...].astype(F32)
    for ref in sum_refs[1:]:
        grad += ref[...].astype(F32)
    root = lax.rsqrt(jnp.sum(values * values, axis=0, keepdims=True) * (1.0 / width) + EPSILON)
    scaled = grad * gain
    centre = jnp.sum(scaled * values, axis=0, keepdims=True) * (1.0 / width)
    total = root * scaled - values * (root * root * root * centre)
    grad_ref[...] = (total + branch_ref[...].astype(F32)).T
    out_ref[...] = rows + result_ref[...].astype(F32).T


def finish(block_input, gain, branch, result, sums):
    shape = jax.ShapeDtypeStruct(block_input.shape, F32)
    operands = (block_input, gain, branch, result, *sums)
    return pl.pallas_call(
        finish_kernel,
        grid=(1,),
        out_shape=(shape, shape),
        in_specs=whole_specs(operands),
        out_specs=tuple(whole_specs((shape, shape))),
        compiler_params=pltpu.CompilerParams(vmem_limit_bytes=VMEM_BYTES),
        name="finish",
    )(*operands)


def split_low(values):
    high = values.astype(BF16)
    return high, (values - high.astype(F32)).astype(BF16)


def load_tile(ref, first, count, *place):
    return jnp.concatenate([ref[(first + m, *place)] for m in range(count)], axis=-1)


def expert_kernel(parts, own_ref, *refs):
    state_refs = refs[:parts]
    (grad_ref, other_ref, in_ref, in_t_ref, out_ref, gain_ref) = refs[parts : parts + 6]
    (
        kept_ref,
        sent_ref,
        normed_ref,
        act_ref,
        pre_ref,
        gate_ref,
        router_sum,
        state_ref,
        full_ref,
        back_ref,
        joint_ref,
    ) = refs[parts + 6 :]

    @pl.when(pl.program_id(0) == 0)
    def _():
        router_sum[...] = jnp.zeros_like(router_sum)

    width = gain_ref.shape[0]
    share = width // parts
    hidden = act_ref.shape[1]
    experts = router_sum.shape[0]
    expert, own = own_ref[0], own_ref[1]
    chains, columns = state_ref.shape[0], state_ref.shape[-1]
    merged = kept_ref.shape[1] // chains
    slots = columns // merged
    gain = gain_ref[...]
    for a in range(chains):
        for k in range(parts):
            state_ref[a, own ^ k] = load_tile(state_refs[k], a * merged, merged)
            near = 2 * (k // 2) + ((own & 1) ^ (k & 1))
            full_ref[a, near] = load_tile(
                other_ref if k & 1 else grad_ref, a * merged, merged, k // 2
            )
    for a in range(chains):
        state = state_ref[a].reshape(width, columns).astype(F32)
        root = lax.rsqrt(jnp.sum(state * state, axis=0, keepdims=True) * (1.0 / width) + EPSILON)
        normed = (state * root * gain).astype(BF16)
        normed_ref[a] = normed
        both = dot(in_t_ref[...], normed)
        pre_act, logits = both[:hidden], both[hidden : hidden + experts]
        act_grad = dot(out_ref[...], full_ref[a].reshape(width, columns))
        raised = jnp.exp(logits - jnp.max(logits, axis=0, keepdims=True))
        router_probs = raised / jnp.sum(raised, axis=0, keepdims=True)
        chosen = lax.broadcasted_iota(jnp.int32, logits.shape, 0) == expert
        gate = jnp.sum(jnp.where(chosen, router_probs, 0.0), axis=0, keepdims=True)
        gate_ref[a] = gate
        square = pre_act * pre_act
        cdf = 0.5 + 0.5 * jnp.tanh(pre_act * (GELU_A + (GELU_A * GELU_B) * square))
        activated = pre_act * cdf
        act_ref[a] = activated.astype(BF16)
        rise = (2.0 * GELU_A) + (6.0 * GELU_A * GELU_B) * square
        pre_grad = act_grad * (cdf + activated * (1.0 - cdf) * rise)
        low_grad = pre_grad.astype(BF16)
        pre_ref[a] = low_grad
        gate_grad = jnp.sum(activated * act_grad, axis=0, keepdims=True)
        logit_grad = gate_grad * (chosen.astype(F32) - router_probs)
        centre = jnp.sum(pre_grad * pre_act, axis=0, keepdims=True)
        centre += jnp.sum(logit_grad * logits, axis=0, keepdims=True)
        joint_ref[a, :hidden, :] = low_grad
        joint_ref[a, hidden:, :] = jnp.concatenate(split_low(logit_grad), axis=0)
        high, low = split_low(logit_grad * gate)
        router_sum[...] += dot_rows(high, normed) + dot_rows(low, normed)
        normed_grad = dot(in_ref[...], joint_ref[a])
        state = state_ref[a].reshape(width, columns).astype(F32)
        back = (root * gate) * (normed_grad * gain - state * (root * centre * (1.0 / width)))
        back_ref[a] = back.astype(BF16).reshape(parts, share, columns)
        for k in range(parts):
            block = back_ref[a, own ^ k]
            target = sent_ref if k & 1 else kept_ref
            for m in range(merged):
                target[k // 2, a * merged + m] = block[:, m * slots : (m + 1) * slots]


def result_kernel(parts, own_ref, *refs):
    chunks = (len(refs) - 11) // 4
    sets = [refs[4 * c : 4 * c + 4] for c in range(chunks)]
    (
        grad_ref,
        other_ref,
        in_ref,
        out_t_ref,
        kept_ref,
        sent_ref,
        in_sum,
        out_sum,
        gain_sum,
        result_ref,
        full_ref,
    ) = refs[4 * chunks :]

    @pl.when(pl.program_id(0) == 0)
    def _():
        in_sum[...] = jnp.zeros_like(in_sum)
        out_sum[...] = jnp.zeros_like(out_sum)

    own = own_ref[1]
    width = out_t_ref.shape[0]
    share = width // parts
    merged = kept_ref.shape[1]
    for c in range(chunks):
        normed_ref, act_ref, pre_ref, gate_ref = sets[c]
        gate, activated = gate_ref[0], act_ref[0]
        columns = activated.shape[-1]
        slots = columns // merged
        for k in range(parts):
            near = 2 * (k // 2) + ((own & 1) ^ (k & 1))
            source = other_ref if k & 1 else grad_ref
            full_ref[c, near] = jnp.concatenate(
                [source[m, k // 2, :, c * slots : (c + 1) * slots] for m in range(merged)], axis=-1
            )
        result = dot(out_t_ref[...], activated) * gate
        result_ref[c] = result.astype(BF16).reshape(parts, share, columns)
        for k in range(parts):
            block = result_ref[c, own ^ k]
            target = sent_ref if k & 1 else kept_ref
            for m in range(merged):
                target[k // 2, m, :, c * slots : (c + 1) * slots] = block[
                    :, m * slots : (m + 1) * slots
                ]
        normed = (normed_ref[0].astype(F32) * gate).astype(BF16)
        in_sum[...] += dot_rows(normed, pre_ref[0])
        scaled = (full_ref[c].reshape(width, columns).astype(F32) * gate).astype(BF16)
        out_sum[...] += dot_rows(activated, scaled)

    @pl.when(pl.program_id(0) == pl.num_programs(0) - 1)
    def _():
        gain_sum[...] = jnp.sum(in_sum[...] * in_ref[...].astype(F32), axis=1, keepdims=True)


def fixed_spec(shape):
    return pl.BlockSpec(shape, lambda g: (0,) * len(shape))


def run_expert(own, states, grads, chunk, merged, chains, weights):
    parts = len(states)
    count, share, slots = states[0].shape
    width = share * parts
    columns = merged * slots
    steps = count // merged
    hidden = weights[2].shape[0]
    joint = weights[0].shape[1]
    experts = (joint - hidden) // 2
    half = parts // 2
    taken = merged * chains
    piece = pl.BlockSpec((taken, share, slots), lambda g: (g, 0, 0))
    grad_piece = pl.BlockSpec((taken, half, share, slots), lambda g: (g, 0, 0, chunk))
    split = pl.BlockSpec((half, taken, share, slots), lambda g: (0, g, 0, 0))
    wide = pl.BlockSpec((chains, width, columns), lambda g: (g, 0, 0))
    deep = pl.BlockSpec((chains, hidden, columns), lambda g: (g, 0, 0))
    flat = pl.BlockSpec((chains, 1, columns), lambda g: (g, 0, 0))
    return pl.pallas_call(
        functools.partial(expert_kernel, parts),
        grid=(steps // chains,),
        out_shape=(
            jax.ShapeDtypeStruct((half, count, share, slots), BF16),
            jax.ShapeDtypeStruct((half, count, share, slots), BF16),
            jax.ShapeDtypeStruct((steps, width, columns), BF16),
            jax.ShapeDtypeStruct((steps, hidden, columns), BF16),
            jax.ShapeDtypeStruct((steps, hidden, columns), BF16),
            jax.ShapeDtypeStruct((steps, 1, columns), F32),
            jax.ShapeDtypeStruct((experts, width), F32),
        ),
        in_specs=[pl.BlockSpec(memory_space=pltpu.SMEM)]
        + [piece] * parts
        + [grad_piece] * 2
        + [fixed_spec(weight.shape) for weight in weights],
        out_specs=(split, split, wide, deep, deep, flat, fixed_spec((experts, width))),
        scratch_shapes=[
            pltpu.VMEM((chains, parts, share, columns), BF16),
            pltpu.VMEM((chains, parts, share, columns), BF16),
            pltpu.VMEM((chains, parts, share, columns), BF16),
            pltpu.VMEM((chains, joint, columns), BF16),
        ],
        compiler_params=pltpu.CompilerParams(vmem_limit_bytes=VMEM_BYTES),
        cost_estimate=pl.CostEstimate(
            flops=16 * steps * columns * width * hidden,
            bytes_accessed=16 * steps * columns * width,
            transcendentals=steps * columns * hidden,
        ),
        name="expert",
    )(own, *states, *grads, *weights)


def run_result(own, saved, grads, merged, weights):
    chunks = len(saved)
    steps, width, columns = saved[0][0].shape
    hidden = saved[0][1].shape[1]
    _, half, share, _ = grads[0].shape
    parts = 2 * half
    slots = columns // merged
    wide = pl.BlockSpec((1, width, columns), lambda g: (g, 0, 0))
    deep = pl.BlockSpec((1, hidden, columns), lambda g: (g, 0, 0))
    flat = pl.BlockSpec((1, 1, columns), lambda g: (g, 0, 0))
    grad_piece = pl.BlockSpec((merged, half, share, slots * chunks), lambda g: (g, 0, 0, 0))
    split = pl.BlockSpec((half, merged, share, slots * chunks), lambda g: (0, g, 0, 0))
    total = jax.ShapeDtypeStruct((half, steps * merged, share, slots * chunks), BF16)
    return pl.pallas_call(
        functools.partial(result_kernel, parts),
        grid=(steps,),
        out_shape=(
            total,
            total,
            jax.ShapeDtypeStruct((width, hidden), F32),
            jax.ShapeDtypeStruct((hidden, width), F32),
            jax.ShapeDtypeStruct((width, 1), F32),
        ),
        in_specs=[pl.BlockSpec(memory_space=pltpu.SMEM)]
        + [wide, deep, deep, flat] * chunks
        + [grad_piece] * 2
        + [fixed_spec(weight.shape) for weight in weights],
        out_specs=(
            split,
            split,
            fixed_spec((width, hidden)),
            fixed_spec((hidden, width)),
            fixed_spec((width, 1)),
        ),
        scratch_shapes=[
            pltpu.VMEM((chunks, parts, share, columns), BF16),
            pltpu.VMEM((chunks, parts, share, columns), BF16),
        ],
        compiler_params=pltpu.CompilerParams(vmem_limit_bytes=VMEM_BYTES),
        cost_estimate=pl.CostEstimate(
            flops=16 * chunks * steps * columns * width * hidden,
            bytes_accessed=12 * chunks * steps * columns * width,
            transcendentals=0,
        ),
        name="result",
    )(own, *[array for arrays in saved for array in arrays], *grads, *weights)


def shards(
    block_input,
    attn_in_weight,
    attn_out_weight,
    position_bias,
    norm_gains,
    router_weight,
    expert_in,
    expert_out,
    segment_ids,
    expert_ids,
    out_grad,
):
    tensor_count, seq_count = lax.axis_size("tensor"), lax.axis_size("seq")
    tensor_place, seq_place = lax.axis_index("tensor"), lax.axis_index("seq")
    grid_count = lax.axis_size("dp") * seq_count
    grid_place = lax.axis_index("dp") * seq_count + seq_place
    local_count, width = block_input.shape
    group_count = local_count * tensor_count
    share = width // tensor_count
    bucket_count, heads = position_bias.shape
    head_cols = attn_in_weight.shape[2]
    experts = router_weight.shape[1]
    capacity = max(2, 2 * group_count // experts)
    tiles = group_count // TILE
    key_tiles = tiles * seq_count
    fast = seq_count == 2 and local_count == TILE and grid_count == 8

    def tiled(pieces):
        pieces = reorder(pieces, tensor_place)
        if local_count == TILE:
            return jnp.stack(pieces)
        return jnp.concatenate(pieces, axis=-1)[None]

    half = tensor_count // 2
    core = tensor_place & 1
    own_rows = jnp.concatenate(
        [
            jnp.transpose(block_input.astype(BF16)),
            jnp.pad(segment_ids.astype(BF16), ((0, 15), (0, 0))),
        ]
    )
    weight_piece = jnp.concatenate(
        [attn_in_weight[0], attn_in_weight[1], attn_in_weight[2], jnp.transpose(attn_out_weight)],
        axis=1,
    )
    grad_rows = jnp.transpose(out_grad.astype(BF16)).reshape(half, 2, share, local_count)
    grad_mine = lax.dynamic_index_in_dim(grad_rows, core, 1, keepdims=False)
    grad_theirs = lax.dynamic_index_in_dim(grad_rows, core ^ 1, 1, keepdims=False)
    in_plain, out_plain = expert_in[0], expert_out[0]
    if fast:
        far_rows = swap(own_rows, "seq", 1)
        near_two = swap(own_rows, "tensor", 2)
        columns = [weight_piece] + [swap(weight_piece, "dp", k) for k in range(1, grid_count // 2)]
        grad_other = swap(grad_theirs, "tensor", 1)
        far_rows, near_two, columns, grad_other, position_bias, expert_ids, in_plain, out_plain = (
            lax.optimization_barrier(
                (
                    far_rows,
                    near_two,
                    columns,
                    grad_other,
                    position_bias,
                    expert_ids,
                    in_plain,
                    out_plain,
                )
            )
        )
        far_two = swap(far_rows, "tensor", 2)
        near_columns = swap(weight_piece, "seq", 1)
        far_columns = swap(jnp.stack(columns[1:]), "seq", 1)
        near_one, near_three = swap(own_rows, "tensor", 1), swap(near_two, "tensor", 1)
    else:
        grad_other = swap(grad_theirs, "tensor", 1)
        both_rows = lax.all_gather(own_rows, "seq", axis=0, tiled=False)
        row_pieces = gather_relative(both_rows, "tensor")
        own_first = seq_place * tiles
        row_pieces = jnp.concatenate(reorder(row_pieces, tensor_place), axis=-1)
        row_pieces = row_pieces.reshape(seq_count, -1, tiles, TILE)
        row_pieces = [jnp.moveaxis(row_pieces, 2, 1).reshape(key_tiles, -1, TILE)]
        weight_pieces = [lax.all_gather(weight_piece, ("dp", "seq"), axis=0, tiled=True)]

    bias = bias_tiles(position_bias)
    in_t, out_t = jnp.transpose(in_plain), jnp.transpose(out_plain)
    router_t = jnp.transpose(router_weight)
    in_joint = jnp.concatenate([in_plain, router_weight, router_weight], axis=1)
    in_t = jnp.concatenate([in_t, router_t, router_t])
    route_all = expert_ids[:, 0]
    expert_range = jnp.arange(experts, dtype=jnp.int32)
    route_hot = (route_all[:, None] == expert_range[None, :]).astype(jnp.int32)
    slot_rank = jnp.sum(jnp.cumsum(route_hot, axis=0) * route_hot, axis=-1) - 1
    target = (route_all * capacity + slot_rank).reshape(1, tiles, TILE, 1)
    places = jnp.arange(experts * capacity, dtype=jnp.int32).reshape(experts, 1, 1, capacity)
    chunks = 2 if capacity >= TILE else 1
    slots = capacity // chunks
    spread = max(1, TILE // capacity)
    merged = max(1, TILE // (slots * spread))

    def exchange(values):
        return lax.all_to_all(values, ("dp", "seq"), split_axis=0, concat_axis=0, tiled=True)

    def joined(values):
        if spread == 1:
            return values
        shape = values.shape
        values = values.reshape((-1, spread) + shape[1:])
        return jnp.moveaxis(values, 1, -2).reshape(
            (shape[0] // spread,) + shape[1:-1] + (spread * shape[-1],)
        )

    def parted(values):
        if spread == 1:
            return values
        shape = values.shape
        values = values.reshape(shape[:-1] + (spread, shape[-1] // spread))
        return jnp.moveaxis(values, -2, 1).reshape((-1,) + shape[1:-1] + (shape[-1] // spread,))


    gain_one = norm_gains[0][:, None]
    gain_two = norm_gains[1][:, None]
    if fast:
        (
            far_two,
            far_columns,
            gain_one,
            bias,
            in_t,
            in_joint,
            out_t,
            target,
            gain_two,
            grad_mine,
            grad_other,
        ) = lax.optimization_barrier(
            (
                far_two,
                far_columns,
                gain_one,
                bias,
                in_t,
                in_joint,
                out_t,
                target,
                gain_two,
                grad_mine,
                grad_other,
            )
        )
        far_one, far_three = swap(far_rows, "tensor", 1), swap(far_two, "tensor", 1)
        row_pieces = [own_rows, near_one, near_two, near_three]
        row_pieces += [far_rows, far_one, far_two, far_three]
        row_pieces = [rows[None] for rows in row_pieces]
        weight_pieces = [weight_piece, near_columns]
        for k in range(1, grid_count // 2):
            weight_pieces += [columns[k], far_columns[k - 1]]
        own_first = jnp.int32(0)
    own = jnp.stack([grid_place, tensor_place, seq_place, own_first]).astype(jnp.int32)
    onehot = (target == places).astype(BF16)
    grad_pair = swap(jnp.stack([grad_mine, grad_other]), "tensor", 2)
    grad_here = tiled([grad_mine, grad_other, grad_pair[0], grad_pair[1]])
    grad_buffer = einsum("nkdq,enqs->ekds", grad_here, onehot).astype(BF16)
    meta, queries, keys_values, normed_tiles, input_share, in_flat, out_blocks, out_t_blocks = (
        project(own, row_pieces, weight_pieces, gain_one, tiles, key_tiles, share)
    )
    queries, grad_buffer = lax.optimization_barrier((queries, grad_buffer))
    grad_arrived = joined(exchange(grad_buffer))
    exact, attended, logs, attn_even, attn_odd = attend(
        meta, queries, keys_values, bias, out_blocks
    )
    attn_share = sum_tensor(attn_even, attn_odd)
    state_share = (input_share.astype(F32) + attn_share).astype(BF16)
    state_share, grad_arrived = lax.optimization_barrier((state_share, grad_arrived))
    grad_near = swap(grad_arrived, "tensor", 1)

    weights = (in_joint, in_t, expert_out[0], gain_two)
    grads = (grad_arrived, grad_near)
    buffers = [
        einsum("ndq,enqs->eds", state_share, onehot[..., c * slots : (c + 1) * slots]).astype(BF16)
        for c in range(chunks)
    ]
    buffers = list(lax.optimization_barrier(tuple(buffers)))
    arrivals = [joined(exchange(buffer)) for buffer in buffers]
    chains = 2 if arrivals[0].shape[0] // merged % 2 == 0 else 1
    gathered = []
    for arrival in arrivals:
        gathered.append(
            [arrival, swap(arrival, "tensor", 1), swap(arrival, "tensor", 2)]
        )
    gathered[0][0], gathered[-1][0] = lax.optimization_barrier((gathered[0][0], gathered[-1][0]))
    saved, halves, crossed = [], [], []
    small = jnp.zeros((experts, width), F32)
    for c in range(chunks):
        gathered[c].append(swap(gathered[c][2], "tensor", 1))
        kept, sent, normed_two, activated, pre_grad, gate, router_sum = run_expert(
            own, gathered[c], grads, c, merged, chains, weights
        )
        saved.append((normed_two, activated, pre_grad, gate))
        if c + 1 < chunks:
            sent, gathered[c + 1][2] = lax.optimization_barrier((sent, gathered[c + 1][2]))
        if c > 0:
            sent, crossed[c - 1] = lax.optimization_barrier((sent, crossed[c - 1]))
        near, got, to_send = core_step(kept, sent)
        if c + 1 == chunks:
            own_late, to_send = lax.optimization_barrier((own, to_send))
        halves.append((near, got))
        crossed.append(swap(to_send, "tensor", 2))
        small = small + router_sum
    returned = [
        exchange(parted(chip_step(*halves[c], crossed[c]).astype(BF16)))
        for c in range(chunks - 1)
    ]
    result_even, result_odd, grad_expert_in, grad_expert_out, in_gain = run_result(
        own_late, saved, grads, merged, (expert_in[0], out_t)
    )
    tied = lax.optimization_barrier((result_odd, crossed[-1], *returned))
    result_odd, crossed[-1], returned = tied[0], tied[1], list(tied[2:])
    returned.append(exchange(parted(chip_step(*halves[-1], crossed[-1]).astype(BF16))))
    gain_part = in_gain[:, 0] + jnp.sum(small * router_t.astype(F32), axis=0)
    router_gains = jnp.concatenate([small, (gain_part / norm_gains[1])[None]])
    state_grad = lax.dynamic_index_in_dim(grad_here, tensor_place // 2, 1, keepdims=False)
    state_grad = state_grad.astype(F32)
    for c in range(chunks):
        state_grad = state_grad + einsum(
            "eds,enqs->ndq", returned[c], onehot[..., c * slots : (c + 1) * slots]
        )
    state_grad = state_grad.astype(BF16)
    result_near, result_got, result_sent = core_step(result_even, result_odd)
    result_far = swap(result_sent, "tensor", 2)

    branch = [state_grad, swap(state_grad, "tensor", 1), swap(state_grad, "tensor", 2)]
    result_far, branch[2] = lax.optimization_barrier((result_far, branch[2]))
    branch.append(swap(branch[2], "tensor", 1))
    result_total = chip_step(result_near, result_got, result_far).astype(BF16)
    result_back = exchange(parted(result_total))
    dq, dkv, bias_rows = attend_back(
        meta, queries, keys_values, bias, out_t_blocks, exact, logs, branch, bucket_count
    )
    dq, dkv, bias_rows, result_back = lax.optimization_barrier((dq, dkv, bias_rows, result_back))

    def joined_small():
        bias_padded = lax.dynamic_update_slice_in_dim(
            jnp.zeros((heads * tensor_count, bucket_count), F32),
            jnp.sum(bias_rows, axis=2),
            tensor_place * heads,
            0,
        )
        return jnp.concatenate(
            [router_gains.reshape(-1), gain_part[:, 0] / norm_gains[0], bias_padded.reshape(-1)]
        )

    def result_rows_of():
        shares = attn_share + einsum("eds,enqs->ndq", result_back, onehot)
        return jnp.moveaxis(shares.astype(BF16), 0, 1).reshape(share, tensor_count, local_count)

    if fast:
        far_even, far_odd, own_even, own_odd, weight_even, weight_odd, gain_part = project_back(
            True, own, dq, dkv, normed_tiles, in_flat, attended, branch, grid_count
        )
        far_near, far_got, far_send = core_step(far_even, far_odd)
        own_near, own_got, own_send = core_step(own_even, own_odd)
        weight_sent = swap(weight_odd, "seq", 1)
        far_send, own_send, gain_part, result_back = lax.optimization_barrier(
            (far_send, own_send, gain_part, result_back)
        )
        far_sent = swap(far_send, "tensor", 2)
        small = sum_all(joined_small(), ("seq",))
        result_share = result_rows_of()
        far_sent, weight_sent, small, result_share, own_send = lax.optimization_barrier(
            (far_sent, weight_sent, small, result_share, own_send)
        )
        own_sent = swap(own_send, "tensor", 2)
        far_sum = chip_step(far_near, far_got, far_sent).astype(BF16)
        sums = [own_near, own_got, own_sent, swap(far_sum, "seq", 1)]
        weight_half = weight_even.astype(F32) + weight_sent.astype(F32)
        weight_grad = weight_half[0]
        for k in range(1, grid_count // 2):
            weight_grad = weight_grad + swap(weight_half[k].astype(BF16), "dp", k).astype(F32)
    else:
        row_part, weight_part, gain_part = project_back(
            False, own, dq, dkv, normed_tiles, in_flat, attended, branch, grid_count
        )
        row_part = lax.psum_scatter(row_part, "seq", scatter_dimension=0, tiled=True)
        row_part = jnp.moveaxis(row_part, 0, 1).reshape(width, tensor_count, local_count)
        blocks = [
            lax.dynamic_index_in_dim(row_part, tensor_place ^ k, 1, keepdims=False)
            for k in range(tensor_count)
        ]
        sums = [sum_tensor(jnp.stack(blocks[0::2]), jnp.stack(blocks[1::2]))]
        small = sum_all(joined_small(), ("seq",))
        result_share = result_rows_of()
        weight_grad = lax.psum_scatter(
            weight_part, ("dp", "seq"), scatter_dimension=0, tiled=True
        ).astype(F32)
    grad_attn_in = jnp.stack(
        [weight_grad[:, c * head_cols : (c + 1) * head_cols] for c in range(3)]
    )
    grad_attn_out = jnp.transpose(weight_grad[:, 3 * head_cols :])

    small = sum_all(small, ("dp", "tensor"))
    first, second = experts * width, (experts + 1) * width
    grad_router = jnp.transpose(small[:first].reshape(experts, width))
    grad_gains = jnp.stack([small[second : second + width], small[first:second]])
    bias_sum = small[second + width :].reshape(heads * tensor_count, bucket_count)
    grad_bias = jnp.transpose(lax.dynamic_slice_in_dim(bias_sum, tensor_place * heads, heads, 0))

    result_rows = lax.all_to_all(
        jnp.moveaxis(result_share, 1, 0), "tensor", split_axis=0, concat_axis=0, tiled=True
    ).reshape(width, local_count)
    if local_count == TILE:
        own_branch = [
            lax.dynamic_index_in_dim(piece, tensor_place, 0, keepdims=False) for piece in branch
        ]
    else:
        own_branch = [
            lax.dynamic_slice_in_dim(piece[0], tensor_place * local_count, local_count, 1)
            for piece in branch
        ]
    own_branch = jnp.concatenate(reorder(own_branch, tensor_place))
    block_out, input_grad = finish(block_input, gain_one, own_branch, result_rows, sums)
    return (
        block_out,
        input_grad,
        grad_attn_in,
        grad_attn_out,
        grad_bias,
        grad_gains,
        grad_router,
        grad_expert_in[None],
        grad_expert_out[None],
    )


def solution(mesh):
    return jax.shard_map(
        shards,
        mesh=mesh,
        in_specs=(
            P(("dp", "seq", "tensor"), None),
            P(None, ("dp", "seq"), "tensor"),
            P("tensor", ("dp", "seq")),
            P(None, "tensor"),
            P(),
            P(),
            P(("dp", "seq"), None, "tensor"),
            P(("dp", "seq"), "tensor", None),
            P("dp", ("seq", "tensor")),
            P(("dp", "seq"), None),
            P(("dp", "seq", "tensor"), None),
        ),
        out_specs=(
            P(("dp", "seq", "tensor"), None),
            P(("dp", "seq", "tensor"), None),
            P(None, ("dp", "seq"), "tensor"),
            P("tensor", ("dp", "seq")),
            P(None, "tensor"),
            P(),
            P(),
            P(("dp", "seq"), None, "tensor"),
            P(("dp", "seq"), "tensor", None),
        ),
        check_vma=False,
    )
```

```python
import functools
import math

import jax
import jax.numpy as jnp
from jax import lax
from jax.experimental import pallas as pl
from jax.experimental.pallas import tpu as pltpu
from jax.sharding import PartitionSpec as P

EPSILON = 1e-06
EDGES = (1, 2, 3, 4, 5, 6, 7, 8, 12, 16, 23, 32, 46, 64, 91)
TILE = 256
HALF = TILE // 2
LOG2E = math.log2(math.e)
SCALE = 0.125
MASKED = -1e30
LOWEST = -1e29
EXTRA = 16
VMEM_BYTES = 60 * 1024 * 1024
GELU_A = math.sqrt(2.0 / math.pi)
GELU_B = 0.044715
BF16 = jnp.bfloat16
F32 = jnp.float32


def dot(left_side, right_side):
    return jnp.dot(left_side, right_side, preferred_element_type=F32)


def dot_rows(left_side, right_side):
    return lax.dot_general(
        left_side, right_side, (((1,), (1,)), ((), ())), preferred_element_type=F32
    )


def einsum(formula, *operands):
    return jnp.einsum(formula, *operands, preferred_element_type=F32)


def swap(values, axis, bit):
    count = lax.axis_size(axis)
    return lax.ppermute(values, axis, [(i, i ^ bit) for i in range(count)])


def bits_of(count):
    return [1 << i for i in range(count.bit_length() - 1)]


def gather_relative(values, axis):
    pieces = {0: values}
    for bit in reversed(bits_of(lax.axis_size(axis))):
        for place in list(pieces):
            pieces[place ^ bit] = swap(pieces[place], axis, bit)
    return [pieces[place] for place in range(len(pieces))]


def core_step(kept, sent):
    got = swap(sent, "tensor", 1)
    to_send = (kept[1].astype(F32) + got[1].astype(F32)).astype(BF16)
    return kept[0], got[0], to_send


def chip_step(near, got, far):
    return near.astype(F32) + got.astype(F32) + far.astype(F32)


def sum_tensor(kept, sent):
    near, got, to_send = core_step(kept, sent)
    return chip_step(near, got, swap(to_send, "tensor", 2))


def reorder(pieces, own_index):
    for bit in bits_of(len(pieces)):
        flip = (own_index & bit) != 0
        pieces = [
            jnp.where(flip, pieces[place ^ bit], pieces[place]) for place in range(len(pieces))
        ]
    return pieces


def sum_all(values, axes):
    for axis in axes:
        for bit in bits_of(lax.axis_size(axis)):
            values = values + swap(values, axis, bit)
    return values


def bucket_of(relative, half_count):
    magnitude = jnp.abs(relative)
    counted = jnp.zeros(relative.shape, jnp.int32)
    for edge_value in EDGES:
        counted = counted + (magnitude >= edge_value).astype(jnp.int32)
    return counted + jnp.where(relative > 0, half_count, 0).astype(jnp.int32)


KINDS = ((0, 0, 0, 0), (0, 0, 1, 0), (2, 1, 3, 2), (4, 3, 4, 4), (4, 4, 4, 4))


def near_tiles(table_ref, near_ref):
    heads = near_ref.shape[0]
    bucket_count = table_ref.shape[0] // heads
    half_count = bucket_count // 2
    offset = lax.broadcasted_iota(jnp.int32, (HALF, HALF), 0) - lax.broadcasted_iota(
        jnp.int32, (HALF, HALF), 1
    )
    near_of = (range(1, half_count), range(bucket_count), range(half_count + 1, bucket_count))
    for shift, buckets in enumerate(near_of):
        grid = bucket_of(offset + (shift - 1) * HALF, half_count)
        for h in range(heads):
            total = jnp.zeros((HALF, HALF), F32)
            for bucket_index in buckets:
                value = table_ref[bucket_index * heads + h] * LOG2E
                total = jnp.where(grid == bucket_index, value, total)
            near_ref[h, 1 + shift] = total
    for h in range(heads):
        for kind, bucket_index in ((0, half_count - 1), (4, bucket_count - 1)):
            value = table_ref[bucket_index * heads + h] * LOG2E
            near_ref[h, kind] = jnp.full((HALF, HALF), value, F32)


def fill_tiles(near_ref, bias_ref):
    for kind, blocks in enumerate(KINDS):
        for h in range(near_ref.shape[0]):
            for place, block in enumerate(blocks):
                row, column = place // 2 * HALF, place % 2 * HALF
                bias_ref[kind, h, row : row + HALF, column : column + HALF] = near_ref[h, block]


def span_of(meta_ref, query_tile, key_tiles):
    opening, closing = meta_ref[1], meta_ref[2]
    first = query_tile * TILE
    last = first + TILE - 1
    begin = jnp.where(first < opening, 0, jnp.where(first < closing, opening, closing))
    end = jnp.where(last < opening, opening, jnp.where(last < closing, closing, key_tiles * TILE))
    return begin // TILE, (end + TILE - 1) // TILE


def document_row(meta_ref, tile):
    place = tile * TILE + lax.broadcasted_iota(jnp.int32, (EXTRA, TILE), 1)
    return (place >= meta_ref[1]).astype(jnp.int32) + (place >= meta_ref[2]).astype(jnp.int32)


def key_rows(meta_ref, tile):
    row = lax.broadcasted_iota(jnp.int32, (EXTRA, TILE), 0)
    differs = jnp.where(document_row(meta_ref, tile) != row, MASKED, 0.0)
    return jnp.where(row < 3, differs, jnp.where(row < 6, 1.0, 0.0)).astype(BF16)


def query_rows(meta_ref, tile, terms):
    row = lax.broadcasted_iota(jnp.int32, (EXTRA, TILE), 0)
    agrees = jnp.where(document_row(meta_ref, tile) == row, 1.0, 0.0)
    return jnp.where(row < 3, agrees, three_rows(row - 3, terms)).astype(BF16)


def three_rows(row, terms):
    result = jnp.zeros(row.shape, F32)
    for i, term in enumerate(terms):
        result = jnp.where(row == i, term, result)
    return result


def split_three(values):
    first = values.astype(BF16).astype(F32)
    second = (values - first).astype(BF16).astype(F32)
    return first, second, values - first - second


def attend_kernel(
    meta_ref,
    q_ref,
    kv_ref,
    near_ref,
    weight_ref,
    exact_ref,
    out_ref,
    log_ref,
    even_ref,
    odd_ref,
    key_ref,
    query_ref,
    sum_ref,
    bias_ref,
):
    key_tiles = kv_ref.shape[0]
    heads = near_ref.shape[0]
    fill_tiles(near_ref, bias_ref)
    size = q_ref.shape[1] // heads

    def turn(j, carry):
        kept = meta_ref[3 + j]
        extra = key_rows(meta_ref, j)
        for h in range(heads):
            rows = kv_ref[kept, h * size : (h + 1) * size, :]
            key_ref[kept, h] = jnp.concatenate([rows, extra], axis=0).T
        return carry

    lax.fori_loop(0, key_tiles, turn, 0)
    ones = jnp.ones((EXTRA, TILE), BF16)

    def query_body(i, carry):
        tile = meta_ref[3 + key_tiles + i]
        place = tile % meta_ref[0]
        begin, end = span_of(meta_ref, tile, key_tiles)
        extra = query_rows(meta_ref, tile, ())
        for h in range(heads):
            rows = q_ref[i, h * size : (h + 1) * size, :]
            query_ref[h] = jnp.concatenate([rows, extra], axis=0)
        sum_ref[...] = jnp.zeros_like(sum_ref)

        def key_body(j, peaks):
            kept = meta_ref[3 + j]
            kind = jnp.clip(j - tile, -2, 2) + 2
            scores = [
                dot(key_ref[kept, h], query_ref[h]) + bias_ref[kind, h] for h in range(heads)
            ]
            new_peaks = [
                jnp.maximum(peaks[h], jnp.max(scores[h], axis=0, keepdims=True))
                for h in range(heads)
            ]
            weights = [jnp.exp2(scores[h] - new_peaks[h]).astype(BF16) for h in range(heads)]
            added = []
            for h in range(heads):
                values = kv_ref[kept, (heads + h) * size : (heads + h + 1) * size, :]
                added.append(dot(jnp.concatenate([values, ones], axis=0), weights[h]))
            for h in range(heads):
                sum_ref[h] = sum_ref[h] * jnp.exp2(peaks[h] - new_peaks[h]) + added[h]
            return tuple(new_peaks)

        start = tuple(jnp.full((1, TILE), LOWEST, F32) for _ in range(heads))
        peaks = lax.fori_loop(begin, end, key_body, start)
        for h in range(heads):
            rows = slice(h * size, (h + 1) * size)
            total = sum_ref[h, size : size + 1, :]
            result = sum_ref[h, :size, :] * (1.0 / total)
            exact_ref[i, rows, :] = result
            out_ref[place, rows, :] = result.astype(BF16)
            log_ref[i, h] = peaks[h] + jnp.log2(total)
        attended = out_ref[place]
        for k in range(weight_ref.shape[0]):
            block = dot(weight_ref[k], attended).astype(BF16)
            (odd_ref if k & 1 else even_ref)[k // 2, place] = block
        return carry

    lax.fori_loop(0, q_ref.shape[0], query_body, 0)


def estimate(queries, key_tiles, products):
    pairs = queries.shape[0] * TILE * key_tiles * TILE
    return pl.CostEstimate(
        flops=2 * products * pairs * queries.shape[1],
        bytes_accessed=8 * pairs,
        transcendentals=3 * pairs,
    )


def whole_specs(arrays):
    return [pl.BlockSpec(array.shape, functools.partial(origin, len(array.shape))) for array in arrays]


def origin(dimensions, step):
    return (0,) * dimensions


def attend(meta, queries, keys_values, near, out_blocks):
    query_tiles, width, _ = queries.shape
    key_tiles = keys_values.shape[0]
    heads = near.shape[0]
    parts, share, _ = out_blocks.shape
    blocks = jax.ShapeDtypeStruct((parts // 2, query_tiles, share, TILE), BF16)
    shapes = (
        jax.ShapeDtypeStruct(queries.shape, F32),
        jax.ShapeDtypeStruct(queries.shape, BF16),
        jax.ShapeDtypeStruct((query_tiles, heads, 1, TILE), F32),
        blocks,
        blocks,
    )
    operands = (queries, keys_values, near, out_blocks)
    return pl.pallas_call(
        attend_kernel,
        grid=(1,),
        out_shape=shapes,
        in_specs=[pl.BlockSpec(memory_space=pltpu.SMEM)] + whole_specs(operands),
        out_specs=tuple(whole_specs(shapes)),
        scratch_shapes=[
            pltpu.VMEM((key_tiles, heads, TILE, width // heads + EXTRA), BF16),
            pltpu.VMEM((heads, width // heads + EXTRA, TILE), BF16),
            pltpu.VMEM((heads, width // heads + EXTRA, TILE), F32),
            pltpu.VMEM((len(KINDS), heads, TILE, TILE), F32),
        ],
        compiler_params=pltpu.CompilerParams(vmem_limit_bytes=VMEM_BYTES),
        cost_estimate=estimate(queries, key_tiles, 2),
        name="attend",
    )(meta, *operands)


def bucket_rows(tiles_ref, rows_ref):
    heads, bucket_count = rows_ref.shape[:2]
    half_count = bucket_count // 2
    offset = lax.broadcasted_iota(jnp.int32, (HALF, HALF), 0) - lax.broadcasted_iota(
        jnp.int32, (HALF, HALF), 1
    )
    grids = [bucket_of(offset + shift * HALF, half_count) for shift in (-1, 0, 1)]
    first, last = slice(0, HALF), slice(HALF, TILE)

    def column_sums(values):
        return jnp.sum(values, axis=0, keepdims=True)

    def head_body(h, carry):
        before = tiles_ref[2, h, first, last] + tiles_ref[1, h, last, first]
        same = tiles_ref[2, h, first, first] + tiles_ref[2, h, last, last]
        after = tiles_ref[2, h, last, first] + tiles_ref[3, h, first, last]
        far_before = column_sums(tiles_ref[0, h, :, first] + tiles_ref[0, h, :, last])
        far_before += column_sums(tiles_ref[1, h, first, first] + tiles_ref[1, h, first, last])
        far_before += column_sums(tiles_ref[1, h, last, last])
        far_after = column_sums(tiles_ref[4, h, :, first] + tiles_ref[4, h, :, last])
        far_after += column_sums(tiles_ref[3, h, last, first] + tiles_ref[3, h, last, last])
        far_after += column_sums(tiles_ref[3, h, first, first])
        for bucket_index in range(bucket_count):
            row = column_sums(jnp.where(grids[1] == bucket_index, same, 0.0))
            if 0 < bucket_index < half_count:
                row += column_sums(jnp.where(grids[0] == bucket_index, before, 0.0))
            if bucket_index > half_count:
                row += column_sums(jnp.where(grids[2] == bucket_index, after, 0.0))
            if bucket_index == half_count - 1:
                row += far_before
            if bucket_index == bucket_count - 1:
                row += far_after
            rows_ref[h, bucket_index : bucket_index + 1, :] = row
        return carry

    lax.fori_loop(0, heads, head_body, 0)


def attend_back_kernel(
    meta_ref,
    q_ref,
    kv_ref,
    near_ref,
    weight_ref,
    exact_ref,
    log_ref,
    *refs,
):
    parts = weight_ref.shape[0]
    branch_refs = refs[:parts]
    (
        dq_ref,
        dkv_ref,
        rows_ref,
        tiles_ref,
        key_ref,
        value_ref,
        query_ref,
        grad_ref,
        dq_sum,
        dkv_sum,
        bias_ref,
    ) = refs[parts:]
    key_tiles = kv_ref.shape[0]
    heads = near_ref.shape[0]
    fill_tiles(near_ref, bias_ref)
    size = q_ref.shape[1] // heads

    row = lax.broadcasted_iota(jnp.int32, (EXTRA, TILE), 0)
    ones = jnp.where(row < 3, 1.0, 0.0).astype(BF16)

    def turn(j, carry):
        kept = meta_ref[3 + j]
        extra = key_rows(meta_ref, j)
        for h in range(heads):
            rows = kv_ref[kept, h * size : (h + 1) * size, :]
            key_ref[kept, h] = jnp.concatenate([rows, extra], axis=0).T
            rows = kv_ref[kept, (heads + h) * size : (heads + h + 1) * size, :]
            value_ref[kept, h] = jnp.concatenate([rows, ones], axis=0).T
        return carry

    lax.fori_loop(0, key_tiles, turn, 0)
    dkv_sum[...] = jnp.zeros_like(dkv_sum)
    tiles_ref[...] = jnp.zeros_like(tiles_ref)

    def query_body(i, carry):
        tile = meta_ref[3 + key_tiles + i]
        place = tile % meta_ref[0]
        begin, end = span_of(meta_ref, tile, key_tiles)
        dq_sum[...] = jnp.zeros_like(dq_sum)
        grad_sum = dot(weight_ref[0], branch_refs[0][place])
        for k in range(1, parts):
            grad_sum += dot(weight_ref[k], branch_refs[k][place])
        for h in range(heads):
            rows = slice(h * size, (h + 1) * size)
            grad = grad_sum[rows].astype(BF16)
            centre = jnp.sum(grad.astype(F32) * exact_ref[i, rows, :], axis=0, keepdims=True)
            extra = three_rows(row, split_three(-centre)).astype(BF16)
            grad_ref[h] = jnp.concatenate([grad, extra], axis=0)
            extra = query_rows(meta_ref, tile, split_three(-log_ref[i, h]))
            query_ref[h] = jnp.concatenate([q_ref[i, rows, :], extra], axis=0)

        def key_body(j, inner):
            kept = meta_ref[3 + j]
            kind = jnp.clip(j - tile, -2, 2) + 2
            probs = [
                jnp.exp2(dot(key_ref[kept, h], query_ref[h]) + bias_ref[kind, h])
                for h in range(heads)
            ]
            score_grads = [probs[h] * dot(value_ref[kept, h], grad_ref[h]) for h in range(heads)]
            low_probs = [prob.astype(BF16) for prob in probs]
            low_grads = [score_grad.astype(BF16) for score_grad in score_grads]
            key_adds, value_adds, query_adds = [], [], []
            for h in range(heads):
                rows = slice(h * size, (h + 1) * size)
                key_adds.append(dot_rows(q_ref[i, rows, :], low_grads[h]))
                value_adds.append(dot_rows(grad_ref[h, :size, :], low_probs[h]))
                query_adds.append(dot(kv_ref[kept, rows, :], low_grads[h]))
            for h in range(heads):
                rows = slice(h * size, (h + 1) * size)
                value_rows = slice((heads + h) * size, (heads + h + 1) * size)
                tiles_ref[kind, h] += score_grads[h]
                dkv_sum[kept, rows, :] += key_adds[h]
                dkv_sum[kept, value_rows, :] += value_adds[h]
                dq_sum[rows, :] += query_adds[h]
            return inner

        lax.fori_loop(begin, end, key_body, 0)
        dq_ref[i] = (dq_sum[...] * SCALE).astype(BF16)
        return carry

    lax.fori_loop(0, q_ref.shape[0], query_body, 0)
    middle = heads * size
    dkv_ref[:, :middle, :] = (dkv_sum[:, :middle, :] * (1.0 / LOG2E)).astype(BF16)
    dkv_ref[:, middle:, :] = dkv_sum[:, middle:, :].astype(BF16)
    bucket_rows(tiles_ref, rows_ref)


def attend_back(meta, queries, keys_values, near, out_blocks, exact, logs, branch, buckets):
    key_tiles = keys_values.shape[0]
    heads = near.shape[0]
    size = queries.shape[1] // heads
    shapes = (
        jax.ShapeDtypeStruct(queries.shape, BF16),
        jax.ShapeDtypeStruct(keys_values.shape, BF16),
        jax.ShapeDtypeStruct((heads, buckets, HALF), F32),
    )
    operands = (queries, keys_values, near, out_blocks, exact, logs, *branch)
    return pl.pallas_call(
        attend_back_kernel,
        grid=(1,),
        out_shape=shapes,
        in_specs=[pl.BlockSpec(memory_space=pltpu.SMEM)] + whole_specs(operands),
        out_specs=tuple(whole_specs(shapes)),
        scratch_shapes=[
            pltpu.VMEM((len(KINDS), heads, TILE, TILE), F32),
            pltpu.VMEM((key_tiles, heads, TILE, size + EXTRA), BF16),
            pltpu.VMEM((key_tiles, heads, TILE, size + EXTRA), BF16),
            pltpu.VMEM((heads, size + EXTRA, TILE), BF16),
            pltpu.VMEM((heads, size + EXTRA, TILE), BF16),
            pltpu.VMEM(queries.shape[1:], F32),
            pltpu.VMEM(keys_values.shape, F32),
            pltpu.VMEM((len(KINDS), heads, TILE, TILE), F32),
        ],
        compiler_params=pltpu.CompilerParams(vmem_limit_bytes=VMEM_BYTES),
        cost_estimate=estimate(queries, key_tiles, 5),
        name="attend_back",
    )(meta, *operands)


def project_kernel(piece_count, weight_count, tiles, share, own_ref, table_ref, *refs):
    piece_refs = refs[:piece_count]
    weight_refs = refs[piece_count : piece_count + weight_count]
    gain_ref = refs[piece_count + weight_count]
    (
        meta_ref,
        q_ref,
        kv_ref,
        normed_ref,
        input_ref,
        in_ref,
        out_ref,
        out_t_ref,
        near_ref,
        block_ref,
        turned_ref,
    ) = refs[piece_count + weight_count + 1 :]
    grid_place, tensor_place, seq_place, own_first = (own_ref[i] for i in range(4))
    width = gain_ref.shape[0]
    head_cols = q_ref.shape[1]
    columns = turned_ref.shape[0]
    for k in range(weight_count):
        place = grid_place ^ k if weight_count > 1 else 0
        block_ref[place] = weight_refs[k][...]
    full = block_ref[...].reshape(width, columns)
    in_ref[...] = full[:, : 3 * head_cols]
    turned_ref[...] = full.T
    blocks_here = width // share
    tall = block_ref.shape[1]
    per = share // tall if weight_count > 1 else 1
    for k in range(blocks_here):
        if weight_count > 1:
            block = block_ref[pl.ds((tensor_place ^ k) * per, per), :, 3 * head_cols :]
            block = block.reshape(share, head_cols)
        else:
            start = pl.multiple_of((tensor_place ^ k) * share, share)
            block = block_ref[0, pl.ds(start, share), 3 * head_cols :]
        out_ref[k] = block
        out_t_ref[k] = block.T
    key_tiles = kv_ref.shape[0]
    near_tiles(table_ref, near_ref)
    early = jnp.zeros((1, TILE), F32)
    late = jnp.zeros((1, TILE), F32)
    gain = gain_ref[...]
    for k in range(piece_count):
        for s in range(piece_refs[0].shape[0]):
            kept = s + k
            rows = piece_refs[k][s, :width, :].astype(F32)
            ids = piece_refs[k][s, width : width + 16, :][:1].astype(F32)
            early += (ids < 0.5).astype(F32)
            late += (ids < 1.5).astype(F32)
            root = lax.rsqrt(jnp.sum(rows * rows, axis=0, keepdims=True) * (1.0 / width) + EPSILON)
            normed = (rows * root * gain).astype(BF16)
            normed_ref[kept] = normed
            kv_ref[kept] = dot(turned_ref[head_cols : 3 * head_cols, :], normed).astype(BF16)
    for i in range(tiles):
        normed = normed_ref[own_first + i]
        q_ref[i] = (dot(turned_ref[:head_cols, :], normed) * (SCALE * LOG2E)).astype(BF16)
        start = pl.multiple_of(tensor_place * share, share)
        if piece_count > 1:
            input_ref[tensor_place ^ i] = piece_refs[i][0, pl.ds(start, share), :]
        else:
            input_ref[i] = piece_refs[0][own_first + i, pl.ds(start, share), :]
    meta_ref[0] = tiles
    meta_ref[1] = jnp.sum(early).astype(jnp.int32)
    meta_ref[2] = jnp.sum(late).astype(jnp.int32)
    for j in range(key_tiles):
        if piece_count > 1:
            meta_ref[3 + j] = ((j // tiles) ^ seq_place) * tiles + ((j % tiles) ^ tensor_place)
        else:
            meta_ref[3 + j] = j
    for i in range(tiles):
        shift = tensor_place ^ i if piece_count > 1 else i
        meta_ref[3 + key_tiles + i] = seq_place * tiles + shift


def project(own, table, pieces, weight_pieces, gain, tiles, key_tiles, share, heads):
    width = gain.shape[0]
    columns = weight_pieces[0].shape[1]
    head_cols = columns // 4
    parts = width // share
    shapes = (
        jax.ShapeDtypeStruct((tiles, head_cols, TILE), BF16),
        jax.ShapeDtypeStruct((key_tiles, 2 * head_cols, TILE), BF16),
        jax.ShapeDtypeStruct((key_tiles, width, TILE), BF16),
        jax.ShapeDtypeStruct((tiles, share, TILE), BF16),
        jax.ShapeDtypeStruct((width, 3 * head_cols), BF16),
        jax.ShapeDtypeStruct((parts, share, head_cols), BF16),
        jax.ShapeDtypeStruct((parts, head_cols, share), BF16),
        jax.ShapeDtypeStruct((heads, len(KINDS), HALF, HALF), F32),
    )
    operands = (*pieces, *weight_pieces, gain)
    return pl.pallas_call(
        functools.partial(project_kernel, len(pieces), len(weight_pieces), tiles, share),
        grid=(1,),
        out_shape=(jax.ShapeDtypeStruct((3 + key_tiles + tiles,), jnp.int32),) + shapes,
        in_specs=[pl.BlockSpec(memory_space=pltpu.SMEM)] * 2 + whole_specs(operands),
        out_specs=(pl.BlockSpec(memory_space=pltpu.SMEM),) + tuple(whole_specs(shapes)),
        scratch_shapes=[
            pltpu.VMEM((len(weight_pieces),) + weight_pieces[0].shape, BF16),
            pltpu.VMEM((columns, width), BF16),
        ],
        compiler_params=pltpu.CompilerParams(vmem_limit_bytes=VMEM_BYTES),
        cost_estimate=pl.CostEstimate(
            flops=6 * key_tiles * TILE * width * head_cols,
            bytes_accessed=8 * key_tiles * TILE * width,
            transcendentals=0,
        ),
        name="project",
    )(own, table, *operands)


def project_back_kernel(fast, parts, own_ref, dq_ref, dkv_ref, normed_ref, in_ref, attended_ref, *refs):
    branch_refs = refs[:parts]
    if fast:
        far_even, far_odd, own_even, own_odd, weight_even, weight_odd, gain_ref, full_ref = refs[
            parts:
        ]
    else:
        part_ref, weight_ref, gain_ref, full_ref = refs[parts:]
    grid_place, tensor_place, seq_place, own_first = (own_ref[i] for i in range(4))
    tiles, head_cols, _ = dq_ref.shape
    key_tiles = dkv_ref.shape[0]
    width = in_ref.shape[0]
    share = width // parts
    key_weight = in_ref[:, head_cols:]
    query_weight = in_ref[:, :head_cols]
    if fast:
        for n in range(tiles):
            block = dot(key_weight, dkv_ref[tiles + n]).astype(BF16)
            (far_odd if n & 1 else far_even)[n // 2] = block
        for n in range(tiles):
            block = dot(key_weight, dkv_ref[n]) + dot(query_weight, dq_ref[n])
            (own_odd if n & 1 else own_even)[n // 2] = block.astype(BF16)
    else:
        for n in range(key_tiles):
            part_ref[n] = dot(key_weight, dkv_ref[n]).astype(BF16)
        for n in range(tiles):
            block = part_ref[own_first + n].astype(F32) + dot(query_weight, dq_ref[n])
            part_ref[own_first + n] = block.astype(BF16)
    query_sum = dot_rows(normed_ref[own_first], dq_ref[0])
    for n in range(1, tiles):
        query_sum += dot_rows(normed_ref[own_first + n], dq_ref[n])
    key_sum = dot_rows(normed_ref[0], dkv_ref[0])
    for n in range(1, key_tiles):
        key_sum += dot_rows(normed_ref[n], dkv_ref[n])
    gain_ref[...] = jnp.sum(
        query_sum * query_weight.astype(F32), axis=1, keepdims=True
    ) + jnp.sum(key_sum * key_weight.astype(F32), axis=1, keepdims=True)
    full_ref[:, :head_cols] = query_sum.astype(BF16)
    full_ref[:, head_cols : 3 * head_cols] = key_sum.astype(BF16)
    for k in range(parts):
        block = dot_rows(branch_refs[k][0], attended_ref[0])
        for n in range(1, tiles):
            block += dot_rows(branch_refs[k][n], attended_ref[n])
        start = pl.multiple_of((tensor_place ^ k) * share, share)
        full_ref[pl.ds(start, share), 3 * head_cols :] = block.astype(BF16)
    if fast:
        tall = weight_even.shape[1]
        for k in range(weight_even.shape[0]):
            place = grid_place ^ (2 * k)
            weight_even[k] = full_ref[pl.ds(pl.multiple_of(place * tall, tall), tall), :]
            weight_odd[k] = full_ref[pl.ds(pl.multiple_of((place ^ 1) * tall, tall), tall), :]
    else:
        weight_ref[...] = full_ref[...]


def project_back(fast, own, dq, dkv, normed, in_flat, attended, branch, grid_count):
    tiles, head_cols, _ = dq.shape
    key_tiles = dkv.shape[0]
    width = in_flat.shape[0]
    parts = len(branch)
    columns = 4 * head_cols
    if fast:
        block = jax.ShapeDtypeStruct((parts // 2, width, TILE), BF16)
        weight = jax.ShapeDtypeStruct((grid_count // 2, width // grid_count, columns), BF16)
        shapes = (block,) * 4 + (weight,) * 2
    else:
        shapes = (
            jax.ShapeDtypeStruct((key_tiles, width, TILE), BF16),
            jax.ShapeDtypeStruct((width, columns), BF16),
        )
    shapes = shapes + (jax.ShapeDtypeStruct((width, 1), F32),)
    operands = (dq, dkv, normed, in_flat, attended, *branch)
    return pl.pallas_call(
        functools.partial(project_back_kernel, fast, parts),
        grid=(1,),
        out_shape=shapes,
        in_specs=[pl.BlockSpec(memory_space=pltpu.SMEM)] + whole_specs(operands),
        out_specs=tuple(whole_specs(shapes)),
        scratch_shapes=[pltpu.VMEM((width, columns), BF16)],
        compiler_params=pltpu.CompilerParams(vmem_limit_bytes=VMEM_BYTES),
        cost_estimate=pl.CostEstimate(
            flops=12 * key_tiles * TILE * width * head_cols,
            bytes_accessed=8 * key_tiles * TILE * width,
            transcendentals=0,
        ),
        name="project_back",
    )(own, *operands)


def finish_kernel(input_ref, gain_ref, branch_ref, result_ref, *refs):
    sum_refs = refs[:-2]
    out_ref, grad_ref = refs[-2:]
    rows = input_ref[...]
    width = rows.shape[1]
    values = rows.T
    gain = gain_ref[...]
    grad = sum_refs[0][...].astype(F32)
    for ref in sum_refs[1:]:
        grad += ref[...].astype(F32)
    root = lax.rsqrt(jnp.sum(values * values, axis=0, keepdims=True) * (1.0 / width) + EPSILON)
    scaled = grad * gain
    centre = jnp.sum(scaled * values, axis=0, keepdims=True) * (1.0 / width)
    total = root * scaled - values * (root * root * root * centre)
    grad_ref[...] = (total + branch_ref[...].astype(F32)).T
    out_ref[...] = rows + result_ref[...].astype(F32).T


def finish(block_input, gain, branch, result, sums):
    shape = jax.ShapeDtypeStruct(block_input.shape, F32)
    operands = (block_input, gain, branch, result, *sums)
    return pl.pallas_call(
        finish_kernel,
        grid=(1,),
        out_shape=(shape, shape),
        in_specs=whole_specs(operands),
        out_specs=tuple(whole_specs((shape, shape))),
        compiler_params=pltpu.CompilerParams(vmem_limit_bytes=VMEM_BYTES),
        name="finish",
    )(*operands)


def split_low(values):
    high = values.astype(BF16)
    return high, (values - high.astype(F32)).astype(BF16)


def load_tile(ref, first, count, *place):
    return jnp.concatenate([ref[(first + m, *place)] for m in range(count)], axis=-1)


def expert_kernel(parts, own_ref, *refs):
    state_refs = refs[:parts]
    (grad_ref, other_ref, in_ref, in_t_ref, out_ref, gain_ref) = refs[parts : parts + 6]
    (
        kept_ref,
        sent_ref,
        normed_ref,
        act_ref,
        pre_ref,
        gate_ref,
        router_sum,
        state_ref,
        full_ref,
        back_ref,
        joint_ref,
    ) = refs[parts + 6 :]

    @pl.when(pl.program_id(0) == 0)
    def _():
        router_sum[...] = jnp.zeros_like(router_sum)

    width = gain_ref.shape[0]
    share = width // parts
    hidden = act_ref.shape[1]
    experts = router_sum.shape[0]
    expert, own = own_ref[0], own_ref[1]
    chains, columns = state_ref.shape[0], state_ref.shape[-1]
    merged = kept_ref.shape[1] // chains
    slots = columns // merged
    gain = gain_ref[...]
    for a in range(chains):
        for k in range(parts):
            state_ref[a, own ^ k] = load_tile(state_refs[k], a * merged, merged)
            near = 2 * (k // 2) + ((own & 1) ^ (k & 1))
            full_ref[a, near] = load_tile(
                other_ref if k & 1 else grad_ref, a * merged, merged, k // 2
            )
    for a in range(chains):
        state = state_ref[a].reshape(width, columns).astype(F32)
        root = lax.rsqrt(jnp.sum(state * state, axis=0, keepdims=True) * (1.0 / width) + EPSILON)
        normed = (state * root * gain).astype(BF16)
        normed_ref[a] = normed
        both = dot(in_t_ref[...], normed)
        pre_act, logits = both[:hidden], both[hidden : hidden + experts]
        act_grad = dot(out_ref[...], full_ref[a].reshape(width, columns))
        raised = jnp.exp(logits - jnp.max(logits, axis=0, keepdims=True))
        router_probs = raised / jnp.sum(raised, axis=0, keepdims=True)
        chosen = lax.broadcasted_iota(jnp.int32, logits.shape, 0) == expert
        gate = jnp.sum(jnp.where(chosen, router_probs, 0.0), axis=0, keepdims=True)
        gate_ref[a] = gate
        square = pre_act * pre_act
        cdf = 0.5 + 0.5 * jnp.tanh(pre_act * (GELU_A + (GELU_A * GELU_B) * square))
        activated = pre_act * cdf
        act_ref[a] = activated.astype(BF16)
        rise = (2.0 * GELU_A) + (6.0 * GELU_A * GELU_B) * square
        pre_grad = act_grad * (cdf + activated * (1.0 - cdf) * rise)
        low_grad = pre_grad.astype(BF16)
        pre_ref[a] = low_grad
        gate_grad = jnp.sum(activated * act_grad, axis=0, keepdims=True)
        logit_grad = gate_grad * (chosen.astype(F32) - router_probs)
        centre = jnp.sum(pre_grad * pre_act, axis=0, keepdims=True)
        centre += jnp.sum(logit_grad * logits, axis=0, keepdims=True)
        joint_ref[a, :hidden, :] = low_grad
        joint_ref[a, hidden:, :] = jnp.concatenate(split_low(logit_grad), axis=0)
        high, low = split_low(logit_grad * gate)
        router_sum[...] += dot_rows(high, normed) + dot_rows(low, normed)
        normed_grad = dot(in_ref[...], joint_ref[a])
        state = state_ref[a].reshape(width, columns).astype(F32)
        back = (root * gate) * (normed_grad * gain - state * (root * centre * (1.0 / width)))
        back_ref[a] = back.astype(BF16).reshape(parts, share, columns)
        for k in range(parts):
            block = back_ref[a, own ^ k]
            target = sent_ref if k & 1 else kept_ref
            for m in range(merged):
                target[k // 2, a * merged + m] = block[:, m * slots : (m + 1) * slots]


def result_kernel(parts, own_ref, *refs):
    out_t_ref, kept_ref, sent_ref, result_ref = refs[-4:]
    chunks = (len(refs) - 4) // 2
    own = own_ref[1]
    width = out_t_ref.shape[0]
    share = width // parts
    merged = kept_ref.shape[1]
    for c in range(chunks):
        gate, activated = refs[2 * c + 1][0], refs[2 * c][0]
        slots = activated.shape[-1] // merged
        result = dot(out_t_ref[...], activated) * gate
        result_ref[c] = result.astype(BF16).reshape(parts, share, -1)
        for k in range(parts):
            block = result_ref[c, own ^ k]
            target = sent_ref if k & 1 else kept_ref
            for m in range(merged):
                target[k // 2, m, :, c * slots : (c + 1) * slots] = block[
                    :, m * slots : (m + 1) * slots
                ]


def grads_kernel(parts, merged, own_ref, *refs):
    grad_ref, other_ref, in_ref, in_sum, out_sum, gain_sum, full_ref = refs[-7:]
    chunks = (len(refs) - 7) // 4

    @pl.when(pl.program_id(0) == 0)
    def _():
        in_sum[...] = jnp.zeros_like(in_sum)
        out_sum[...] = jnp.zeros_like(out_sum)

    own = own_ref[1]
    width = in_ref.shape[0]
    for c in range(chunks):
        normed_ref, act_ref, pre_ref, gate_ref = refs[4 * c : 4 * c + 4]
        gate = gate_ref[0]
        columns = gate.shape[-1]
        slots = columns // merged
        for k in range(parts):
            near = 2 * (k // 2) + ((own & 1) ^ (k & 1))
            source = other_ref if k & 1 else grad_ref
            full_ref[c, near] = jnp.concatenate(
                [source[m, k // 2, :, c * slots : (c + 1) * slots] for m in range(merged)], axis=-1
            )
        normed = (normed_ref[0].astype(F32) * gate).astype(BF16)
        in_sum[...] += dot_rows(normed, pre_ref[0])
        scaled = (full_ref[c].reshape(width, columns).astype(F32) * gate).astype(BF16)
        out_sum[...] += dot_rows(act_ref[0], scaled)

    @pl.when(pl.program_id(0) == pl.num_programs(0) - 1)
    def _():
        gain_sum[...] = jnp.sum(in_sum[...] * in_ref[...].astype(F32), axis=1, keepdims=True)


def fixed_spec(shape):
    return pl.BlockSpec(shape, lambda g: (0,) * len(shape))


def run_expert(own, states, grads, chunk, merged, chains, weights):
    parts = len(states)
    count, share, slots = states[0].shape
    width = share * parts
    columns = merged * slots
    steps = count // merged
    hidden = weights[2].shape[0]
    joint = weights[0].shape[1]
    experts = (joint - hidden) // 2
    half = parts // 2
    taken = merged * chains
    piece = pl.BlockSpec((taken, share, slots), lambda g: (g, 0, 0))
    grad_piece = pl.BlockSpec((taken, half, share, slots), lambda g: (g, 0, 0, chunk))
    split = pl.BlockSpec((half, taken, share, slots), lambda g: (0, g, 0, 0))
    wide = pl.BlockSpec((chains, width, columns), lambda g: (g, 0, 0))
    deep = pl.BlockSpec((chains, hidden, columns), lambda g: (g, 0, 0))
    flat = pl.BlockSpec((chains, 1, columns), lambda g: (g, 0, 0))
    return pl.pallas_call(
        functools.partial(expert_kernel, parts),
        grid=(steps // chains,),
        out_shape=(
            jax.ShapeDtypeStruct((half, count, share, slots), BF16),
            jax.ShapeDtypeStruct((half, count, share, slots), BF16),
            jax.ShapeDtypeStruct((steps, width, columns), BF16),
            jax.ShapeDtypeStruct((steps, hidden, columns), BF16),
            jax.ShapeDtypeStruct((steps, hidden, columns), BF16),
            jax.ShapeDtypeStruct((steps, 1, columns), F32),
            jax.ShapeDtypeStruct((experts, width), F32),
        ),
        in_specs=[pl.BlockSpec(memory_space=pltpu.SMEM)]
        + [piece] * parts
        + [grad_piece] * 2
        + [fixed_spec(weight.shape) for weight in weights],
        out_specs=(split, split, wide, deep, deep, flat, fixed_spec((experts, width))),
        scratch_shapes=[
            pltpu.VMEM((chains, parts, share, columns), BF16),
            pltpu.VMEM((chains, parts, share, columns), BF16),
            pltpu.VMEM((chains, parts, share, columns), BF16),
            pltpu.VMEM((chains, joint, columns), BF16),
        ],
        compiler_params=pltpu.CompilerParams(vmem_limit_bytes=VMEM_BYTES),
        cost_estimate=pl.CostEstimate(
            flops=16 * steps * columns * width * hidden,
            bytes_accessed=16 * steps * columns * width,
            transcendentals=steps * columns * hidden,
        ),
        name="expert",
    )(own, *states, *grads, *weights)


def run_result(own, saved, parts, merged, out_t):
    chunks = len(saved)
    steps, hidden, columns = saved[0][0].shape
    width = out_t.shape[0]
    share, half, slots = width // parts, parts // 2, columns // merged
    deep = pl.BlockSpec((1, hidden, columns), lambda g: (g, 0, 0))
    flat = pl.BlockSpec((1, 1, columns), lambda g: (g, 0, 0))
    split = pl.BlockSpec((half, merged, share, slots * chunks), lambda g: (0, g, 0, 0))
    total = jax.ShapeDtypeStruct((half, steps * merged, share, slots * chunks), BF16)
    return pl.pallas_call(
        functools.partial(result_kernel, parts),
        grid=(steps,),
        out_shape=(total, total),
        in_specs=[pl.BlockSpec(memory_space=pltpu.SMEM)]
        + [deep, flat] * chunks
        + [fixed_spec(out_t.shape)],
        out_specs=(split, split),
        scratch_shapes=[pltpu.VMEM((chunks, parts, share, columns), BF16)],
        compiler_params=pltpu.CompilerParams(vmem_limit_bytes=VMEM_BYTES),
        cost_estimate=pl.CostEstimate(
            flops=6 * chunks * steps * columns * width * hidden,
            bytes_accessed=6 * chunks * steps * columns * width,
            transcendentals=0,
        ),
        name="result",
    )(own, *[array for arrays in saved for array in arrays], out_t)


def run_grads(own, saved, grads, merged, weight):
    chunks = len(saved)
    steps, width, columns = saved[0][0].shape
    hidden = saved[0][1].shape[1]
    _, half, share, _ = grads[0].shape
    parts = 2 * half
    wide = pl.BlockSpec((1, width, columns), lambda g: (g, 0, 0))
    deep = pl.BlockSpec((1, hidden, columns), lambda g: (g, 0, 0))
    flat = pl.BlockSpec((1, 1, columns), lambda g: (g, 0, 0))
    grad_piece = pl.BlockSpec((merged,) + grads[0].shape[1:], lambda g: (g, 0, 0, 0))
    return pl.pallas_call(
        functools.partial(grads_kernel, parts, merged),
        grid=(steps,),
        out_shape=(
            jax.ShapeDtypeStruct((width, hidden), F32),
            jax.ShapeDtypeStruct((hidden, width), F32),
            jax.ShapeDtypeStruct((width, 1), F32),
        ),
        in_specs=[pl.BlockSpec(memory_space=pltpu.SMEM)]
        + [wide, deep, deep, flat] * chunks
        + [grad_piece] * 2
        + [fixed_spec(weight.shape)],
        out_specs=(
            fixed_spec((width, hidden)),
            fixed_spec((hidden, width)),
            fixed_spec((width, 1)),
        ),
        scratch_shapes=[pltpu.VMEM((chunks, parts, share, columns), BF16)],
        compiler_params=pltpu.CompilerParams(vmem_limit_bytes=VMEM_BYTES),
        cost_estimate=pl.CostEstimate(
            flops=8 * chunks * steps * columns * width * hidden,
            bytes_accessed=8 * chunks * steps * columns * width,
            transcendentals=0,
        ),
        name="grads",
    )(own, *[array for arrays in saved for array in arrays], *grads, weight)


def shards(
    block_input,
    attn_in_weight,
    attn_out_weight,
    position_bias,
    norm_gains,
    router_weight,
    expert_in,
    expert_out,
    segment_ids,
    expert_ids,
    out_grad,
):
    tensor_count, seq_count = lax.axis_size("tensor"), lax.axis_size("seq")
    tensor_place, seq_place = lax.axis_index("tensor"), lax.axis_index("seq")
    grid_count = lax.axis_size("dp") * seq_count
    grid_place = lax.axis_index("dp") * seq_count + seq_place
    local_count, width = block_input.shape
    group_count = local_count * tensor_count
    share = width // tensor_count
    bucket_count, heads = position_bias.shape
    head_cols = attn_in_weight.shape[2]
    experts = router_weight.shape[1]
    capacity = max(2, 2 * group_count // experts)
    tiles = group_count // TILE
    key_tiles = tiles * seq_count
    fast = seq_count == 2 and local_count == TILE and grid_count == 8

    def tiled(pieces):
        pieces = reorder(pieces, tensor_place)
        if local_count == TILE:
            return jnp.stack(pieces)
        return jnp.concatenate(pieces, axis=-1)[None]

    half = tensor_count // 2
    core = tensor_place & 1
    own_rows = jnp.concatenate(
        [
            jnp.transpose(block_input.astype(BF16)),
            jnp.pad(segment_ids.astype(BF16), ((0, 15), (0, 0))),
        ]
    )
    weight_piece = jnp.concatenate(
        [attn_in_weight[0], attn_in_weight[1], attn_in_weight[2], jnp.transpose(attn_out_weight)],
        axis=1,
    )
    grad_rows = jnp.transpose(out_grad.astype(BF16)).reshape(half, 2, share, local_count)
    grad_mine = lax.dynamic_index_in_dim(grad_rows, core, 1, keepdims=False)
    grad_theirs = lax.dynamic_index_in_dim(grad_rows, core ^ 1, 1, keepdims=False)
    in_plain, out_plain = expert_in[0], expert_out[0]
    if fast:
        far_rows = swap(own_rows, "seq", 1)
        near_two = swap(own_rows, "tensor", 2)
        columns = [weight_piece] + [swap(weight_piece, "dp", k) for k in range(1, grid_count // 2)]
        grad_other = swap(grad_theirs, "tensor", 1)
        far_rows, near_two, columns, grad_other, expert_ids, in_plain, out_plain = (
            lax.optimization_barrier(
                (
                    far_rows,
                    near_two,
                    columns,
                    grad_other,
                    expert_ids,
                    in_plain,
                    out_plain,
                )
            )
        )
        far_two = swap(far_rows, "tensor", 2)
        near_columns = swap(weight_piece, "seq", 1)
        far_columns = swap(jnp.stack(columns[1:]), "seq", 1)
        near_one, near_three = swap(own_rows, "tensor", 1), swap(near_two, "tensor", 1)
    else:
        grad_other = swap(grad_theirs, "tensor", 1)
        both_rows = lax.all_gather(own_rows, "seq", axis=0, tiled=False)
        row_pieces = gather_relative(both_rows, "tensor")
        own_first = seq_place * tiles
        row_pieces = jnp.concatenate(reorder(row_pieces, tensor_place), axis=-1)
        row_pieces = row_pieces.reshape(seq_count, -1, tiles, TILE)
        row_pieces = [jnp.moveaxis(row_pieces, 2, 1).reshape(key_tiles, -1, TILE)]
        weight_pieces = [lax.all_gather(weight_piece, ("dp", "seq"), axis=0, tiled=True)]

    in_t, out_t = jnp.transpose(in_plain), jnp.transpose(out_plain)
    router_t = jnp.transpose(router_weight)
    in_joint = jnp.concatenate([in_plain, router_weight, router_weight], axis=1)
    in_t = jnp.concatenate([in_t, router_t, router_t])
    route_all = expert_ids[:, 0]
    expert_range = jnp.arange(experts, dtype=jnp.int32)
    route_hot = (route_all[:, None] == expert_range[None, :]).astype(jnp.int32)
    slot_rank = jnp.sum(jnp.cumsum(route_hot, axis=0) * route_hot, axis=-1) - 1
    target = (route_all * capacity + slot_rank).reshape(1, tiles, TILE, 1)
    places = jnp.arange(experts * capacity, dtype=jnp.int32).reshape(experts, 1, 1, capacity)
    chunks = 2 if capacity >= TILE else 1
    slots = capacity // chunks
    spread = max(1, TILE // capacity)
    merged = max(1, TILE // (slots * spread))

    def exchange(values):
        return lax.all_to_all(values, ("dp", "seq"), split_axis=0, concat_axis=0, tiled=True)

    def joined(values):
        if spread == 1:
            return values
        shape = values.shape
        values = values.reshape((-1, spread) + shape[1:])
        return jnp.moveaxis(values, 1, -2).reshape(
            (shape[0] // spread,) + shape[1:-1] + (spread * shape[-1],)
        )

    def parted(values):
        if spread == 1:
            return values
        shape = values.shape
        values = values.reshape(shape[:-1] + (spread, shape[-1] // spread))
        return jnp.moveaxis(values, -2, 1).reshape((-1,) + shape[1:-1] + (shape[-1] // spread,))


    gain_one = norm_gains[0][:, None]
    gain_two = norm_gains[1][:, None]
    if fast:
        (
            far_two,
            far_columns,
            gain_one,
            in_t,
            in_joint,
            out_t,
            target,
            gain_two,
            grad_mine,
            grad_other,
        ) = lax.optimization_barrier(
            (
                far_two,
                far_columns,
                gain_one,
                in_t,
                in_joint,
                out_t,
                target,
                gain_two,
                grad_mine,
                grad_other,
            )
        )
        far_one, far_three = swap(far_rows, "tensor", 1), swap(far_two, "tensor", 1)
        row_pieces = [own_rows, near_one, near_two, near_three]
        row_pieces += [far_rows, far_one, far_two, far_three]
        row_pieces = [rows[None] for rows in row_pieces]
        weight_pieces = [weight_piece, near_columns]
        for k in range(1, grid_count // 2):
            weight_pieces += [columns[k], far_columns[k - 1]]
        own_first = jnp.int32(0)
    own = jnp.stack([grid_place, tensor_place, seq_place, own_first]).astype(jnp.int32)
    onehot = (target == places).astype(BF16)
    grad_pair = swap(jnp.stack([grad_mine, grad_other]), "tensor", 2)
    grad_here = tiled([grad_mine, grad_other, grad_pair[0], grad_pair[1]])
    grad_buffer = einsum("nkdq,enqs->ekds", grad_here, onehot).astype(BF16)
    (
        meta,
        queries,
        keys_values,
        normed_tiles,
        input_share,
        in_flat,
        out_blocks,
        out_t_blocks,
        near,
    ) = project(
        own,
        position_bias.reshape(-1),
        row_pieces,
        weight_pieces,
        gain_one,
        tiles,
        key_tiles,
        share,
        heads,
    )
    queries, grad_buffer = lax.optimization_barrier((queries, grad_buffer))
    grad_arrived = joined(exchange(grad_buffer))
    exact, attended, logs, attn_even, attn_odd = attend(
        meta, queries, keys_values, near, out_blocks
    )
    attn_share = sum_tensor(attn_even, attn_odd)
    state_share = (input_share.astype(F32) + attn_share).astype(BF16)
    state_share, grad_arrived = lax.optimization_barrier((state_share, grad_arrived))
    grad_near = swap(grad_arrived, "tensor", 1)

    weights = (in_joint, in_t, expert_out[0], gain_two)
    grads = (grad_arrived, grad_near)
    buffers = [
        einsum("ndq,enqs->eds", state_share, onehot[..., c * slots : (c + 1) * slots]).astype(BF16)
        for c in range(chunks)
    ]
    buffers = list(lax.optimization_barrier(tuple(buffers)))
    arrivals = [joined(exchange(buffer)) for buffer in buffers]
    chains = 2 if arrivals[0].shape[0] // merged % 2 == 0 else 1
    gathered = []
    for arrival in arrivals:
        gathered.append(
            [arrival, swap(arrival, "tensor", 1), swap(arrival, "tensor", 2)]
        )
    gathered[0][0], gathered[-1][0] = lax.optimization_barrier((gathered[0][0], gathered[-1][0]))
    saved, halves, crossed = [], [], []
    small = jnp.zeros((experts, width), F32)
    for c in range(chunks):
        gathered[c].append(swap(gathered[c][2], "tensor", 1))
        kept, sent, normed_two, activated, pre_grad, gate, router_sum = run_expert(
            own, gathered[c], grads, c, merged, chains, weights
        )
        saved.append((normed_two, activated, pre_grad, gate))
        if c + 1 < chunks:
            sent, gathered[c + 1][2] = lax.optimization_barrier((sent, gathered[c + 1][2]))
        if c > 0:
            sent, crossed[c - 1] = lax.optimization_barrier((sent, crossed[c - 1]))
        stayed, got, to_send = core_step(kept, sent)
        if c + 1 == chunks:
            own_late, to_send = lax.optimization_barrier((own, to_send))
        halves.append((stayed, got))
        crossed.append(swap(to_send, "tensor", 2))
        small = small + router_sum
    returned = [
        exchange(parted(chip_step(*halves[c], crossed[c]).astype(BF16)))
        for c in range(chunks - 1)
    ]
    result_even, result_odd = run_result(
        own_late, [(arrays[1], arrays[3]) for arrays in saved], tensor_count, merged, out_t
    )
    tied = lax.optimization_barrier((result_odd, crossed[-1], *returned))
    result_odd, crossed[-1], returned = tied[0], tied[1], list(tied[2:])
    returned.append(exchange(parted(chip_step(*halves[-1], crossed[-1]).astype(BF16))))
    result_near, result_got, result_sent = core_step(result_even, result_odd)
    result_far = swap(result_sent, "tensor", 2)
    own_late, result_sent = lax.optimization_barrier((own, result_sent))
    grad_expert_in, grad_expert_out, in_gain = run_grads(
        own_late, saved, grads, merged, expert_in[0]
    )
    in_gain, returned[-1] = lax.optimization_barrier((in_gain, returned[-1]))
    gain_part = in_gain[:, 0] + jnp.sum(small * router_t.astype(F32), axis=0)
    router_gains = jnp.concatenate([small, (gain_part / norm_gains[1])[None]])
    state_grad = lax.dynamic_index_in_dim(grad_here, tensor_place // 2, 1, keepdims=False)
    state_grad = state_grad.astype(F32)
    for c in range(chunks):
        state_grad = state_grad + einsum(
            "eds,enqs->ndq", returned[c], onehot[..., c * slots : (c + 1) * slots]
        )
    state_grad = state_grad.astype(BF16)

    branch = [state_grad, swap(state_grad, "tensor", 1), swap(state_grad, "tensor", 2)]
    result_far, branch[2] = lax.optimization_barrier((result_far, branch[2]))
    branch.append(swap(branch[2], "tensor", 1))
    result_total = chip_step(result_near, result_got, result_far).astype(BF16)
    result_back = exchange(parted(result_total))
    dq, dkv, bias_rows = attend_back(
        meta, queries, keys_values, near, out_t_blocks, exact, logs, branch, bucket_count
    )
    dq, dkv, bias_rows, result_back = lax.optimization_barrier((dq, dkv, bias_rows, result_back))

    def joined_small():
        bias_padded = lax.dynamic_update_slice_in_dim(
            jnp.zeros((heads * tensor_count, bucket_count), F32),
            jnp.sum(bias_rows, axis=2),
            tensor_place * heads,
            0,
        )
        return jnp.concatenate(
            [router_gains.reshape(-1), gain_part[:, 0] / norm_gains[0], bias_padded.reshape(-1)]
        )

    def result_rows_of():
        shares = attn_share + einsum("eds,enqs->ndq", result_back, onehot)
        return jnp.moveaxis(shares.astype(BF16), 0, 1).reshape(share, tensor_count, local_count)

    if fast:
        far_even, far_odd, own_even, own_odd, weight_even, weight_odd, gain_part = project_back(
            True, own, dq, dkv, normed_tiles, in_flat, attended, branch, grid_count
        )
        far_near, far_got, far_send = core_step(far_even, far_odd)
        own_near, own_got, own_send = core_step(own_even, own_odd)
        weight_sent = swap(weight_odd, "seq", 1)
        far_send, own_send, gain_part, result_back = lax.optimization_barrier(
            (far_send, own_send, gain_part, result_back)
        )
        far_sent = swap(far_send, "tensor", 2)
        small = sum_all(joined_small(), ("dp",))
        result_share = result_rows_of()
        own_send, far_sent = lax.optimization_barrier((own_send, far_sent))
        own_sent = swap(own_send, "tensor", 2)
        far_sent, weight_sent, small, result_share, branch = lax.optimization_barrier(
            (far_sent, weight_sent, small, result_share, branch)
        )
        far_sum = chip_step(far_near, far_got, far_sent).astype(BF16)
        sums = [own_near, own_got, own_sent, swap(far_sum, "seq", 1)]
        weight_half = weight_even.astype(F32) + weight_sent.astype(F32)
        weight_grad = weight_half[0]
        for k in range(1, grid_count // 2):
            weight_grad = weight_grad + swap(weight_half[k].astype(BF16), "dp", k).astype(F32)
    else:
        row_part, weight_part, gain_part = project_back(
            False, own, dq, dkv, normed_tiles, in_flat, attended, branch, grid_count
        )
        row_part = lax.psum_scatter(row_part, "seq", scatter_dimension=0, tiled=True)
        row_part = jnp.moveaxis(row_part, 0, 1).reshape(width, tensor_count, local_count)
        blocks = [
            lax.dynamic_index_in_dim(row_part, tensor_place ^ k, 1, keepdims=False)
            for k in range(tensor_count)
        ]
        sums = [sum_tensor(jnp.stack(blocks[0::2]), jnp.stack(blocks[1::2]))]
        small = sum_all(joined_small(), ("dp",))
        result_share = result_rows_of()
        weight_grad = lax.psum_scatter(
            weight_part, ("dp", "seq"), scatter_dimension=0, tiled=True
        ).astype(F32)
    grad_attn_in = jnp.stack(
        [weight_grad[:, c * head_cols : (c + 1) * head_cols] for c in range(3)]
    )
    grad_attn_out = jnp.transpose(weight_grad[:, 3 * head_cols :])

    small = sum_all(small, ("seq", "tensor"))
    first, second = experts * width, (experts + 1) * width
    grad_router = jnp.transpose(small[:first].reshape(experts, width))
    grad_gains = jnp.stack([small[second : second + width], small[first:second]])
    bias_sum = small[second + width :].reshape(heads * tensor_count, bucket_count)
    grad_bias = jnp.transpose(lax.dynamic_slice_in_dim(bias_sum, tensor_place * heads, heads, 0))

    result_rows = lax.all_to_all(
        jnp.moveaxis(result_share, 1, 0), "tensor", split_axis=0, concat_axis=0, tiled=True
    ).reshape(width, local_count)
    if local_count == TILE:
        own_branch = [
            lax.dynamic_index_in_dim(piece, tensor_place, 0, keepdims=False) for piece in branch
        ]
    else:
        own_branch = [
            lax.dynamic_slice_in_dim(piece[0], tensor_place * local_count, local_count, 1)
            for piece in branch
        ]
    own_branch = jnp.concatenate(reorder(own_branch, tensor_place))
    block_out, input_grad = finish(block_input, gain_one, own_branch, result_rows, sums)
    return (
        block_out,
        input_grad,
        grad_attn_in,
        grad_attn_out,
        grad_bias,
        grad_gains,
        grad_router,
        grad_expert_in[None],
        grad_expert_out[None],
    )


def solution(mesh):
    return jax.shard_map(
        shards,
        mesh=mesh,
        in_specs=(
            P(("dp", "seq", "tensor"), None),
            P(None, ("dp", "seq"), "tensor"),
            P("tensor", ("dp", "seq")),
            P(None, "tensor"),
            P(),
            P(),
            P(("dp", "seq"), None, "tensor"),
            P(("dp", "seq"), "tensor", None),
            P("dp", ("seq", "tensor")),
            P(("dp", "seq"), None),
            P(("dp", "seq", "tensor"), None),
        ),
        out_specs=(
            P(("dp", "seq", "tensor"), None),
            P(("dp", "seq", "tensor"), None),
            P(None, ("dp", "seq"), "tensor"),
            P("tensor", ("dp", "seq")),
            P(None, "tensor"),
            P(),
            P(),
            P(("dp", "seq"), None, "tensor"),
            P(("dp", "seq"), "tensor", None),
        ),
        check_vma=False,
    )
```

```python
import functools
import math

import jax
import jax.numpy as jnp
from jax import lax
from jax.experimental import pallas as pl
from jax.experimental.pallas import tpu as pltpu
from jax.sharding import PartitionSpec as P

EPSILON = 1e-06
EDGES = (1, 2, 3, 4, 5, 6, 7, 8, 12, 16, 23, 32, 46, 64, 91)
TILE = 256
HALF = TILE // 2
LOG2E = math.log2(math.e)
SCALE = 0.125
MASKED = -1e30
LOWEST = -1e29
EXTRA = 16
VMEM_BYTES = 60 * 1024 * 1024
GELU_A = math.sqrt(2.0 / math.pi)
GELU_B = 0.044715
BF16 = jnp.bfloat16
F32 = jnp.float32


def dot(left_side, right_side):
    return jnp.dot(left_side, right_side, preferred_element_type=F32)


def dot_rows(left_side, right_side):
    return lax.dot_general(
        left_side, right_side, (((1,), (1,)), ((), ())), preferred_element_type=F32
    )


def einsum(formula, *operands):
    return jnp.einsum(formula, *operands, preferred_element_type=F32)


def swap(values, axis, bit):
    count = lax.axis_size(axis)
    return lax.ppermute(values, axis, [(i, i ^ bit) for i in range(count)])


def bits_of(count):
    return [1 << i for i in range(count.bit_length() - 1)]


def gather_relative(values, axis):
    pieces = {0: values}
    for bit in reversed(bits_of(lax.axis_size(axis))):
        for place in list(pieces):
            pieces[place ^ bit] = swap(pieces[place], axis, bit)
    return [pieces[place] for place in range(len(pieces))]


def core_step(kept, sent):
    got = swap(sent, "tensor", 1)
    to_send = (kept[1].astype(F32) + got[1].astype(F32)).astype(BF16)
    return kept[0], got[0], to_send


def chip_step(near, got, far):
    return near.astype(F32) + got.astype(F32) + far.astype(F32)


def sum_tensor(kept, sent):
    near, got, to_send = core_step(kept, sent)
    return chip_step(near, got, swap(to_send, "tensor", 2))


def reorder(pieces, own_index):
    for bit in bits_of(len(pieces)):
        flip = (own_index & bit) != 0
        pieces = [
            jnp.where(flip, pieces[place ^ bit], pieces[place]) for place in range(len(pieces))
        ]
    return pieces


def sum_all(values, axes):
    for axis in axes:
        for bit in bits_of(lax.axis_size(axis)):
            values = values + swap(values, axis, bit)
    return values


def bucket_of(relative, half_count):
    magnitude = jnp.abs(relative)
    counted = jnp.zeros(relative.shape, jnp.int32)
    for edge_value in EDGES:
        counted = counted + (magnitude >= edge_value).astype(jnp.int32)
    return counted + jnp.where(relative > 0, half_count, 0).astype(jnp.int32)


KINDS = ((0, 0, 0, 0), (0, 0, 1, 0), (2, 1, 3, 2), (4, 3, 4, 4), (4, 4, 4, 4))


def near_tiles(table_ref, near_ref):
    heads = near_ref.shape[0]
    bucket_count = table_ref.shape[0] // heads
    half_count = bucket_count // 2
    offset = lax.broadcasted_iota(jnp.int32, (HALF, HALF), 0) - lax.broadcasted_iota(
        jnp.int32, (HALF, HALF), 1
    )
    near_of = (range(1, half_count), range(bucket_count), range(half_count + 1, bucket_count))
    for shift, buckets in enumerate(near_of):
        grid = bucket_of(offset + (shift - 1) * HALF, half_count)
        for h in range(heads):
            total = jnp.zeros((HALF, HALF), F32)
            for bucket_index in buckets:
                value = table_ref[bucket_index * heads + h] * LOG2E
                total = jnp.where(grid == bucket_index, value, total)
            near_ref[h, 1 + shift] = total
    for h in range(heads):
        for kind, bucket_index in ((0, half_count - 1), (4, bucket_count - 1)):
            value = table_ref[bucket_index * heads + h] * LOG2E
            near_ref[h, kind] = jnp.full((HALF, HALF), value, F32)


def fill_tiles(near_ref, bias_ref):
    for kind, blocks in enumerate(KINDS):
        for h in range(near_ref.shape[0]):
            for place, block in enumerate(blocks):
                row, column = place // 2 * HALF, place % 2 * HALF
                bias_ref[kind, h, row : row + HALF, column : column + HALF] = near_ref[h, block]


def span_of(meta_ref, query_tile, key_tiles):
    opening, closing = meta_ref[1], meta_ref[2]
    first = query_tile * TILE
    last = first + TILE - 1
    begin = jnp.where(first < opening, 0, jnp.where(first < closing, opening, closing))
    end = jnp.where(last < opening, opening, jnp.where(last < closing, closing, key_tiles * TILE))
    return begin // TILE, (end + TILE - 1) // TILE


def document_row(meta_ref, tile):
    place = tile * TILE + lax.broadcasted_iota(jnp.int32, (EXTRA, TILE), 1)
    return (place >= meta_ref[1]).astype(jnp.int32) + (place >= meta_ref[2]).astype(jnp.int32)


def key_rows(meta_ref, tile):
    row = lax.broadcasted_iota(jnp.int32, (EXTRA, TILE), 0)
    differs = jnp.where(document_row(meta_ref, tile) != row, MASKED, 0.0)
    return jnp.where(row < 3, differs, jnp.where(row < 6, 1.0, 0.0)).astype(BF16)


def query_rows(meta_ref, tile, terms):
    row = lax.broadcasted_iota(jnp.int32, (EXTRA, TILE), 0)
    agrees = jnp.where(document_row(meta_ref, tile) == row, 1.0, 0.0)
    return jnp.where(row < 3, agrees, three_rows(row - 3, terms)).astype(BF16)


def three_rows(row, terms):
    result = jnp.zeros(row.shape, F32)
    for i, term in enumerate(terms):
        result = jnp.where(row == i, term, result)
    return result


def split_three(values):
    first = values.astype(BF16).astype(F32)
    second = (values - first).astype(BF16).astype(F32)
    return first, second, values - first - second


def attend_kernel(
    meta_ref,
    q_ref,
    kv_ref,
    near_ref,
    weight_ref,
    exact_ref,
    out_ref,
    log_ref,
    even_ref,
    odd_ref,
    key_ref,
    query_ref,
    sum_ref,
    bias_ref,
):
    key_tiles = kv_ref.shape[0]
    heads = near_ref.shape[0]
    fill_tiles(near_ref, bias_ref)
    size = q_ref.shape[1] // heads

    def turn(j, carry):
        kept = meta_ref[3 + j]
        extra = key_rows(meta_ref, j)
        for h in range(heads):
            rows = kv_ref[kept, h * size : (h + 1) * size, :]
            key_ref[kept, h] = jnp.concatenate([rows, extra], axis=0).T
        return carry

    lax.fori_loop(0, key_tiles, turn, 0)
    ones = jnp.ones((EXTRA, TILE), BF16)

    def query_body(i, carry):
        tile = meta_ref[3 + key_tiles + i]
        place = tile % meta_ref[0]
        begin, end = span_of(meta_ref, tile, key_tiles)
        extra = query_rows(meta_ref, tile, ())
        for h in range(heads):
            rows = q_ref[i, h * size : (h + 1) * size, :]
            query_ref[h] = jnp.concatenate([rows, extra], axis=0)
        sum_ref[...] = jnp.zeros_like(sum_ref)

        def key_body(j, peaks):
            kept = meta_ref[3 + j]
            kind = jnp.clip(j - tile, -2, 2) + 2
            scores = [
                dot(key_ref[kept, h], query_ref[h]) + bias_ref[kind, h] for h in range(heads)
            ]
            new_peaks = [
                jnp.maximum(peaks[h], jnp.max(scores[h], axis=0, keepdims=True))
                for h in range(heads)
            ]
            weights = [jnp.exp2(scores[h] - new_peaks[h]).astype(BF16) for h in range(heads)]
            added = []
            for h in range(heads):
                values = kv_ref[kept, (heads + h) * size : (heads + h + 1) * size, :]
                added.append(dot(jnp.concatenate([values, ones], axis=0), weights[h]))
            for h in range(heads):
                sum_ref[h] = sum_ref[h] * jnp.exp2(peaks[h] - new_peaks[h]) + added[h]
            return tuple(new_peaks)

        start = tuple(jnp.full((1, TILE), LOWEST, F32) for _ in range(heads))
        peaks = lax.fori_loop(begin, end, key_body, start)
        for h in range(heads):
            rows = slice(h * size, (h + 1) * size)
            total = sum_ref[h, size : size + 1, :]
            result = sum_ref[h, :size, :] * (1.0 / total)
            exact_ref[i, rows, :] = result
            out_ref[place, rows, :] = result.astype(BF16)
            log_ref[i, h] = peaks[h] + jnp.log2(total)
        attended = out_ref[place]
        for k in range(weight_ref.shape[0]):
            block = dot(weight_ref[k], attended).astype(BF16)
            (odd_ref if k & 1 else even_ref)[k // 2, place] = block
        return carry

    lax.fori_loop(0, q_ref.shape[0], query_body, 0)


def estimate(queries, key_tiles, products):
    pairs = queries.shape[0] * TILE * key_tiles * TILE
    return pl.CostEstimate(
        flops=2 * products * pairs * queries.shape[1],
        bytes_accessed=8 * pairs,
        transcendentals=3 * pairs,
    )


def whole_specs(arrays):
    return [pl.BlockSpec(array.shape, functools.partial(origin, len(array.shape))) for array in arrays]


def origin(dimensions, step):
    return (0,) * dimensions


def attend(meta, queries, keys_values, near, out_blocks):
    query_tiles, width, _ = queries.shape
    key_tiles = keys_values.shape[0]
    heads = near.shape[0]
    parts, share, _ = out_blocks.shape
    blocks = jax.ShapeDtypeStruct((parts // 2, query_tiles, share, TILE), BF16)
    shapes = (
        jax.ShapeDtypeStruct(queries.shape, F32),
        jax.ShapeDtypeStruct(queries.shape, BF16),
        jax.ShapeDtypeStruct((query_tiles, heads, 1, TILE), F32),
        blocks,
        blocks,
    )
    operands = (queries, keys_values, near, out_blocks)
    return pl.pallas_call(
        attend_kernel,
        grid=(1,),
        out_shape=shapes,
        in_specs=[pl.BlockSpec(memory_space=pltpu.SMEM)] + whole_specs(operands),
        out_specs=tuple(whole_specs(shapes)),
        scratch_shapes=[
            pltpu.VMEM((key_tiles, heads, TILE, width // heads + EXTRA), BF16),
            pltpu.VMEM((heads, width // heads + EXTRA, TILE), BF16),
            pltpu.VMEM((heads, width // heads + EXTRA, TILE), F32),
            pltpu.VMEM((len(KINDS), heads, TILE, TILE), F32),
        ],
        compiler_params=pltpu.CompilerParams(vmem_limit_bytes=VMEM_BYTES),
        cost_estimate=estimate(queries, key_tiles, 2),
        name="attend",
    )(meta, *operands)


def bucket_rows(tiles_ref, rows_ref):
    heads, bucket_count = rows_ref.shape[:2]
    half_count = bucket_count // 2
    offset = lax.broadcasted_iota(jnp.int32, (HALF, HALF), 0) - lax.broadcasted_iota(
        jnp.int32, (HALF, HALF), 1
    )
    grids = [bucket_of(offset + shift * HALF, half_count) for shift in (-1, 0, 1)]
    first, last = slice(0, HALF), slice(HALF, TILE)

    def column_sums(values):
        return jnp.sum(values, axis=0, keepdims=True)

    def head_body(h, carry):
        before = tiles_ref[2, h, first, last] + tiles_ref[1, h, last, first]
        same = tiles_ref[2, h, first, first] + tiles_ref[2, h, last, last]
        after = tiles_ref[2, h, last, first] + tiles_ref[3, h, first, last]
        far_before = column_sums(tiles_ref[0, h, :, first] + tiles_ref[0, h, :, last])
        far_before += column_sums(tiles_ref[1, h, first, first] + tiles_ref[1, h, first, last])
        far_before += column_sums(tiles_ref[1, h, last, last])
        far_after = column_sums(tiles_ref[4, h, :, first] + tiles_ref[4, h, :, last])
        far_after += column_sums(tiles_ref[3, h, last, first] + tiles_ref[3, h, last, last])
        far_after += column_sums(tiles_ref[3, h, first, first])
        for bucket_index in range(bucket_count):
            row = column_sums(jnp.where(grids[1] == bucket_index, same, 0.0))
            if 0 < bucket_index < half_count:
                row += column_sums(jnp.where(grids[0] == bucket_index, before, 0.0))
            if bucket_index > half_count:
                row += column_sums(jnp.where(grids[2] == bucket_index, after, 0.0))
            if bucket_index == half_count - 1:
                row += far_before
            if bucket_index == bucket_count - 1:
                row += far_after
            rows_ref[h, bucket_index : bucket_index + 1, :] = row
        return carry

    lax.fori_loop(0, heads, head_body, 0)


def attend_back_kernel(
    meta_ref,
    q_ref,
    kv_ref,
    near_ref,
    weight_ref,
    exact_ref,
    log_ref,
    *refs,
):
    parts = weight_ref.shape[0]
    branch_refs = refs[:parts]
    (
        dq_ref,
        dkv_ref,
        rows_ref,
        tiles_ref,
        key_ref,
        value_ref,
        query_ref,
        grad_ref,
        dq_sum,
        dkv_sum,
        bias_ref,
    ) = refs[parts:]
    key_tiles = kv_ref.shape[0]
    heads = near_ref.shape[0]
    fill_tiles(near_ref, bias_ref)
    size = q_ref.shape[1] // heads

    row = lax.broadcasted_iota(jnp.int32, (EXTRA, TILE), 0)
    ones = jnp.where(row < 3, 1.0, 0.0).astype(BF16)

    def turn(j, carry):
        kept = meta_ref[3 + j]
        extra = key_rows(meta_ref, j)
        for h in range(heads):
            rows = kv_ref[kept, h * size : (h + 1) * size, :]
            key_ref[kept, h] = jnp.concatenate([rows, extra], axis=0).T
            rows = kv_ref[kept, (heads + h) * size : (heads + h + 1) * size, :]
            value_ref[kept, h] = jnp.concatenate([rows, ones], axis=0).T
        return carry

    lax.fori_loop(0, key_tiles, turn, 0)
    dkv_sum[...] = jnp.zeros_like(dkv_sum)
    tiles_ref[...] = jnp.zeros_like(tiles_ref)

    def query_body(i, carry):
        tile = meta_ref[3 + key_tiles + i]
        place = tile % meta_ref[0]
        begin, end = span_of(meta_ref, tile, key_tiles)
        dq_sum[...] = jnp.zeros_like(dq_sum)
        grad_sum = dot(weight_ref[0], branch_refs[0][place])
        for k in range(1, parts):
            grad_sum += dot(weight_ref[k], branch_refs[k][place])
        for h in range(heads):
            rows = slice(h * size, (h + 1) * size)
            grad = grad_sum[rows].astype(BF16)
            centre = jnp.sum(grad.astype(F32) * exact_ref[i, rows, :], axis=0, keepdims=True)
            extra = three_rows(row, split_three(-centre)).astype(BF16)
            grad_ref[h] = jnp.concatenate([grad, extra], axis=0)
            extra = query_rows(meta_ref, tile, split_three(-log_ref[i, h]))
            query_ref[h] = jnp.concatenate([q_ref[i, rows, :], extra], axis=0)

        def key_body(j, inner):
            kept = meta_ref[3 + j]
            kind = jnp.clip(j - tile, -2, 2) + 2
            probs = [
                jnp.exp2(dot(key_ref[kept, h], query_ref[h]) + bias_ref[kind, h])
                for h in range(heads)
            ]
            score_grads = [probs[h] * dot(value_ref[kept, h], grad_ref[h]) for h in range(heads)]
            low_probs = [prob.astype(BF16) for prob in probs]
            low_grads = [score_grad.astype(BF16) for score_grad in score_grads]
            key_adds, value_adds, query_adds = [], [], []
            for h in range(heads):
                rows = slice(h * size, (h + 1) * size)
                key_adds.append(dot_rows(q_ref[i, rows, :], low_grads[h]))
                value_adds.append(dot_rows(grad_ref[h, :size, :], low_probs[h]))
                query_adds.append(dot(kv_ref[kept, rows, :], low_grads[h]))
            for h in range(heads):
                rows = slice(h * size, (h + 1) * size)
                value_rows = slice((heads + h) * size, (heads + h + 1) * size)
                tiles_ref[kind, h] += score_grads[h]
                dkv_sum[kept, rows, :] += key_adds[h]
                dkv_sum[kept, value_rows, :] += value_adds[h]
                dq_sum[rows, :] += query_adds[h]
            return inner

        lax.fori_loop(begin, end, key_body, 0)
        dq_ref[i] = (dq_sum[...] * SCALE).astype(BF16)
        return carry

    lax.fori_loop(0, q_ref.shape[0], query_body, 0)
    middle = heads * size
    dkv_ref[:, :middle, :] = (dkv_sum[:, :middle, :] * (1.0 / LOG2E)).astype(BF16)
    dkv_ref[:, middle:, :] = dkv_sum[:, middle:, :].astype(BF16)
    bucket_rows(tiles_ref, rows_ref)


def attend_back(meta, queries, keys_values, near, out_blocks, exact, logs, branch, buckets):
    key_tiles = keys_values.shape[0]
    heads = near.shape[0]
    size = queries.shape[1] // heads
    shapes = (
        jax.ShapeDtypeStruct(queries.shape, BF16),
        jax.ShapeDtypeStruct(keys_values.shape, BF16),
        jax.ShapeDtypeStruct((heads, buckets, HALF), F32),
    )
    operands = (queries, keys_values, near, out_blocks, exact, logs, *branch)
    return pl.pallas_call(
        attend_back_kernel,
        grid=(1,),
        out_shape=shapes,
        in_specs=[pl.BlockSpec(memory_space=pltpu.SMEM)] + whole_specs(operands),
        out_specs=tuple(whole_specs(shapes)),
        scratch_shapes=[
            pltpu.VMEM((len(KINDS), heads, TILE, TILE), F32),
            pltpu.VMEM((key_tiles, heads, TILE, size + EXTRA), BF16),
            pltpu.VMEM((key_tiles, heads, TILE, size + EXTRA), BF16),
            pltpu.VMEM((heads, size + EXTRA, TILE), BF16),
            pltpu.VMEM((heads, size + EXTRA, TILE), BF16),
            pltpu.VMEM(queries.shape[1:], F32),
            pltpu.VMEM(keys_values.shape, F32),
            pltpu.VMEM((len(KINDS), heads, TILE, TILE), F32),
        ],
        compiler_params=pltpu.CompilerParams(vmem_limit_bytes=VMEM_BYTES),
        cost_estimate=estimate(queries, key_tiles, 5),
        name="attend_back",
    )(meta, *operands)


def project_kernel(piece_count, weight_count, tiles, share, own_ref, table_ref, *refs):
    piece_refs = refs[:piece_count]
    weight_refs = refs[piece_count : piece_count + weight_count]
    gain_ref = refs[piece_count + weight_count]
    (
        meta_ref,
        q_ref,
        kv_ref,
        normed_ref,
        input_ref,
        in_ref,
        out_ref,
        out_t_ref,
        near_ref,
        block_ref,
        turned_ref,
    ) = refs[piece_count + weight_count + 1 :]
    grid_place, tensor_place, seq_place, own_first = (own_ref[i] for i in range(4))
    width = gain_ref.shape[0]
    head_cols = q_ref.shape[1]
    columns = turned_ref.shape[0]
    for k in range(weight_count):
        place = grid_place ^ k if weight_count > 1 else 0
        block_ref[place] = weight_refs[k][...]
    full = block_ref[...].reshape(width, columns)
    in_ref[...] = full[:, : 3 * head_cols]
    turned_ref[...] = full.T
    blocks_here = width // share
    tall = block_ref.shape[1]
    per = share // tall if weight_count > 1 else 1
    for k in range(blocks_here):
        if weight_count > 1:
            block = block_ref[pl.ds((tensor_place ^ k) * per, per), :, 3 * head_cols :]
            block = block.reshape(share, head_cols)
        else:
            start = pl.multiple_of((tensor_place ^ k) * share, share)
            block = block_ref[0, pl.ds(start, share), 3 * head_cols :]
        out_ref[k] = block
        out_t_ref[k] = block.T
    key_tiles = kv_ref.shape[0]
    near_tiles(table_ref, near_ref)
    early = jnp.zeros((1, TILE), F32)
    late = jnp.zeros((1, TILE), F32)
    gain = gain_ref[...]
    for k in range(piece_count):
        for s in range(piece_refs[0].shape[0]):
            kept = s + k
            rows = piece_refs[k][s, :width, :].astype(F32)
            ids = piece_refs[k][s, width : width + 16, :][:1].astype(F32)
            early += (ids < 0.5).astype(F32)
            late += (ids < 1.5).astype(F32)
            root = lax.rsqrt(jnp.sum(rows * rows, axis=0, keepdims=True) * (1.0 / width) + EPSILON)
            normed = (rows * root * gain).astype(BF16)
            normed_ref[kept] = normed
            kv_ref[kept] = dot(turned_ref[head_cols : 3 * head_cols, :], normed).astype(BF16)
    for i in range(tiles):
        normed = normed_ref[own_first + i]
        q_ref[i] = (dot(turned_ref[:head_cols, :], normed) * (SCALE * LOG2E)).astype(BF16)
        start = pl.multiple_of(tensor_place * share, share)
        if piece_count > 1:
            input_ref[tensor_place ^ i] = piece_refs[i][0, pl.ds(start, share), :]
        else:
            input_ref[i] = piece_refs[0][own_first + i, pl.ds(start, share), :]
    meta_ref[0] = tiles
    meta_ref[1] = jnp.sum(early).astype(jnp.int32)
    meta_ref[2] = jnp.sum(late).astype(jnp.int32)
    for j in range(key_tiles):
        if piece_count > 1:
            meta_ref[3 + j] = ((j // tiles) ^ seq_place) * tiles + ((j % tiles) ^ tensor_place)
        else:
            meta_ref[3 + j] = j
    for i in range(tiles):
        shift = tensor_place ^ i if piece_count > 1 else i
        meta_ref[3 + key_tiles + i] = seq_place * tiles + shift


def project(own, table, pieces, weight_pieces, gain, tiles, key_tiles, share, heads):
    width = gain.shape[0]
    columns = weight_pieces[0].shape[1]
    head_cols = columns // 4
    parts = width // share
    shapes = (
        jax.ShapeDtypeStruct((tiles, head_cols, TILE), BF16),
        jax.ShapeDtypeStruct((key_tiles, 2 * head_cols, TILE), BF16),
        jax.ShapeDtypeStruct((key_tiles, width, TILE), BF16),
        jax.ShapeDtypeStruct((tiles, share, TILE), BF16),
        jax.ShapeDtypeStruct((width, 3 * head_cols), BF16),
        jax.ShapeDtypeStruct((parts, share, head_cols), BF16),
        jax.ShapeDtypeStruct((parts, head_cols, share), BF16),
        jax.ShapeDtypeStruct((heads, len(KINDS), HALF, HALF), F32),
    )
    operands = (*pieces, *weight_pieces, gain)
    return pl.pallas_call(
        functools.partial(project_kernel, len(pieces), len(weight_pieces), tiles, share),
        grid=(1,),
        out_shape=(jax.ShapeDtypeStruct((3 + key_tiles + tiles,), jnp.int32),) + shapes,
        in_specs=[pl.BlockSpec(memory_space=pltpu.SMEM)] * 2 + whole_specs(operands),
        out_specs=(pl.BlockSpec(memory_space=pltpu.SMEM),) + tuple(whole_specs(shapes)),
        scratch_shapes=[
            pltpu.VMEM((len(weight_pieces),) + weight_pieces[0].shape, BF16),
            pltpu.VMEM((columns, width), BF16),
        ],
        compiler_params=pltpu.CompilerParams(vmem_limit_bytes=VMEM_BYTES),
        cost_estimate=pl.CostEstimate(
            flops=6 * key_tiles * TILE * width * head_cols,
            bytes_accessed=8 * key_tiles * TILE * width,
            transcendentals=0,
        ),
        name="project",
    )(own, table, *operands)


def project_back_kernel(fast, parts, own_ref, dq_ref, dkv_ref, normed_ref, in_ref, attended_ref, *refs):
    branch_refs = refs[:parts]
    if fast:
        far_even, far_odd, own_even, own_odd, weight_even, weight_odd, gain_ref, full_ref = refs[
            parts:
        ]
    else:
        part_ref, weight_ref, gain_ref, full_ref = refs[parts:]
    grid_place, tensor_place, seq_place, own_first = (own_ref[i] for i in range(4))
    tiles, head_cols, _ = dq_ref.shape
    key_tiles = dkv_ref.shape[0]
    width = in_ref.shape[0]
    share = width // parts
    key_weight = in_ref[:, head_cols:]
    query_weight = in_ref[:, :head_cols]
    if fast:
        for n in range(tiles):
            block = dot(key_weight, dkv_ref[tiles + n]).astype(BF16)
            (far_odd if n & 1 else far_even)[n // 2] = block
        for n in range(tiles):
            block = dot(key_weight, dkv_ref[n]) + dot(query_weight, dq_ref[n])
            (own_odd if n & 1 else own_even)[n // 2] = block.astype(BF16)
    else:
        for n in range(key_tiles):
            part_ref[n] = dot(key_weight, dkv_ref[n]).astype(BF16)
        for n in range(tiles):
            block = part_ref[own_first + n].astype(F32) + dot(query_weight, dq_ref[n])
            part_ref[own_first + n] = block.astype(BF16)
    query_sum = dot_rows(normed_ref[own_first], dq_ref[0])
    for n in range(1, tiles):
        query_sum += dot_rows(normed_ref[own_first + n], dq_ref[n])
    key_sum = dot_rows(normed_ref[0], dkv_ref[0])
    for n in range(1, key_tiles):
        key_sum += dot_rows(normed_ref[n], dkv_ref[n])
    gain_ref[...] = jnp.sum(
        query_sum * query_weight.astype(F32), axis=1, keepdims=True
    ) + jnp.sum(key_sum * key_weight.astype(F32), axis=1, keepdims=True)
    full_ref[:, :head_cols] = query_sum.astype(BF16)
    full_ref[:, head_cols : 3 * head_cols] = key_sum.astype(BF16)
    for k in range(parts):
        block = dot_rows(branch_refs[k][0], attended_ref[0])
        for n in range(1, tiles):
            block += dot_rows(branch_refs[k][n], attended_ref[n])
        start = pl.multiple_of((tensor_place ^ k) * share, share)
        full_ref[pl.ds(start, share), 3 * head_cols :] = block.astype(BF16)
    if fast:
        tall = weight_even.shape[1]
        for k in range(weight_even.shape[0]):
            place = grid_place ^ (2 * k)
            weight_even[k] = full_ref[pl.ds(pl.multiple_of(place * tall, tall), tall), :]
            weight_odd[k] = full_ref[pl.ds(pl.multiple_of((place ^ 1) * tall, tall), tall), :]
    else:
        weight_ref[...] = full_ref[...]


def project_back(fast, own, dq, dkv, normed, in_flat, attended, branch, grid_count):
    tiles, head_cols, _ = dq.shape
    key_tiles = dkv.shape[0]
    width = in_flat.shape[0]
    parts = len(branch)
    columns = 4 * head_cols
    if fast:
        block = jax.ShapeDtypeStruct((parts // 2, width, TILE), BF16)
        weight = jax.ShapeDtypeStruct((grid_count // 2, width // grid_count, columns), BF16)
        shapes = (block,) * 4 + (weight,) * 2
    else:
        shapes = (
            jax.ShapeDtypeStruct((key_tiles, width, TILE), BF16),
            jax.ShapeDtypeStruct((width, columns), BF16),
        )
    shapes = shapes + (jax.ShapeDtypeStruct((width, 1), F32),)
    operands = (dq, dkv, normed, in_flat, attended, *branch)
    return pl.pallas_call(
        functools.partial(project_back_kernel, fast, parts),
        grid=(1,),
        out_shape=shapes,
        in_specs=[pl.BlockSpec(memory_space=pltpu.SMEM)] + whole_specs(operands),
        out_specs=tuple(whole_specs(shapes)),
        scratch_shapes=[pltpu.VMEM((width, columns), BF16)],
        compiler_params=pltpu.CompilerParams(vmem_limit_bytes=VMEM_BYTES),
        cost_estimate=pl.CostEstimate(
            flops=12 * key_tiles * TILE * width * head_cols,
            bytes_accessed=8 * key_tiles * TILE * width,
            transcendentals=0,
        ),
        name="project_back",
    )(own, *operands)


def finish_kernel(input_ref, gain_ref, branch_ref, result_ref, *refs):
    sum_refs = refs[:-2]
    out_ref, grad_ref = refs[-2:]
    rows = input_ref[...]
    width = rows.shape[1]
    values = rows.T
    gain = gain_ref[...]
    grad = sum_refs[0][0].astype(F32)
    for ref in sum_refs[1:]:
        grad += ref[0].astype(F32)
    root = lax.rsqrt(jnp.sum(values * values, axis=0, keepdims=True) * (1.0 / width) + EPSILON)
    scaled = grad * gain
    centre = jnp.sum(scaled * values, axis=0, keepdims=True) * (1.0 / width)
    total = root * scaled - values * (root * root * root * centre)
    grad_ref[...] = (total + branch_ref[...].astype(F32)).T
    out_ref[...] = rows + result_ref[...].astype(F32).T


def finish(block_input, gain, branch, result, sums):
    shape = jax.ShapeDtypeStruct(block_input.shape, F32)
    operands = (block_input, gain, branch, result, *sums)
    first = pl.BlockSpec((1,) + sums[0].shape[1:], functools.partial(origin, 3))
    return pl.pallas_call(
        finish_kernel,
        grid=(1,),
        out_shape=(shape, shape),
        in_specs=whole_specs(operands[:4]) + [first] * len(sums),
        out_specs=tuple(whole_specs((shape, shape))),
        compiler_params=pltpu.CompilerParams(vmem_limit_bytes=VMEM_BYTES),
        name="finish",
    )(*operands)


def split_low(values):
    high = values.astype(BF16)
    return high, (values - high.astype(F32)).astype(BF16)


def load_tile(ref, first, count, *place):
    return jnp.concatenate([ref[(first + m, *place)] for m in range(count)], axis=-1)


def expert_kernel(parts, own_ref, *refs):
    state_refs = refs[:parts]
    (grad_ref, other_ref, in_ref, in_t_ref, out_ref, gain_ref) = refs[parts : parts + 6]
    (
        kept_ref,
        sent_ref,
        normed_ref,
        act_ref,
        pre_ref,
        gate_ref,
        router_sum,
        state_ref,
        full_ref,
        back_ref,
        joint_ref,
    ) = refs[parts + 6 :]

    @pl.when(pl.program_id(0) == 0)
    def _():
        router_sum[...] = jnp.zeros_like(router_sum)

    width = gain_ref.shape[0]
    share = width // parts
    hidden = act_ref.shape[1]
    experts = router_sum.shape[0]
    expert, own = own_ref[0], own_ref[1]
    chains, columns = state_ref.shape[0], state_ref.shape[-1]
    merged = kept_ref.shape[1] // chains
    slots = columns // merged
    gain = gain_ref[...]
    for a in range(chains):
        for k in range(parts):
            state_ref[a, own ^ k] = load_tile(state_refs[k], a * merged, merged)
            near = 2 * (k // 2) + ((own & 1) ^ (k & 1))
            full_ref[a, near] = load_tile(
                other_ref if k & 1 else grad_ref, a * merged, merged, k // 2
            )
    for a in range(chains):
        state = state_ref[a].reshape(width, columns).astype(F32)
        root = lax.rsqrt(jnp.sum(state * state, axis=0, keepdims=True) * (1.0 / width) + EPSILON)
        normed = (state * root * gain).astype(BF16)
        normed_ref[a] = normed
        both = dot(in_t_ref[...], normed)
        pre_act, logits = both[:hidden], both[hidden : hidden + experts]
        act_grad = dot(out_ref[...], full_ref[a].reshape(width, columns))
        raised = jnp.exp(logits - jnp.max(logits, axis=0, keepdims=True))
        router_probs = raised / jnp.sum(raised, axis=0, keepdims=True)
        chosen = lax.broadcasted_iota(jnp.int32, logits.shape, 0) == expert
        gate = jnp.sum(jnp.where(chosen, router_probs, 0.0), axis=0, keepdims=True)
        gate_ref[a] = gate
        square = pre_act * pre_act
        cdf = 0.5 + 0.5 * jnp.tanh(pre_act * (GELU_A + (GELU_A * GELU_B) * square))
        activated = pre_act * cdf
        act_ref[a] = activated.astype(BF16)
        rise = (2.0 * GELU_A) + (6.0 * GELU_A * GELU_B) * square
        pre_grad = act_grad * (cdf + activated * (1.0 - cdf) * rise)
        low_grad = pre_grad.astype(BF16)
        pre_ref[a] = low_grad
        gate_grad = jnp.sum(activated * act_grad, axis=0, keepdims=True)
        logit_grad = gate_grad * (chosen.astype(F32) - router_probs)
        centre = jnp.sum(pre_grad * pre_act, axis=0, keepdims=True)
        centre += jnp.sum(logit_grad * logits, axis=0, keepdims=True)
        joint_ref[a, :hidden, :] = low_grad
        joint_ref[a, hidden:, :] = jnp.concatenate(split_low(logit_grad), axis=0)
        high, low = split_low(logit_grad * gate)
        router_sum[...] += dot_rows(high, normed) + dot_rows(low, normed)
        normed_grad = dot(in_ref[...], joint_ref[a])
        state = state_ref[a].reshape(width, columns).astype(F32)
        back = (root * gate) * (normed_grad * gain - state * (root * centre * (1.0 / width)))
        back_ref[a] = back.astype(BF16).reshape(parts, share, columns)
        for k in range(parts):
            block = back_ref[a, own ^ k]
            target = sent_ref if k & 1 else kept_ref
            for m in range(merged):
                target[k // 2, a * merged + m] = block[:, m * slots : (m + 1) * slots]


def result_kernel(parts, own_ref, *refs):
    out_t_ref, kept_ref, sent_ref, result_ref = refs[-4:]
    chunks = (len(refs) - 4) // 2
    own = own_ref[1]
    width = out_t_ref.shape[0]
    share = width // parts
    merged = kept_ref.shape[1]
    for c in range(chunks):
        gate, activated = refs[2 * c + 1][0], refs[2 * c][0]
        slots = activated.shape[-1] // merged
        result = dot(out_t_ref[...], activated) * gate
        result_ref[c] = result.astype(BF16).reshape(parts, share, -1)
        for k in range(parts):
            block = result_ref[c, own ^ k]
            target = sent_ref if k & 1 else kept_ref
            for m in range(merged):
                target[k // 2, m, :, c * slots : (c + 1) * slots] = block[
                    :, m * slots : (m + 1) * slots
                ]


def grads_kernel(parts, merged, own_ref, *refs):
    grad_ref, other_ref, in_ref, in_sum, out_sum, gain_sum, full_ref = refs[-7:]
    chunks = (len(refs) - 7) // 4

    @pl.when(pl.program_id(0) == 0)
    def _():
        in_sum[...] = jnp.zeros_like(in_sum)
        out_sum[...] = jnp.zeros_like(out_sum)

    own = own_ref[1]
    width = in_ref.shape[0]
    for c in range(chunks):
        normed_ref, act_ref, pre_ref, gate_ref = refs[4 * c : 4 * c + 4]
        gate = gate_ref[0]
        columns = gate.shape[-1]
        slots = columns // merged
        for k in range(parts):
            near = 2 * (k // 2) + ((own & 1) ^ (k & 1))
            source = other_ref if k & 1 else grad_ref
            full_ref[c, near] = jnp.concatenate(
                [source[m, k // 2, :, c * slots : (c + 1) * slots] for m in range(merged)], axis=-1
            )
        normed = (normed_ref[0].astype(F32) * gate).astype(BF16)
        in_sum[...] += dot_rows(normed, pre_ref[0])
        scaled = (full_ref[c].reshape(width, columns).astype(F32) * gate).astype(BF16)
        out_sum[...] += dot_rows(act_ref[0], scaled)

    @pl.when(pl.program_id(0) == pl.num_programs(0) - 1)
    def _():
        gain_sum[...] = jnp.sum(in_sum[...] * in_ref[...].astype(F32), axis=1, keepdims=True)


def fixed_spec(shape):
    return pl.BlockSpec(shape, lambda g: (0,) * len(shape))


def run_expert(own, states, grads, chunk, merged, chains, weights):
    parts = len(states)
    count, share, slots = states[0].shape
    width = share * parts
    columns = merged * slots
    steps = count // merged
    hidden = weights[2].shape[0]
    joint = weights[0].shape[1]
    experts = (joint - hidden) // 2
    half = parts // 2
    taken = merged * chains
    piece = pl.BlockSpec((taken, share, slots), lambda g: (g, 0, 0))
    grad_piece = pl.BlockSpec((taken, half, share, slots), lambda g: (g, 0, 0, chunk))
    split = pl.BlockSpec((half, taken, share, slots), lambda g: (0, g, 0, 0))
    wide = pl.BlockSpec((chains, width, columns), lambda g: (g, 0, 0))
    deep = pl.BlockSpec((chains, hidden, columns), lambda g: (g, 0, 0))
    flat = pl.BlockSpec((chains, 1, columns), lambda g: (g, 0, 0))
    return pl.pallas_call(
        functools.partial(expert_kernel, parts),
        grid=(steps // chains,),
        out_shape=(
            jax.ShapeDtypeStruct((half, count, share, slots), BF16),
            jax.ShapeDtypeStruct((half, count, share, slots), BF16),
            jax.ShapeDtypeStruct((steps, width, columns), BF16),
            jax.ShapeDtypeStruct((steps, hidden, columns), BF16),
            jax.ShapeDtypeStruct((steps, hidden, columns), BF16),
            jax.ShapeDtypeStruct((steps, 1, columns), F32),
            jax.ShapeDtypeStruct((experts, width), F32),
        ),
        in_specs=[pl.BlockSpec(memory_space=pltpu.SMEM)]
        + [piece] * parts
        + [grad_piece] * 2
        + [fixed_spec(weight.shape) for weight in weights],
        out_specs=(split, split, wide, deep, deep, flat, fixed_spec((experts, width))),
        scratch_shapes=[
            pltpu.VMEM((chains, parts, share, columns), BF16),
            pltpu.VMEM((chains, parts, share, columns), BF16),
            pltpu.VMEM((chains, parts, share, columns), BF16),
            pltpu.VMEM((chains, joint, columns), BF16),
        ],
        compiler_params=pltpu.CompilerParams(vmem_limit_bytes=VMEM_BYTES),
        cost_estimate=pl.CostEstimate(
            flops=16 * steps * columns * width * hidden,
            bytes_accessed=16 * steps * columns * width,
            transcendentals=steps * columns * hidden,
        ),
        name="expert",
    )(own, *states, *grads, *weights)


def run_result(own, saved, parts, merged, out_t):
    chunks = len(saved)
    steps, hidden, columns = saved[0][0].shape
    width = out_t.shape[0]
    share, half, slots = width // parts, parts // 2, columns // merged
    deep = pl.BlockSpec((1, hidden, columns), lambda g: (g, 0, 0))
    flat = pl.BlockSpec((1, 1, columns), lambda g: (g, 0, 0))
    split = pl.BlockSpec((half, merged, share, slots * chunks), lambda g: (0, g, 0, 0))
    total = jax.ShapeDtypeStruct((half, steps * merged, share, slots * chunks), BF16)
    return pl.pallas_call(
        functools.partial(result_kernel, parts),
        grid=(steps,),
        out_shape=(total, total),
        in_specs=[pl.BlockSpec(memory_space=pltpu.SMEM)]
        + [deep, flat] * chunks
        + [fixed_spec(out_t.shape)],
        out_specs=(split, split),
        scratch_shapes=[pltpu.VMEM((chunks, parts, share, columns), BF16)],
        compiler_params=pltpu.CompilerParams(vmem_limit_bytes=VMEM_BYTES),
        cost_estimate=pl.CostEstimate(
            flops=6 * chunks * steps * columns * width * hidden,
            bytes_accessed=6 * chunks * steps * columns * width,
            transcendentals=0,
        ),
        name="result",
    )(own, *[array for arrays in saved for array in arrays], out_t)


def run_grads(own, saved, grads, merged, weight):
    chunks = len(saved)
    steps, width, columns = saved[0][0].shape
    hidden = saved[0][1].shape[1]
    _, half, share, _ = grads[0].shape
    parts = 2 * half
    wide = pl.BlockSpec((1, width, columns), lambda g: (g, 0, 0))
    deep = pl.BlockSpec((1, hidden, columns), lambda g: (g, 0, 0))
    flat = pl.BlockSpec((1, 1, columns), lambda g: (g, 0, 0))
    grad_piece = pl.BlockSpec((merged,) + grads[0].shape[1:], lambda g: (g, 0, 0, 0))
    return pl.pallas_call(
        functools.partial(grads_kernel, parts, merged),
        grid=(steps,),
        out_shape=(
            jax.ShapeDtypeStruct((width, hidden), F32),
            jax.ShapeDtypeStruct((hidden, width), F32),
            jax.ShapeDtypeStruct((width, 1), F32),
        ),
        in_specs=[pl.BlockSpec(memory_space=pltpu.SMEM)]
        + [wide, deep, deep, flat] * chunks
        + [grad_piece] * 2
        + [fixed_spec(weight.shape)],
        out_specs=(
            fixed_spec((width, hidden)),
            fixed_spec((hidden, width)),
            fixed_spec((width, 1)),
        ),
        scratch_shapes=[pltpu.VMEM((chunks, parts, share, columns), BF16)],
        compiler_params=pltpu.CompilerParams(vmem_limit_bytes=VMEM_BYTES),
        cost_estimate=pl.CostEstimate(
            flops=8 * chunks * steps * columns * width * hidden,
            bytes_accessed=8 * chunks * steps * columns * width,
            transcendentals=0,
        ),
        name="grads",
    )(own, *[array for arrays in saved for array in arrays], *grads, weight)


def shards(
    block_input,
    attn_in_weight,
    attn_out_weight,
    position_bias,
    norm_gains,
    router_weight,
    expert_in,
    expert_out,
    segment_ids,
    expert_ids,
    out_grad,
):
    tensor_count, seq_count = lax.axis_size("tensor"), lax.axis_size("seq")
    tensor_place, seq_place = lax.axis_index("tensor"), lax.axis_index("seq")
    grid_count = lax.axis_size("dp") * seq_count
    grid_place = lax.axis_index("dp") * seq_count + seq_place
    local_count, width = block_input.shape
    group_count = local_count * tensor_count
    share = width // tensor_count
    bucket_count, heads = position_bias.shape
    head_cols = attn_in_weight.shape[2]
    experts = router_weight.shape[1]
    capacity = max(2, 2 * group_count // experts)
    tiles = group_count // TILE
    key_tiles = tiles * seq_count
    fast = seq_count == 2 and local_count == TILE and grid_count == 8

    def tiled(pieces):
        pieces = reorder(pieces, tensor_place)
        if local_count == TILE:
            return jnp.stack(pieces)
        return jnp.concatenate(pieces, axis=-1)[None]

    half = tensor_count // 2
    core = tensor_place & 1
    own_rows = jnp.concatenate(
        [
            jnp.transpose(block_input.astype(BF16)),
            jnp.pad(segment_ids.astype(BF16), ((0, 15), (0, 0))),
        ]
    )
    weight_piece = jnp.concatenate(
        [attn_in_weight[0], attn_in_weight[1], attn_in_weight[2], jnp.transpose(attn_out_weight)],
        axis=1,
    )
    grad_rows = jnp.transpose(out_grad.astype(BF16)).reshape(half, 2, share, local_count)
    grad_mine = lax.dynamic_index_in_dim(grad_rows, core, 1, keepdims=False)
    grad_theirs = lax.dynamic_index_in_dim(grad_rows, core ^ 1, 1, keepdims=False)
    in_plain, out_plain = expert_in[0], expert_out[0]
    if fast:
        far_rows = swap(own_rows, "seq", 1)
        near_two = swap(own_rows, "tensor", 2)
        columns = [weight_piece] + [swap(weight_piece, "dp", k) for k in range(1, grid_count // 2)]
        grad_other = swap(grad_theirs, "tensor", 1)
        far_rows, near_two, columns, grad_other, expert_ids, in_plain, out_plain = (
            lax.optimization_barrier(
                (
                    far_rows,
                    near_two,
                    columns,
                    grad_other,
                    expert_ids,
                    in_plain,
                    out_plain,
                )
            )
        )
        far_two = swap(far_rows, "tensor", 2)
        near_columns = swap(weight_piece, "seq", 1)
        far_columns = swap(jnp.stack(columns[1:]), "seq", 1)
        near_one, near_three = swap(own_rows, "tensor", 1), swap(near_two, "tensor", 1)
    else:
        grad_other = swap(grad_theirs, "tensor", 1)
        both_rows = lax.all_gather(own_rows, "seq", axis=0, tiled=False)
        row_pieces = gather_relative(both_rows, "tensor")
        own_first = seq_place * tiles
        row_pieces = jnp.concatenate(reorder(row_pieces, tensor_place), axis=-1)
        row_pieces = row_pieces.reshape(seq_count, -1, tiles, TILE)
        row_pieces = [jnp.moveaxis(row_pieces, 2, 1).reshape(key_tiles, -1, TILE)]
        weight_pieces = [lax.all_gather(weight_piece, ("dp", "seq"), axis=0, tiled=True)]

    in_t, out_t = jnp.transpose(in_plain), jnp.transpose(out_plain)
    router_t = jnp.transpose(router_weight)
    in_joint = jnp.concatenate([in_plain, router_weight, router_weight], axis=1)
    in_t = jnp.concatenate([in_t, router_t, router_t])
    route_all = expert_ids[:, 0]
    expert_range = jnp.arange(experts, dtype=jnp.int32)
    route_hot = (route_all[:, None] == expert_range[None, :]).astype(jnp.int32)
    slot_rank = jnp.sum(jnp.cumsum(route_hot, axis=0) * route_hot, axis=-1) - 1
    target = (route_all * capacity + slot_rank).reshape(1, tiles, TILE, 1)
    places = jnp.arange(experts * capacity, dtype=jnp.int32).reshape(experts, 1, 1, capacity)
    chunks = 2 if capacity >= TILE else 1
    slots = capacity // chunks
    spread = max(1, TILE // capacity)
    merged = max(1, TILE // (slots * spread))

    def exchange(values):
        return lax.all_to_all(values, ("dp", "seq"), split_axis=0, concat_axis=0, tiled=True)

    def joined(values):
        if spread == 1:
            return values
        shape = values.shape
        values = values.reshape((-1, spread) + shape[1:])
        return jnp.moveaxis(values, 1, -2).reshape(
            (shape[0] // spread,) + shape[1:-1] + (spread * shape[-1],)
        )

    def parted(values):
        if spread == 1:
            return values
        shape = values.shape
        values = values.reshape(shape[:-1] + (spread, shape[-1] // spread))
        return jnp.moveaxis(values, -2, 1).reshape((-1,) + shape[1:-1] + (shape[-1] // spread,))


    gain_one = norm_gains[0][:, None]
    gain_two = norm_gains[1][:, None]
    if fast:
        (
            far_two,
            far_columns,
            gain_one,
            in_t,
            in_joint,
            out_t,
            target,
            gain_two,
            grad_mine,
            grad_other,
        ) = lax.optimization_barrier(
            (
                far_two,
                far_columns,
                gain_one,
                in_t,
                in_joint,
                out_t,
                target,
                gain_two,
                grad_mine,
                grad_other,
            )
        )
        far_one, far_three = swap(far_rows, "tensor", 1), swap(far_two, "tensor", 1)
        row_pieces = [own_rows, near_one, near_two, near_three]
        row_pieces += [far_rows, far_one, far_two, far_three]
        row_pieces = [rows[None] for rows in row_pieces]
        weight_pieces = [weight_piece, near_columns]
        for k in range(1, grid_count // 2):
            weight_pieces += [columns[k], far_columns[k - 1]]
        own_first = jnp.int32(0)
    own = jnp.stack([grid_place, tensor_place, seq_place, own_first]).astype(jnp.int32)
    onehot = (target == places).astype(BF16)
    grad_pair = swap(jnp.stack([grad_mine, grad_other]), "tensor", 2)
    (
        meta,
        queries,
        keys_values,
        normed_tiles,
        input_share,
        in_flat,
        out_blocks,
        out_t_blocks,
        near,
    ) = project(
        own,
        position_bias.reshape(-1),
        row_pieces,
        weight_pieces,
        gain_one,
        tiles,
        key_tiles,
        share,
        heads,
    )
    queries, grad_pair = lax.optimization_barrier((queries, grad_pair))
    grad_here = tiled([grad_mine, grad_other, grad_pair[0], grad_pair[1]])
    grad_buffer = einsum("nkdq,enqs->ekds", grad_here, onehot).astype(BF16)
    queries, grad_buffer = lax.optimization_barrier((queries, grad_buffer))
    grad_arrived = joined(exchange(grad_buffer))
    exact, attended, logs, attn_even, attn_odd = attend(
        meta, queries, keys_values, near, out_blocks
    )
    attn_share = sum_tensor(attn_even, attn_odd)
    state_share = (input_share.astype(F32) + attn_share).astype(BF16)
    state_share, grad_arrived = lax.optimization_barrier((state_share, grad_arrived))
    grad_near = swap(grad_arrived, "tensor", 1)

    weights = (in_joint, in_t, expert_out[0], gain_two)
    grads = (grad_arrived, grad_near)
    buffers = [
        einsum("ndq,enqs->eds", state_share, onehot[..., c * slots : (c + 1) * slots]).astype(BF16)
        for c in range(chunks)
    ]
    buffers = list(lax.optimization_barrier(tuple(buffers)))
    arrivals = [joined(exchange(buffer)) for buffer in buffers]
    chains = 2 if arrivals[0].shape[0] // merged % 2 == 0 else 1
    gathered = []
    for arrival in arrivals:
        gathered.append(
            [arrival, swap(arrival, "tensor", 1), swap(arrival, "tensor", 2)]
        )
    gathered[0][0], gathered[-1][0] = lax.optimization_barrier((gathered[0][0], gathered[-1][0]))
    saved, halves, crossed = [], [], []
    small = jnp.zeros((experts, width), F32)
    for c in range(chunks):
        gathered[c].append(swap(gathered[c][2], "tensor", 1))
        kept, sent, normed_two, activated, pre_grad, gate, router_sum = run_expert(
            own, gathered[c], grads, c, merged, chains, weights
        )
        saved.append((normed_two, activated, pre_grad, gate))
        if c + 1 < chunks:
            sent, gathered[c + 1][2] = lax.optimization_barrier((sent, gathered[c + 1][2]))
        if c > 0:
            sent, crossed[c - 1] = lax.optimization_barrier((sent, crossed[c - 1]))
        stayed, got, to_send = core_step(kept, sent)
        if c + 1 == chunks:
            own_late, to_send = lax.optimization_barrier((own, to_send))
        halves.append((stayed, got))
        crossed.append(swap(to_send, "tensor", 2))
        small = small + router_sum
    returned = [
        exchange(parted(chip_step(*halves[c], crossed[c]).astype(BF16)))
        for c in range(chunks - 1)
    ]
    result_even, result_odd = run_result(
        own_late, [(arrays[1], arrays[3]) for arrays in saved], tensor_count, merged, out_t
    )
    tied = lax.optimization_barrier((result_odd, crossed[-1], *returned))
    result_odd, crossed[-1], returned = tied[0], tied[1], list(tied[2:])
    returned.append(exchange(parted(chip_step(*halves[-1], crossed[-1]).astype(BF16))))
    result_near, result_got, result_sent = core_step(result_even, result_odd)
    result_far = swap(result_sent, "tensor", 2)
    own_late, result_sent = lax.optimization_barrier((own, result_sent))
    grad_expert_in, grad_expert_out, in_gain = run_grads(
        own_late, saved, grads, merged, expert_in[0]
    )
    in_gain, returned[-1] = lax.optimization_barrier((in_gain, returned[-1]))
    gain_part = in_gain[:, 0] + jnp.sum(small * router_t.astype(F32), axis=0)
    router_gains = jnp.concatenate([small, (gain_part / norm_gains[1])[None]])
    state_grad = lax.dynamic_index_in_dim(grad_here, tensor_place // 2, 1, keepdims=False)
    state_grad = state_grad.astype(F32)
    for c in range(chunks):
        state_grad = state_grad + einsum(
            "eds,enqs->ndq", returned[c], onehot[..., c * slots : (c + 1) * slots]
        )
    state_grad = state_grad.astype(BF16)

    branch = [state_grad, swap(state_grad, "tensor", 1), swap(state_grad, "tensor", 2)]
    result_total = chip_step(result_near, result_got, result_far).astype(BF16)
    result_total, branch[2] = lax.optimization_barrier((result_total, branch[2]))
    branch.append(swap(branch[2], "tensor", 1))
    result_back = exchange(parted(result_total))
    dq, dkv, bias_rows = attend_back(
        meta, queries, keys_values, near, out_t_blocks, exact, logs, branch, bucket_count
    )
    dq, dkv, bias_rows, result_back = lax.optimization_barrier((dq, dkv, bias_rows, result_back))

    def joined_small():
        bias_padded = lax.dynamic_update_slice_in_dim(
            jnp.zeros((heads * tensor_count, bucket_count), F32),
            jnp.sum(bias_rows, axis=2),
            tensor_place * heads,
            0,
        )
        return jnp.concatenate(
            [router_gains.reshape(-1), gain_part[:, 0] / norm_gains[0], bias_padded.reshape(-1)]
        )

    def result_rows_of():
        shares = attn_share + einsum("eds,enqs->ndq", result_back, onehot)
        return jnp.moveaxis(shares.astype(BF16), 0, 1).reshape(share, tensor_count, local_count)

    if fast:
        far_even, far_odd, own_even, own_odd, weight_even, weight_odd, gain_part = project_back(
            True, own, dq, dkv, normed_tiles, in_flat, attended, branch, grid_count
        )
        far_near, far_got, far_send = core_step(far_even, far_odd)
        own_got = swap(own_odd, "tensor", 1)
        own_send = (own_even[1].astype(F32) + own_got[1].astype(F32)).astype(BF16)
        weight_sent = swap(weight_odd, "seq", 1)
        far_send, own_send, gain_part, result_back = lax.optimization_barrier(
            (far_send, own_send, gain_part, result_back)
        )
        far_sent = swap(far_send, "tensor", 2)
        small = sum_all(joined_small(), ("dp",))
        result_share = result_rows_of()
        own_send, result_share = lax.optimization_barrier((own_send, result_share))
        own_sent = swap(own_send, "tensor", 2)
        far_sent, weight_sent, small, result_share, branch = lax.optimization_barrier(
            (far_sent, weight_sent, small, result_share, branch)
        )
        far_sum = chip_step(far_near, far_got, far_sent).astype(BF16)
        sums = [own_even, own_got, own_sent[None], swap(far_sum, "seq", 1)[None]]
        weight_half = weight_even.astype(F32) + weight_sent.astype(F32)
        weight_grad = weight_half[0]
        for k in range(1, grid_count // 2):
            weight_grad = weight_grad + swap(weight_half[k].astype(BF16), "dp", k).astype(F32)
    else:
        row_part, weight_part, gain_part = project_back(
            False, own, dq, dkv, normed_tiles, in_flat, attended, branch, grid_count
        )
        row_part = lax.psum_scatter(row_part, "seq", scatter_dimension=0, tiled=True)
        row_part = jnp.moveaxis(row_part, 0, 1).reshape(width, tensor_count, local_count)
        blocks = [
            lax.dynamic_index_in_dim(row_part, tensor_place ^ k, 1, keepdims=False)
            for k in range(tensor_count)
        ]
        sums = [sum_tensor(jnp.stack(blocks[0::2]), jnp.stack(blocks[1::2]))[None]]
        small = sum_all(joined_small(), ("dp",))
        result_share = result_rows_of()
        weight_grad = lax.psum_scatter(
            weight_part, ("dp", "seq"), scatter_dimension=0, tiled=True
        ).astype(F32)
    grad_attn_in = jnp.stack(
        [weight_grad[:, c * head_cols : (c + 1) * head_cols] for c in range(3)]
    )
    grad_attn_out = jnp.transpose(weight_grad[:, 3 * head_cols :])

    small = sum_all(small, ("seq", "tensor"))
    first, second = experts * width, (experts + 1) * width
    grad_router = jnp.transpose(small[:first].reshape(experts, width))
    grad_gains = jnp.stack([small[second : second + width], small[first:second]])
    bias_sum = small[second + width :].reshape(heads * tensor_count, bucket_count)
    grad_bias = jnp.transpose(lax.dynamic_slice_in_dim(bias_sum, tensor_place * heads, heads, 0))

    result_rows = lax.all_to_all(
        jnp.moveaxis(result_share, 1, 0), "tensor", split_axis=0, concat_axis=0, tiled=True
    ).reshape(width, local_count)
    if local_count == TILE:
        own_branch = [
            lax.dynamic_index_in_dim(piece, tensor_place, 0, keepdims=False) for piece in branch
        ]
    else:
        own_branch = [
            lax.dynamic_slice_in_dim(piece[0], tensor_place * local_count, local_count, 1)
            for piece in branch
        ]
    own_branch = jnp.concatenate(reorder(own_branch, tensor_place))
    block_out, input_grad = finish(block_input, gain_one, own_branch, result_rows, sums)
    return (
        block_out,
        input_grad,
        grad_attn_in,
        grad_attn_out,
        grad_bias,
        grad_gains,
        grad_router,
        grad_expert_in[None],
        grad_expert_out[None],
    )


def solution(mesh):
    return jax.shard_map(
        shards,
        mesh=mesh,
        in_specs=(
            P(("dp", "seq", "tensor"), None),
            P(None, ("dp", "seq"), "tensor"),
            P("tensor", ("dp", "seq")),
            P(None, "tensor"),
            P(),
            P(),
            P(("dp", "seq"), None, "tensor"),
            P(("dp", "seq"), "tensor", None),
            P("dp", ("seq", "tensor")),
            P(("dp", "seq"), None),
            P(("dp", "seq", "tensor"), None),
        ),
        out_specs=(
            P(("dp", "seq", "tensor"), None),
            P(("dp", "seq", "tensor"), None),
            P(None, ("dp", "seq"), "tensor"),
            P("tensor", ("dp", "seq")),
            P(None, "tensor"),
            P(),
            P(),
            P(("dp", "seq"), None, "tensor"),
            P(("dp", "seq"), "tensor", None),
        ),
        check_vma=False,
    )
```

```python
import functools
import math

import jax
import jax.numpy as jnp
from jax import lax
from jax.experimental import pallas as pl
from jax.experimental.pallas import tpu as pltpu
from jax.sharding import PartitionSpec as P

EPSILON = 1e-06
EDGES = (1, 2, 3, 4, 5, 6, 7, 8, 12, 16, 23, 32, 46, 64, 91)
TILE = 256
HALF = TILE // 2
LOG2E = math.log2(math.e)
SCALE = 0.125
MASKED = -1e30
LOWEST = -1e29
EXTRA = 16
VMEM_BYTES = 60 * 1024 * 1024
GELU_A = math.sqrt(2.0 / math.pi)
GELU_B = 0.044715
BF16 = jnp.bfloat16
F32 = jnp.float32


def dot(left_side, right_side):
    return jnp.dot(left_side, right_side, preferred_element_type=F32)


def dot_rows(left_side, right_side):
    return lax.dot_general(
        left_side, right_side, (((1,), (1,)), ((), ())), preferred_element_type=F32
    )


def einsum(formula, *operands):
    return jnp.einsum(formula, *operands, preferred_element_type=F32)


def swap(values, axis, bit):
    count = lax.axis_size(axis)
    return lax.ppermute(values, axis, [(i, i ^ bit) for i in range(count)])


def bits_of(count):
    return [1 << i for i in range(count.bit_length() - 1)]


def gather_relative(values, axis):
    pieces = {0: values}
    for bit in reversed(bits_of(lax.axis_size(axis))):
        for place in list(pieces):
            pieces[place ^ bit] = swap(pieces[place], axis, bit)
    return [pieces[place] for place in range(len(pieces))]


def core_step(kept, sent):
    got = swap(sent, "tensor", 1)
    to_send = (kept[1].astype(F32) + got[1].astype(F32)).astype(BF16)
    return kept[0], got[0], to_send


def chip_step(near, got, far):
    return near.astype(F32) + got.astype(F32) + far.astype(F32)


def sum_tensor(kept, sent):
    near, got, to_send = core_step(kept, sent)
    return chip_step(near, got, swap(to_send, "tensor", 2))


def reorder(pieces, own_index):
    for bit in bits_of(len(pieces)):
        flip = (own_index & bit) != 0
        pieces = [
            jnp.where(flip, pieces[place ^ bit], pieces[place]) for place in range(len(pieces))
        ]
    return pieces


def sum_all(values, axes):
    for axis in axes:
        for bit in bits_of(lax.axis_size(axis)):
            values = values + swap(values, axis, bit)
    return values


def bucket_of(relative, half_count):
    magnitude = jnp.abs(relative)
    counted = jnp.zeros(relative.shape, jnp.int32)
    for edge_value in EDGES:
        counted = counted + (magnitude >= edge_value).astype(jnp.int32)
    return counted + jnp.where(relative > 0, half_count, 0).astype(jnp.int32)


KINDS = ((0, 0, 1, 0), (2, 1, 3, 2), (4, 3, 4, 4))


def near_tiles(table_ref, near_ref):
    heads = near_ref.shape[0]
    bucket_count = table_ref.shape[0] // heads
    half_count = bucket_count // 2
    offset = lax.broadcasted_iota(jnp.int32, (HALF, HALF), 0) - lax.broadcasted_iota(
        jnp.int32, (HALF, HALF), 1
    )
    near_of = (range(1, half_count), range(bucket_count), range(half_count + 1, bucket_count))
    for shift, buckets in enumerate(near_of):
        grid = bucket_of(offset + (shift - 1) * HALF, half_count)
        for h in range(heads):
            total = jnp.zeros((HALF, HALF), F32)
            for bucket_index in buckets:
                value = table_ref[bucket_index * heads + h] * LOG2E
                total = jnp.where(grid == bucket_index, value, total)
            near_ref[h, 1 + shift] = total
    for h in range(heads):
        for kind, bucket_index in ((0, half_count - 1), (4, bucket_count - 1)):
            value = table_ref[bucket_index * heads + h] * LOG2E
            near_ref[h, kind] = jnp.full((HALF, HALF), value, F32)


def fill_tiles(near_ref, bias_ref):
    for kind, blocks in enumerate(KINDS):
        for h in range(near_ref.shape[0]):
            for place, block in enumerate(blocks):
                row, column = place // 2 * HALF, place % 2 * HALF
                bias_ref[kind, h, row : row + HALF, column : column + HALF] = near_ref[h, block]


def span_of(meta_ref, query_tile, key_tiles):
    opening, closing = meta_ref[1], meta_ref[2]
    first = query_tile * TILE
    last = first + TILE - 1
    begin = jnp.where(first < opening, 0, jnp.where(first < closing, opening, closing))
    end = jnp.where(last < opening, opening, jnp.where(last < closing, closing, key_tiles * TILE))
    return begin // TILE, (end + TILE - 1) // TILE


def run_tiles(begin, end, tile, key_body, carry):
    first = jnp.clip(tile - 1, begin, end)
    last = jnp.clip(tile + 2, begin, end)
    carry = lax.fori_loop(begin, first, functools.partial(key_body, 0), carry)
    carry = lax.fori_loop(first, last, functools.partial(key_body, None), carry)
    return lax.fori_loop(last, end, functools.partial(key_body, 4), carry)


def bias_of(near_ref, bias_ref, far, kind, h):
    if far is None:
        return bias_ref[kind, h]
    return near_ref[h, far, 0:1, 0:1]


def document_row(meta_ref, tile):
    place = tile * TILE + lax.broadcasted_iota(jnp.int32, (EXTRA, TILE), 1)
    return (place >= meta_ref[1]).astype(jnp.int32) + (place >= meta_ref[2]).astype(jnp.int32)


def key_rows(meta_ref, tile):
    row = lax.broadcasted_iota(jnp.int32, (EXTRA, TILE), 0)
    differs = jnp.where(document_row(meta_ref, tile) != row, MASKED, 0.0)
    return jnp.where(row < 3, differs, jnp.where(row < 6, 1.0, 0.0)).astype(BF16)


def query_rows(meta_ref, tile, terms):
    row = lax.broadcasted_iota(jnp.int32, (EXTRA, TILE), 0)
    agrees = jnp.where(document_row(meta_ref, tile) == row, 1.0, 0.0)
    return jnp.where(row < 3, agrees, three_rows(row - 3, terms)).astype(BF16)


def three_rows(row, terms):
    result = jnp.zeros(row.shape, F32)
    for i, term in enumerate(terms):
        result = jnp.where(row == i, term, result)
    return result


def split_three(values):
    first = values.astype(BF16).astype(F32)
    second = (values - first).astype(BF16).astype(F32)
    return first, second, values - first - second


def attend_kernel(
    meta_ref,
    q_ref,
    kv_ref,
    near_ref,
    weight_ref,
    exact_ref,
    out_ref,
    log_ref,
    even_ref,
    odd_ref,
    key_ref,
    query_ref,
    sum_ref,
    bias_ref,
):
    key_tiles = kv_ref.shape[0]
    heads = near_ref.shape[0]
    fill_tiles(near_ref, bias_ref)
    size = q_ref.shape[1] // heads

    def turn(j, carry):
        kept = meta_ref[3 + j]
        extra = key_rows(meta_ref, j)
        for h in range(heads):
            rows = kv_ref[kept, h * size : (h + 1) * size, :]
            key_ref[kept, h] = jnp.concatenate([rows, extra], axis=0).T
        return carry

    lax.fori_loop(0, key_tiles, turn, 0)
    ones = jnp.ones((EXTRA, TILE), BF16)

    def query_body(i, carry):
        tile = meta_ref[3 + key_tiles + i]
        place = tile % meta_ref[0]
        begin, end = span_of(meta_ref, tile, key_tiles)
        extra = query_rows(meta_ref, tile, ())
        for h in range(heads):
            rows = q_ref[i, h * size : (h + 1) * size, :]
            query_ref[h] = jnp.concatenate([rows, extra], axis=0)
        sum_ref[...] = jnp.zeros_like(sum_ref)

        def key_body(far, j, peaks):
            kept = meta_ref[3 + j]
            kind = j - tile + 1
            scores = [
                dot(key_ref[kept, h], query_ref[h]) + bias_of(near_ref, bias_ref, far, kind, h)
                for h in range(heads)
            ]
            new_peaks = [
                jnp.maximum(peaks[h], jnp.max(scores[h], axis=0, keepdims=True))
                for h in range(heads)
            ]
            weights = [jnp.exp2(scores[h] - new_peaks[h]).astype(BF16) for h in range(heads)]
            added = []
            for h in range(heads):
                values = kv_ref[kept, (heads + h) * size : (heads + h + 1) * size, :]
                added.append(dot(jnp.concatenate([values, ones], axis=0), weights[h]))
            for h in range(heads):
                sum_ref[h] = sum_ref[h] * jnp.exp2(peaks[h] - new_peaks[h]) + added[h]
            return tuple(new_peaks)

        start = tuple(jnp.full((1, TILE), LOWEST, F32) for _ in range(heads))
        peaks = run_tiles(begin, end, tile, key_body, start)
        for h in range(heads):
            rows = slice(h * size, (h + 1) * size)
            total = sum_ref[h, size : size + 1, :]
            result = sum_ref[h, :size, :] * (1.0 / total)
            exact_ref[i, rows, :] = result
            out_ref[place, rows, :] = result.astype(BF16)
            log_ref[i, h] = peaks[h] + jnp.log2(total)
        attended = out_ref[place]
        for k in range(weight_ref.shape[0]):
            block = dot(weight_ref[k], attended).astype(BF16)
            (odd_ref if k & 1 else even_ref)[k // 2, place] = block
        return carry

    lax.fori_loop(0, q_ref.shape[0], query_body, 0)


def estimate(queries, key_tiles, products):
    pairs = queries.shape[0] * TILE * key_tiles * TILE
    return pl.CostEstimate(
        flops=2 * products * pairs * queries.shape[1],
        bytes_accessed=8 * pairs,
        transcendentals=3 * pairs,
    )


def whole_specs(arrays):
    return [pl.BlockSpec(array.shape, functools.partial(origin, len(array.shape))) for array in arrays]


def origin(dimensions, step):
    return (0,) * dimensions


def attend(meta, queries, keys_values, near, out_blocks):
    query_tiles, width, _ = queries.shape
    key_tiles = keys_values.shape[0]
    heads = near.shape[0]
    parts, share, _ = out_blocks.shape
    blocks = jax.ShapeDtypeStruct((parts // 2, query_tiles, share, TILE), BF16)
    shapes = (
        jax.ShapeDtypeStruct(queries.shape, F32),
        jax.ShapeDtypeStruct(queries.shape, BF16),
        jax.ShapeDtypeStruct((query_tiles, heads, 1, TILE), F32),
        blocks,
        blocks,
    )
    operands = (queries, keys_values, near, out_blocks)
    return pl.pallas_call(
        attend_kernel,
        grid=(1,),
        out_shape=shapes,
        in_specs=[pl.BlockSpec(memory_space=pltpu.SMEM)] + whole_specs(operands),
        out_specs=tuple(whole_specs(shapes)),
        scratch_shapes=[
            pltpu.VMEM((key_tiles, heads, TILE, width // heads + EXTRA), BF16),
            pltpu.VMEM((heads, width // heads + EXTRA, TILE), BF16),
            pltpu.VMEM((heads, width // heads + EXTRA, TILE), F32),
            pltpu.VMEM((len(KINDS), heads, TILE, TILE), F32),
        ],
        compiler_params=pltpu.CompilerParams(vmem_limit_bytes=VMEM_BYTES),
        cost_estimate=estimate(queries, key_tiles, 2),
        name="attend",
    )(meta, *operands)


def bucket_rows(tiles_ref, far_ref, rows_ref):
    heads, bucket_count = rows_ref.shape[:2]
    half_count = bucket_count // 2
    offset = lax.broadcasted_iota(jnp.int32, (HALF, HALF), 0) - lax.broadcasted_iota(
        jnp.int32, (HALF, HALF), 1
    )
    grids = [bucket_of(offset + shift * HALF, half_count) for shift in (-1, 0, 1)]
    first, last = slice(0, HALF), slice(HALF, TILE)

    def column_sums(values):
        return jnp.sum(values, axis=0, keepdims=True)

    def head_body(h, carry):
        before = tiles_ref[1, h, first, last] + tiles_ref[0, h, last, first]
        same = tiles_ref[1, h, first, first] + tiles_ref[1, h, last, last]
        after = tiles_ref[1, h, last, first] + tiles_ref[2, h, first, last]
        far_before = column_sums(far_ref[0, h, :, first] + far_ref[0, h, :, last])
        far_before += column_sums(tiles_ref[0, h, first, first] + tiles_ref[0, h, first, last])
        far_before += column_sums(tiles_ref[0, h, last, last])
        far_after = column_sums(far_ref[1, h, :, first] + far_ref[1, h, :, last])
        far_after += column_sums(tiles_ref[2, h, last, first] + tiles_ref[2, h, last, last])
        far_after += column_sums(tiles_ref[2, h, first, first])
        for bucket_index in range(bucket_count):
            row = column_sums(jnp.where(grids[1] == bucket_index, same, 0.0))
            if 0 < bucket_index < half_count:
                row += column_sums(jnp.where(grids[0] == bucket_index, before, 0.0))
            if bucket_index > half_count:
                row += column_sums(jnp.where(grids[2] == bucket_index, after, 0.0))
            if bucket_index == half_count - 1:
                row += far_before
            if bucket_index == bucket_count - 1:
                row += far_after
            rows_ref[h, bucket_index : bucket_index + 1, :] = row
        return carry

    lax.fori_loop(0, heads, head_body, 0)


def attend_back_kernel(
    meta_ref,
    q_ref,
    kv_ref,
    near_ref,
    weight_ref,
    exact_ref,
    log_ref,
    *refs,
):
    parts = weight_ref.shape[0]
    branch_refs = refs[:parts]
    (
        dq_ref,
        dkv_ref,
        rows_ref,
        tiles_ref,
        key_ref,
        value_ref,
        query_ref,
        grad_ref,
        dq_sum,
        dkv_sum,
        bias_ref,
        far_ref,
    ) = refs[parts:]
    key_tiles = kv_ref.shape[0]
    heads = near_ref.shape[0]
    fill_tiles(near_ref, bias_ref)
    size = q_ref.shape[1] // heads

    row = lax.broadcasted_iota(jnp.int32, (EXTRA, TILE), 0)
    ones = jnp.where(row < 3, 1.0, 0.0).astype(BF16)

    def turn(j, carry):
        kept = meta_ref[3 + j]
        extra = key_rows(meta_ref, j)
        for h in range(heads):
            rows = kv_ref[kept, h * size : (h + 1) * size, :]
            key_ref[kept, h] = jnp.concatenate([rows, extra], axis=0).T
            rows = kv_ref[kept, (heads + h) * size : (heads + h + 1) * size, :]
            value_ref[kept, h] = jnp.concatenate([rows, ones], axis=0).T
        return carry

    lax.fori_loop(0, key_tiles, turn, 0)
    dkv_sum[...] = jnp.zeros_like(dkv_sum)
    tiles_ref[...] = jnp.zeros_like(tiles_ref)
    far_ref[...] = jnp.zeros_like(far_ref)

    def query_body(i, carry):
        tile = meta_ref[3 + key_tiles + i]
        place = tile % meta_ref[0]
        begin, end = span_of(meta_ref, tile, key_tiles)
        dq_sum[...] = jnp.zeros_like(dq_sum)
        grad_sum = dot(weight_ref[0], branch_refs[0][place])
        for k in range(1, parts):
            grad_sum += dot(weight_ref[k], branch_refs[k][place])
        for h in range(heads):
            rows = slice(h * size, (h + 1) * size)
            grad = grad_sum[rows].astype(BF16)
            centre = jnp.sum(grad.astype(F32) * exact_ref[i, rows, :], axis=0, keepdims=True)
            extra = three_rows(row, split_three(-centre)).astype(BF16)
            grad_ref[h] = jnp.concatenate([grad, extra], axis=0)
            extra = query_rows(meta_ref, tile, split_three(-log_ref[i, h]))
            query_ref[h] = jnp.concatenate([q_ref[i, rows, :], extra], axis=0)

        def key_body(far, j, inner):
            kept = meta_ref[3 + j]
            kind = j - tile + 1
            probs = [
                jnp.exp2(
                    dot(key_ref[kept, h], query_ref[h])
                    + bias_of(near_ref, bias_ref, far, kind, h)
                )
                for h in range(heads)
            ]
            score_grads = [probs[h] * dot(value_ref[kept, h], grad_ref[h]) for h in range(heads)]
            low_probs = [prob.astype(BF16) for prob in probs]
            low_grads = [score_grad.astype(BF16) for score_grad in score_grads]
            key_adds, value_adds, query_adds = [], [], []
            for h in range(heads):
                rows = slice(h * size, (h + 1) * size)
                key_adds.append(dot_rows(q_ref[i, rows, :], low_grads[h]))
                value_adds.append(dot_rows(grad_ref[h, :size, :], low_probs[h]))
                query_adds.append(dot(kv_ref[kept, rows, :], low_grads[h]))
            for h in range(heads):
                rows = slice(h * size, (h + 1) * size)
                value_rows = slice((heads + h) * size, (heads + h + 1) * size)
                if far is None:
                    tiles_ref[kind, h] += score_grads[h]
                else:
                    far_ref[far // 4, h] += jnp.sum(
                        score_grads[h].reshape(TILE // 8, 8, TILE), axis=0
                    )
                dkv_sum[kept, rows, :] += key_adds[h]
                dkv_sum[kept, value_rows, :] += value_adds[h]
                dq_sum[rows, :] += query_adds[h]
            return inner

        run_tiles(begin, end, tile, key_body, 0)
        dq_ref[i] = (dq_sum[...] * SCALE).astype(BF16)
        return carry

    lax.fori_loop(0, q_ref.shape[0], query_body, 0)
    middle = heads * size
    dkv_ref[:, :middle, :] = (dkv_sum[:, :middle, :] * (1.0 / LOG2E)).astype(BF16)
    dkv_ref[:, middle:, :] = dkv_sum[:, middle:, :].astype(BF16)
    bucket_rows(tiles_ref, far_ref, rows_ref)


def attend_back(meta, queries, keys_values, near, out_blocks, exact, logs, branch, buckets):
    key_tiles = keys_values.shape[0]
    heads = near.shape[0]
    size = queries.shape[1] // heads
    shapes = (
        jax.ShapeDtypeStruct(queries.shape, BF16),
        jax.ShapeDtypeStruct(keys_values.shape, BF16),
        jax.ShapeDtypeStruct((heads, buckets, HALF), F32),
    )
    operands = (queries, keys_values, near, out_blocks, exact, logs, *branch)
    return pl.pallas_call(
        attend_back_kernel,
        grid=(1,),
        out_shape=shapes,
        in_specs=[pl.BlockSpec(memory_space=pltpu.SMEM)] + whole_specs(operands),
        out_specs=tuple(whole_specs(shapes)),
        scratch_shapes=[
            pltpu.VMEM((len(KINDS), heads, TILE, TILE), F32),
            pltpu.VMEM((key_tiles, heads, TILE, size + EXTRA), BF16),
            pltpu.VMEM((key_tiles, heads, TILE, size + EXTRA), BF16),
            pltpu.VMEM((heads, size + EXTRA, TILE), BF16),
            pltpu.VMEM((heads, size + EXTRA, TILE), BF16),
            pltpu.VMEM(queries.shape[1:], F32),
            pltpu.VMEM(keys_values.shape, F32),
            pltpu.VMEM((len(KINDS), heads, TILE, TILE), F32),
            pltpu.VMEM((2, heads, 8, TILE), F32),
        ],
        compiler_params=pltpu.CompilerParams(vmem_limit_bytes=VMEM_BYTES),
        cost_estimate=estimate(queries, key_tiles, 5),
        name="attend_back",
    )(meta, *operands)


def project_kernel(piece_count, weight_count, tiles, share, own_ref, table_ref, *refs):
    piece_refs = refs[:piece_count]
    weight_refs = refs[piece_count : piece_count + weight_count]
    gain_ref = refs[piece_count + weight_count]
    (
        meta_ref,
        q_ref,
        kv_ref,
        normed_ref,
        input_ref,
        in_ref,
        out_ref,
        out_t_ref,
        near_ref,
        block_ref,
        turned_ref,
    ) = refs[piece_count + weight_count + 1 :]
    grid_place, tensor_place, seq_place, own_first = (own_ref[i] for i in range(4))
    width = gain_ref.shape[0]
    head_cols = q_ref.shape[1]
    columns = turned_ref.shape[0]
    for k in range(weight_count):
        place = grid_place ^ k if weight_count > 1 else 0
        block_ref[place] = weight_refs[k][...]
    full = block_ref[...].reshape(width, columns)
    in_ref[...] = full[:, : 3 * head_cols]
    turned_ref[...] = full.T
    blocks_here = width // share
    tall = block_ref.shape[1]
    per = share // tall if weight_count > 1 else 1
    for k in range(blocks_here):
        if weight_count > 1:
            block = block_ref[pl.ds((tensor_place ^ k) * per, per), :, 3 * head_cols :]
            block = block.reshape(share, head_cols)
        else:
            start = pl.multiple_of((tensor_place ^ k) * share, share)
            block = block_ref[0, pl.ds(start, share), 3 * head_cols :]
        out_ref[k] = block
        out_t_ref[k] = block.T
    key_tiles = kv_ref.shape[0]
    near_tiles(table_ref, near_ref)
    early = jnp.zeros((1, TILE), F32)
    late = jnp.zeros((1, TILE), F32)
    gain = gain_ref[...]
    for k in range(piece_count):
        for s in range(piece_refs[0].shape[0]):
            kept = s + k
            rows = piece_refs[k][s, :width, :].astype(F32)
            ids = piece_refs[k][s, width : width + 16, :][:1].astype(F32)
            early += (ids < 0.5).astype(F32)
            late += (ids < 1.5).astype(F32)
            root = lax.rsqrt(jnp.sum(rows * rows, axis=0, keepdims=True) * (1.0 / width) + EPSILON)
            normed = (rows * root * gain).astype(BF16)
            normed_ref[kept] = normed
            kv_ref[kept] = dot(turned_ref[head_cols : 3 * head_cols, :], normed).astype(BF16)
    for i in range(tiles):
        normed = normed_ref[own_first + i]
        q_ref[i] = (dot(turned_ref[:head_cols, :], normed) * (SCALE * LOG2E)).astype(BF16)
        start = pl.multiple_of(tensor_place * share, share)
        if piece_count > 1:
            input_ref[tensor_place ^ i] = piece_refs[i][0, pl.ds(start, share), :]
        else:
            input_ref[i] = piece_refs[0][own_first + i, pl.ds(start, share), :]
    meta_ref[0] = tiles
    meta_ref[1] = jnp.sum(early).astype(jnp.int32)
    meta_ref[2] = jnp.sum(late).astype(jnp.int32)
    for j in range(key_tiles):
        if piece_count > 1:
            meta_ref[3 + j] = ((j // tiles) ^ seq_place) * tiles + ((j % tiles) ^ tensor_place)
        else:
            meta_ref[3 + j] = j
    for i in range(tiles):
        shift = tensor_place ^ i if piece_count > 1 else i
        meta_ref[3 + key_tiles + i] = seq_place * tiles + shift


def project(own, table, pieces, weight_pieces, gain, tiles, key_tiles, share, heads):
    width = gain.shape[0]
    columns = weight_pieces[0].shape[1]
    head_cols = columns // 4
    parts = width // share
    shapes = (
        jax.ShapeDtypeStruct((tiles, head_cols, TILE), BF16),
        jax.ShapeDtypeStruct((key_tiles, 2 * head_cols, TILE), BF16),
        jax.ShapeDtypeStruct((key_tiles, width, TILE), BF16),
        jax.ShapeDtypeStruct((tiles, share, TILE), BF16),
        jax.ShapeDtypeStruct((width, 3 * head_cols), BF16),
        jax.ShapeDtypeStruct((parts, share, head_cols), BF16),
        jax.ShapeDtypeStruct((parts, head_cols, share), BF16),
        jax.ShapeDtypeStruct((heads, 5, HALF, HALF), F32),
    )
    operands = (*pieces, *weight_pieces, gain)
    return pl.pallas_call(
        functools.partial(project_kernel, len(pieces), len(weight_pieces), tiles, share),
        grid=(1,),
        out_shape=(jax.ShapeDtypeStruct((3 + key_tiles + tiles,), jnp.int32),) + shapes,
        in_specs=[pl.BlockSpec(memory_space=pltpu.SMEM)] * 2 + whole_specs(operands),
        out_specs=(pl.BlockSpec(memory_space=pltpu.SMEM),) + tuple(whole_specs(shapes)),
        scratch_shapes=[
            pltpu.VMEM((len(weight_pieces),) + weight_pieces[0].shape, BF16),
            pltpu.VMEM((columns, width), BF16),
        ],
        compiler_params=pltpu.CompilerParams(vmem_limit_bytes=VMEM_BYTES),
        cost_estimate=pl.CostEstimate(
            flops=6 * key_tiles * TILE * width * head_cols,
            bytes_accessed=8 * key_tiles * TILE * width,
            transcendentals=0,
        ),
        name="project",
    )(own, table, *operands)


def project_back_kernel(fast, parts, own_ref, dq_ref, dkv_ref, normed_ref, in_ref, attended_ref, *refs):
    branch_refs = refs[:parts]
    if fast:
        far_even, far_odd, own_even, own_odd, weight_even, weight_odd, gain_ref, full_ref = refs[
            parts:
        ]
    else:
        part_ref, weight_ref, gain_ref, full_ref = refs[parts:]
    grid_place, tensor_place, seq_place, own_first = (own_ref[i] for i in range(4))
    tiles, head_cols, _ = dq_ref.shape
    key_tiles = dkv_ref.shape[0]
    width = in_ref.shape[0]
    share = width // parts
    key_weight = in_ref[:, head_cols:]
    query_weight = in_ref[:, :head_cols]
    if fast:
        for n in range(tiles):
            block = dot(key_weight, dkv_ref[tiles + n]).astype(BF16)
            (far_odd if n & 1 else far_even)[n // 2] = block
        for n in range(tiles):
            block = dot(key_weight, dkv_ref[n]) + dot(query_weight, dq_ref[n])
            (own_odd if n & 1 else own_even)[n // 2] = block.astype(BF16)
    else:
        for n in range(key_tiles):
            part_ref[n] = dot(key_weight, dkv_ref[n]).astype(BF16)
        for n in range(tiles):
            block = part_ref[own_first + n].astype(F32) + dot(query_weight, dq_ref[n])
            part_ref[own_first + n] = block.astype(BF16)
    query_sum = dot_rows(normed_ref[own_first], dq_ref[0])
    for n in range(1, tiles):
        query_sum += dot_rows(normed_ref[own_first + n], dq_ref[n])
    key_sum = dot_rows(normed_ref[0], dkv_ref[0])
    for n in range(1, key_tiles):
        key_sum += dot_rows(normed_ref[n], dkv_ref[n])
    gain_ref[...] = jnp.sum(
        query_sum * query_weight.astype(F32), axis=1, keepdims=True
    ) + jnp.sum(key_sum * key_weight.astype(F32), axis=1, keepdims=True)
    full_ref[:, :head_cols] = query_sum.astype(BF16)
    full_ref[:, head_cols : 3 * head_cols] = key_sum.astype(BF16)
    for k in range(parts):
        block = dot_rows(branch_refs[k][0], attended_ref[0])
        for n in range(1, tiles):
            block += dot_rows(branch_refs[k][n], attended_ref[n])
        start = pl.multiple_of((tensor_place ^ k) * share, share)
        full_ref[pl.ds(start, share), 3 * head_cols :] = block.astype(BF16)
    if fast:
        tall = weight_even.shape[1]
        for k in range(weight_even.shape[0]):
            place = grid_place ^ (2 * k)
            weight_even[k] = full_ref[pl.ds(pl.multiple_of(place * tall, tall), tall), :]
            weight_odd[k] = full_ref[pl.ds(pl.multiple_of((place ^ 1) * tall, tall), tall), :]
    else:
        weight_ref[...] = full_ref[...]


def project_back(fast, own, dq, dkv, normed, in_flat, attended, branch, grid_count):
    tiles, head_cols, _ = dq.shape
    key_tiles = dkv.shape[0]
    width = in_flat.shape[0]
    parts = len(branch)
    columns = 4 * head_cols
    if fast:
        block = jax.ShapeDtypeStruct((parts // 2, width, TILE), BF16)
        weight = jax.ShapeDtypeStruct((grid_count // 2, width // grid_count, columns), BF16)
        shapes = (block,) * 4 + (weight,) * 2
    else:
        shapes = (
            jax.ShapeDtypeStruct((key_tiles, width, TILE), BF16),
            jax.ShapeDtypeStruct((width, columns), BF16),
        )
    shapes = shapes + (jax.ShapeDtypeStruct((width, 1), F32),)
    operands = (dq, dkv, normed, in_flat, attended, *branch)
    return pl.pallas_call(
        functools.partial(project_back_kernel, fast, parts),
        grid=(1,),
        out_shape=shapes,
        in_specs=[pl.BlockSpec(memory_space=pltpu.SMEM)] + whole_specs(operands),
        out_specs=tuple(whole_specs(shapes)),
        scratch_shapes=[pltpu.VMEM((width, columns), BF16)],
        compiler_params=pltpu.CompilerParams(vmem_limit_bytes=VMEM_BYTES),
        cost_estimate=pl.CostEstimate(
            flops=12 * key_tiles * TILE * width * head_cols,
            bytes_accessed=8 * key_tiles * TILE * width,
            transcendentals=0,
        ),
        name="project_back",
    )(own, *operands)


def finish_kernel(input_ref, gain_ref, branch_ref, result_ref, *refs):
    sum_refs = refs[:-2]
    out_ref, grad_ref = refs[-2:]
    rows = input_ref[...]
    width = rows.shape[1]
    values = rows.T
    gain = gain_ref[...]
    grad = sum_refs[0][0].astype(F32)
    for ref in sum_refs[1:]:
        grad += ref[0].astype(F32)
    root = lax.rsqrt(jnp.sum(values * values, axis=0, keepdims=True) * (1.0 / width) + EPSILON)
    scaled = grad * gain
    centre = jnp.sum(scaled * values, axis=0, keepdims=True) * (1.0 / width)
    total = root * scaled - values * (root * root * root * centre)
    grad_ref[...] = (total + branch_ref[...].astype(F32)).T
    out_ref[...] = rows + result_ref[...].astype(F32).T


def finish(block_input, gain, branch, result, sums):
    shape = jax.ShapeDtypeStruct(block_input.shape, F32)
    operands = (block_input, gain, branch, result, *sums)
    first = pl.BlockSpec((1,) + sums[0].shape[1:], functools.partial(origin, 3))
    return pl.pallas_call(
        finish_kernel,
        grid=(1,),
        out_shape=(shape, shape),
        in_specs=whole_specs(operands[:4]) + [first] * len(sums),
        out_specs=tuple(whole_specs((shape, shape))),
        compiler_params=pltpu.CompilerParams(vmem_limit_bytes=VMEM_BYTES),
        name="finish",
    )(*operands)


def split_low(values):
    high = values.astype(BF16)
    return high, (values - high.astype(F32)).astype(BF16)


def load_tile(ref, first, count, *place):
    return jnp.concatenate([ref[(first + m, *place)] for m in range(count)], axis=-1)


def expert_kernel(parts, own_ref, *refs):
    state_refs = refs[:parts]
    (grad_ref, other_ref, in_ref, in_t_ref, out_ref, gain_ref) = refs[parts : parts + 6]
    (
        kept_ref,
        sent_ref,
        normed_ref,
        act_ref,
        pre_ref,
        gate_ref,
        router_sum,
        state_ref,
        full_ref,
        back_ref,
        joint_ref,
    ) = refs[parts + 6 :]

    @pl.when(pl.program_id(0) == 0)
    def _():
        router_sum[...] = jnp.zeros_like(router_sum)

    width = gain_ref.shape[0]
    share = width // parts
    hidden = act_ref.shape[1]
    experts = router_sum.shape[0]
    expert, own = own_ref[0], own_ref[1]
    chains, columns = state_ref.shape[0], state_ref.shape[-1]
    merged = kept_ref.shape[1] // chains
    slots = columns // merged
    gain = gain_ref[...]
    for a in range(chains):
        for k in range(parts):
            state_ref[a, own ^ k] = load_tile(state_refs[k], a * merged, merged)
            near = 2 * (k // 2) + ((own & 1) ^ (k & 1))
            full_ref[a, near] = load_tile(
                other_ref if k & 1 else grad_ref, a * merged, merged, k // 2
            )
    for a in range(chains):
        state = state_ref[a].reshape(width, columns).astype(F32)
        root = lax.rsqrt(jnp.sum(state * state, axis=0, keepdims=True) * (1.0 / width) + EPSILON)
        normed = (state * root * gain).astype(BF16)
        normed_ref[a] = normed
        both = dot(in_t_ref[...], normed)
        pre_act, logits = both[:hidden], both[hidden : hidden + experts]
        act_grad = dot(out_ref[...], full_ref[a].reshape(width, columns))
        raised = jnp.exp(logits - jnp.max(logits, axis=0, keepdims=True))
        router_probs = raised / jnp.sum(raised, axis=0, keepdims=True)
        chosen = lax.broadcasted_iota(jnp.int32, logits.shape, 0) == expert
        gate = jnp.sum(jnp.where(chosen, router_probs, 0.0), axis=0, keepdims=True)
        gate_ref[a] = gate
        square = pre_act * pre_act
        cdf = 0.5 + 0.5 * jnp.tanh(pre_act * (GELU_A + (GELU_A * GELU_B) * square))
        activated = pre_act * cdf
        act_ref[a] = activated.astype(BF16)
        rise = (2.0 * GELU_A) + (6.0 * GELU_A * GELU_B) * square
        pre_grad = act_grad * (cdf + activated * (1.0 - cdf) * rise)
        low_grad = pre_grad.astype(BF16)
        pre_ref[a] = low_grad
        gate_grad = jnp.sum(activated * act_grad, axis=0, keepdims=True)
        logit_grad = gate_grad * (chosen.astype(F32) - router_probs)
        centre = jnp.sum(pre_grad * pre_act, axis=0, keepdims=True)
        centre += jnp.sum(logit_grad * logits, axis=0, keepdims=True)
        joint_ref[a, :hidden, :] = low_grad
        joint_ref[a, hidden:, :] = jnp.concatenate(split_low(logit_grad), axis=0)
        high, low = split_low(logit_grad * gate)
        router_sum[...] += dot_rows(high, normed) + dot_rows(low, normed)
        normed_grad = dot(in_ref[...], joint_ref[a])
        state = state_ref[a].reshape(width, columns).astype(F32)
        back = (root * gate) * (normed_grad * gain - state * (root * centre * (1.0 / width)))
        back_ref[a] = back.astype(BF16).reshape(parts, share, columns)
        for k in range(parts):
            block = back_ref[a, own ^ k]
            target = sent_ref if k & 1 else kept_ref
            for m in range(merged):
                target[k // 2, a * merged + m] = block[:, m * slots : (m + 1) * slots]


def result_kernel(parts, own_ref, *refs):
    out_t_ref, kept_ref, sent_ref, result_ref = refs[-4:]
    chunks = (len(refs) - 4) // 2
    own = own_ref[1]
    width = out_t_ref.shape[0]
    share = width // parts
    merged = kept_ref.shape[1]
    for c in range(chunks):
        gate, activated = refs[2 * c + 1][0], refs[2 * c][0]
        slots = activated.shape[-1] // merged
        result = dot(out_t_ref[...], activated) * gate
        result_ref[c] = result.astype(BF16).reshape(parts, share, -1)
        for k in range(parts):
            block = result_ref[c, own ^ k]
            target = sent_ref if k & 1 else kept_ref
            for m in range(merged):
                target[k // 2, m, :, c * slots : (c + 1) * slots] = block[
                    :, m * slots : (m + 1) * slots
                ]


def grads_kernel(parts, merged, own_ref, *refs):
    grad_ref, other_ref, in_ref, in_sum, out_sum, gain_sum, full_ref = refs[-7:]
    chunks = (len(refs) - 7) // 4

    @pl.when(pl.program_id(0) == 0)
    def _():
        in_sum[...] = jnp.zeros_like(in_sum)
        out_sum[...] = jnp.zeros_like(out_sum)

    own = own_ref[1]
    width = in_ref.shape[0]
    normed, pre, activated, scaled = [], [], [], []
    for c in range(chunks):
        normed_ref, act_ref, pre_ref, gate_ref = refs[4 * c : 4 * c + 4]
        for t in range(gate_ref.shape[0]):
            gate = gate_ref[t]
            columns = gate.shape[-1]
            slots = columns // merged
            for k in range(parts):
                near = 2 * (k // 2) + ((own & 1) ^ (k & 1))
                source = other_ref if k & 1 else grad_ref
                pieces = [
                    source[t * merged + m, k // 2, :, c * slots : (c + 1) * slots]
                    for m in range(merged)
                ]
                full_ref[c, t, near] = jnp.concatenate(pieces, axis=-1)
            full = full_ref[c, t].reshape(width, columns).astype(F32)
            normed.append((normed_ref[t].astype(F32) * gate).astype(BF16))
            scaled.append((full * gate).astype(BF16))
            pre.append(pre_ref[t])
            activated.append(act_ref[t])
    in_sum[...] += dot_rows(jnp.concatenate(normed, axis=1), jnp.concatenate(pre, axis=1))
    out_sum[...] += dot_rows(jnp.concatenate(activated, axis=1), jnp.concatenate(scaled, axis=1))

    @pl.when(pl.program_id(0) == pl.num_programs(0) - 1)
    def _():
        gain_sum[...] = jnp.sum(in_sum[...] * in_ref[...].astype(F32), axis=1, keepdims=True)


def fixed_spec(shape):
    return pl.BlockSpec(shape, lambda g: (0,) * len(shape))


def run_expert(own, states, grads, chunk, merged, chains, weights):
    parts = len(states)
    count, share, slots = states[0].shape
    width = share * parts
    columns = merged * slots
    steps = count // merged
    hidden = weights[2].shape[0]
    joint = weights[0].shape[1]
    experts = (joint - hidden) // 2
    half = parts // 2
    taken = merged * chains
    piece = pl.BlockSpec((taken, share, slots), lambda g: (g, 0, 0))
    grad_piece = pl.BlockSpec((taken, half, share, slots), lambda g: (g, 0, 0, chunk))
    split = pl.BlockSpec((half, taken, share, slots), lambda g: (0, g, 0, 0))
    wide = pl.BlockSpec((chains, width, columns), lambda g: (g, 0, 0))
    deep = pl.BlockSpec((chains, hidden, columns), lambda g: (g, 0, 0))
    flat = pl.BlockSpec((chains, 1, columns), lambda g: (g, 0, 0))
    return pl.pallas_call(
        functools.partial(expert_kernel, parts),
        grid=(steps // chains,),
        out_shape=(
            jax.ShapeDtypeStruct((half, count, share, slots), BF16),
            jax.ShapeDtypeStruct((half, count, share, slots), BF16),
            jax.ShapeDtypeStruct((steps, width, columns), BF16),
            jax.ShapeDtypeStruct((steps, hidden, columns), BF16),
            jax.ShapeDtypeStruct((steps, hidden, columns), BF16),
            jax.ShapeDtypeStruct((steps, 1, columns), F32),
            jax.ShapeDtypeStruct((experts, width), F32),
        ),
        in_specs=[pl.BlockSpec(memory_space=pltpu.SMEM)]
        + [piece] * parts
        + [grad_piece] * 2
        + [fixed_spec(weight.shape) for weight in weights],
        out_specs=(split, split, wide, deep, deep, flat, fixed_spec((experts, width))),
        scratch_shapes=[
            pltpu.VMEM((chains, parts, share, columns), BF16),
            pltpu.VMEM((chains, parts, share, columns), BF16),
            pltpu.VMEM((chains, parts, share, columns), BF16),
            pltpu.VMEM((chains, joint, columns), BF16),
        ],
        compiler_params=pltpu.CompilerParams(vmem_limit_bytes=VMEM_BYTES),
        cost_estimate=pl.CostEstimate(
            flops=16 * steps * columns * width * hidden,
            bytes_accessed=16 * steps * columns * width,
            transcendentals=steps * columns * hidden,
        ),
        name="expert",
    )(own, *states, *grads, *weights)


def run_result(own, saved, parts, merged, out_t):
    chunks = len(saved)
    steps, hidden, columns = saved[0][0].shape
    width = out_t.shape[0]
    share, half, slots = width // parts, parts // 2, columns // merged
    deep = pl.BlockSpec((1, hidden, columns), lambda g: (g, 0, 0))
    flat = pl.BlockSpec((1, 1, columns), lambda g: (g, 0, 0))
    split = pl.BlockSpec((half, merged, share, slots * chunks), lambda g: (0, g, 0, 0))
    total = jax.ShapeDtypeStruct((half, steps * merged, share, slots * chunks), BF16)
    return pl.pallas_call(
        functools.partial(result_kernel, parts),
        grid=(steps,),
        out_shape=(total, total),
        in_specs=[pl.BlockSpec(memory_space=pltpu.SMEM)]
        + [deep, flat] * chunks
        + [fixed_spec(out_t.shape)],
        out_specs=(split, split),
        scratch_shapes=[pltpu.VMEM((chunks, parts, share, columns), BF16)],
        compiler_params=pltpu.CompilerParams(vmem_limit_bytes=VMEM_BYTES),
        cost_estimate=pl.CostEstimate(
            flops=6 * chunks * steps * columns * width * hidden,
            bytes_accessed=6 * chunks * steps * columns * width,
            transcendentals=0,
        ),
        name="result",
    )(own, *[array for arrays in saved for array in arrays], out_t)


def run_grads(own, saved, grads, merged, weight):
    chunks = len(saved)
    steps, width, columns = saved[0][0].shape
    hidden = saved[0][1].shape[1]
    _, half, share, _ = grads[0].shape
    parts = 2 * half
    taken = 2 if steps % 2 == 0 else 1
    wide = pl.BlockSpec((taken, width, columns), lambda g: (g, 0, 0))
    deep = pl.BlockSpec((taken, hidden, columns), lambda g: (g, 0, 0))
    flat = pl.BlockSpec((taken, 1, columns), lambda g: (g, 0, 0))
    grad_piece = pl.BlockSpec((taken * merged,) + grads[0].shape[1:], lambda g: (g, 0, 0, 0))
    return pl.pallas_call(
        functools.partial(grads_kernel, parts, merged),
        grid=(steps // taken,),
        out_shape=(
            jax.ShapeDtypeStruct((width, hidden), F32),
            jax.ShapeDtypeStruct((hidden, width), F32),
            jax.ShapeDtypeStruct((width, 1), F32),
        ),
        in_specs=[pl.BlockSpec(memory_space=pltpu.SMEM)]
        + [wide, deep, deep, flat] * chunks
        + [grad_piece] * 2
        + [fixed_spec(weight.shape)],
        out_specs=(
            fixed_spec((width, hidden)),
            fixed_spec((hidden, width)),
            fixed_spec((width, 1)),
        ),
        scratch_shapes=[pltpu.VMEM((chunks, taken, parts, share, columns), BF16)],
        compiler_params=pltpu.CompilerParams(vmem_limit_bytes=VMEM_BYTES),
        cost_estimate=pl.CostEstimate(
            flops=8 * chunks * steps * columns * width * hidden,
            bytes_accessed=8 * chunks * steps * columns * width,
            transcendentals=0,
        ),
        name="grads",
    )(own, *[array for arrays in saved for array in arrays], *grads, weight)


def shards(
    block_input,
    attn_in_weight,
    attn_out_weight,
    position_bias,
    norm_gains,
    router_weight,
    expert_in,
    expert_out,
    segment_ids,
    expert_ids,
    out_grad,
):
    tensor_count, seq_count = lax.axis_size("tensor"), lax.axis_size("seq")
    tensor_place, seq_place = lax.axis_index("tensor"), lax.axis_index("seq")
    grid_count = lax.axis_size("dp") * seq_count
    grid_place = lax.axis_index("dp") * seq_count + seq_place
    local_count, width = block_input.shape
    group_count = local_count * tensor_count
    share = width // tensor_count
    bucket_count, heads = position_bias.shape
    head_cols = attn_in_weight.shape[2]
    experts = router_weight.shape[1]
    capacity = max(2, 2 * group_count // experts)
    tiles = group_count // TILE
    key_tiles = tiles * seq_count
    fast = seq_count == 2 and local_count == TILE and grid_count == 8

    def tiled(pieces):
        pieces = reorder(pieces, tensor_place)
        if local_count == TILE:
            return jnp.stack(pieces)
        return jnp.concatenate(pieces, axis=-1)[None]

    half = tensor_count // 2
    core = tensor_place & 1
    own_rows = jnp.concatenate(
        [
            jnp.transpose(block_input.astype(BF16)),
            jnp.pad(segment_ids.astype(BF16), ((0, 15), (0, 0))),
        ]
    )
    weight_piece = jnp.concatenate(
        [attn_in_weight[0], attn_in_weight[1], attn_in_weight[2], jnp.transpose(attn_out_weight)],
        axis=1,
    )
    grad_rows = jnp.transpose(out_grad.astype(BF16)).reshape(half, 2, share, local_count)
    grad_mine = lax.dynamic_index_in_dim(grad_rows, core, 1, keepdims=False)
    grad_theirs = lax.dynamic_index_in_dim(grad_rows, core ^ 1, 1, keepdims=False)
    in_plain, out_plain = expert_in[0], expert_out[0]
    if fast:
        far_rows = swap(own_rows, "seq", 1)
        near_two = swap(own_rows, "tensor", 2)
        columns = [weight_piece] + [swap(weight_piece, "dp", k) for k in range(1, grid_count // 2)]
        grad_other = swap(grad_theirs, "tensor", 1)
        far_rows, near_two, columns, grad_other, expert_ids, in_plain, out_plain = (
            lax.optimization_barrier(
                (
                    far_rows,
                    near_two,
                    columns,
                    grad_other,
                    expert_ids,
                    in_plain,
                    out_plain,
                )
            )
        )
        far_two = swap(far_rows, "tensor", 2)
        near_columns = swap(weight_piece, "seq", 1)
        far_columns = swap(jnp.stack(columns[1:]), "seq", 1)
        near_one, near_three = swap(own_rows, "tensor", 1), swap(near_two, "tensor", 1)
    else:
        grad_other = swap(grad_theirs, "tensor", 1)
        both_rows = lax.all_gather(own_rows, "seq", axis=0, tiled=False)
        row_pieces = gather_relative(both_rows, "tensor")
        own_first = seq_place * tiles
        row_pieces = jnp.concatenate(reorder(row_pieces, tensor_place), axis=-1)
        row_pieces = row_pieces.reshape(seq_count, -1, tiles, TILE)
        row_pieces = [jnp.moveaxis(row_pieces, 2, 1).reshape(key_tiles, -1, TILE)]
        weight_pieces = [lax.all_gather(weight_piece, ("dp", "seq"), axis=0, tiled=True)]

    in_t, out_t = jnp.transpose(in_plain), jnp.transpose(out_plain)
    router_t = jnp.transpose(router_weight)
    in_joint = jnp.concatenate([in_plain, router_weight, router_weight], axis=1)
    in_t = jnp.concatenate([in_t, router_t, router_t])
    route_all = expert_ids[:, 0]
    expert_range = jnp.arange(experts, dtype=jnp.int32)
    route_hot = (route_all[:, None] == expert_range[None, :]).astype(jnp.int32)
    slot_rank = jnp.sum(jnp.cumsum(route_hot, axis=0) * route_hot, axis=-1) - 1
    target = (route_all * capacity + slot_rank).reshape(1, tiles, TILE, 1)
    places = jnp.arange(experts * capacity, dtype=jnp.int32).reshape(experts, 1, 1, capacity)
    chunks = 2 if capacity >= TILE else 1
    slots = capacity // chunks
    spread = max(1, TILE // capacity)
    merged = max(1, TILE // (slots * spread))

    def exchange(values):
        return lax.all_to_all(values, ("dp", "seq"), split_axis=0, concat_axis=0, tiled=True)

    def joined(values):
        if spread == 1:
            return values
        shape = values.shape
        values = values.reshape((-1, spread) + shape[1:])
        return jnp.moveaxis(values, 1, -2).reshape(
            (shape[0] // spread,) + shape[1:-1] + (spread * shape[-1],)
        )

    def parted(values):
        if spread == 1:
            return values
        shape = values.shape
        values = values.reshape(shape[:-1] + (spread, shape[-1] // spread))
        return jnp.moveaxis(values, -2, 1).reshape((-1,) + shape[1:-1] + (shape[-1] // spread,))


    gain_one = norm_gains[0][:, None]
    gain_two = norm_gains[1][:, None]
    if fast:
        (
            far_two,
            far_columns,
            gain_one,
            in_t,
            in_joint,
            out_t,
            target,
            gain_two,
            grad_mine,
            grad_other,
        ) = lax.optimization_barrier(
            (
                far_two,
                far_columns,
                gain_one,
                in_t,
                in_joint,
                out_t,
                target,
                gain_two,
                grad_mine,
                grad_other,
            )
        )
        far_one, far_three = swap(far_rows, "tensor", 1), swap(far_two, "tensor", 1)
        row_pieces = [own_rows, near_one, near_two, near_three]
        row_pieces += [far_rows, far_one, far_two, far_three]
        row_pieces = [rows[None] for rows in row_pieces]
        weight_pieces = [weight_piece, near_columns]
        for k in range(1, grid_count // 2):
            weight_pieces += [columns[k], far_columns[k - 1]]
        own_first = jnp.int32(0)
    own = jnp.stack([grid_place, tensor_place, seq_place, own_first]).astype(jnp.int32)
    onehot = (target == places).astype(BF16)
    grad_pair = swap(jnp.stack([grad_mine, grad_other]), "tensor", 2)
    (
        meta,
        queries,
        keys_values,
        normed_tiles,
        input_share,
        in_flat,
        out_blocks,
        out_t_blocks,
        near,
    ) = project(
        own,
        position_bias.reshape(-1),
        row_pieces,
        weight_pieces,
        gain_one,
        tiles,
        key_tiles,
        share,
        heads,
    )
    queries, grad_pair = lax.optimization_barrier((queries, grad_pair))
    grad_here = tiled([grad_mine, grad_other, grad_pair[0], grad_pair[1]])
    grad_buffer = einsum("nkdq,enqs->ekds", grad_here, onehot).astype(BF16)
    queries, grad_buffer = lax.optimization_barrier((queries, grad_buffer))
    grad_arrived = joined(exchange(grad_buffer))
    exact, attended, logs, attn_even, attn_odd = attend(
        meta, queries, keys_values, near, out_blocks
    )
    attn_share = sum_tensor(attn_even, attn_odd)
    state_share = (input_share.astype(F32) + attn_share).astype(BF16)
    state_share, grad_arrived = lax.optimization_barrier((state_share, grad_arrived))
    grad_near = swap(grad_arrived, "tensor", 1)

    weights = (in_joint, in_t, expert_out[0], gain_two)
    grads = (grad_arrived, grad_near)
    buffers = [
        einsum("ndq,enqs->eds", state_share, onehot[..., c * slots : (c + 1) * slots]).astype(BF16)
        for c in range(chunks)
    ]
    buffers = list(lax.optimization_barrier(tuple(buffers)))
    arrivals = [joined(exchange(buffer)) for buffer in buffers]
    chains = 2 if arrivals[0].shape[0] // merged % 2 == 0 else 1
    gathered = []
    for arrival in arrivals:
        gathered.append(
            [arrival, swap(arrival, "tensor", 1), swap(arrival, "tensor", 2)]
        )
    gathered[0][0], gathered[-1][0] = lax.optimization_barrier((gathered[0][0], gathered[-1][0]))
    saved, halves, crossed = [], [], []
    small = jnp.zeros((experts, width), F32)
    for c in range(chunks):
        gathered[c].append(swap(gathered[c][2], "tensor", 1))
        kept, sent, normed_two, activated, pre_grad, gate, router_sum = run_expert(
            own, gathered[c], grads, c, merged, chains, weights
        )
        saved.append((normed_two, activated, pre_grad, gate))
        if c + 1 < chunks:
            sent, gathered[c + 1][2] = lax.optimization_barrier((sent, gathered[c + 1][2]))
        if c > 0:
            sent, crossed[c - 1] = lax.optimization_barrier((sent, crossed[c - 1]))
        stayed, got, to_send = core_step(kept, sent)
        if c + 1 == chunks:
            own_late, to_send = lax.optimization_barrier((own, to_send))
        halves.append((stayed, got))
        crossed.append(swap(to_send, "tensor", 2))
        small = small + router_sum
    returned = [
        exchange(parted(chip_step(*halves[c], crossed[c]).astype(BF16)))
        for c in range(chunks - 1)
    ]
    result_even, result_odd = run_result(
        own_late, [(arrays[1], arrays[3]) for arrays in saved], tensor_count, merged, out_t
    )
    tied = lax.optimization_barrier((result_odd, crossed[-1], *returned))
    result_odd, crossed[-1], returned = tied[0], tied[1], list(tied[2:])
    returned.append(exchange(parted(chip_step(*halves[-1], crossed[-1]).astype(BF16))))
    result_near, result_got, result_sent = core_step(result_even, result_odd)
    result_far = swap(result_sent, "tensor", 2)
    own_late, result_sent = lax.optimization_barrier((own, result_sent))
    grad_expert_in, grad_expert_out, in_gain = run_grads(
        own_late, saved, grads, merged, expert_in[0]
    )
    in_gain, returned[-1] = lax.optimization_barrier((in_gain, returned[-1]))
    gain_part = in_gain[:, 0] + jnp.sum(small * router_t.astype(F32), axis=0)
    router_gains = jnp.concatenate([small, (gain_part / norm_gains[1])[None]])
    state_grad = lax.dynamic_index_in_dim(grad_here, tensor_place // 2, 1, keepdims=False)
    state_grad = state_grad.astype(F32)
    for c in range(chunks):
        state_grad = state_grad + einsum(
            "eds,enqs->ndq", returned[c], onehot[..., c * slots : (c + 1) * slots]
        )
    state_grad = state_grad.astype(BF16)

    branch = [state_grad, swap(state_grad, "tensor", 1), swap(state_grad, "tensor", 2)]
    result_total = chip_step(result_near, result_got, result_far).astype(BF16)
    result_total, branch[2] = lax.optimization_barrier((result_total, branch[2]))
    branch.append(swap(branch[2], "tensor", 1))
    result_back = exchange(parted(result_total))
    dq, dkv, bias_rows = attend_back(
        meta, queries, keys_values, near, out_t_blocks, exact, logs, branch, bucket_count
    )
    dq, dkv, bias_rows, result_back = lax.optimization_barrier((dq, dkv, bias_rows, result_back))

    def joined_small():
        bias_padded = lax.dynamic_update_slice_in_dim(
            jnp.zeros((heads * tensor_count, bucket_count), F32),
            jnp.sum(bias_rows, axis=2),
            tensor_place * heads,
            0,
        )
        return jnp.concatenate(
            [router_gains.reshape(-1), gain_part[:, 0] / norm_gains[0], bias_padded.reshape(-1)]
        )

    def result_rows_of():
        shares = attn_share + einsum("eds,enqs->ndq", result_back, onehot)
        return jnp.moveaxis(shares.astype(BF16), 0, 1).reshape(share, tensor_count, local_count)

    if fast:
        far_even, far_odd, own_even, own_odd, weight_even, weight_odd, gain_part = project_back(
            True, own, dq, dkv, normed_tiles, in_flat, attended, branch, grid_count
        )
        far_near, far_got, far_send = core_step(far_even, far_odd)
        own_got = swap(own_odd, "tensor", 1)
        own_send = (own_even[1].astype(F32) + own_got[1].astype(F32)).astype(BF16)
        weight_sent = swap(weight_odd, "seq", 1)
        far_send, own_send, gain_part, result_back = lax.optimization_barrier(
            (far_send, own_send, gain_part, result_back)
        )
        far_sent = swap(far_send, "tensor", 2)
        result_share = result_rows_of()
        own_send, result_share = lax.optimization_barrier((own_send, result_share))
        own_sent = swap(own_send, "tensor", 2)
        far_sent, result_share, gain_part, bias_rows = lax.optimization_barrier(
            (far_sent, result_share, gain_part, bias_rows)
        )
        small = sum_all(joined_small(), ("dp",))
        far_sent, weight_sent, branch = lax.optimization_barrier((far_sent, weight_sent, branch))
        far_sum = chip_step(far_near, far_got, far_sent).astype(BF16)
        far_back = swap(far_sum, "seq", 1)
        small, far_back = lax.optimization_barrier((small, far_back))
        sums = [own_even, own_got, own_sent[None], far_back[None]]
        weight_half = weight_even.astype(F32) + weight_sent.astype(F32)
        weight_grad = weight_half[0]
        for k in range(1, grid_count // 2):
            weight_grad = weight_grad + swap(weight_half[k].astype(BF16), "dp", k).astype(F32)
    else:
        row_part, weight_part, gain_part = project_back(
            False, own, dq, dkv, normed_tiles, in_flat, attended, branch, grid_count
        )
        row_part = lax.psum_scatter(row_part, "seq", scatter_dimension=0, tiled=True)
        row_part = jnp.moveaxis(row_part, 0, 1).reshape(width, tensor_count, local_count)
        blocks = [
            lax.dynamic_index_in_dim(row_part, tensor_place ^ k, 1, keepdims=False)
            for k in range(tensor_count)
        ]
        sums = [sum_tensor(jnp.stack(blocks[0::2]), jnp.stack(blocks[1::2]))[None]]
        small = sum_all(joined_small(), ("dp",))
        result_share = result_rows_of()
        weight_grad = lax.psum_scatter(
            weight_part, ("dp", "seq"), scatter_dimension=0, tiled=True
        ).astype(F32)
    grad_attn_in = jnp.stack(
        [weight_grad[:, c * head_cols : (c + 1) * head_cols] for c in range(3)]
    )
    grad_attn_out = jnp.transpose(weight_grad[:, 3 * head_cols :])

    small = sum_all(small, ("seq", "tensor"))
    first, second = experts * width, (experts + 1) * width
    grad_router = jnp.transpose(small[:first].reshape(experts, width))
    grad_gains = jnp.stack([small[second : second + width], small[first:second]])
    bias_sum = small[second + width :].reshape(heads * tensor_count, bucket_count)
    grad_bias = jnp.transpose(lax.dynamic_slice_in_dim(bias_sum, tensor_place * heads, heads, 0))

    result_rows = lax.all_to_all(
        jnp.moveaxis(result_share, 1, 0), "tensor", split_axis=0, concat_axis=0, tiled=True
    ).reshape(width, local_count)
    if local_count == TILE:
        own_branch = [
            lax.dynamic_index_in_dim(piece, tensor_place, 0, keepdims=False) for piece in branch
        ]
    else:
        own_branch = [
            lax.dynamic_slice_in_dim(piece[0], tensor_place * local_count, local_count, 1)
            for piece in branch
        ]
    own_branch = jnp.concatenate(reorder(own_branch, tensor_place))
    block_out, input_grad = finish(block_input, gain_one, own_branch, result_rows, sums)
    return (
        block_out,
        input_grad,
        grad_attn_in,
        grad_attn_out,
        grad_bias,
        grad_gains,
        grad_router,
        grad_expert_in[None],
        grad_expert_out[None],
    )


def solution(mesh):
    return jax.shard_map(
        shards,
        mesh=mesh,
        in_specs=(
            P(("dp", "seq", "tensor"), None),
            P(None, ("dp", "seq"), "tensor"),
            P("tensor", ("dp", "seq")),
            P(None, "tensor"),
            P(),
            P(),
            P(("dp", "seq"), None, "tensor"),
            P(("dp", "seq"), "tensor", None),
            P("dp", ("seq", "tensor")),
            P(("dp", "seq"), None),
            P(("dp", "seq", "tensor"), None),
        ),
        out_specs=(
            P(("dp", "seq", "tensor"), None),
            P(("dp", "seq", "tensor"), None),
            P(None, ("dp", "seq"), "tensor"),
            P("tensor", ("dp", "seq")),
            P(None, "tensor"),
            P(),
            P(),
            P(("dp", "seq"), None, "tensor"),
            P(("dp", "seq"), "tensor", None),
        ),
        check_vma=False,
    )
```

```python
import functools
import math

import jax
import jax.numpy as jnp
from jax import lax
from jax.experimental import pallas as pl
from jax.experimental.pallas import tpu as pltpu
from jax.sharding import PartitionSpec as P

EPSILON = 1e-06
EDGES = (1, 2, 3, 4, 5, 6, 7, 8, 12, 16, 23, 32, 46, 64, 91)
TILE = 256
HALF = TILE // 2
LOG2E = math.log2(math.e)
SCALE = 0.125
MASKED = -1e30
LOWEST = -1e29
EXTRA = 16
VMEM_BYTES = 60 * 1024 * 1024
GELU_A = math.sqrt(2.0 / math.pi)
GELU_B = 0.044715
BF16 = jnp.bfloat16
F32 = jnp.float32


def dot(left_side, right_side):
    return jnp.dot(left_side, right_side, preferred_element_type=F32)


def dot_rows(left_side, right_side):
    return lax.dot_general(
        left_side, right_side, (((1,), (1,)), ((), ())), preferred_element_type=F32
    )


def einsum(formula, *operands):
    return jnp.einsum(formula, *operands, preferred_element_type=F32)


def swap(values, axis, bit):
    count = lax.axis_size(axis)
    return lax.ppermute(values, axis, [(i, i ^ bit) for i in range(count)])


def bits_of(count):
    return [1 << i for i in range(count.bit_length() - 1)]


def gather_relative(values, axis):
    pieces = {0: values}
    for bit in reversed(bits_of(lax.axis_size(axis))):
        for place in list(pieces):
            pieces[place ^ bit] = swap(pieces[place], axis, bit)
    return [pieces[place] for place in range(len(pieces))]


def core_step(kept, sent):
    got = swap(sent, "tensor", 1)
    to_send = (kept[1].astype(F32) + got[1].astype(F32)).astype(BF16)
    return kept[0], got[0], to_send


def chip_step(near, got, far):
    return near.astype(F32) + got.astype(F32) + far.astype(F32)


def sum_tensor(kept, sent):
    near, got, to_send = core_step(kept, sent)
    return chip_step(near, got, swap(to_send, "tensor", 2))


def reorder(pieces, own_index):
    for bit in bits_of(len(pieces)):
        flip = (own_index & bit) != 0
        pieces = [
            jnp.where(flip, pieces[place ^ bit], pieces[place]) for place in range(len(pieces))
        ]
    return pieces


def sum_all(values, axes):
    for axis in axes:
        for bit in bits_of(lax.axis_size(axis)):
            values = values + swap(values, axis, bit)
    return values


def bucket_of(relative, half_count):
    magnitude = jnp.abs(relative)
    counted = jnp.zeros(relative.shape, jnp.int32)
    for edge_value in EDGES:
        counted = counted + (magnitude >= edge_value).astype(jnp.int32)
    return counted + jnp.where(relative > 0, half_count, 0).astype(jnp.int32)


KINDS = ((0, 0, 0, 0), (0, 0, 1, 0), (2, 1, 3, 2), (4, 3, 4, 4), (4, 4, 4, 4))


def near_tiles(table_ref, near_ref):
    heads = near_ref.shape[0]
    bucket_count = table_ref.shape[0] // heads
    half_count = bucket_count // 2
    offset = lax.broadcasted_iota(jnp.int32, (HALF, HALF), 0) - lax.broadcasted_iota(
        jnp.int32, (HALF, HALF), 1
    )
    near_of = (range(1, half_count), range(bucket_count), range(half_count + 1, bucket_count))
    for shift, buckets in enumerate(near_of):
        grid = bucket_of(offset + (shift - 1) * HALF, half_count)
        for h in range(heads):
            total = jnp.zeros((HALF, HALF), F32)
            for bucket_index in buckets:
                value = table_ref[bucket_index * heads + h] * LOG2E
                total = jnp.where(grid == bucket_index, value, total)
            near_ref[h, 1 + shift] = total
    for h in range(heads):
        for kind, bucket_index in ((0, half_count - 1), (4, bucket_count - 1)):
            value = table_ref[bucket_index * heads + h] * LOG2E
            near_ref[h, kind] = jnp.full((HALF, HALF), value, F32)


def fill_tiles(near_ref, bias_ref):
    for kind, blocks in enumerate(KINDS):
        for h in range(near_ref.shape[0]):
            for place, block in enumerate(blocks):
                row, column = place // 2 * HALF, place % 2 * HALF
                bias_ref[kind, h, row : row + HALF, column : column + HALF] = near_ref[h, block]


def span_of(meta_ref, query_tile, key_tiles):
    opening, closing = meta_ref[1], meta_ref[2]
    first = query_tile * TILE
    last = first + TILE - 1
    begin = jnp.where(first < opening, 0, jnp.where(first < closing, opening, closing))
    end = jnp.where(last < opening, opening, jnp.where(last < closing, closing, key_tiles * TILE))
    return begin // TILE, (end + TILE - 1) // TILE


def document_row(meta_ref, tile):
    place = tile * TILE + lax.broadcasted_iota(jnp.int32, (EXTRA, TILE), 1)
    return (place >= meta_ref[1]).astype(jnp.int32) + (place >= meta_ref[2]).astype(jnp.int32)


def key_rows(meta_ref, tile):
    row = lax.broadcasted_iota(jnp.int32, (EXTRA, TILE), 0)
    differs = jnp.where(document_row(meta_ref, tile) != row, MASKED, 0.0)
    return jnp.where(row < 3, differs, jnp.where(row < 6, 1.0, 0.0)).astype(BF16)


def query_rows(meta_ref, tile, terms):
    row = lax.broadcasted_iota(jnp.int32, (EXTRA, TILE), 0)
    agrees = jnp.where(document_row(meta_ref, tile) == row, 1.0, 0.0)
    return jnp.where(row < 3, agrees, three_rows(row - 3, terms)).astype(BF16)


def three_rows(row, terms):
    result = jnp.zeros(row.shape, F32)
    for i, term in enumerate(terms):
        result = jnp.where(row == i, term, result)
    return result


def split_three(values):
    first = values.astype(BF16).astype(F32)
    second = (values - first).astype(BF16).astype(F32)
    return first, second, values - first - second


def attend_kernel(
    meta_ref,
    q_ref,
    kv_ref,
    near_ref,
    weight_ref,
    exact_ref,
    out_ref,
    log_ref,
    even_ref,
    odd_ref,
    key_ref,
    query_ref,
    sum_ref,
    bias_ref,
):
    key_tiles = kv_ref.shape[0]
    heads = near_ref.shape[0]
    fill_tiles(near_ref, bias_ref)
    size = q_ref.shape[1] // heads

    def turn(j, carry):
        kept = meta_ref[3 + j]
        extra = key_rows(meta_ref, j)
        for h in range(heads):
            rows = kv_ref[kept, h * size : (h + 1) * size, :]
            key_ref[kept, h] = jnp.concatenate([rows, extra], axis=0).T
        return carry

    lax.fori_loop(0, key_tiles, turn, 0)
    ones = jnp.ones((EXTRA, TILE), BF16)

    def query_body(i, carry):
        tile = meta_ref[3 + key_tiles + i]
        place = tile % meta_ref[0]
        begin, end = span_of(meta_ref, tile, key_tiles)
        extra = query_rows(meta_ref, tile, ())
        for h in range(heads):
            rows = q_ref[i, h * size : (h + 1) * size, :]
            query_ref[h] = jnp.concatenate([rows, extra], axis=0)
        sum_ref[...] = jnp.zeros_like(sum_ref)

        def key_body(j, peaks):
            kept = meta_ref[3 + j]
            kind = jnp.clip(j - tile, -2, 2) + 2
            scores = [
                dot(key_ref[kept, h], query_ref[h]) + bias_ref[kind, h] for h in range(heads)
            ]
            new_peaks = [
                jnp.maximum(peaks[h], jnp.max(scores[h], axis=0, keepdims=True))
                for h in range(heads)
            ]
            weights = [jnp.exp2(scores[h] - new_peaks[h]).astype(BF16) for h in range(heads)]
            added = []
            for h in range(heads):
                values = kv_ref[kept, (heads + h) * size : (heads + h + 1) * size, :]
                added.append(dot(jnp.concatenate([values, ones], axis=0), weights[h]))
            for h in range(heads):
                sum_ref[h] = sum_ref[h] * jnp.exp2(peaks[h] - new_peaks[h]) + added[h]
            return tuple(new_peaks)

        start = tuple(jnp.full((1, TILE), LOWEST, F32) for _ in range(heads))
        peaks = lax.fori_loop(begin, end, key_body, start)
        for h in range(heads):
            rows = slice(h * size, (h + 1) * size)
            total = sum_ref[h, size : size + 1, :]
            result = sum_ref[h, :size, :] * (1.0 / total)
            exact_ref[i, rows, :] = result
            out_ref[place, rows, :] = result.astype(BF16)
            log_ref[i, h] = peaks[h] + jnp.log2(total)
        attended = out_ref[place]
        for k in range(weight_ref.shape[0]):
            block = dot(weight_ref[k], attended).astype(BF16)
            (odd_ref if k & 1 else even_ref)[k // 2, place] = block
        return carry

    lax.fori_loop(0, q_ref.shape[0], query_body, 0)


def estimate(queries, key_tiles, products):
    pairs = queries.shape[0] * TILE * key_tiles * TILE
    return pl.CostEstimate(
        flops=2 * products * pairs * queries.shape[1],
        bytes_accessed=8 * pairs,
        transcendentals=3 * pairs,
    )


def whole_specs(arrays):
    return [pl.BlockSpec(array.shape, functools.partial(origin, len(array.shape))) for array in arrays]


def origin(dimensions, step):
    return (0,) * dimensions


def attend(meta, queries, keys_values, near, out_blocks):
    query_tiles, width, _ = queries.shape
    key_tiles = keys_values.shape[0]
    heads = near.shape[0]
    parts, share, _ = out_blocks.shape
    blocks = jax.ShapeDtypeStruct((parts // 2, query_tiles, share, TILE), BF16)
    shapes = (
        jax.ShapeDtypeStruct(queries.shape, F32),
        jax.ShapeDtypeStruct(queries.shape, BF16),
        jax.ShapeDtypeStruct((query_tiles, heads, 1, TILE), F32),
        blocks,
        blocks,
    )
    operands = (queries, keys_values, near, out_blocks)
    return pl.pallas_call(
        attend_kernel,
        grid=(1,),
        out_shape=shapes,
        in_specs=[pl.BlockSpec(memory_space=pltpu.SMEM)] + whole_specs(operands),
        out_specs=tuple(whole_specs(shapes)),
        scratch_shapes=[
            pltpu.VMEM((key_tiles, heads, TILE, width // heads + EXTRA), BF16),
            pltpu.VMEM((heads, width // heads + EXTRA, TILE), BF16),
            pltpu.VMEM((heads, width // heads + EXTRA, TILE), F32),
            pltpu.VMEM((len(KINDS), heads, TILE, TILE), F32),
        ],
        compiler_params=pltpu.CompilerParams(vmem_limit_bytes=VMEM_BYTES),
        cost_estimate=estimate(queries, key_tiles, 2),
        name="attend",
    )(meta, *operands)


def bucket_rows(tiles_ref, rows_ref):
    heads, bucket_count = rows_ref.shape[:2]
    half_count = bucket_count // 2
    offset = lax.broadcasted_iota(jnp.int32, (HALF, HALF), 0) - lax.broadcasted_iota(
        jnp.int32, (HALF, HALF), 1
    )
    grids = [bucket_of(offset + shift * HALF, half_count) for shift in (-1, 0, 1)]
    first, last = slice(0, HALF), slice(HALF, TILE)

    def column_sums(values):
        return jnp.sum(values, axis=0, keepdims=True)

    def head_body(h, carry):
        before = tiles_ref[2, h, first, last] + tiles_ref[1, h, last, first]
        same = tiles_ref[2, h, first, first] + tiles_ref[2, h, last, last]
        after = tiles_ref[2, h, last, first] + tiles_ref[3, h, first, last]
        far_before = column_sums(tiles_ref[0, h, :, first] + tiles_ref[0, h, :, last])
        far_before += column_sums(tiles_ref[1, h, first, first] + tiles_ref[1, h, first, last])
        far_before += column_sums(tiles_ref[1, h, last, last])
        far_after = column_sums(tiles_ref[4, h, :, first] + tiles_ref[4, h, :, last])
        far_after += column_sums(tiles_ref[3, h, last, first] + tiles_ref[3, h, last, last])
        far_after += column_sums(tiles_ref[3, h, first, first])
        for bucket_index in range(bucket_count):
            row = column_sums(jnp.where(grids[1] == bucket_index, same, 0.0))
            if 0 < bucket_index < half_count:
                row += column_sums(jnp.where(grids[0] == bucket_index, before, 0.0))
            if bucket_index > half_count:
                row += column_sums(jnp.where(grids[2] == bucket_index, after, 0.0))
            if bucket_index == half_count - 1:
                row += far_before
            if bucket_index == bucket_count - 1:
                row += far_after
            rows_ref[h, bucket_index : bucket_index + 1, :] = row
        return carry

    lax.fori_loop(0, heads, head_body, 0)


def attend_back_kernel(
    meta_ref,
    q_ref,
    kv_ref,
    near_ref,
    weight_ref,
    exact_ref,
    log_ref,
    *refs,
):
    parts = weight_ref.shape[0]
    branch_refs = refs[:parts]
    (
        dq_ref,
        dkv_ref,
        rows_ref,
        tiles_ref,
        key_ref,
        value_ref,
        query_ref,
        grad_ref,
        dq_sum,
        dkv_sum,
        bias_ref,
    ) = refs[parts:]
    key_tiles = kv_ref.shape[0]
    heads = near_ref.shape[0]
    fill_tiles(near_ref, bias_ref)
    size = q_ref.shape[1] // heads

    row = lax.broadcasted_iota(jnp.int32, (EXTRA, TILE), 0)
    ones = jnp.where(row < 3, 1.0, 0.0).astype(BF16)

    def turn(j, carry):
        kept = meta_ref[3 + j]
        extra = key_rows(meta_ref, j)
        for h in range(heads):
            rows = kv_ref[kept, h * size : (h + 1) * size, :]
            key_ref[kept, h] = jnp.concatenate([rows, extra], axis=0).T
            rows = kv_ref[kept, (heads + h) * size : (heads + h + 1) * size, :]
            value_ref[kept, h] = jnp.concatenate([rows, ones], axis=0).T
        return carry

    lax.fori_loop(0, key_tiles, turn, 0)
    dkv_sum[...] = jnp.zeros_like(dkv_sum)
    tiles_ref[...] = jnp.zeros_like(tiles_ref)

    def query_body(i, carry):
        tile = meta_ref[3 + key_tiles + i]
        place = tile % meta_ref[0]
        begin, end = span_of(meta_ref, tile, key_tiles)
        dq_sum[...] = jnp.zeros_like(dq_sum)
        grad_sum = dot(weight_ref[0], branch_refs[0][place])
        for k in range(1, parts):
            grad_sum += dot(weight_ref[k], branch_refs[k][place])
        for h in range(heads):
            rows = slice(h * size, (h + 1) * size)
            grad = grad_sum[rows].astype(BF16)
            centre = jnp.sum(grad.astype(F32) * exact_ref[i, rows, :], axis=0, keepdims=True)
            extra = three_rows(row, split_three(-centre)).astype(BF16)
            grad_ref[h] = jnp.concatenate([grad, extra], axis=0)
            extra = query_rows(meta_ref, tile, split_three(-log_ref[i, h]))
            query_ref[h] = jnp.concatenate([q_ref[i, rows, :], extra], axis=0)

        def key_body(j, inner):
            kept = meta_ref[3 + j]
            kind = jnp.clip(j - tile, -2, 2) + 2
            probs = [
                jnp.exp2(dot(key_ref[kept, h], query_ref[h]) + bias_ref[kind, h])
                for h in range(heads)
            ]
            score_grads = [probs[h] * dot(value_ref[kept, h], grad_ref[h]) for h in range(heads)]
            low_probs = [prob.astype(BF16) for prob in probs]
            low_grads = [score_grad.astype(BF16) for score_grad in score_grads]
            key_adds, value_adds, query_adds = [], [], []
            for h in range(heads):
                rows = slice(h * size, (h + 1) * size)
                key_adds.append(dot_rows(q_ref[i, rows, :], low_grads[h]))
                value_adds.append(dot_rows(grad_ref[h, :size, :], low_probs[h]))
                query_adds.append(dot(kv_ref[kept, rows, :], low_grads[h]))
            for h in range(heads):
                rows = slice(h * size, (h + 1) * size)
                value_rows = slice((heads + h) * size, (heads + h + 1) * size)
                tiles_ref[kind, h] += score_grads[h]
                dkv_sum[kept, rows, :] += key_adds[h]
                dkv_sum[kept, value_rows, :] += value_adds[h]
                dq_sum[rows, :] += query_adds[h]
            return inner

        lax.fori_loop(begin, end, key_body, 0)
        dq_ref[i] = (dq_sum[...] * SCALE).astype(BF16)
        return carry

    lax.fori_loop(0, q_ref.shape[0], query_body, 0)
    middle = heads * size
    dkv_ref[:, :middle, :] = (dkv_sum[:, :middle, :] * (1.0 / LOG2E)).astype(BF16)
    dkv_ref[:, middle:, :] = dkv_sum[:, middle:, :].astype(BF16)
    bucket_rows(tiles_ref, rows_ref)


def attend_back(meta, queries, keys_values, near, out_blocks, exact, logs, branch, buckets):
    key_tiles = keys_values.shape[0]
    heads = near.shape[0]
    size = queries.shape[1] // heads
    shapes = (
        jax.ShapeDtypeStruct(queries.shape, BF16),
        jax.ShapeDtypeStruct(keys_values.shape, BF16),
        jax.ShapeDtypeStruct((heads, buckets, HALF), F32),
    )
    operands = (queries, keys_values, near, out_blocks, exact, logs, *branch)
    return pl.pallas_call(
        attend_back_kernel,
        grid=(1,),
        out_shape=shapes,
        in_specs=[pl.BlockSpec(memory_space=pltpu.SMEM)] + whole_specs(operands),
        out_specs=tuple(whole_specs(shapes)),
        scratch_shapes=[
            pltpu.VMEM((len(KINDS), heads, TILE, TILE), F32),
            pltpu.VMEM((key_tiles, heads, TILE, size + EXTRA), BF16),
            pltpu.VMEM((key_tiles, heads, TILE, size + EXTRA), BF16),
            pltpu.VMEM((heads, size + EXTRA, TILE), BF16),
            pltpu.VMEM((heads, size + EXTRA, TILE), BF16),
            pltpu.VMEM(queries.shape[1:], F32),
            pltpu.VMEM(keys_values.shape, F32),
            pltpu.VMEM((len(KINDS), heads, TILE, TILE), F32),
        ],
        compiler_params=pltpu.CompilerParams(vmem_limit_bytes=VMEM_BYTES),
        cost_estimate=estimate(queries, key_tiles, 5),
        name="attend_back",
    )(meta, *operands)


def project_kernel(piece_count, weight_count, tiles, share, own_ref, table_ref, *refs):
    piece_refs = refs[:piece_count]
    weight_refs = refs[piece_count : piece_count + weight_count]
    gain_ref = refs[piece_count + weight_count]
    (
        meta_ref,
        q_ref,
        kv_ref,
        normed_ref,
        input_ref,
        in_ref,
        out_ref,
        out_t_ref,
        near_ref,
        block_ref,
        turned_ref,
    ) = refs[piece_count + weight_count + 1 :]
    grid_place, tensor_place, seq_place, own_first = (own_ref[i] for i in range(4))
    width = gain_ref.shape[0]
    head_cols = q_ref.shape[1]
    columns = turned_ref.shape[0]
    for k in range(weight_count):
        place = grid_place ^ k if weight_count > 1 else 0
        block_ref[place] = weight_refs[k][...]
    full = block_ref[...].reshape(width, columns)
    in_ref[...] = full[:, : 3 * head_cols]
    turned_ref[...] = full.T
    blocks_here = width // share
    tall = block_ref.shape[1]
    per = share // tall if weight_count > 1 else 1
    for k in range(blocks_here):
        if weight_count > 1:
            block = block_ref[pl.ds((tensor_place ^ k) * per, per), :, 3 * head_cols :]
            block = block.reshape(share, head_cols)
        else:
            start = pl.multiple_of((tensor_place ^ k) * share, share)
            block = block_ref[0, pl.ds(start, share), 3 * head_cols :]
        out_ref[k] = block
        out_t_ref[k] = block.T
    key_tiles = kv_ref.shape[0]
    near_tiles(table_ref, near_ref)
    early = jnp.zeros((1, TILE), F32)
    late = jnp.zeros((1, TILE), F32)
    gain = gain_ref[...]
    for k in range(piece_count):
        for s in range(piece_refs[0].shape[0]):
            kept = s + k
            rows = piece_refs[k][s, :width, :].astype(F32)
            ids = piece_refs[k][s, width : width + 16, :][:1].astype(F32)
            early += (ids < 0.5).astype(F32)
            late += (ids < 1.5).astype(F32)
            root = lax.rsqrt(jnp.sum(rows * rows, axis=0, keepdims=True) * (1.0 / width) + EPSILON)
            normed = (rows * root * gain).astype(BF16)
            normed_ref[kept] = normed
            kv_ref[kept] = dot(turned_ref[head_cols : 3 * head_cols, :], normed).astype(BF16)
    for i in range(tiles):
        normed = normed_ref[own_first + i]
        q_ref[i] = (dot(turned_ref[:head_cols, :], normed) * (SCALE * LOG2E)).astype(BF16)
        start = pl.multiple_of(tensor_place * share, share)
        if piece_count > 1:
            input_ref[tensor_place ^ i] = piece_refs[i][0, pl.ds(start, share), :]
        else:
            input_ref[i] = piece_refs[0][own_first + i, pl.ds(start, share), :]
    meta_ref[0] = tiles
    meta_ref[1] = jnp.sum(early).astype(jnp.int32)
    meta_ref[2] = jnp.sum(late).astype(jnp.int32)
    for j in range(key_tiles):
        if piece_count > 1:
            meta_ref[3 + j] = ((j // tiles) ^ seq_place) * tiles + ((j % tiles) ^ tensor_place)
        else:
            meta_ref[3 + j] = j
    for i in range(tiles):
        shift = tensor_place ^ i if piece_count > 1 else i
        meta_ref[3 + key_tiles + i] = seq_place * tiles + shift


def project(own, table, pieces, weight_pieces, gain, tiles, key_tiles, share, heads):
    width = gain.shape[0]
    columns = weight_pieces[0].shape[1]
    head_cols = columns // 4
    parts = width // share
    shapes = (
        jax.ShapeDtypeStruct((tiles, head_cols, TILE), BF16),
        jax.ShapeDtypeStruct((key_tiles, 2 * head_cols, TILE), BF16),
        jax.ShapeDtypeStruct((key_tiles, width, TILE), BF16),
        jax.ShapeDtypeStruct((tiles, share, TILE), BF16),
        jax.ShapeDtypeStruct((width, 3 * head_cols), BF16),
        jax.ShapeDtypeStruct((parts, share, head_cols), BF16),
        jax.ShapeDtypeStruct((parts, head_cols, share), BF16),
        jax.ShapeDtypeStruct((heads, len(KINDS), HALF, HALF), F32),
    )
    operands = (*pieces, *weight_pieces, gain)
    return pl.pallas_call(
        functools.partial(project_kernel, len(pieces), len(weight_pieces), tiles, share),
        grid=(1,),
        out_shape=(jax.ShapeDtypeStruct((3 + key_tiles + tiles,), jnp.int32),) + shapes,
        in_specs=[pl.BlockSpec(memory_space=pltpu.SMEM)] * 2 + whole_specs(operands),
        out_specs=(pl.BlockSpec(memory_space=pltpu.SMEM),) + tuple(whole_specs(shapes)),
        scratch_shapes=[
            pltpu.VMEM((len(weight_pieces),) + weight_pieces[0].shape, BF16),
            pltpu.VMEM((columns, width), BF16),
        ],
        compiler_params=pltpu.CompilerParams(vmem_limit_bytes=VMEM_BYTES),
        cost_estimate=pl.CostEstimate(
            flops=6 * key_tiles * TILE * width * head_cols,
            bytes_accessed=8 * key_tiles * TILE * width,
            transcendentals=0,
        ),
        name="project",
    )(own, table, *operands)


def project_back_kernel(fast, parts, own_ref, dq_ref, dkv_ref, normed_ref, in_ref, attended_ref, *refs):
    branch_refs = refs[:parts]
    if fast:
        far_even, far_odd, own_even, own_odd, weight_even, weight_odd, gain_ref, full_ref = refs[
            parts:
        ]
    else:
        part_ref, weight_ref, gain_ref, full_ref = refs[parts:]
    grid_place, tensor_place, seq_place, own_first = (own_ref[i] for i in range(4))
    tiles, head_cols, _ = dq_ref.shape
    key_tiles = dkv_ref.shape[0]
    width = in_ref.shape[0]
    share = width // parts
    key_weight = in_ref[:, head_cols:]
    query_weight = in_ref[:, :head_cols]
    if fast:
        for n in range(tiles):
            block = dot(key_weight, dkv_ref[tiles + n]).astype(BF16)
            (far_odd if n & 1 else far_even)[n // 2] = block
        for n in range(tiles):
            block = dot(key_weight, dkv_ref[n]) + dot(query_weight, dq_ref[n])
            (own_odd if n & 1 else own_even)[n // 2] = block.astype(BF16)
    else:
        for n in range(key_tiles):
            part_ref[n] = dot(key_weight, dkv_ref[n]).astype(BF16)
        for n in range(tiles):
            block = part_ref[own_first + n].astype(F32) + dot(query_weight, dq_ref[n])
            part_ref[own_first + n] = block.astype(BF16)
    query_sum = dot_rows(normed_ref[own_first], dq_ref[0])
    for n in range(1, tiles):
        query_sum += dot_rows(normed_ref[own_first + n], dq_ref[n])
    key_sum = dot_rows(normed_ref[0], dkv_ref[0])
    for n in range(1, key_tiles):
        key_sum += dot_rows(normed_ref[n], dkv_ref[n])
    gain_ref[...] = jnp.sum(
        query_sum * query_weight.astype(F32), axis=1, keepdims=True
    ) + jnp.sum(key_sum * key_weight.astype(F32), axis=1, keepdims=True)
    full_ref[:, :head_cols] = query_sum.astype(BF16)
    full_ref[:, head_cols : 3 * head_cols] = key_sum.astype(BF16)
    for k in range(parts):
        block = dot_rows(branch_refs[k][0], attended_ref[0])
        for n in range(1, tiles):
            block += dot_rows(branch_refs[k][n], attended_ref[n])
        start = pl.multiple_of((tensor_place ^ k) * share, share)
        full_ref[pl.ds(start, share), 3 * head_cols :] = block.astype(BF16)
    if fast:
        tall = weight_even.shape[1]
        for k in range(weight_even.shape[0]):
            place = grid_place ^ (2 * k)
            weight_even[k] = full_ref[pl.ds(pl.multiple_of(place * tall, tall), tall), :]
            weight_odd[k] = full_ref[pl.ds(pl.multiple_of((place ^ 1) * tall, tall), tall), :]
    else:
        weight_ref[...] = full_ref[...]


def project_back(fast, own, dq, dkv, normed, in_flat, attended, branch, grid_count):
    tiles, head_cols, _ = dq.shape
    key_tiles = dkv.shape[0]
    width = in_flat.shape[0]
    parts = len(branch)
    columns = 4 * head_cols
    if fast:
        block = jax.ShapeDtypeStruct((parts // 2, width, TILE), BF16)
        weight = jax.ShapeDtypeStruct((grid_count // 2, width // grid_count, columns), BF16)
        shapes = (block,) * 4 + (weight,) * 2
    else:
        shapes = (
            jax.ShapeDtypeStruct((key_tiles, width, TILE), BF16),
            jax.ShapeDtypeStruct((width, columns), BF16),
        )
    shapes = shapes + (jax.ShapeDtypeStruct((width, 1), F32),)
    operands = (dq, dkv, normed, in_flat, attended, *branch)
    return pl.pallas_call(
        functools.partial(project_back_kernel, fast, parts),
        grid=(1,),
        out_shape=shapes,
        in_specs=[pl.BlockSpec(memory_space=pltpu.SMEM)] + whole_specs(operands),
        out_specs=tuple(whole_specs(shapes)),
        scratch_shapes=[pltpu.VMEM((width, columns), BF16)],
        compiler_params=pltpu.CompilerParams(vmem_limit_bytes=VMEM_BYTES),
        cost_estimate=pl.CostEstimate(
            flops=12 * key_tiles * TILE * width * head_cols,
            bytes_accessed=8 * key_tiles * TILE * width,
            transcendentals=0,
        ),
        name="project_back",
    )(own, *operands)


def finish_kernel(input_ref, gain_ref, branch_ref, result_ref, *refs):
    sum_refs = refs[:-2]
    out_ref, grad_ref = refs[-2:]
    rows = input_ref[...]
    width = rows.shape[1]
    values = rows.T
    gain = gain_ref[...]
    grad = sum_refs[0][0].astype(F32)
    for ref in sum_refs[1:]:
        grad += ref[0].astype(F32)
    root = lax.rsqrt(jnp.sum(values * values, axis=0, keepdims=True) * (1.0 / width) + EPSILON)
    scaled = grad * gain
    centre = jnp.sum(scaled * values, axis=0, keepdims=True) * (1.0 / width)
    total = root * scaled - values * (root * root * root * centre)
    grad_ref[...] = (total + branch_ref[...].astype(F32)).T
    out_ref[...] = rows + result_ref[...].astype(F32).T


def finish(block_input, gain, branch, result, sums):
    shape = jax.ShapeDtypeStruct(block_input.shape, F32)
    operands = (block_input, gain, branch, result, *sums)
    first = pl.BlockSpec((1,) + sums[0].shape[1:], functools.partial(origin, 3))
    return pl.pallas_call(
        finish_kernel,
        grid=(1,),
        out_shape=(shape, shape),
        in_specs=whole_specs(operands[:4]) + [first] * len(sums),
        out_specs=tuple(whole_specs((shape, shape))),
        compiler_params=pltpu.CompilerParams(vmem_limit_bytes=VMEM_BYTES),
        name="finish",
    )(*operands)


def split_low(values):
    high = values.astype(BF16)
    return high, (values - high.astype(F32)).astype(BF16)


def load_tile(ref, first, count, *place):
    return jnp.concatenate([ref[(first + m, *place)] for m in range(count)], axis=-1)


def expert_kernel(parts, own_ref, *refs):
    state_refs = refs[:parts]
    (grad_ref, other_ref, in_ref, in_t_ref, out_ref, gain_ref) = refs[parts : parts + 6]
    (
        kept_ref,
        sent_ref,
        normed_ref,
        act_ref,
        pre_ref,
        gate_ref,
        router_sum,
        state_ref,
        full_ref,
        back_ref,
        joint_ref,
    ) = refs[parts + 6 :]

    @pl.when(pl.program_id(0) == 0)
    def _():
        router_sum[...] = jnp.zeros_like(router_sum)

    width = gain_ref.shape[0]
    share = width // parts
    hidden = act_ref.shape[1]
    experts = router_sum.shape[0]
    expert, own = own_ref[0], own_ref[1]
    chains, columns = state_ref.shape[0], state_ref.shape[-1]
    merged = kept_ref.shape[1] // chains
    slots = columns // merged
    gain = gain_ref[...]
    for a in range(chains):
        for k in range(parts):
            state_ref[a, own ^ k] = load_tile(state_refs[k], a * merged, merged)
            near = 2 * (k // 2) + ((own & 1) ^ (k & 1))
            full_ref[a, near] = load_tile(
                other_ref if k & 1 else grad_ref, a * merged, merged, k // 2
            )
    for a in range(chains):
        state = state_ref[a].reshape(width, columns).astype(F32)
        root = lax.rsqrt(jnp.sum(state * state, axis=0, keepdims=True) * (1.0 / width) + EPSILON)
        normed = (state * root * gain).astype(BF16)
        normed_ref[a] = normed
        both = dot(in_t_ref[...], normed)
        pre_act, logits = both[:hidden], both[hidden : hidden + experts]
        act_grad = dot(out_ref[...], full_ref[a].reshape(width, columns))
        raised = jnp.exp(logits - jnp.max(logits, axis=0, keepdims=True))
        router_probs = raised / jnp.sum(raised, axis=0, keepdims=True)
        chosen = lax.broadcasted_iota(jnp.int32, logits.shape, 0) == expert
        gate = jnp.sum(jnp.where(chosen, router_probs, 0.0), axis=0, keepdims=True)
        gate_ref[a] = gate
        square = pre_act * pre_act
        cdf = 0.5 + 0.5 * jnp.tanh(pre_act * (GELU_A + (GELU_A * GELU_B) * square))
        activated = pre_act * cdf
        act_ref[a] = activated.astype(BF16)
        rise = (2.0 * GELU_A) + (6.0 * GELU_A * GELU_B) * square
        pre_grad = act_grad * (cdf + activated * (1.0 - cdf) * rise)
        low_grad = pre_grad.astype(BF16)
        pre_ref[a] = low_grad
        gate_grad = jnp.sum(activated * act_grad, axis=0, keepdims=True)
        logit_grad = gate_grad * (chosen.astype(F32) - router_probs)
        centre = jnp.sum(pre_grad * pre_act, axis=0, keepdims=True)
        centre += jnp.sum(logit_grad * logits, axis=0, keepdims=True)
        joint_ref[a, :hidden, :] = low_grad
        joint_ref[a, hidden:, :] = jnp.concatenate(split_low(logit_grad), axis=0)
        high, low = split_low(logit_grad * gate)
        router_sum[...] += dot_rows(high, normed) + dot_rows(low, normed)
        normed_grad = dot(in_ref[...], joint_ref[a])
        state = state_ref[a].reshape(width, columns).astype(F32)
        back = (root * gate) * (normed_grad * gain - state * (root * centre * (1.0 / width)))
        back_ref[a] = back.astype(BF16).reshape(parts, share, columns)
        for k in range(parts):
            block = back_ref[a, own ^ k]
            target = sent_ref if k & 1 else kept_ref
            for m in range(merged):
                target[k // 2, a * merged + m] = block[:, m * slots : (m + 1) * slots]


def result_kernel(parts, own_ref, *refs):
    out_t_ref, kept_ref, sent_ref, result_ref = refs[-4:]
    chunks = (len(refs) - 4) // 2
    own = own_ref[1]
    width = out_t_ref.shape[0]
    share = width // parts
    merged = kept_ref.shape[1]
    for c in range(chunks):
        gate, activated = refs[2 * c + 1][0], refs[2 * c][0]
        slots = activated.shape[-1] // merged
        result = dot(out_t_ref[...], activated) * gate
        result_ref[c] = result.astype(BF16).reshape(parts, share, -1)
        for k in range(parts):
            block = result_ref[c, own ^ k]
            target = sent_ref if k & 1 else kept_ref
            for m in range(merged):
                target[k // 2, m, :, c * slots : (c + 1) * slots] = block[
                    :, m * slots : (m + 1) * slots
                ]


def grads_kernel(parts, merged, own_ref, *refs):
    grad_ref, other_ref, in_ref, in_sum, out_sum, gain_sum, full_ref = refs[-7:]
    chunks = (len(refs) - 7) // 4

    @pl.when(pl.program_id(0) == 0)
    def _():
        in_sum[...] = jnp.zeros_like(in_sum)
        out_sum[...] = jnp.zeros_like(out_sum)

    own = own_ref[1]
    width = in_ref.shape[0]
    for c in range(chunks):
        normed_ref, act_ref, pre_ref, gate_ref = refs[4 * c : 4 * c + 4]
        gate = gate_ref[0]
        columns = gate.shape[-1]
        slots = columns // merged
        for k in range(parts):
            near = 2 * (k // 2) + ((own & 1) ^ (k & 1))
            source = other_ref if k & 1 else grad_ref
            full_ref[c, near] = jnp.concatenate(
                [source[m, k // 2, :, c * slots : (c + 1) * slots] for m in range(merged)], axis=-1
            )
        normed = (normed_ref[0].astype(F32) * gate).astype(BF16)
        in_sum[...] += dot_rows(normed, pre_ref[0])
        scaled = (full_ref[c].reshape(width, columns).astype(F32) * gate).astype(BF16)
        out_sum[...] += dot_rows(act_ref[0], scaled)

    @pl.when(pl.program_id(0) == pl.num_programs(0) - 1)
    def _():
        gain_sum[...] = jnp.sum(in_sum[...] * in_ref[...].astype(F32), axis=1, keepdims=True)


def fixed_spec(shape):
    return pl.BlockSpec(shape, lambda g: (0,) * len(shape))


def run_expert(own, states, grads, chunk, merged, chains, weights):
    parts = len(states)
    count, share, slots = states[0].shape
    width = share * parts
    columns = merged * slots
    steps = count // merged
    hidden = weights[2].shape[0]
    joint = weights[0].shape[1]
    experts = (joint - hidden) // 2
    half = parts // 2
    taken = merged * chains
    piece = pl.BlockSpec((taken, share, slots), lambda g: (g, 0, 0))
    grad_piece = pl.BlockSpec((taken, half, share, slots), lambda g: (g, 0, 0, chunk))
    split = pl.BlockSpec((half, taken, share, slots), lambda g: (0, g, 0, 0))
    wide = pl.BlockSpec((chains, width, columns), lambda g: (g, 0, 0))
    deep = pl.BlockSpec((chains, hidden, columns), lambda g: (g, 0, 0))
    flat = pl.BlockSpec((chains, 1, columns), lambda g: (g, 0, 0))
    return pl.pallas_call(
        functools.partial(expert_kernel, parts),
        grid=(steps // chains,),
        out_shape=(
            jax.ShapeDtypeStruct((half, count, share, slots), BF16),
            jax.ShapeDtypeStruct((half, count, share, slots), BF16),
            jax.ShapeDtypeStruct((steps, width, columns), BF16),
            jax.ShapeDtypeStruct((steps, hidden, columns), BF16),
            jax.ShapeDtypeStruct((steps, hidden, columns), BF16),
            jax.ShapeDtypeStruct((steps, 1, columns), F32),
            jax.ShapeDtypeStruct((experts, width), F32),
        ),
        in_specs=[pl.BlockSpec(memory_space=pltpu.SMEM)]
        + [piece] * parts
        + [grad_piece] * 2
        + [fixed_spec(weight.shape) for weight in weights],
        out_specs=(split, split, wide, deep, deep, flat, fixed_spec((experts, width))),
        scratch_shapes=[
            pltpu.VMEM((chains, parts, share, columns), BF16),
            pltpu.VMEM((chains, parts, share, columns), BF16),
            pltpu.VMEM((chains, parts, share, columns), BF16),
            pltpu.VMEM((chains, joint, columns), BF16),
        ],
        compiler_params=pltpu.CompilerParams(vmem_limit_bytes=VMEM_BYTES),
        cost_estimate=pl.CostEstimate(
            flops=16 * steps * columns * width * hidden,
            bytes_accessed=16 * steps * columns * width,
            transcendentals=steps * columns * hidden,
        ),
        name="expert",
    )(own, *states, *grads, *weights)


def run_result(own, saved, parts, merged, out_t):
    chunks = len(saved)
    steps, hidden, columns = saved[0][0].shape
    width = out_t.shape[0]
    share, half, slots = width // parts, parts // 2, columns // merged
    deep = pl.BlockSpec((1, hidden, columns), lambda g: (g, 0, 0))
    flat = pl.BlockSpec((1, 1, columns), lambda g: (g, 0, 0))
    split = pl.BlockSpec((half, merged, share, slots * chunks), lambda g: (0, g, 0, 0))
    total = jax.ShapeDtypeStruct((half, steps * merged, share, slots * chunks), BF16)
    return pl.pallas_call(
        functools.partial(result_kernel, parts),
        grid=(steps,),
        out_shape=(total, total),
        in_specs=[pl.BlockSpec(memory_space=pltpu.SMEM)]
        + [deep, flat] * chunks
        + [fixed_spec(out_t.shape)],
        out_specs=(split, split),
        scratch_shapes=[pltpu.VMEM((chunks, parts, share, columns), BF16)],
        compiler_params=pltpu.CompilerParams(vmem_limit_bytes=VMEM_BYTES),
        cost_estimate=pl.CostEstimate(
            flops=6 * chunks * steps * columns * width * hidden,
            bytes_accessed=6 * chunks * steps * columns * width,
            transcendentals=0,
        ),
        name="result",
    )(own, *[array for arrays in saved for array in arrays], out_t)


def run_grads(own, saved, grads, merged, weight):
    chunks = len(saved)
    steps, width, columns = saved[0][0].shape
    hidden = saved[0][1].shape[1]
    _, half, share, _ = grads[0].shape
    parts = 2 * half
    wide = pl.BlockSpec((1, width, columns), lambda g: (g, 0, 0))
    deep = pl.BlockSpec((1, hidden, columns), lambda g: (g, 0, 0))
    flat = pl.BlockSpec((1, 1, columns), lambda g: (g, 0, 0))
    grad_piece = pl.BlockSpec((merged,) + grads[0].shape[1:], lambda g: (g, 0, 0, 0))
    return pl.pallas_call(
        functools.partial(grads_kernel, parts, merged),
        grid=(steps,),
        out_shape=(
            jax.ShapeDtypeStruct((width, hidden), F32),
            jax.ShapeDtypeStruct((hidden, width), F32),
            jax.ShapeDtypeStruct((width, 1), F32),
        ),
        in_specs=[pl.BlockSpec(memory_space=pltpu.SMEM)]
        + [wide, deep, deep, flat] * chunks
        + [grad_piece] * 2
        + [fixed_spec(weight.shape)],
        out_specs=(
            fixed_spec((width, hidden)),
            fixed_spec((hidden, width)),
            fixed_spec((width, 1)),
        ),
        scratch_shapes=[pltpu.VMEM((chunks, parts, share, columns), BF16)],
        compiler_params=pltpu.CompilerParams(vmem_limit_bytes=VMEM_BYTES),
        cost_estimate=pl.CostEstimate(
            flops=8 * chunks * steps * columns * width * hidden,
            bytes_accessed=8 * chunks * steps * columns * width,
            transcendentals=0,
        ),
        name="grads",
    )(own, *[array for arrays in saved for array in arrays], *grads, weight)


def shards(
    block_input,
    attn_in_weight,
    attn_out_weight,
    position_bias,
    norm_gains,
    router_weight,
    expert_in,
    expert_out,
    segment_ids,
    expert_ids,
    out_grad,
):
    tensor_count, seq_count = lax.axis_size("tensor"), lax.axis_size("seq")
    tensor_place, seq_place = lax.axis_index("tensor"), lax.axis_index("seq")
    grid_count = lax.axis_size("dp") * seq_count
    grid_place = lax.axis_index("dp") * seq_count + seq_place
    local_count, width = block_input.shape
    group_count = local_count * tensor_count
    share = width // tensor_count
    bucket_count, heads = position_bias.shape
    head_cols = attn_in_weight.shape[2]
    experts = router_weight.shape[1]
    capacity = max(2, 2 * group_count // experts)
    tiles = group_count // TILE
    key_tiles = tiles * seq_count
    fast = seq_count == 2 and local_count == TILE and grid_count == 8

    def tiled(pieces):
        pieces = reorder(pieces, tensor_place)
        if local_count == TILE:
            return jnp.stack(pieces)
        return jnp.concatenate(pieces, axis=-1)[None]

    half = tensor_count // 2
    core = tensor_place & 1
    own_rows = jnp.concatenate(
        [
            jnp.transpose(block_input.astype(BF16)),
            jnp.pad(segment_ids.astype(BF16), ((0, 15), (0, 0))),
        ]
    )
    weight_piece = jnp.concatenate(
        [attn_in_weight[0], attn_in_weight[1], attn_in_weight[2], jnp.transpose(attn_out_weight)],
        axis=1,
    )
    grad_rows = jnp.transpose(out_grad.astype(BF16)).reshape(half, 2, share, local_count)
    grad_mine = lax.dynamic_index_in_dim(grad_rows, core, 1, keepdims=False)
    grad_theirs = lax.dynamic_index_in_dim(grad_rows, core ^ 1, 1, keepdims=False)
    in_plain, out_plain = expert_in[0], expert_out[0]
    if fast:
        far_rows = swap(own_rows, "seq", 1)
        near_two = swap(own_rows, "tensor", 2)
        columns = [weight_piece] + [swap(weight_piece, "dp", k) for k in range(1, grid_count // 2)]
        grad_other = swap(grad_theirs, "tensor", 1)
        far_rows, near_two, columns, grad_other, expert_ids, in_plain, out_plain = (
            lax.optimization_barrier(
                (
                    far_rows,
                    near_two,
                    columns,
                    grad_other,
                    expert_ids,
                    in_plain,
                    out_plain,
                )
            )
        )
        far_two = swap(far_rows, "tensor", 2)
        near_columns = swap(weight_piece, "seq", 1)
        far_columns = swap(jnp.stack(columns[1:]), "seq", 1)
        near_one, near_three = swap(own_rows, "tensor", 1), swap(near_two, "tensor", 1)
    else:
        grad_other = swap(grad_theirs, "tensor", 1)
        both_rows = lax.all_gather(own_rows, "seq", axis=0, tiled=False)
        row_pieces = gather_relative(both_rows, "tensor")
        own_first = seq_place * tiles
        row_pieces = jnp.concatenate(reorder(row_pieces, tensor_place), axis=-1)
        row_pieces = row_pieces.reshape(seq_count, -1, tiles, TILE)
        row_pieces = [jnp.moveaxis(row_pieces, 2, 1).reshape(key_tiles, -1, TILE)]
        weight_pieces = [lax.all_gather(weight_piece, ("dp", "seq"), axis=0, tiled=True)]

    in_t, out_t = jnp.transpose(in_plain), jnp.transpose(out_plain)
    router_t = jnp.transpose(router_weight)
    in_joint = jnp.concatenate([in_plain, router_weight, router_weight], axis=1)
    in_t = jnp.concatenate([in_t, router_t, router_t])
    route_all = expert_ids[:, 0]
    expert_range = jnp.arange(experts, dtype=jnp.int32)
    route_hot = (route_all[:, None] == expert_range[None, :]).astype(jnp.int32)
    slot_rank = jnp.sum(jnp.cumsum(route_hot, axis=0) * route_hot, axis=-1) - 1
    target = (route_all * capacity + slot_rank).reshape(1, tiles, TILE, 1)
    places = jnp.arange(experts * capacity, dtype=jnp.int32).reshape(experts, 1, 1, capacity)
    chunks = 2 if capacity >= TILE else 1
    slots = capacity // chunks
    spread = max(1, TILE // capacity)
    merged = max(1, TILE // (slots * spread))

    def exchange(values):
        return lax.all_to_all(values, ("dp", "seq"), split_axis=0, concat_axis=0, tiled=True)

    def joined(values):
        if spread == 1:
            return values
        shape = values.shape
        values = values.reshape((-1, spread) + shape[1:])
        return jnp.moveaxis(values, 1, -2).reshape(
            (shape[0] // spread,) + shape[1:-1] + (spread * shape[-1],)
        )

    def parted(values):
        if spread == 1:
            return values
        shape = values.shape
        values = values.reshape(shape[:-1] + (spread, shape[-1] // spread))
        return jnp.moveaxis(values, -2, 1).reshape((-1,) + shape[1:-1] + (shape[-1] // spread,))


    gain_one = norm_gains[0][:, None]
    gain_two = norm_gains[1][:, None]
    if fast:
        (
            far_two,
            far_columns,
            gain_one,
            in_t,
            in_joint,
            out_t,
            target,
            gain_two,
            grad_mine,
            grad_other,
        ) = lax.optimization_barrier(
            (
                far_two,
                far_columns,
                gain_one,
                in_t,
                in_joint,
                out_t,
                target,
                gain_two,
                grad_mine,
                grad_other,
            )
        )
        far_one, far_three = swap(far_rows, "tensor", 1), swap(far_two, "tensor", 1)
        row_pieces = [own_rows, near_one, near_two, near_three]
        row_pieces += [far_rows, far_one, far_two, far_three]
        row_pieces = [rows[None] for rows in row_pieces]
        weight_pieces = [weight_piece, near_columns]
        for k in range(1, grid_count // 2):
            weight_pieces += [columns[k], far_columns[k - 1]]
        own_first = jnp.int32(0)
    own = jnp.stack([grid_place, tensor_place, seq_place, own_first]).astype(jnp.int32)
    onehot = (target == places).astype(BF16)
    onehot_parts = [
        (target == places[..., c * slots : (c + 1) * slots]).astype(BF16) for c in range(chunks)
    ]
    onehot, onehot_parts, gain_one = lax.optimization_barrier((onehot, onehot_parts, gain_one))
    grad_pair = swap(jnp.stack([grad_mine, grad_other]), "tensor", 2)
    (
        meta,
        queries,
        keys_values,
        normed_tiles,
        input_share,
        in_flat,
        out_blocks,
        out_t_blocks,
        near,
    ) = project(
        own,
        position_bias.reshape(-1),
        row_pieces,
        weight_pieces,
        gain_one,
        tiles,
        key_tiles,
        share,
        heads,
    )
    queries, grad_pair = lax.optimization_barrier((queries, grad_pair))
    grad_here = tiled([grad_mine, grad_other, grad_pair[0], grad_pair[1]])
    grad_buffer = einsum("nkdq,enqs->ekds", grad_here, onehot).astype(BF16)
    queries, grad_buffer = lax.optimization_barrier((queries, grad_buffer))
    grad_arrived = joined(exchange(grad_buffer))
    exact, attended, logs, attn_even, attn_odd = attend(
        meta, queries, keys_values, near, out_blocks
    )
    attn_share = sum_tensor(attn_even, attn_odd)
    state_share = (input_share.astype(F32) + attn_share).astype(BF16)
    state_share, grad_arrived = lax.optimization_barrier((state_share, grad_arrived))
    grad_near = swap(grad_arrived, "tensor", 1)

    weights = (in_joint, in_t, expert_out[0], gain_two)
    grads = (grad_arrived, grad_near)
    buffers = [
        einsum("ndq,enqs->eds", state_share, onehot_parts[c]).astype(BF16)
        for c in range(chunks)
    ]
    buffers = list(lax.optimization_barrier(tuple(buffers)))
    arrivals = [joined(exchange(buffer)) for buffer in buffers]
    chains = 2 if arrivals[0].shape[0] // merged % 2 == 0 else 1
    gathered = []
    for arrival in arrivals:
        gathered.append(
            [arrival, swap(arrival, "tensor", 1), swap(arrival, "tensor", 2)]
        )
    gathered[0][0], gathered[-1][0] = lax.optimization_barrier((gathered[0][0], gathered[-1][0]))
    saved, halves, crossed = [], [], []
    small = jnp.zeros((experts, width), F32)
    for c in range(chunks):
        gathered[c].append(swap(gathered[c][2], "tensor", 1))
        kept, sent, normed_two, activated, pre_grad, gate, router_sum = run_expert(
            own, gathered[c], grads, c, merged, chains, weights
        )
        saved.append((normed_two, activated, pre_grad, gate))
        if c + 1 < chunks:
            sent, gathered[c + 1][2] = lax.optimization_barrier((sent, gathered[c + 1][2]))
        if c > 0:
            sent, crossed[c - 1] = lax.optimization_barrier((sent, crossed[c - 1]))
        stayed, got, to_send = core_step(kept, sent)
        if c + 1 == chunks:
            own_late, to_send = lax.optimization_barrier((own, to_send))
        halves.append((stayed, got))
        crossed.append(swap(to_send, "tensor", 2))
        small = small + router_sum
    returned = [
        exchange(parted(chip_step(*halves[c], crossed[c]).astype(BF16)))
        for c in range(chunks - 1)
    ]
    result_even, result_odd = run_result(
        own_late, [(arrays[1], arrays[3]) for arrays in saved], tensor_count, merged, out_t
    )
    tied = lax.optimization_barrier((result_odd, crossed[-1], *returned))
    result_odd, crossed[-1], returned = tied[0], tied[1], list(tied[2:])
    returned.append(exchange(parted(chip_step(*halves[-1], crossed[-1]).astype(BF16))))
    result_near, result_got, result_sent = core_step(result_even, result_odd)
    result_far = swap(result_sent, "tensor", 2)
    own_late, result_sent = lax.optimization_barrier((own, result_sent))
    grad_expert_in, grad_expert_out, in_gain = run_grads(
        own_late, saved, grads, merged, expert_in[0]
    )
    in_gain, returned[-1] = lax.optimization_barrier((in_gain, returned[-1]))
    gain_part = in_gain[:, 0] + jnp.sum(small * router_t.astype(F32), axis=0)
    router_gains = jnp.concatenate([small, (gain_part / norm_gains[1])[None]])
    state_grad = lax.dynamic_index_in_dim(grad_here, tensor_place // 2, 1, keepdims=False)
    state_grad = state_grad.astype(F32)
    for c in range(chunks):
        state_grad = state_grad + einsum(
            "eds,enqs->ndq", returned[c], onehot_parts[c]
        )
    state_grad = state_grad.astype(BF16)

    branch = [state_grad, swap(state_grad, "tensor", 1), swap(state_grad, "tensor", 2)]
    result_total = chip_step(result_near, result_got, result_far).astype(BF16)
    result_total, branch[2] = lax.optimization_barrier((result_total, branch[2]))
    branch.append(swap(branch[2], "tensor", 1))
    result_back = exchange(parted(result_total))
    dq, dkv, bias_rows = attend_back(
        meta, queries, keys_values, near, out_t_blocks, exact, logs, branch, bucket_count
    )
    dq, dkv, bias_rows, result_back = lax.optimization_barrier((dq, dkv, bias_rows, result_back))

    def joined_small():
        bias_padded = lax.dynamic_update_slice_in_dim(
            jnp.zeros((heads * tensor_count, bucket_count), F32),
            jnp.sum(bias_rows, axis=2),
            tensor_place * heads,
            0,
        )
        return jnp.concatenate(
            [router_gains.reshape(-1), gain_part[:, 0] / norm_gains[0], bias_padded.reshape(-1)]
        )

    def result_rows_of():
        shares = attn_share + einsum("eds,enqs->ndq", result_back, onehot)
        return jnp.moveaxis(shares.astype(BF16), 0, 1).reshape(share, tensor_count, local_count)

    if fast:
        far_even, far_odd, own_even, own_odd, weight_even, weight_odd, gain_part = project_back(
            True, own, dq, dkv, normed_tiles, in_flat, attended, branch, grid_count
        )
        far_near, far_got, far_send = core_step(far_even, far_odd)
        own_got = swap(own_odd, "tensor", 1)
        own_send = (own_even[1].astype(F32) + own_got[1].astype(F32)).astype(BF16)
        weight_sent = swap(weight_odd, "seq", 1)
        far_send, own_send, gain_part, result_back = lax.optimization_barrier(
            (far_send, own_send, gain_part, result_back)
        )
        far_sent = swap(far_send, "tensor", 2)
        small = sum_all(joined_small(), ("dp",))
        result_share = result_rows_of()
        own_send, result_share = lax.optimization_barrier((own_send, result_share))
        own_sent = swap(own_send, "tensor", 2)
        far_sent, weight_sent, small, result_share, branch = lax.optimization_barrier(
            (far_sent, weight_sent, small, result_share, branch)
        )
        far_sum = chip_step(far_near, far_got, far_sent).astype(BF16)
        sums = [own_even, own_got, own_sent[None], swap(far_sum, "seq", 1)[None]]
        weight_half = weight_even.astype(F32) + weight_sent.astype(F32)
        weight_grad = weight_half[0]
        for k in range(1, grid_count // 2):
            weight_grad = weight_grad + swap(weight_half[k].astype(BF16), "dp", k).astype(F32)
    else:
        row_part, weight_part, gain_part = project_back(
            False, own, dq, dkv, normed_tiles, in_flat, attended, branch, grid_count
        )
        row_part = lax.psum_scatter(row_part, "seq", scatter_dimension=0, tiled=True)
        row_part = jnp.moveaxis(row_part, 0, 1).reshape(width, tensor_count, local_count)
        blocks = [
            lax.dynamic_index_in_dim(row_part, tensor_place ^ k, 1, keepdims=False)
            for k in range(tensor_count)
        ]
        sums = [sum_tensor(jnp.stack(blocks[0::2]), jnp.stack(blocks[1::2]))[None]]
        small = sum_all(joined_small(), ("dp",))
        result_share = result_rows_of()
        weight_grad = lax.psum_scatter(
            weight_part, ("dp", "seq"), scatter_dimension=0, tiled=True
        ).astype(F32)
    grad_attn_in = jnp.stack(
        [weight_grad[:, c * head_cols : (c + 1) * head_cols] for c in range(3)]
    )
    grad_attn_out = jnp.transpose(weight_grad[:, 3 * head_cols :])

    small = sum_all(small, ("seq", "tensor"))
    first, second = experts * width, (experts + 1) * width
    grad_router = jnp.transpose(small[:first].reshape(experts, width))
    grad_gains = jnp.stack([small[second : second + width], small[first:second]])
    bias_sum = small[second + width :].reshape(heads * tensor_count, bucket_count)
    grad_bias = jnp.transpose(lax.dynamic_slice_in_dim(bias_sum, tensor_place * heads, heads, 0))

    result_rows = lax.all_to_all(
        jnp.moveaxis(result_share, 1, 0), "tensor", split_axis=0, concat_axis=0, tiled=True
    ).reshape(width, local_count)
    if local_count == TILE:
        own_branch = [
            lax.dynamic_index_in_dim(piece, tensor_place, 0, keepdims=False) for piece in branch
        ]
    else:
        own_branch = [
            lax.dynamic_slice_in_dim(piece[0], tensor_place * local_count, local_count, 1)
            for piece in branch
        ]
    own_branch = jnp.concatenate(reorder(own_branch, tensor_place))
    block_out, input_grad = finish(block_input, gain_one, own_branch, result_rows, sums)
    return (
        block_out,
        input_grad,
        grad_attn_in,
        grad_attn_out,
        grad_bias,
        grad_gains,
        grad_router,
        grad_expert_in[None],
        grad_expert_out[None],
    )


def solution(mesh):
    return jax.shard_map(
        shards,
        mesh=mesh,
        in_specs=(
            P(("dp", "seq", "tensor"), None),
            P(None, ("dp", "seq"), "tensor"),
            P("tensor", ("dp", "seq")),
            P(None, "tensor"),
            P(),
            P(),
            P(("dp", "seq"), None, "tensor"),
            P(("dp", "seq"), "tensor", None),
            P("dp", ("seq", "tensor")),
            P(("dp", "seq"), None),
            P(("dp", "seq", "tensor"), None),
        ),
        out_specs=(
            P(("dp", "seq", "tensor"), None),
            P(("dp", "seq", "tensor"), None),
            P(None, ("dp", "seq"), "tensor"),
            P("tensor", ("dp", "seq")),
            P(None, "tensor"),
            P(),
            P(),
            P(("dp", "seq"), None, "tensor"),
            P(("dp", "seq"), "tensor", None),
        ),
        check_vma=False,
    )
```
